32 devices in a mesh: row: 16 (over z, y, x), col: 2 (over core).
Axes of the slice: x: 2, y: 2, z: 4, core: 2. Of those that a mesh axis runs over, the one named last changes fastest.
Arguments:
- tokens: bfloat16 [2, 2048, 2048], P(None, 'row'), may hold values from -6 to 6
- cotangent: bfloat16 [2, 2048, 2048], P(None, 'row'), may hold values from -6 to 6
- deal_order: int32 [2, 2048], P(None, 'row'), may hold values from 0 to 2047, as said below
- seq_lengths: int32 [2, 16, 3], P(None, 'row'), may hold values from 1 to 96, 128 in all within a row
- mixer_norm_gain: float32 [2048], replicated, may hold values from 0.5 to 1.5
- mamba_gate_weight: bfloat16 [2048, 3072], P('row', 'col'), may hold values from -0.125 to 0.125
- mamba_input_weight: bfloat16 [2048, 3072], P('row', 'col'), may hold values from -0.125 to 0.125
- state_weight: bfloat16 [2048, 512], P('row'), may hold values from -0.125 to 0.125
- step_weight: bfloat16 [2048, 48], P('row', 'col'), may hold values from -0.0625 to 0.0625
- conv_input: float32 [4, 3072], P(None, 'col'), may hold values from -3 to 3
- conv_input_bias: float32 [3072], P('col'), may hold values from -2 to 2
- conv_state: float32 [4, 512], replicated, may hold values from -3 to 3
- conv_state_bias: float32 [512], replicated, may hold values from -2 to 2
- step_bias: float32 [48], P('col'), may hold values from -4.5 to -2
- decay_log: float32 [48], P('col'), may hold values from -3 to 1
- skip_scale: float32 [48], P('col'), may hold values from 0.5 to 1.5
- mamba_out_weight: bfloat16 [3072, 2048], P('col', 'row'), may hold values from -0.109375 to 0.109375
- query_weight: bfloat16 [2048, 1024], P('row', 'col'), may hold values from -0.125 to 0.125
- key_weight: bfloat16 [2048, 256], P('row', 'col'), may hold values from -0.125 to 0.125
- value_weight: bfloat16 [2048, 256], P('row', 'col'), may hold values from -0.125 to 0.125
- attn_out_weight: bfloat16 [1024, 2048], P('col', 'row'), may hold values from -0.5 to 0.5
- ff_norm_gain: float32 [2048], replicated, may hold values from 0.5 to 1.5
- gate_weight: bfloat16 [2048, 4096], P('row', 'col'), may hold values from -0.125 to 0.125
- up_weight: bfloat16 [2048, 4096], P('row', 'col'), may hold values from -0.125 to 0.125
- down_weight: bfloat16 [4096, 2048], P('col', 'row'), may hold values from -0.09375 to 0.09375
Outputs:
- output: bfloat16 [2, 2048, 2048], P(None, 'row')
- grad_tokens: bfloat16 [2, 2048, 2048], P(None, 'row')
- grad_mixer_norm_gain: float32 [2048], replicated
- grad_mamba_gate_weight: float32 [2048, 3072], P('row', 'col')
- grad_mamba_input_weight: float32 [2048, 3072], P('row', 'col')
- grad_state_weight: float32 [2048, 512], P('row')
- grad_step_weight: float32 [2048, 48], P('row', 'col')
- grad_conv_input: float32 [4, 3072], P(None, 'col')
- grad_conv_input_bias: float32 [3072], P('col')
- grad_conv_state: float32 [4, 512], replicated
- grad_conv_state_bias: float32 [512], replicated
- grad_step_bias: float32 [48], P('col')
- grad_decay_log: float32 [48], P('col')
- grad_skip_scale: float32 [48], P('col')
- grad_mamba_out_weight: float32 [3072, 2048], P('col', 'row')
- grad_query_weight: float32 [2048, 1024], P('row', 'col')
- grad_key_weight: float32 [2048, 256], P('row', 'col')
- grad_value_weight: float32 [2048, 256], P('row', 'col')
- grad_attn_out_weight: float32 [1024, 2048], P('col', 'row')
- grad_ff_norm_gain: float32 [2048], replicated
- grad_gate_weight: float32 [2048, 4096], P('row', 'col')
- grad_up_weight: float32 [2048, 4096], P('row', 'col')
- grad_down_weight: float32 [4096, 2048], P('col', 'row')
The draws below stay inside these ranges and needn't reach their ends.
Inputs may be any that keep to these rules, and one draw needn't show every extreme that they name: For each micro-batch, deal_order names every token of it once; the slots of each device take exactly 8 tokens from the rows of each device. `seq_lengths`: the 3 lengths of one device and micro-batch sum to 128.
All inputs are finite; a program needn't handle non-finite values.
Results may differ from the reference program's by a relative error of at most 0.018.
Values may be sent and summed in bfloat16 or wider, within the bound.
A program may use at most 320 MiB of HBM per device.

```python
import math
import jax
import jax.numpy as jnp
import numpy as np
from jax import lax

D = 2048
MH = 48
NS = 256
AH = 8
AK = 2
HD = 128
FF = 4096
KW = 4
MB = 2
SEGS = 3
TOK_MB = 128
DI = 3072
LONGEST = 96
TOKM = 2048
N_ROW = 16


def draw_deal_order(key, part):
    per_peer = TOK_MB // N_ROW

    def one_batch(batch_key):
        pick_key, place_key = jax.random.split(batch_key)
        picks = jax.vmap(lambda inner_key: jax.random.permutation(inner_key, TOK_MB))(jax.random.split(pick_key, N_ROW))
        chosen = picks.astype(jnp.int32).reshape(N_ROW, N_ROW, per_peer)
        sources = jnp.arange(N_ROW, dtype=jnp.int32)[:, None, None] * TOK_MB + chosen
        sources = jnp.transpose(sources, (1, 0, 2)).reshape(N_ROW, TOK_MB)
        places = jax.vmap(lambda inner_key: jax.random.permutation(inner_key, TOK_MB))(jax.random.split(place_key, N_ROW))
        slots = jax.vmap(lambda source_row, place_row: jnp.zeros((TOK_MB,), jnp.int32).at[place_row].set(source_row))(sources, places.astype(jnp.int32))
        return slots.reshape(N_ROW * TOK_MB)
    return jax.vmap(one_batch)(jax.random.split(key, MB))


def steps_of(rng, dims, cuts, smallest, largest):
    def one(dim, parts):
        heights = jax.random.uniform(jax.random.fold_in(jax.random.fold_in(rng, 6), dim), (parts,), jnp.float32, smallest / len(cuts), largest / len(cuts))
        return jnp.repeat(jnp.exp(heights), dims[dim] // parts).reshape((-1,) + (1,) * (len(dims) - dim - 1))

    gain = one(*cuts[0])
    for cut in cuts[1:]:
        gain = gain * one(*cut)
    return gain


def length_profile(count, total, most, lean):
    loads = [(1 << 20) // math.isqrt(rank ** lean) + 1 for rank in range(2, count + 1)]
    surplus, counts = total - most - (count - 1), [1] * (count - 1)
    while surplus > 0:
        free = [i for i in range(count - 1) if counts[i] < most]
        mass, left = sum([loads[i] for i in free]), surplus
        for i in free:
            extra = min(most - counts[i], max(1, left * loads[i] // mass), surplus)
            counts[i] = counts[i] + extra
            surplus = surplus - extra
    return np.array([most] + counts)


def uneven_parts(rng, count, total, limit, slope):
    if count == 2:
        one = jax.random.randint(rng, (), max(1, total - limit), min(limit, total - 1) + 1)
        return jnp.stack([one, total - one])
    tallies = jnp.asarray(length_profile(count, total, limit, slope), jnp.int32)
    pairs = (count - 1) // 2
    giver, sink = tallies[1:1 + 2 * pairs:2], tallies[2:2 + 2 * pairs:2]
    slack = jnp.minimum(giver - 1, limit - sink)
    moved = jax.random.randint(jax.random.fold_in(rng, 1), (pairs,), 0, 1 << 20) % (slack + 1)
    tallies = tallies.at[1:1 + 2 * pairs:2].set(giver - moved).at[2:2 + 2 * pairs:2].set(sink + moved)
    return tallies[jax.random.permutation(jax.random.fold_in(rng, 2), count)]


def centred(key, dims, width, limit, cuts=(), held_as=jnp.bfloat16):
    array = width * jax.random.normal(key, dims, jnp.float32)
    if cuts:
        array = array * steps_of(key, dims, cuts, -0.22, 0.18)
    return jnp.clip(array, -limit, limit).astype(held_as)


def setup_inputs(seed: int = 0) -> dict:
    arg_keys = jax.random.split(jax.random.key(seed), 26)
    return {
        "tokens": centred(arg_keys[0], (MB, TOKM, D), 1.0, 6.0, ((1, 16),)),
        "cotangent": centred(arg_keys[1], (MB, TOKM, D), 1.0, 6.0, ((1, 16),)),
        "deal_order": draw_deal_order(jax.random.fold_in(arg_keys[25], 71), 0),
        "seq_lengths": jax.vmap(lambda own: uneven_parts(own, SEGS, TOK_MB, LONGEST, 1))(jax.random.split(arg_keys[3], MB * N_ROW)).reshape((MB, N_ROW, SEGS)).astype(jnp.int32),
        "mixer_norm_gain": jnp.clip(1.0 + 0.1 * jax.random.normal(arg_keys[4], (D,), jnp.float32), 0.5, 1.5),
        "mamba_gate_weight": centred(arg_keys[5], (D, DI), D ** -0.5, 0.125, ((0, 16), (1, 2))),
        "mamba_input_weight": centred(arg_keys[6], (D, DI), D ** -0.5, 0.125, ((0, 16), (1, 2))),
        "state_weight": centred(arg_keys[7], (D, 2 * NS), D ** -0.5, 0.125, ((0, 16),)),
        "step_weight": centred(arg_keys[8], (D, MH), (4 * D) ** -0.5, 0.0625, ((0, 16), (1, 2))),
        "conv_input": centred(arg_keys[9], (KW, DI), 0.5, 3.0, ((1, 2),), jnp.float32),
        "conv_input_bias": centred(arg_keys[10], (DI,), 0.3, 2.0, ((0, 2),), jnp.float32),
        "conv_state": centred(arg_keys[11], (KW, 2 * NS), 0.5, 3.0, (), jnp.float32),
        "conv_state_bias": centred(arg_keys[12], (2 * NS,), 0.3, 2.0, (), jnp.float32),
        "step_bias": jnp.clip(-4.5 + 2.5 * jax.random.uniform(arg_keys[13], (MH,), jnp.float32) ** steps_of(arg_keys[13], (MH,), ((0, 2),), -0.2, 0.2), -4.5, -2.0),
        "decay_log": jnp.clip(-3.0 + 4.0 * jax.random.uniform(arg_keys[14], (MH,), jnp.float32) ** steps_of(arg_keys[14], (MH,), ((0, 2),), -0.2, 0.2), -3.0, 1.0),
        "skip_scale": jnp.clip(0.5 + 1.0 * jax.random.uniform(arg_keys[15], (MH,), jnp.float32) ** steps_of(arg_keys[15], (MH,), ((0, 2),), -0.2, 0.2), 0.5, 1.5),
        "mamba_out_weight": centred(arg_keys[16], (DI, D), DI ** -0.5, 0.109375, ((0, 2), (1, 16))),
        "query_weight": centred(arg_keys[17], (D, AH * HD), D ** -0.5, 0.125, ((0, 16), (1, 2))),
        "key_weight": centred(arg_keys[18], (D, AK * HD), D ** -0.5, 0.125, ((0, 16), (1, 2))),
        "value_weight": centred(arg_keys[19], (D, AK * HD), D ** -0.5, 0.125, ((0, 16), (1, 2))),
        "attn_out_weight": centred(arg_keys[20], (AH * HD, D), (AH * HD // 8) ** -0.5, 0.5, ((0, 2), (1, 16))),
        "ff_norm_gain": jnp.clip(1.0 + 0.1 * jax.random.normal(arg_keys[21], (D,), jnp.float32), 0.5, 1.5),
        "gate_weight": centred(arg_keys[22], (D, FF), D ** -0.5, 0.125, ((0, 16), (1, 2))),
        "up_weight": centred(arg_keys[23], (D, FF), D ** -0.5, 0.125, ((0, 16), (1, 2))),
        "down_weight": centred(arg_keys[24], (FF, D), FF ** -0.5, 0.09375, ((0, 2), (1, 16))),
    }


EPS = 1e-05
NEG_LARGE = -1e+30
ROPE_BASE = 100000000000.0
HIGH = lax.Precision.HIGHEST

@jax.custom_vjp
def low(v):
    return lax.optimization_barrier(v.astype(jnp.bfloat16)).astype(jnp.float32)

@jax.custom_vjp
def low_back(v):
    return v

def low_keep(v):
    return (low(v), None)

def low_pass(kept, grad):
    return (grad,)

def back_keep(v):
    return (v, None)

def back_low(kept, grad):
    return (low(grad),)
low.defvjp(low_keep, low_pass)
low_back.defvjp(back_keep, back_low)

def matmul(first_op, second_op):
    return jnp.dot(first_op, second_op, precision=HIGH, preferred_element_type=jnp.float32)

def rms_scale(values, gain_vec):
    return values * lax.rsqrt(lax.optimization_barrier(jnp.mean(values * values, axis=-1, keepdims=True)) + EPS) * gain_vec

def layout(lengths, slot_count):
    seg_ends = jnp.cumsum(lengths).astype(jnp.int32)
    starts = (seg_ends - lengths).astype(jnp.int32)
    places = jnp.arange(slot_count, dtype=jnp.int32)
    segment = lax.optimization_barrier(jnp.sum((places[:, None] >= seg_ends[None, :]).astype(jnp.int32), axis=1)).astype(jnp.int32)
    member = segment[:, None] == jnp.arange(lengths.shape[0], dtype=jnp.int32)[None, :]
    within = places - lax.optimization_barrier(jnp.sum(jnp.where(member, starts[None, :], 0), axis=1)).astype(jnp.int32)
    allowed = (segment[:, None] == segment[None, :]) & (places[:, None] >= places[None, :])
    return (segment, within, allowed)

def causal_conv(values_in, kernel, bias_vec, segment):
    slot_count, channels = values_in.shape
    kernel_len = kernel.shape[0]
    summed = bias_vec[None, :] + kernel[kernel_len - 1][None, :] * values_in
    for shift_by in range(1, kernel_len):
        shifted = jnp.concatenate([jnp.zeros((shift_by, channels), values_in.dtype), values_in[:slot_count - shift_by]], axis=0)
        earlier = jnp.concatenate([jnp.full((shift_by,), -1, jnp.int32), segment[:slot_count - shift_by]], axis=0)
        shifted = jnp.where((earlier == segment)[:, None], shifted, 0.0)
        summed = summed + kernel[kernel_len - 1 - shift_by][None, :] * shifted
    return jax.nn.silu(summed)

def decay_mix(intersection, step_raw, step_bias, decay_log, allowed):
    step_size = jax.nn.softplus(step_raw + step_bias[None, :])
    rates = -jnp.exp(decay_log)
    levels = jnp.cumsum(step_size * rates[None, :], axis=0).T
    spread = levels[:, :, None] - levels[:, None, :]
    decays = jnp.where(allowed[None], jnp.exp(jnp.where(allowed[None], spread, 0.0)), 0.0)
    return intersection[None] * decays * step_size.T[:, None, :]

def gate_mix(scanned, conv_out, mamba_gate, skip_scale):
    slot_count, channels = conv_out.shape
    per_head = channels // skip_scale.shape[0]
    mixed_out = scanned.reshape(slot_count, channels) + conv_out * jnp.repeat(skip_scale, per_head)[None, :]
    return mixed_out * jax.nn.silu(mamba_gate)

def rotary(vectors, within, heads):
    slot_count = vectors.shape[0]
    head_dim = vectors.shape[1] // heads
    half_dim = head_dim // 2
    inverse = ROPE_BASE ** (-2.0 * jnp.arange(half_dim, dtype=jnp.float32) / head_dim)
    angles = within.astype(jnp.float32)[:, None] * inverse[None, :]
    cosine = jnp.concatenate([jnp.cos(angles), jnp.cos(angles)], axis=1)[:, None, :]
    sine = jnp.concatenate([jnp.sin(angles), jnp.sin(angles)], axis=1)[:, None, :]
    shaped = vectors.reshape(slot_count, heads, head_dim)
    turned = jnp.concatenate([-shaped[..., half_dim:], shaped[..., :half_dim]], axis=-1)
    return (shaped * cosine + turned * sine).reshape(slot_count, heads * head_dim)

def swiglu(ff_gate, ff_up):
    return jax.nn.silu(ff_gate) * ff_up

def layer_block(params, block_tokens, lengths):
    mixer_norm_gain, mamba_gate_weight, mamba_input_weight, state_weight, step_weight, conv_input, conv_input_bias, conv_state, conv_state_bias, step_bias, decay_log, skip_scale, mamba_out_weight, query_weight, key_weight, value_weight, attn_out_weight, ff_norm_gain, gate_weight, up_weight, down_weight = params
    slot_count = block_tokens.shape[0]
    segment, within, allowed = layout(lengths, slot_count)
    normed_one = low(rms_scale(block_tokens, mixer_norm_gain))
    mamba_gate = low_back(matmul(normed_one, mamba_gate_weight))
    conv_in = low_back(matmul(normed_one, mamba_input_weight))
    state_raw = low_back(matmul(normed_one, state_weight))
    step_raw = low_back(matmul(normed_one, step_weight))
    conv_out = causal_conv(conv_in, conv_input, conv_input_bias, segment)
    state_act = causal_conv(state_raw, conv_state, conv_state_bias, segment)
    state_dim = state_act.shape[1] // 2
    state_in = low(state_act[:, :state_dim])
    state_out = low(state_act[:, state_dim:])
    intersection = low_back(matmul(state_out, state_in.T))
    mixing = decay_mix(intersection, step_raw, step_bias, decay_log, allowed)
    heads = step_raw.shape[1]
    conv_heads = low(conv_out).reshape(slot_count, heads, -1)
    scanned = low_back(jnp.einsum('hij,jhp->ihp', low(mixing), conv_heads, precision=HIGH))
    gated = gate_mix(scanned, conv_out, mamba_gate, skip_scale)
    mamba_part = low_back(matmul(low(gated), mamba_out_weight))
    queries = low_back(matmul(normed_one, query_weight))
    keys_raw = low_back(matmul(normed_one, key_weight))
    values_raw = low_back(matmul(normed_one, value_weight))
    q_heads = queries.shape[1] // HD
    kv_heads = keys_raw.shape[1] // HD
    group_size = q_heads // kv_heads
    query_rot = low(rotary(queries, within, q_heads)).reshape(slot_count, kv_heads, group_size, HD)
    key_rot = low(rotary(keys_raw, within, kv_heads)).reshape(slot_count, kv_heads, HD)
    value_low = low(values_raw).reshape(slot_count, kv_heads, HD)
    raw_scores = low_back(jnp.einsum('ikrd,jkd->krij', query_rot, key_rot, precision=HIGH))
    scores = jnp.where(allowed[None, None], raw_scores * HD ** (-0.5), NEG_LARGE)
    peaks = lax.optimization_barrier(jnp.max(scores, axis=-1, keepdims=True))
    exp_terms = jnp.exp(scores - peaks)
    attn_probs = exp_terms / lax.optimization_barrier(jnp.sum(exp_terms, axis=-1, keepdims=True))
    attended = low_back(jnp.einsum('krij,jkd->ikrd', low(attn_probs), value_low, precision=HIGH)).reshape(slot_count, -1)
    attn_part = low_back(matmul(low(attended), attn_out_weight))
    hidden_mid = block_tokens + mamba_part + attn_part
    normed_two = low(rms_scale(hidden_mid, ff_norm_gain))
    ff_gate = low_back(matmul(normed_two, gate_weight))
    ff_up = low_back(matmul(normed_two, up_weight))
    ff_hidden = low(swiglu(ff_gate, ff_up))
    return hidden_mid + low_back(matmul(ff_hidden, down_weight))

def reference(tokens, cotangent, deal_order, seq_lengths, mixer_norm_gain, mamba_gate_weight, mamba_input_weight, state_weight, step_weight, conv_input, conv_input_bias, conv_state, conv_state_bias, step_bias, decay_log, skip_scale, mamba_out_weight, query_weight, key_weight, value_weight, attn_out_weight, ff_norm_gain, gate_weight, up_weight, down_weight):
    params = (mixer_norm_gain.astype(jnp.float32), mamba_gate_weight.astype(jnp.float32), mamba_input_weight.astype(jnp.float32), state_weight.astype(jnp.float32), step_weight.astype(jnp.float32), conv_input.astype(jnp.float32), conv_input_bias.astype(jnp.float32), conv_state.astype(jnp.float32), conv_state_bias.astype(jnp.float32), step_bias.astype(jnp.float32), decay_log.astype(jnp.float32), skip_scale.astype(jnp.float32), mamba_out_weight.astype(jnp.float32), query_weight.astype(jnp.float32), key_weight.astype(jnp.float32), value_weight.astype(jnp.float32), attn_out_weight.astype(jnp.float32), ff_norm_gain.astype(jnp.float32), gate_weight.astype(jnp.float32), up_weight.astype(jnp.float32), down_weight.astype(jnp.float32))

    def forward(token_values, layer_params):
        dealt = jax.vmap(lambda rows_in, picked: rows_in[picked])(token_values, deal_order)
        blocks = dealt.reshape(MB * N_ROW, TOK_MB, D)
        lengths_all = seq_lengths.reshape(MB * N_ROW, SEGS)
        checked = jax.checkpoint(layer_block)

        def advance(state_carry, inputs_pair):
            return (state_carry, checked(layer_params, inputs_pair[0], inputs_pair[1]))
        unused_carry, outputs = lax.scan(advance, jnp.zeros((), jnp.float32), (blocks, lengths_all))
        outputs = outputs.reshape(MB, N_ROW * TOK_MB, D)
        return jax.vmap(lambda placed, picked: jnp.zeros_like(placed).at[picked].set(placed))(outputs, deal_order)
    result, pullback = jax.vjp(forward, tokens.astype(jnp.float32), params)
    grad_input, grad_params = pullback(cotangent.astype(jnp.float32))
    grad_mixer_norm_gain, grad_mamba_gate_weight, grad_mamba_input_weight, grad_state_weight, grad_step_weight, grad_conv_input, grad_conv_input_bias, grad_conv_state, grad_conv_state_bias, grad_step_bias, grad_decay_log, grad_skip_scale, grad_mamba_out_weight, grad_query_weight, grad_key_weight, grad_value_weight, grad_attn_out_weight, grad_ff_norm_gain, grad_gate_weight, grad_up_weight, grad_down_weight = grad_params
    return (result.astype(jnp.bfloat16), grad_input.astype(jnp.bfloat16), grad_mixer_norm_gain, grad_mamba_gate_weight, grad_mamba_input_weight, grad_state_weight, grad_step_weight, grad_conv_input, grad_conv_input_bias, grad_conv_state, grad_conv_state_bias, grad_step_bias, grad_decay_log, grad_skip_scale, grad_mamba_out_weight, grad_query_weight, grad_key_weight, grad_value_weight, grad_attn_out_weight, grad_ff_norm_gain, grad_gate_weight, grad_up_weight, grad_down_weight)
```

```python
from functools import partial

import jax
import jax.numpy as jnp
from jax import lax
from jax.experimental import pallas as pl
from jax.experimental.pallas import tpu as pltpu
from jax.sharding import PartitionSpec as P

HD = 128
TP = 4
GROUP = 2 * TP
CHUNK = 16
EPS = 1e-05
NEG_LARGE = -1e30
ROPE_BASE = 100000000000.0
MESH = pl.DeviceIdType.MESH
HIGH = lax.Precision.HIGHEST
VMEM = pltpu.VMEM
ANY = pl.ANY


def matmul(first_op, second_op):
    return jnp.dot(first_op, second_op, preferred_element_type=jnp.float32)


def matmul_trans(first_op, second_op):
    return lax.dot_general(
        first_op, second_op, (((1,), (1,)), ((), ())), preferred_element_type=jnp.float32
    )


def matmul_left(first_op, second_op):
    return lax.dot_general(
        first_op, second_op, (((0,), (0,)), ((), ())), preferred_element_type=jnp.float32
    )


def place():
    r = lax.axis_index("row")
    c = lax.axis_index("col")
    t = lax.rem(r, TP)
    return r, c, r - t, t


def partner(t, m):
    if m == 0:
        return t
    if m == 1:
        return t + 1 - 2 * lax.rem(t, 2)
    if m == 2:
        return lax.rem(t + 2, TP)
    return TP - 1 - t


def remote(src, dst, send, recv, row, col):
    return pltpu.make_async_remote_copy(
        src_ref=src, dst_ref=dst, send_sem=send, recv_sem=recv, device_id=(row, col), device_id_type=MESH
    )


def greet_group(cross=False):
    r, c, base, t = place()
    barrier = pltpu.get_barrier_semaphore()
    pl.semaphore_signal(barrier, inc=1, device_id=(r, 1 - c), device_id_type=MESH)
    count = 1
    for m in (1, 2, 3):
        pl.semaphore_signal(barrier, inc=1, device_id=(base + partner(t, m), c), device_id_type=MESH)
        count += 1
        if cross:
            pl.semaphore_signal(
                barrier, inc=1, device_id=(base + partner(t, m), 1 - c), device_id_type=MESH
            )
            count += 1
    pl.semaphore_wait(barrier, count)


def gather_start(src, out, send, recv, here):
    r, c, base, t = place()
    mine = out.at[t * 2 + c]
    local = pltpu.make_async_copy(src, mine, here)
    peers = [
        remote(src, mine, send.at[m], recv.at[m], base + partner(t, m), c) for m in (1, 2, 3)
    ]
    sibling = remote(src, mine, send.at[0], recv.at[0], r, 1 - c)
    for copy in (peers[2], peers[0], peers[1], sibling, local):
        copy.start()
    return peers, sibling, local


def gather_finish(started, out, send, recv):
    r, c, base, t = place()
    peers, sibling, local = started
    forwards = []
    for m in (1, 2, 3):
        peers[m - 1].wait_recv()
        block = out.at[partner(t, m) * 2 + c]
        forward = remote(block, block, send.at[3 + m], recv.at[3 + m], r, 1 - c)
        forward.start()
        forwards.append(forward)
    local.wait()
    sibling.wait()
    for copy in peers:
        copy.wait_send()
    for copy in forwards:
        copy.wait()


ROWS = 16


def by_rows(count, body):
    def step(i, carry):
        body(pl.ds(pl.multiple_of(i * ROWS, ROWS), ROWS))
        return carry

    lax.fori_loop(0, count // ROWS, step, 0)


def scatter_sum(parts, near, out2, far, s1, r1, s2, r2, total):
    r, c, base, t = place()
    order = (3, 1, 2, 0)
    first = {}
    for m in order:
        first[m] = remote(
            parts.at[partner(t, m) * 2 + 1 - c], near.at[m], s1.at[m], r1.at[m], r, 1 - c
        )
        first[m].start()
    second = {}
    for m in order[:3]:
        first[m].wait_recv()
        block = partner(t, m) * 2 + c

        def add(rows, m=m, block=block):
            out2[m - 1, rows, :] = (
                parts[block, rows, :].astype(jnp.float32) + near[m, rows, :].astype(jnp.float32)
            ).astype(jnp.bfloat16)

        by_rows(total.shape[0], add)
        second[m] = remote(
            out2.at[m - 1], far.at[m - 1], s2.at[m - 1], r2.at[m - 1], base + partner(t, m), c
        )
        second[m].start()
    first[0].wait_recv()
    own = t * 2 + c
    for m in (1, 2, 3):
        second[m].wait_recv()

    def fold(rows):
        total[rows, :] = (
            parts[own, rows, :].astype(jnp.float32)
            + near[0, rows, :].astype(jnp.float32)
            + far[0, rows, :].astype(jnp.float32)
            + far[1, rows, :].astype(jnp.float32)
            + far[2, rows, :].astype(jnp.float32)
        )

    by_rows(total.shape[0], fold)
    for m in order:
        first[m].wait_send()
    for m in (1, 2, 3):
        second[m].wait_send()


def scatter_scratch(slots, width):
    return [
        VMEM((TP, slots, width), jnp.bfloat16),
        VMEM((TP - 1, slots, width), jnp.bfloat16),
        VMEM((TP - 1, slots, width), jnp.bfloat16),
        pltpu.SemaphoreType.DMA((TP,)),
        pltpu.SemaphoreType.DMA((TP,)),
        pltpu.SemaphoreType.DMA((TP - 1,)),
        pltpu.SemaphoreType.DMA((TP - 1,)),
    ]


def gather_scratch():
    return [
        pltpu.SemaphoreType.DMA((7,)),
        pltpu.SemaphoreType.DMA((7,)),
        pltpu.SemaphoreType.DMA,
    ]


def exchange_rows(buf, land, send, recv):
    r, c, base, t = place()
    n_row = lax.axis_size("row")

    def copy(other):
        return remote(
            buf.at[other], land.at[r], send.at[other], recv.at[r], other, c
        )

    def start(off, carry):
        copy(lax.rem(r + off, n_row)).start()
        return carry

    lax.fori_loop(1, n_row, start, 0)


def finish_rows(buf, land, send, recv):
    r, c, base, t = place()
    n_row = lax.axis_size("row")

    def finish(off, carry):
        other = lax.rem(r + off, n_row)
        copy = remote(buf.at[other], land.at[other], send.at[other], recv.at[other], other, c)
        copy.wait_send()
        copy.wait_recv()
        return carry

    lax.fori_loop(1, n_row, finish, 0)


def greet_rows():
    r, c, base, t = place()
    n_row = lax.axis_size("row")
    barrier = pltpu.get_barrier_semaphore()

    def greet(off, carry):
        pl.semaphore_signal(
            barrier, inc=1, device_id=(lax.rem(r + off, n_row), c), device_id_type=MESH
        )
        return carry

    lax.fori_loop(1, n_row, greet, 0)
    pl.semaphore_signal(barrier, inc=1, device_id=(r, 1 - c), device_id_type=MESH)
    pl.semaphore_wait(barrier, n_row)


COLS = 512


def permute_out(choice, buf, first, second, slots):
    n_row = buf.shape[0]

    def column(i, carry):
        cols = pl.ds(pl.multiple_of(i * COLS, COLS), COLS)
        picked = matmul(choice[:, :slots], first[:, cols]) + matmul(choice[:, slots:], second[:, cols])
        buf[:, :, cols] = picked.astype(jnp.bfloat16).reshape(n_row, CHUNK, COLS)
        return carry

    lax.fori_loop(0, buf.shape[2] // COLS, column, 0)


def permute_in(choice, land, first, second, slots):
    n_row = land.shape[0]

    def column(i, carry):
        cols = pl.ds(pl.multiple_of(i * COLS, COLS), COLS)
        got = land[:, :, cols].reshape(n_row * CHUNK, COLS)
        first[:, cols] = matmul_left(choice[:, :slots], got).astype(jnp.bfloat16)
        second[:, cols] = matmul_left(choice[:, slots:], got).astype(jnp.bfloat16)
        return carry

    lax.fori_loop(0, land.shape[2] // COLS, column, 0)


def deal_kernel(
    meta, tokens, cotangent, gain,
    meta_all, give, take, x_out, gy_out, normed_all, gy_all,
    x_mine, g_mine, buf, land, normed,
    load, msend, mrecv, csend, crecv, nsend, nrecv, nhere, gsend, grecv, ghere,
):
    r, c, base, t = place()
    n_row = lax.axis_size("row")
    slots = x_mine.shape[0]
    per_peer = slots // n_row
    loads = [
        pltpu.make_async_copy(tokens.at[c], x_mine, load.at[0]),
        pltpu.make_async_copy(cotangent.at[c], g_mine, load.at[1]),
    ]
    for copy in loads:
        copy.start()
    greet_rows()

    def meta_copy(other, slot):
        return remote(meta, meta_all.at[slot], msend.at[other], mrecv.at[slot], other, c)

    def start(off, carry):
        meta_copy(lax.rem(r + off, n_row), r).start()
        return carry

    lax.fori_loop(1, n_row, start, 0)
    meta_all[r] = meta[...]

    def finish(off, carry):
        other = lax.rem(r + off, n_row)
        copy = meta_copy(other, other)
        copy.wait_send()
        copy.wait_recv()
        return carry

    lax.fori_loop(1, n_row, finish, 0)

    shift = slots.bit_length() - 1
    row_no = lax.broadcasted_iota(jnp.int32, (CHUNK, slots), 0)
    wanted = jnp.where(row_no < per_peer, row_no, row_no - per_peer).astype(jnp.float32)
    early = row_no < per_peer
    late = (row_no >= per_peer) & (row_no < 2 * per_peer)
    tri = (
        lax.broadcasted_iota(jnp.int32, (slots, slots), 0)
        < lax.broadcasted_iota(jnp.int32, (slots, slots), 1)
    ).astype(jnp.float32).astype(jnp.bfloat16)
    places = lax.broadcasted_iota(jnp.int32, (slots, slots), 0)

    def order_of(block):
        picked = jnp.where(c == 0, block[0:1, :], block[1:2, :])
        return lax.shift_right_logical(picked, shift), picked - lax.shift_left(
            lax.shift_right_logical(picked, shift), shift
        )

    own_source, own_local = order_of(meta[...])

    def select(mask):
        wide = jnp.broadcast_to(mask.astype(jnp.float32), (CHUNK, slots)).astype(jnp.bfloat16)
        rank = matmul(wide, tri)
        return jnp.where(
            (rank == wanted) & (wide.astype(jnp.float32) > 0.5), 1.0, 0.0
        )

    def build(d, carry):
        rows = pl.ds(pl.multiple_of(d * CHUNK, CHUNK), CHUNK)
        source, local = order_of(meta_all[d])
        chosen = select(source == r).astype(jnp.bfloat16)
        at_home = (places == local).astype(jnp.float32).astype(jnp.bfloat16)
        picks = matmul_trans(chosen, at_home)
        give[rows, :slots] = jnp.where(early, picks, 0.0).astype(jnp.bfloat16)
        give[rows, slots:] = jnp.where(late, picks, 0.0).astype(jnp.bfloat16)
        kept = select(own_source == d)
        take[rows, :slots] = jnp.where(early, kept, 0.0).astype(jnp.bfloat16)
        take[rows, slots:] = jnp.where(late, kept, 0.0).astype(jnp.bfloat16)
        return carry

    lax.fori_loop(0, n_row, build, 0)
    for copy in loads:
        copy.wait()
    permute_out(give, buf, x_mine, g_mine, slots)
    exchange_rows(buf, land, csend, crecv)
    land[r] = buf[r]
    finish_rows(buf, land, csend, crecv)
    permute_in(take, land, x_out, gy_out, slots)

    def norm(rows):
        values = x_out[rows, :].astype(jnp.float32)
        scale = lax.rsqrt(jnp.mean(values * values, axis=-1, keepdims=True) + EPS)
        normed[rows, :] = (values * scale * gain[...]).astype(jnp.bfloat16)

    by_rows(slots, norm)
    first = gather_start(normed, normed_all, nsend, nrecv, nhere)
    second = gather_start(gy_out, gy_all, gsend, grecv, ghere)
    gather_finish(first, normed_all, nsend, nrecv)
    gather_finish(second, gy_all, gsend, grecv)


def deal(meta, tokens, cotangent, gain, n_row):
    slots, width = tokens.shape[1:]
    bf = jnp.bfloat16
    return pl.pallas_call(
        deal_kernel,
        name="deal",
        out_shape=(
            jax.ShapeDtypeStruct((n_row, 8, 128), jnp.int32),
            jax.ShapeDtypeStruct((n_row * CHUNK, 2 * slots), bf),
            jax.ShapeDtypeStruct((n_row * CHUNK, 2 * slots), bf),
            jax.ShapeDtypeStruct((slots, width), bf),
            jax.ShapeDtypeStruct((slots, width), bf),
            jax.ShapeDtypeStruct((GROUP, slots, width), bf),
            jax.ShapeDtypeStruct((GROUP, slots, width), bf),
        ),
        in_specs=[
            pl.BlockSpec(memory_space=VMEM),
            pl.BlockSpec(memory_space=ANY),
            pl.BlockSpec(memory_space=ANY),
            pl.BlockSpec(memory_space=VMEM),
        ],
        out_specs=(pl.BlockSpec(memory_space=VMEM),) * 5 + (pl.BlockSpec(memory_space=ANY),) * 2,
        scratch_shapes=[
            VMEM((slots, width), bf),
            VMEM((slots, width), bf),
            VMEM((n_row, CHUNK, width), bf),
            VMEM((n_row, CHUNK, width), bf),
            VMEM((slots, width), bf),
            pltpu.SemaphoreType.DMA((2,)),
            pltpu.SemaphoreType.DMA((n_row,)),
            pltpu.SemaphoreType.DMA((n_row,)),
            pltpu.SemaphoreType.DMA((n_row,)),
            pltpu.SemaphoreType.DMA((n_row,)),
        ]
        + gather_scratch()
        + gather_scratch(),
        compiler_params=pltpu.CompilerParams(
            collective_id=0, has_side_effects=True, vmem_limit_bytes=40 << 20
        ),
    )(meta, tokens, cotangent, gain)


def middle_kernel(parts, x, gain, mid, normed_all, near, out2, far, s1, r1, s2, r2, normed, nsend, nrecv, nhere):
    greet_group()
    scatter_sum(parts, near, out2, far, s1, r1, s2, r2, mid)

    def norm(rows):
        values = x[rows, :].astype(jnp.float32) + mid[rows, :]
        mid[rows, :] = values
        scale = lax.rsqrt(jnp.mean(values * values, axis=-1, keepdims=True) + EPS)
        normed[rows, :] = (values * scale * gain[...]).astype(jnp.bfloat16)

    by_rows(mid.shape[0], norm)
    started = gather_start(normed, normed_all, nsend, nrecv, nhere)
    gather_finish(started, normed_all, nsend, nrecv)


def middle(parts, x, gain):
    slots, width = x.shape
    return pl.pallas_call(
        middle_kernel,
        name="middle",
        out_shape=(
            jax.ShapeDtypeStruct((slots, width), jnp.float32),
            jax.ShapeDtypeStruct((GROUP, slots, width), jnp.bfloat16),
        ),
        in_specs=[pl.BlockSpec(memory_space=VMEM)] * 3,
        out_specs=(pl.BlockSpec(memory_space=VMEM), pl.BlockSpec(memory_space=ANY)),
        scratch_shapes=scatter_scratch(slots, width)
        + [VMEM((slots, width), jnp.bfloat16)]
        + gather_scratch(),
        compiler_params=pltpu.CompilerParams(
            collective_id=1, has_side_effects=True, vmem_limit_bytes=40 << 20
        ),
    )(parts, x, gain)


def norm_back(values, gain, grad):
    inverse = lax.rsqrt(jnp.mean(values * values, axis=-1, keepdims=True) + EPS)
    scaled = grad * gain
    back = inverse * scaled - values * (
        inverse * inverse * inverse * jnp.mean(values * scaled, axis=-1, keepdims=True)
    )
    return back, jnp.sum(grad * values * inverse, axis=0, keepdims=True)


def turn_kernel(
    parts, ff_parts, mid, gy, gain, d_mid, result, d_gain, branch_all,
    near, out2, far, s1, r1, s2, r2, near_b, out2_b, far_b, s1b, r1b, s2b, r2b, branch, nsend, nrecv, nhere,
):
    greet_group()
    scatter_sum(parts, near, out2, far, s1, r1, s2, r2, d_mid)
    d_gain[...] = jnp.zeros_like(d_gain)

    def back(rows):
        values = mid[rows, :]
        grad, gain_part = norm_back(values, gain[...], d_mid[rows, :])
        grad = gy[rows, :].astype(jnp.float32) + grad
        d_mid[rows, :] = grad
        branch[rows, :] = grad.astype(jnp.bfloat16)
        d_gain[...] += gain_part

    by_rows(mid.shape[0], back)
    started = gather_start(branch, branch_all, nsend, nrecv, nhere)
    scatter_sum(ff_parts, near_b, out2_b, far_b, s1b, r1b, s2b, r2b, result)

    def add(rows):
        result[rows, :] += mid[rows, :]

    by_rows(mid.shape[0], add)
    gather_finish(started, branch_all, nsend, nrecv)


def turn(parts, ff_parts, mid, gy, gain):
    slots, width = mid.shape
    return pl.pallas_call(
        turn_kernel,
        name="turn",
        out_shape=(
            jax.ShapeDtypeStruct((slots, width), jnp.float32),
            jax.ShapeDtypeStruct((slots, width), jnp.float32),
            jax.ShapeDtypeStruct((1, width), jnp.float32),
            jax.ShapeDtypeStruct((GROUP, slots, width), jnp.bfloat16),
        ),
        in_specs=[pl.BlockSpec(memory_space=VMEM)] * 5,
        out_specs=(pl.BlockSpec(memory_space=VMEM),) * 3 + (pl.BlockSpec(memory_space=ANY),),
        scratch_shapes=scatter_scratch(slots, width)
        + scatter_scratch(slots, width)
        + [VMEM((slots, width), jnp.bfloat16)]
        + gather_scratch(),
        compiler_params=pltpu.CompilerParams(
            collective_id=2, has_side_effects=True, vmem_limit_bytes=48 << 20
        ),
    )(parts, ff_parts, mid, gy, gain)


def home_kernel(
    parts, x, d_mid, result, gain, give, take, output, gradient, d_gain,
    near, out2, far, s1, r1, s2, r2, total, first, second, buf, land, csend, crecv, here, osend, orecv,
):
    r, c, base, t = place()
    slots = x.shape[0]
    greet_rows()
    scatter_sum(parts, near, out2, far, s1, r1, s2, r2, total)
    d_gain[...] = jnp.zeros_like(d_gain)

    def back(rows):
        values = x[rows, :].astype(jnp.float32)
        grad, gain_part = norm_back(values, gain[...], total[rows, :])
        second[rows, :] = (d_mid[rows, :] + grad).astype(jnp.bfloat16)
        first[rows, :] = result[rows, :].astype(jnp.bfloat16)
        d_gain[...] += gain_part

    by_rows(slots, back)
    permute_out(take, buf, first, second, slots)
    exchange_rows(buf, land, csend, crecv)
    land[r] = buf[r]
    finish_rows(buf, land, csend, crecv)
    permute_in(give, land, first, second, slots)
    copies = []
    for i, (mine, out) in enumerate(((first, output), (second, gradient))):
        copies.append(pltpu.make_async_copy(mine, out.at[c], here.at[i]))
        copies.append(remote(mine, out.at[c], osend.at[i], orecv.at[i], r, 1 - c))
    for copy in copies:
        copy.start()
    for copy in copies:
        copy.wait()


def send_home(parts, x, d_mid, result, gain, give, take, n_row):
    slots, width = x.shape
    bf = jnp.bfloat16
    return pl.pallas_call(
        home_kernel,
        name="home",
        out_shape=(
            jax.ShapeDtypeStruct((2, slots, width), bf),
            jax.ShapeDtypeStruct((2, slots, width), bf),
            jax.ShapeDtypeStruct((1, width), jnp.float32),
        ),
        in_specs=[pl.BlockSpec(memory_space=VMEM)] * 7,
        out_specs=(pl.BlockSpec(memory_space=ANY),) * 2 + (pl.BlockSpec(memory_space=VMEM),),
        scratch_shapes=scatter_scratch(slots, width)
        + [
            VMEM((slots, width), jnp.float32),
            VMEM((slots, width), bf),
            VMEM((slots, width), bf),
            VMEM((n_row, CHUNK, width), bf),
            VMEM((n_row, CHUNK, width), bf),
            pltpu.SemaphoreType.DMA((n_row,)),
            pltpu.SemaphoreType.DMA((n_row,)),
            pltpu.SemaphoreType.DMA((2,)),
            pltpu.SemaphoreType.DMA((2,)),
            pltpu.SemaphoreType.DMA((2,)),
        ],
        compiler_params=pltpu.CompilerParams(
            collective_id=3, has_side_effects=True, vmem_limit_bytes=48 << 20
        ),
    )(parts, x, d_mid, result, gain, give, take)


def blocks_kernel(parts, total, low, land, mine, s1, r1, s2, r2, here):
    r, c, base, t = place()
    greet_group(cross=True)
    low[...] = parts[...].astype(jnp.bfloat16)
    others = [(m, f) for m in (3, 1, 2) for f in (0, 1)] + [(0, 1)]

    def where(m, f):
        row, col = partner(t, m), (1 - c if f else c)
        return row, col, row * 2 + col

    first = []
    for m, f in others:
        row, col, block = where(m, f)
        k = m * 2 + f
        first.append(remote(low.at[block], land.at[k], s1.at[k], r1.at[k], base + row, col))
        first[-1].start()
    own = t * 2 + c
    for copy in first:
        copy.wait_recv()
    summed = parts[own]
    for m, f in others:
        summed = summed + land[m * 2 + f].astype(jnp.float32)
    mine[...] = summed.astype(jnp.bfloat16)
    local = pltpu.make_async_copy(mine, total.at[own], here)
    local.start()
    second = []
    for m, f in others:
        row, col, block = where(m, f)
        k = m * 2 + f
        second.append(remote(mine, total.at[own], s2.at[k], r2.at[k], base + row, col))
        second[-1].start()
    local.wait()
    for copy in first:
        copy.wait_send()
    for copy in second:
        copy.wait()


def sum_blocks(parts, number):
    slots = parts.shape[1]
    return pl.pallas_call(
        blocks_kernel,
        name=f"blocks{number}",
        out_shape=jax.ShapeDtypeStruct(parts.shape, jnp.bfloat16),
        in_specs=[pl.BlockSpec(memory_space=VMEM)],
        out_specs=pl.BlockSpec(memory_space=VMEM),
        scratch_shapes=[
            VMEM(parts.shape, jnp.bfloat16),
            VMEM(parts.shape, jnp.bfloat16),
            VMEM(parts.shape[1:], jnp.bfloat16),
            pltpu.SemaphoreType.DMA((GROUP,)),
            pltpu.SemaphoreType.DMA((GROUP,)),
            pltpu.SemaphoreType.DMA((GROUP,)),
            pltpu.SemaphoreType.DMA((GROUP,)),
            pltpu.SemaphoreType.DMA,
        ],
        compiler_params=pltpu.CompilerParams(
            collective_id=number, has_side_effects=True, vmem_limit_bytes=16 << 20
        ),
    )(parts)


def layout(lengths, slot_count):
    count = lengths.shape[0]
    ends = [lengths[0]]
    for i in range(1, count):
        ends.append(ends[-1] + lengths[i])
    places = jnp.arange(slot_count, dtype=jnp.int32)
    segment = sum((places >= end).astype(jnp.int32) for end in ends)
    within = places
    for i in range(1, count):
        within = jnp.where(places >= ends[i - 1], places - ends[i - 1], within)
    allowed = (segment[:, None] == segment[None, :]) & (places[:, None] >= places[None, :])
    return (segment, within, allowed)


def causal_conv(values_in, kernel, bias_vec, segment):
    slot_count, channels = values_in.shape
    kernel_len = kernel.shape[0]
    summed = bias_vec[None, :] + kernel[kernel_len - 1][None, :] * values_in
    for shift_by in range(1, kernel_len):
        shifted = jnp.concatenate(
            [jnp.zeros((shift_by, channels), values_in.dtype), values_in[: slot_count - shift_by]],
            axis=0,
        )
        earlier = jnp.concatenate(
            [jnp.full((shift_by,), -1, jnp.int32), segment[: slot_count - shift_by]], axis=0
        )
        shifted = jnp.where((earlier == segment)[:, None], shifted, 0.0)
        summed = summed + kernel[kernel_len - 1 - shift_by][None, :] * shifted
    return jax.nn.silu(summed)


def decay_mix(intersection, step_raw, step_bias, decay_log, allowed):
    slot_count = step_raw.shape[0]
    step_size = jax.nn.softplus(step_raw + step_bias[None, :])
    rates = -jnp.exp(decay_log)
    places = jnp.arange(slot_count)
    tri = (places[:, None] >= places[None, :]).astype(jnp.float32)
    levels = jnp.dot(tri, step_size * rates[None, :], precision=HIGH).T
    spread = levels[:, :, None] - levels[:, None, :]
    decays = jnp.where(allowed[None], jnp.exp(jnp.where(allowed[None], spread, 0.0)), 0.0)
    return intersection[None] * decays * step_size.T[:, None, :]


def gate_mix(scanned, conv_out, mamba_gate, skip_scale):
    slot_count, channels = conv_out.shape
    per_head = channels // skip_scale.shape[0]
    mixed_out = (
        scanned.reshape(slot_count, channels) + conv_out * jnp.repeat(skip_scale, per_head)[None, :]
    )
    return mixed_out * jax.nn.silu(mamba_gate)


def rotary(vectors, cosine, sine):
    half_dim = vectors.shape[1] // 2
    turned = jnp.concatenate([-vectors[:, half_dim:], vectors[:, :half_dim]], axis=-1)
    return vectors * cosine + turned * sine


def rotary_back(vectors, cosine, sine):
    half_dim = vectors.shape[1] // 2
    scaled = vectors * sine
    turned = jnp.concatenate([scaled[:, half_dim:], -scaled[:, :half_dim]], axis=-1)
    return vectors * cosine + turned


def swiglu(ff_gate, ff_up):
    return jax.nn.silu(ff_gate) * ff_up


def cut(array, parts, axis=1):
    rows, cols = array.shape
    return array.reshape(rows, parts, cols // parts).transpose(1, 0, 2)


def local(
    tokens,
    cotangent,
    deal_order,
    seq_lengths,
    mixer_norm_gain,
    mamba_gate_weight,
    mamba_input_weight,
    state_weight,
    step_weight,
    conv_input,
    conv_input_bias,
    conv_state,
    conv_state_bias,
    step_bias,
    decay_log,
    skip_scale,
    mamba_out_weight,
    query_weight,
    key_weight,
    value_weight,
    attn_out_weight,
    ff_norm_gain,
    gate_weight,
    up_weight,
    down_weight,
):
    n_row = lax.axis_size("row")
    r = lax.axis_index("row")
    c = lax.axis_index("col")
    t = lax.rem(r, TP)
    data = n_row // TP
    slots, width = tokens.shape[1:]
    bf = jnp.bfloat16
    plane = [[i * TP + j for j in range(TP)] for i in range(data)]
    along = [[i * TP + j for i in range(data)] for j in range(TP)]

    rows = mamba_gate_weight.shape[0]
    mh = mamba_gate_weight.shape[1] // TP
    qh = query_weight.shape[1] // TP
    kvh = key_weight.shape[1]
    sh = state_weight.shape[1] // (2 * GROUP)
    ph = step_weight.shape[1] // TP
    fh = gate_weight.shape[1] // TP
    used = 2 * mh + qh + 2 * kvh + 2 * sh + ph
    spare = -used % 256

    def wide(array):
        return jnp.broadcast_to(array[None], (TP,) + array.shape)

    half = state_weight.shape[1] // 2
    state_in_part = lax.dynamic_slice_in_dim(state_weight[:, :half], c * (half // 2), half // 2, 1)
    state_out_part = lax.dynamic_slice_in_dim(state_weight[:, half:], c * (half // 2), half // 2, 1)
    packed_in = jnp.concatenate(
        [
            cut(mamba_gate_weight, TP),
            cut(mamba_input_weight, TP),
            cut(query_weight, TP),
            wide(key_weight),
            wide(value_weight),
            cut(state_in_part, TP),
            cut(state_out_part, TP),
            cut(step_weight, TP),
            jnp.zeros((TP, rows, spare), bf),
        ],
        axis=2,
    )
    packed_out = jnp.concatenate([cut(mamba_out_weight.T, TP), cut(attn_out_weight.T, TP)], axis=2)
    packed_ff = jnp.concatenate(
        [cut(gate_weight, TP), cut(up_weight, TP), cut(down_weight.T, TP)], axis=2
    )

    def assemble(packed):
        cols = packed.shape[2]
        mine = lax.all_to_all(
            packed, "row", split_axis=0, concat_axis=0, axis_index_groups=plane, tiled=True
        )
        return lax.all_gather(
            mine.reshape(TP * rows, cols), "row", axis=0, axis_index_groups=along, tiled=True
        )

    def disperse(grad):
        cols = grad.shape[1]
        mine = lax.psum_scatter(
            grad.astype(bf), "row", scatter_dimension=0, axis_index_groups=along, tiled=True
        )
        return lax.all_to_all(
            mine.reshape(TP, rows, cols),
            "row",
            split_axis=0,
            concat_axis=0,
            axis_index_groups=plane,
            tiled=True,
        )

    w_in = assemble(packed_in)
    w_out = assemble(packed_out)
    w_ff = assemble(packed_ff)

    meta = jnp.concatenate(
        [
            deal_order,
            jnp.pad(seq_lengths[:, 0, :], ((0, 0), (0, 128 - seq_lengths.shape[2]))),
            jnp.zeros((4, 128), jnp.int32),
        ],
        axis=0,
    )
    meta_all, give, take, x_home, gy_home, normed_one, gy_all = deal(
        meta, tokens, cotangent, mixer_norm_gain[None, :], n_row
    )
    normed_one = normed_one.reshape(GROUP * slots, width)
    gy_all = gy_all.reshape(GROUP * slots, width)
    group_meta = lax.dynamic_slice_in_dim(meta_all, r - t, TP, 0)
    lengths = group_meta[:, 2:4, : seq_lengths.shape[2]].reshape(GROUP, seq_lengths.shape[2])
    segment, within, allowed = jax.vmap(lambda own: layout(own, slots))(lengths)
    segment = (segment + 8 * jnp.arange(GROUP, dtype=jnp.int32)[:, None]).reshape(-1)
    half_dim = HD // 2
    inverse = ROPE_BASE ** (-2.0 * jnp.arange(half_dim, dtype=jnp.float32) / HD)
    angles = within.reshape(-1).astype(jnp.float32)[:, None] * inverse[None, :]
    cosine = jnp.concatenate([jnp.cos(angles), jnp.cos(angles)], axis=1)
    sine = jnp.concatenate([jnp.sin(angles), jnp.sin(angles)], axis=1)

    def piece(array, size, start):
        return lax.dynamic_slice_in_dim(array, start, size, array.ndim - 1)

    eighth = c * TP + t
    conv_k = piece(conv_input, mh, t * mh)
    conv_b = piece(conv_input_bias, mh, t * mh)
    state_k = jnp.concatenate(
        [piece(conv_state, sh, eighth * sh), piece(conv_state, sh, half + eighth * sh)], axis=1
    )
    state_b = jnp.concatenate(
        [piece(conv_state_bias, sh, eighth * sh), piece(conv_state_bias, sh, half + eighth * sh)]
    )
    bias_h = piece(step_bias, ph, t * ph)
    decay_h = piece(decay_log, ph, t * ph)
    skip_h = piece(skip_scale, ph, t * ph)

    projected = matmul(normed_one, w_in)
    edges = [0, mh, 2 * mh, 2 * mh + qh, 2 * mh + qh + kvh, 2 * mh + qh + 2 * kvh]
    edges = edges + [edges[-1] + 2 * sh, edges[-1] + 2 * sh + ph]
    mamba_gate, conv_in, queries, keys_raw, values_raw, state_raw, step_raw = (
        projected[:, low:high] for low, high in zip(edges[:-1], edges[1:])
    )
    conv_out = causal_conv(conv_in, conv_k, conv_b, segment)
    state_act = causal_conv(state_raw, state_k, state_b, segment)
    state_in_low = state_act[:, :sh].astype(bf).reshape(GROUP, slots, sh)
    state_out_low = state_act[:, sh:].astype(bf).reshape(GROUP, slots, sh)
    cross_part = jnp.einsum(
        "bin,bjn->bij", state_out_low, state_in_low, preferred_element_type=jnp.float32
    )
    intersection = sum_blocks(cross_part, 4).astype(jnp.float32)
    step_blocks = step_raw.reshape(GROUP, slots, ph)

    def mix_all(crossed, step_values, bias_values, decay_values):
        return jax.vmap(
            lambda one, two, three: decay_mix(one, two, bias_values, decay_values, three)
        )(crossed, step_values, allowed)

    mixing, mix_back = jax.vjp(mix_all, intersection, step_blocks, bias_h, decay_h)
    mixing_low = mixing.astype(bf)
    conv_low = conv_out.astype(bf).reshape(GROUP, slots, ph, -1)
    scanned = jnp.einsum(
        "bhij,bjhp->bihp", mixing_low, conv_low, preferred_element_type=jnp.float32
    ).reshape(GROUP * slots, mh)
    gated_low = gate_mix(scanned, conv_out, mamba_gate, skip_h).astype(bf)

    query_rot = rotary(queries, cosine, sine).astype(bf).reshape(GROUP, slots, HD)
    key_rot = rotary(keys_raw, cosine, sine).astype(bf).reshape(GROUP, slots, HD)
    value_low = values_raw.astype(bf).reshape(GROUP, slots, HD)
    raw = jnp.einsum("bid,bjd->bij", query_rot, key_rot, preferred_element_type=jnp.float32)
    scores = jnp.where(allowed, raw * HD ** (-0.5), NEG_LARGE)
    exp_terms = jnp.exp(scores - jnp.max(scores, axis=-1, keepdims=True))
    probs = exp_terms / jnp.sum(exp_terms, axis=-1, keepdims=True)
    attended_low = (
        jnp.einsum("bij,bjd->bid", probs.astype(bf), value_low, preferred_element_type=jnp.float32)
        .astype(bf)
        .reshape(GROUP * slots, HD)
    )
    branch_in = jnp.concatenate([gated_low, attended_low], axis=1)
    branch_part = matmul_trans(branch_in, w_out).astype(bf).reshape(GROUP, slots, width)
    mid, normed_two = middle(branch_part, x_home, ff_norm_gain[None, :])
    normed_two = normed_two.reshape(GROUP * slots, width)

    ff_gate_up = matmul(normed_two, w_ff[:, : 2 * fh])
    ff_gate, ff_up = ff_gate_up[:, :fh], ff_gate_up[:, fh:]
    w_down = w_ff[:, 2 * fh :]
    ff_hidden = swiglu(ff_gate, ff_up).astype(bf)
    ff_part = matmul_trans(ff_hidden, w_down).astype(bf).reshape(GROUP, slots, width)
    grad_hidden = matmul(gy_all, w_down)
    unused_value, pullback = jax.vjp(swiglu, ff_gate, ff_up)
    grad_gate, grad_up = pullback(grad_hidden)
    grad_gate_up = jnp.concatenate([grad_gate.astype(bf), grad_up.astype(bf)], axis=1)
    normed_two_part = (
        matmul_trans(grad_gate_up, w_ff[:, : 2 * fh]).astype(bf).reshape(GROUP, slots, width)
    )
    d_mid, result, delta_ff_gain, branch_all = turn(
        normed_two_part, ff_part, mid, gy_home, ff_norm_gain[None, :]
    )
    branch_all = branch_all.reshape(GROUP * slots, width)
    delta_gate_up = disperse(matmul_left(normed_two, grad_gate_up))
    delta_down = disperse(matmul_left(gy_all, ff_hidden))

    delta_out = disperse(matmul_left(branch_all, branch_in))
    grad_branch_in = matmul(branch_all, w_out)
    grad_gated = grad_branch_in[:, :mh]
    unused_value, pullback = jax.vjp(gate_mix, scanned, conv_out, mamba_gate, skip_h)
    grad_scanned, grad_conv_skip, grad_mamba_gate, delta_skip = pullback(grad_gated)
    grad_scanned = grad_scanned.astype(bf).reshape(GROUP, slots, ph, -1)
    grad_mixing = jnp.einsum(
        "bihp,bjhp->bhij", grad_scanned, conv_low, preferred_element_type=jnp.float32
    )
    grad_conv_out = grad_conv_skip + jnp.einsum(
        "bhij,bihp->bjhp", mixing_low, grad_scanned, preferred_element_type=jnp.float32
    ).reshape(GROUP * slots, mh)
    grad_cross, grad_step, delta_step_bias, delta_decay = mix_back(grad_mixing)
    grad_cross = sum_blocks(grad_cross, 5)
    grad_step = grad_step.reshape(GROUP * slots, ph).astype(bf)

    grad_attended = grad_branch_in[:, mh:].astype(bf).reshape(GROUP, slots, HD)
    grad_probs = jnp.einsum(
        "bid,bjd->bij", grad_attended, value_low, preferred_element_type=jnp.float32
    )
    grad_values = jnp.einsum(
        "bij,bid->bjd", probs.astype(bf), grad_attended, preferred_element_type=jnp.float32
    ).reshape(GROUP * slots, HD)
    grad_raw = probs * (grad_probs - jnp.sum(grad_probs * probs, axis=-1, keepdims=True))
    grad_raw = (grad_raw * HD ** (-0.5)).astype(bf)
    grad_query_rot = jnp.einsum(
        "bij,bjd->bid", grad_raw, key_rot, preferred_element_type=jnp.float32
    ).reshape(GROUP * slots, HD)
    grad_key_rot = jnp.einsum(
        "bij,bid->bjd", grad_raw, query_rot, preferred_element_type=jnp.float32
    ).reshape(GROUP * slots, HD)
    grad_queries = rotary_back(grad_query_rot, cosine, sine)
    grad_keys = rotary_back(grad_key_rot, cosine, sine)

    unused_value, pullback = jax.vjp(partial(causal_conv, segment=segment), conv_in, conv_k, conv_b)
    grad_conv_in, delta_conv_k, delta_conv_b = pullback(grad_conv_out)
    grad_state = jnp.concatenate(
        [
            jnp.einsum("bij,bin->bjn", grad_cross, state_out_low, preferred_element_type=jnp.float32),
            jnp.einsum("bij,bjn->bin", grad_cross, state_in_low, preferred_element_type=jnp.float32),
        ],
        axis=2,
    ).reshape(GROUP * slots, 2 * sh)
    unused_value, pullback = jax.vjp(
        partial(causal_conv, segment=segment), state_raw, state_k, state_b
    )
    grad_state_raw, delta_state_k, delta_state_b = pullback(grad_state)
    grad_projected = jnp.concatenate(
        [
            grad_mamba_gate.astype(bf),
            grad_conv_in.astype(bf),
            grad_queries.astype(bf),
            grad_keys.astype(bf),
            grad_values.astype(bf),
            grad_state_raw.astype(bf),
            grad_step,
            jnp.zeros((GROUP * slots, spare), bf),
        ],
        axis=1,
    )
    normed_one_part = matmul_trans(grad_projected, w_in).astype(bf).reshape(GROUP, slots, width)
    output, grad_tokens, delta_mixer_gain = send_home(
        normed_one_part, x_home, d_mid, result, mixer_norm_gain[None, :], give, take, n_row
    )
    delta_in = disperse(matmul_left(normed_one, grad_projected))

    def join(stacked):
        return stacked.transpose(1, 0, 2).reshape(stacked.shape[1], -1).astype(jnp.float32)

    pieces = [delta_in[:, :, low:high] for low, high in zip(edges[:-1], edges[1:])]
    state_mine = pieces[5]
    state_other = lax.ppermute(state_mine, "col", [(0, 1), (1, 0)])
    state_first = jnp.where(c == 0, state_mine, state_other)
    state_second = jnp.where(c == 0, state_other, state_mine)
    delta_state = jnp.concatenate(
        [
            join(state_first[:, :, :sh]),
            join(state_second[:, :, :sh]),
            join(state_first[:, :, sh:]),
            join(state_second[:, :, sh:]),
        ],
        axis=1,
    )
    delta_key = jnp.sum(pieces[3].astype(jnp.float32), axis=0)
    delta_value = jnp.sum(pieces[4].astype(jnp.float32), axis=0)

    def spread(array, whole, start):
        return lax.dynamic_update_slice_in_dim(
            jnp.zeros(array.shape[:-1] + (whole,), jnp.float32), array, start, array.ndim - 1
        )

    by_col = [
        spread(delta_conv_k, conv_input.shape[1], t * mh),
        spread(delta_conv_b, conv_input_bias.shape[0], t * mh),
        spread(delta_step_bias, step_bias.shape[0], t * ph),
        spread(delta_decay, decay_log.shape[0], t * ph),
        spread(delta_skip, skip_scale.shape[0], t * ph),
    ]
    by_all = [
        spread(delta_state_k[:, :sh], 2 * half, eighth * sh)
        + spread(delta_state_k[:, sh:], 2 * half, half + eighth * sh),
        spread(delta_state_b[:sh], 2 * half, eighth * sh)
        + spread(delta_state_b[sh:], 2 * half, half + eighth * sh),
        delta_mixer_gain[0],
        delta_ff_gain[0],
    ]
    by_col = lax.psum(by_col, "row")
    by_all = lax.psum(by_all, ("row", "col"))

    return (
        output,
        grad_tokens,
        by_all[2],
        join(pieces[0]),
        join(pieces[1]),
        delta_state,
        join(pieces[6]),
        by_col[0],
        by_col[1],
        by_all[0],
        by_all[1],
        by_col[2],
        by_col[3],
        by_col[4],
        join(delta_out[:, :, :mh]).T,
        join(pieces[2]),
        delta_key,
        delta_value,
        join(delta_out[:, :, mh:]).T,
        by_all[3],
        join(delta_gate_up[:, :, :fh]),
        join(delta_gate_up[:, :, fh:]),
        join(delta_down).T,
    )


def solution(mesh):
    both = P("row", "col")
    turned = P("col", "row")
    in_specs = (
        P(None, "row", None),
        P(None, "row", None),
        P(None, "row"),
        P(None, "row", None),
        P(),
        both,
        both,
        P("row", None),
        both,
        P(None, "col"),
        P("col"),
        P(),
        P(),
        P("col"),
        P("col"),
        P("col"),
        turned,
        both,
        both,
        both,
        turned,
        P(),
        both,
        both,
        turned,
    )
    out_specs = (
        P(None, "row", None),
        P(None, "row", None),
        P(),
        both,
        both,
        P("row", None),
        both,
        P(None, "col"),
        P("col"),
        P(),
        P(),
        P("col"),
        P("col"),
        P("col"),
        turned,
        both,
        both,
        both,
        turned,
        P(),
        both,
        both,
        turned,
    )
    return jax.shard_map(local, mesh=mesh, in_specs=in_specs, out_specs=out_specs, check_vma=False)
```

```python
from functools import partial

import jax
import jax.numpy as jnp
from jax import lax
from jax.experimental import pallas as pl
from jax.experimental.pallas import tpu as pltpu
from jax.sharding import PartitionSpec as P

HD = 128
TP = 4
GROUP = 2 * TP
CHUNK = 16
EPS = 1e-05
NEG_LARGE = -1e30
ROPE_BASE = 100000000000.0
MESH = pl.DeviceIdType.MESH
HIGH = lax.Precision.HIGHEST
VMEM = pltpu.VMEM
ANY = pl.ANY


def matmul(first_op, second_op):
    return jnp.dot(first_op, second_op, preferred_element_type=jnp.float32)


def matmul_trans(first_op, second_op):
    return lax.dot_general(
        first_op, second_op, (((1,), (1,)), ((), ())), preferred_element_type=jnp.float32
    )


def matmul_left(first_op, second_op):
    return lax.dot_general(
        first_op, second_op, (((0,), (0,)), ((), ())), preferred_element_type=jnp.float32
    )


TP_BITS = (0, 1)


def data_bits(n_row):
    return [b for b in reversed(range(n_row.bit_length() - 1)) if b not in TP_BITS]


def bit(row, b):
    return lax.rem(lax.div(row, 1 << b), 2)


def flip(row, b):
    return row + (1 << b) * (1 - 2 * bit(row, b))


def member(row):
    return bit(row, TP_BITS[0]) + 2 * bit(row, TP_BITS[1])


def partner(row, m):
    if m & 1:
        row = flip(row, TP_BITS[0])
    if m & 2:
        row = flip(row, TP_BITS[1])
    return row


def turned_row(row, mask):
    for b in range(mask.bit_length()):
        row = flip(row, b) if mask >> b & 1 else row
    return row


def group_of(row, n_row):
    index = 0
    for b in data_bits(n_row):
        index = index * 2 + bit(row, b)
    return index


def spot(row, n_row):
    return group_of(row, n_row) * TP + member(row)


def flips(n_row, mask):
    return [(row, row ^ mask) for row in range(n_row)]


def mask_of(m):
    return (m & 1) * (1 << TP_BITS[0]) + (m // 2) * (1 << TP_BITS[1])


def place():
    r = lax.axis_index("row")
    c = lax.axis_index("col")
    return r, c, member(r)


def block_of(m):
    return member(partner(lax.axis_index("row"), m)) * 2


def params(number, megabytes):
    return pltpu.CompilerParams(
        collective_id=number, has_side_effects=True, vmem_limit_bytes=megabytes << 20
    )


def cost(microseconds):
    return pl.CostEstimate(flops=0, transcendentals=0, bytes_accessed=microseconds * 3_400_000)


def remote(src, dst, send, recv, row, col):
    return pltpu.make_async_remote_copy(
        src_ref=src, dst_ref=dst, send_sem=send, recv_sem=recv, device_id=(row, col), device_id_type=MESH
    )


def greet_group(cross=False):
    r, c, t = place()
    barrier = pltpu.get_barrier_semaphore()
    pl.semaphore_signal(barrier, inc=1, device_id=(r, 1 - c), device_id_type=MESH)
    count = 1
    for m in (1, 2, 3):
        pl.semaphore_signal(barrier, inc=1, device_id=(partner(r, m), c), device_id_type=MESH)
        count += 1
        if cross:
            pl.semaphore_signal(
                barrier, inc=1, device_id=(partner(r, m), 1 - c), device_id_type=MESH
            )
            count += 1
    pl.semaphore_wait(barrier, count)


def gather_start(src, out, send, recv, here):
    r, c, t = place()
    mine = out.at[t * 2 + c]
    local = pltpu.make_async_copy(src, mine, here)
    peers = [
        remote(src, mine, send.at[m], recv.at[m], partner(r, m), c) for m in (1, 2, 3)
    ]
    sibling = remote(src, mine, send.at[0], recv.at[0], r, 1 - c)
    for copy in (peers[2], peers[0], peers[1], sibling, local):
        copy.start()
    return peers, sibling, local


def gather_finish(started, out, send, recv):
    r, c, t = place()
    peers, sibling, local = started
    forwards = []
    for m in (1, 2, 3):
        peers[m - 1].wait_recv()
        block = out.at[block_of(m) + c]
        forward = remote(block, block, send.at[3 + m], recv.at[3 + m], r, 1 - c)
        forward.start()
        forwards.append(forward)
    local.wait()
    sibling.wait()
    for copy in peers:
        copy.wait_send()
    for copy in forwards:
        copy.wait()


ROWS = 16


def by_rows(count, body):
    def step(i, carry):
        body(pl.ds(pl.multiple_of(i * ROWS, ROWS), ROWS))
        return carry

    lax.fori_loop(0, count // ROWS, step, 0)


def scatter_sum(parts, near, out2, far, s1, r1, s2, r2, total):
    r, c, t = place()
    order = (3, 1, 2, 0)
    first = {}
    for m in order:
        first[m] = remote(
            parts.at[block_of(m) + 1 - c], near.at[m], s1.at[m], r1.at[m], r, 1 - c
        )
        first[m].start()
    second = {}
    for m in order[:3]:
        first[m].wait_recv()
        block = block_of(m) + c

        def add(rows, m=m, block=block):
            out2[m - 1, rows, :] = (
                parts[block, rows, :].astype(jnp.float32) + near[m, rows, :].astype(jnp.float32)
            ).astype(jnp.bfloat16)

        by_rows(total.shape[0], add)
        second[m] = remote(
            out2.at[m - 1], far.at[m - 1], s2.at[m - 1], r2.at[m - 1], partner(r, m), c
        )
        second[m].start()
    first[0].wait_recv()
    own = t * 2 + c
    for m in (1, 2, 3):
        second[m].wait_recv()

    def fold(rows):
        total[rows, :] = (
            parts[own, rows, :].astype(jnp.float32)
            + near[0, rows, :].astype(jnp.float32)
            + far[0, rows, :].astype(jnp.float32)
            + far[1, rows, :].astype(jnp.float32)
            + far[2, rows, :].astype(jnp.float32)
        )

    by_rows(total.shape[0], fold)
    for m in order:
        first[m].wait_send()
    for m in (1, 2, 3):
        second[m].wait_send()


def scatter_scratch(slots, width):
    return [
        VMEM((TP, slots, width), jnp.bfloat16),
        VMEM((TP - 1, slots, width), jnp.bfloat16),
        VMEM((TP - 1, slots, width), jnp.bfloat16),
        pltpu.SemaphoreType.DMA((TP,)),
        pltpu.SemaphoreType.DMA((TP,)),
        pltpu.SemaphoreType.DMA((TP - 1,)),
        pltpu.SemaphoreType.DMA((TP - 1,)),
    ]


def gather_scratch():
    return [
        pltpu.SemaphoreType.DMA((7,)),
        pltpu.SemaphoreType.DMA((7,)),
        pltpu.SemaphoreType.DMA,
    ]


def strips(refs, shared, size):
    found, at = [], 0
    for ref, whole in zip(refs, shared):
        count = ref.shape[1] if whole else ref.shape[1] // TP
        found.append((ref, whole, count, at))
        at += count
    return found


def strip_views(refs, shared, owner, piece):
    for ref, whole, count, at in strips(refs, shared, piece.shape[1]):
        cols = slice(None) if whole else pl.ds(pl.multiple_of(owner * count, 128), count)
        yield ref.at[:, cols], piece.at[:, at : at + count]


def cut_start(refs, shared, place_of, send, recv, here):
    r, c, t = place()
    for source, target in strip_views(refs, shared, t, place_of()):
        pltpu.make_async_copy(source, target, here).start()
    for m in (3, 1, 2):
        other = partner(r, m)
        for source, target in strip_views(refs, shared, member(other), place_of()):
            remote(source, target, send.at[m], recv.at[m], other, c).start()


def piece_done(piece, sem):
    pltpu.make_async_copy(piece, piece, sem).wait()


def cut_finish(place_of, send, recv, here):
    piece_done(place_of(), here)
    for m in (3, 1, 2):
        piece_done(place_of(), send.at[m])
        piece_done(place_of(), recv.at[m])


def weight_copy(whole, mask, b, send, recv):
    r, c, t = place()
    n_row = lax.axis_size("row")
    at = whole.at[spot(turned_row(r, mask), n_row)]
    lands = mask | 1 << b
    return remote(at, at, send.at[lands], recv.at[lands], flip(r, b), c)


def weight_forward(masks, whole, send, recv):
    r, c, t = place()
    n_row = lax.axis_size("row")
    bits = data_bits(n_row)
    copies = []
    for mask in masks:
        at = whole.at[spot(turned_row(r, mask), n_row)]
        if mask:
            piece_done(at, recv.at[mask])
        last = max([-1] + [i for i, b in enumerate(bits) if mask >> b & 1])
        for b in bits[last + 1 :]:
            copies.append(weight_copy(whole, mask, b, send, recv))
            copies[-1].start()
    return copies


def weight_masks(n_row):
    held = [mask_of(m) for m in range(TP)]
    rounds = [held[1:]]
    for b in data_bits(n_row):
        rounds.append([mask | 1 << b for mask in held])
        held = held + rounds[-1]
    return rounds


def place_kernel(masks, n_row, *refs):
    slabs, whole, sems = refs[: len(masks)], refs[-2], refs[-1]
    r, c, t = place()
    copies = []
    for i, mask in enumerate(masks):
        at = whole.at[group_of(turned_row(r, mask), n_row)]
        copies.append(pltpu.make_async_copy(slabs[i], at, sems.at[i]))
        copies[-1].start()
    for copy in copies:
        copy.wait()


def place_slabs(masks, slabs, n_row):
    return pl.pallas_call(
        partial(place_kernel, masks, n_row),
        name="place",
        out_shape=jax.ShapeDtypeStruct((len(masks),) + slabs[0].shape, slabs[0].dtype),
        in_specs=[pl.BlockSpec(memory_space=ANY)] * len(masks),
        out_specs=pl.BlockSpec(memory_space=ANY),
        scratch_shapes=[pltpu.SemaphoreType.DMA((len(masks),))],
        compiler_params=pltpu.CompilerParams(vmem_limit_bytes=4 << 20),
        cost_estimate=cost(4),
    )(*slabs)


def exchange_rows(buf, land, send, recv):
    r, c, t = place()
    n_row = lax.axis_size("row")

    def copy(other):
        return remote(
            buf.at[other], land.at[r], send.at[other], recv.at[r], other, c
        )

    def start(off, carry):
        copy(lax.rem(r + off, n_row)).start()
        return carry

    lax.fori_loop(1, n_row, start, 0)


def finish_rows(buf, land, send, recv):
    r, c, t = place()
    n_row = lax.axis_size("row")

    def finish(off, carry):
        other = lax.rem(r + off, n_row)
        copy = remote(buf.at[other], land.at[other], send.at[other], recv.at[other], other, c)
        copy.wait_send()
        copy.wait_recv()
        return carry

    lax.fori_loop(1, n_row, finish, 0)


def greet_rows():
    r, c, t = place()
    n_row = lax.axis_size("row")
    barrier = pltpu.get_barrier_semaphore()

    def greet(off, carry):
        pl.semaphore_signal(
            barrier, inc=1, device_id=(lax.rem(r + off, n_row), c), device_id_type=MESH
        )
        return carry

    lax.fori_loop(1, n_row, greet, 0)
    pl.semaphore_signal(barrier, inc=1, device_id=(r, 1 - c), device_id_type=MESH)
    pl.semaphore_wait(barrier, n_row)


COLS = 512


def permute_out(choice, buf, first, second, slots):
    n_row = buf.shape[0]

    def column(i, carry):
        cols = pl.ds(pl.multiple_of(i * COLS, COLS), COLS)
        picked = matmul(choice[:, :slots], first[:, cols]) + matmul(choice[:, slots:], second[:, cols])
        buf[:, :, cols] = picked.astype(jnp.bfloat16).reshape(n_row, CHUNK, COLS)
        return carry

    lax.fori_loop(0, buf.shape[2] // COLS, column, 0)


def permute_in(choice, land, first, second, slots):
    n_row = land.shape[0]

    def column(i, carry):
        cols = pl.ds(pl.multiple_of(i * COLS, COLS), COLS)
        got = land[:, :, cols].reshape(n_row * CHUNK, COLS)
        first[:, cols] = matmul_left(choice[:, :slots], got).astype(jnp.bfloat16)
        second[:, cols] = matmul_left(choice[:, slots:], got).astype(jnp.bfloat16)
        return carry

    lax.fori_loop(0, land.shape[2] // COLS, column, 0)


def deal_kernel(
    meta, tokens, cotangent, gain, *refs
):
    in_refs, ff_refs, refs = refs[:8], refs[8:11], refs[11:]
    meta_all, give, take, x_out, gy_out, normed_all, gy_all, whole, slab_ff = refs[:9]
    x_mine, g_mine, buf, land, normed = refs[9:14]
    load, msend, mrecv, csend, crecv, nsend, nrecv, nhere, gsend, grecv, ghere = refs[14:25]
    wsend, wrecv, wcut, whole_here, fsend, frecv, fhere = refs[25:]
    r, c, t = place()
    n_row = lax.axis_size("row")
    slots = x_mine.shape[0]
    per_peer = slots // n_row
    loads = [
        pltpu.make_async_copy(tokens.at[c], x_mine, load.at[0]),
        pltpu.make_async_copy(cotangent.at[c], g_mine, load.at[1]),
    ]
    for copy in loads:
        copy.start()
    greet_rows()
    rounds = weight_masks(n_row)
    in_shared = [False, False, False, True, True, False, False, False]

    def in_place():
        return whole.at[spot(r, n_row)]

    def meta_copy(other, slot):
        return remote(meta, meta_all.at[slot], msend.at[other], mrecv.at[slot], other, c)

    def start(off, carry):
        meta_copy(lax.rem(r + off, n_row), r).start()
        return carry

    lax.fori_loop(1, n_row, start, 0)
    meta_all[r] = meta[...]

    def finish(off, carry):
        other = lax.rem(r + off, n_row)
        copy = meta_copy(other, other)
        copy.wait_send()
        copy.wait_recv()
        return carry

    lax.fori_loop(1, n_row, finish, 0)
    for source, target in strip_views(in_refs, in_shared, t, in_place()):
        pltpu.make_async_copy(source, target, whole_here).start()
    for m in (3, 1, 2):
        other = partner(r, m)
        for source, target in strip_views(in_refs, in_shared, member(other), in_place()):
            remote(source, target, wcut.at[m], wrecv.at[mask_of(m)], other, c).start()
    piece_done(in_place(), whole_here)
    forwards = weight_forward([0], whole, wsend, wrecv)

    shift = slots.bit_length() - 1
    row_no = lax.broadcasted_iota(jnp.int32, (CHUNK, slots), 0)
    wanted = jnp.where(row_no < per_peer, row_no, row_no - per_peer).astype(jnp.float32)
    early = row_no < per_peer
    late = (row_no >= per_peer) & (row_no < 2 * per_peer)
    tri = (
        lax.broadcasted_iota(jnp.int32, (slots, slots), 0)
        < lax.broadcasted_iota(jnp.int32, (slots, slots), 1)
    ).astype(jnp.float32).astype(jnp.bfloat16)
    places = lax.broadcasted_iota(jnp.int32, (slots, slots), 0)

    def order_of(block):
        picked = jnp.where(c == 0, block[0:1, :], block[1:2, :])
        return lax.shift_right_logical(picked, shift), picked - lax.shift_left(
            lax.shift_right_logical(picked, shift), shift
        )

    own_source, own_local = order_of(meta[...])

    def select(mask):
        wide = jnp.broadcast_to(mask.astype(jnp.float32), (CHUNK, slots)).astype(jnp.bfloat16)
        rank = matmul(wide, tri)
        return jnp.where(
            (rank == wanted) & (wide.astype(jnp.float32) > 0.5), 1.0, 0.0
        )

    def build(d, carry):
        rows = pl.ds(pl.multiple_of(d * CHUNK, CHUNK), CHUNK)
        source, local = order_of(meta_all[d])
        chosen = select(source == r).astype(jnp.bfloat16)
        at_home = (places == local).astype(jnp.float32).astype(jnp.bfloat16)
        picks = matmul_trans(chosen, at_home)
        give[rows, :slots] = jnp.where(early, picks, 0.0).astype(jnp.bfloat16)
        give[rows, slots:] = jnp.where(late, picks, 0.0).astype(jnp.bfloat16)
        kept = select(own_source == d)
        take[rows, :slots] = jnp.where(early, kept, 0.0).astype(jnp.bfloat16)
        take[rows, slots:] = jnp.where(late, kept, 0.0).astype(jnp.bfloat16)
        return carry

    lax.fori_loop(0, n_row, build, 0)
    for copy in loads:
        copy.wait()
    permute_out(give, buf, x_mine, g_mine, slots)
    exchange_rows(buf, land, csend, crecv)
    land[r] = buf[r]
    forwards = forwards + weight_forward(rounds[0], whole, wsend, wrecv)
    finish_rows(buf, land, csend, crecv)
    permute_in(take, land, x_out, gy_out, slots)

    def norm(rows):
        values = x_out[rows, :].astype(jnp.float32)
        scale = lax.rsqrt(jnp.mean(values * values, axis=-1, keepdims=True) + EPS)
        normed[rows, :] = (values * scale * gain[...]).astype(jnp.bfloat16)

    by_rows(slots, norm)
    first = gather_start(normed, normed_all, nsend, nrecv, nhere)
    cut_start(ff_refs, [False] * 3, lambda: slab_ff.at[t], fsend, frecv, fhere)
    second = gather_start(gy_out, gy_all, gsend, grecv, ghere)
    for masks in rounds[1:]:
        forwards = forwards + weight_forward(masks, whole, wsend, wrecv)
    gather_finish(first, normed_all, nsend, nrecv)
    gather_finish(second, gy_all, gsend, grecv)
    for copy in forwards:
        copy.wait_send()
    for m in (1, 2, 3):
        piece_done(in_place(), wcut.at[m])
    cut_finish(lambda: slab_ff.at[t], fsend, frecv, fhere)


def deal(meta, tokens, cotangent, gain, in_weights, ff_weights, n_row):
    slots, width = tokens.shape[1:]
    bf = jnp.bfloat16
    rows = in_weights[0].shape[0]
    in_cols = sum(
        array.shape[1] // (1 if i in (3, 4) else TP) for i, array in enumerate(in_weights)
    )
    ff_cols = sum(array.shape[1] for array in ff_weights) // TP
    vm, hb = pl.BlockSpec(memory_space=VMEM), pl.BlockSpec(memory_space=ANY)
    dma = pltpu.SemaphoreType.DMA
    return pl.pallas_call(
        deal_kernel,
        name="deal",
        out_shape=(
            jax.ShapeDtypeStruct((n_row, 8, 128), jnp.int32),
            jax.ShapeDtypeStruct((n_row * CHUNK, 2 * slots), bf),
            jax.ShapeDtypeStruct((n_row * CHUNK, 2 * slots), bf),
            jax.ShapeDtypeStruct((slots, width), bf),
            jax.ShapeDtypeStruct((slots, width), bf),
            jax.ShapeDtypeStruct((GROUP, slots, width), bf),
            jax.ShapeDtypeStruct((GROUP, slots, width), bf),
            jax.ShapeDtypeStruct((n_row, rows, in_cols), bf),
            jax.ShapeDtypeStruct((TP, rows, ff_cols), bf),
        ),
        in_specs=[vm, hb, hb, vm] + [hb] * 11,
        out_specs=(vm,) * 5 + (hb,) * 4,
        scratch_shapes=[
            VMEM((slots, width), bf),
            VMEM((slots, width), bf),
            VMEM((n_row, CHUNK, width), bf),
            VMEM((n_row, CHUNK, width), bf),
            VMEM((slots, width), bf),
            dma((2,)),
            dma((n_row,)),
            dma((n_row,)),
            dma((n_row,)),
            dma((n_row,)),
        ]
        + gather_scratch()
        + gather_scratch()
        + [dma((n_row,)), dma((n_row,)), dma((TP,)), dma]
        + [dma((TP,)), dma((TP,)), dma],
        compiler_params=params(0, 40),
        cost_estimate=cost(100),
    )(meta, tokens, cotangent, gain, *in_weights, *ff_weights)


def middle_kernel(parts, x, gain, mid, normed_all, near, out2, far, s1, r1, s2, r2, normed, nsend, nrecv, nhere):
    greet_group()
    scatter_sum(parts, near, out2, far, s1, r1, s2, r2, mid)

    def norm(rows):
        values = x[rows, :].astype(jnp.float32) + mid[rows, :]
        mid[rows, :] = values
        scale = lax.rsqrt(jnp.mean(values * values, axis=-1, keepdims=True) + EPS)
        normed[rows, :] = (values * scale * gain[...]).astype(jnp.bfloat16)

    by_rows(mid.shape[0], norm)
    started = gather_start(normed, normed_all, nsend, nrecv, nhere)
    gather_finish(started, normed_all, nsend, nrecv)


def middle(parts, x, gain):
    slots, width = x.shape
    return pl.pallas_call(
        middle_kernel,
        name="middle",
        out_shape=(
            jax.ShapeDtypeStruct((slots, width), jnp.float32),
            jax.ShapeDtypeStruct((GROUP, slots, width), jnp.bfloat16),
        ),
        in_specs=[pl.BlockSpec(memory_space=VMEM)] * 3,
        out_specs=(pl.BlockSpec(memory_space=VMEM), pl.BlockSpec(memory_space=ANY)),
        scratch_shapes=scatter_scratch(slots, width)
        + [VMEM((slots, width), jnp.bfloat16)]
        + gather_scratch(),
        compiler_params=params(1, 40),
        cost_estimate=cost(60),
    )(parts, x, gain)


def norm_back(values, gain, grad):
    inverse = lax.rsqrt(jnp.mean(values * values, axis=-1, keepdims=True) + EPS)
    scaled = grad * gain
    back = inverse * scaled - values * (
        inverse * inverse * inverse * jnp.mean(values * scaled, axis=-1, keepdims=True)
    )
    return back, jnp.sum(grad * values * inverse, axis=0, keepdims=True)


def turn_kernel(
    parts, mid, gy, gain, d_mid, d_gain, branch_all,
    near, out2, far, s1, r1, s2, r2, branch, nsend, nrecv, nhere,
):
    greet_group()
    scatter_sum(parts, near, out2, far, s1, r1, s2, r2, d_mid)
    d_gain[...] = jnp.zeros_like(d_gain)

    def back(rows):
        values = mid[rows, :]
        grad, gain_part = norm_back(values, gain[...], d_mid[rows, :])
        grad = gy[rows, :].astype(jnp.float32) + grad
        d_mid[rows, :] = grad
        branch[rows, :] = grad.astype(jnp.bfloat16)
        d_gain[...] += gain_part

    by_rows(mid.shape[0], back)
    started = gather_start(branch, branch_all, nsend, nrecv, nhere)
    gather_finish(started, branch_all, nsend, nrecv)


def turn(parts, mid, gy, gain):
    slots, width = mid.shape
    return pl.pallas_call(
        turn_kernel,
        name="turn",
        out_shape=(
            jax.ShapeDtypeStruct((slots, width), jnp.float32),
            jax.ShapeDtypeStruct((1, width), jnp.float32),
            jax.ShapeDtypeStruct((GROUP, slots, width), jnp.bfloat16),
        ),
        in_specs=[pl.BlockSpec(memory_space=VMEM)] * 4,
        out_specs=(pl.BlockSpec(memory_space=VMEM),) * 2 + (pl.BlockSpec(memory_space=ANY),),
        scratch_shapes=scatter_scratch(slots, width)
        + [VMEM((slots, width), jnp.bfloat16)]
        + gather_scratch(),
        compiler_params=params(2, 48),
        cost_estimate=cost(60),
    )(parts, mid, gy, gain)


def home_kernel(
    parts, x, d_mid, result, gain, give, take, small, output, gradient, small_all,
    near, out2, far, s1, r1, s2, r2, total, first, second, buf, land, csend, crecv, here, osend, orecv,
    d_gain, stages, stage_land, tsend, trecv, gsend, grecv, ghere,
):
    r, c, t = place()
    slots, width = x.shape
    bits = data_bits(lax.axis_size("row"))
    greet_rows()
    scatter_sum(parts, near, out2, far, s1, r1, s2, r2, total)
    d_gain[...] = jnp.zeros_like(d_gain)

    def back(rows):
        values = x[rows, :].astype(jnp.float32)
        grad, gain_part = norm_back(values, gain[...], total[rows, :])
        second[rows, :] = (d_mid[rows, :] + grad).astype(jnp.bfloat16)
        first[rows, :] = result[rows, :].astype(jnp.bfloat16)
        d_gain[...] += gain_part

    by_rows(slots, back)
    head = small.shape[0]
    stages[0, :head, :] = small[...]
    for k in range(width // 128):
        stages[0, head + k : head + k + 1, :] = d_gain[:, k * 128 : (k + 1) * 128]

    def stage_copy(i):
        return remote(
            stages.at[i], stage_land.at[i], tsend.at[i], trecv.at[i], flip(r, bits[i]), c
        )

    stage_copy(0).start()
    permute_out(take, buf, first, second, slots)
    exchange_rows(buf, land, csend, crecv)
    land[r] = buf[r]
    for i in range(len(bits)):
        stage_copy(i).wait()
        stages[i + 1] = stages[i] + stage_land[i]
        if i + 1 < len(bits):
            stage_copy(i + 1).start()
    started = gather_start(stages.at[len(bits)], small_all, gsend, grecv, ghere)
    finish_rows(buf, land, csend, crecv)
    permute_in(give, land, first, second, slots)
    copies = []
    for i, (mine, out) in enumerate(((first, output), (second, gradient))):
        copies.append(pltpu.make_async_copy(mine, out.at[c], here.at[i]))
        copies.append(remote(mine, out.at[c], osend.at[i], orecv.at[i], r, 1 - c))
    for copy in copies:
        copy.start()
    gather_finish(started, small_all, gsend, grecv)
    for copy in copies:
        copy.wait()


def send_home(parts, x, d_mid, result, gain, give, take, small, n_row):
    slots, width = x.shape
    bf = jnp.bfloat16
    size = small.shape[0] + width // 128
    phases = len(data_bits(n_row))
    return pl.pallas_call(
        home_kernel,
        name="home",
        out_shape=(
            jax.ShapeDtypeStruct((2, slots, width), bf),
            jax.ShapeDtypeStruct((2, slots, width), bf),
            jax.ShapeDtypeStruct((GROUP, size, 128), jnp.float32),
        ),
        in_specs=[pl.BlockSpec(memory_space=VMEM)] * 8,
        out_specs=(pl.BlockSpec(memory_space=ANY),) * 3,
        scratch_shapes=scatter_scratch(slots, width)
        + [
            VMEM((slots, width), jnp.float32),
            VMEM((slots, width), bf),
            VMEM((slots, width), bf),
            VMEM((n_row, CHUNK, width), bf),
            VMEM((n_row, CHUNK, width), bf),
            pltpu.SemaphoreType.DMA((n_row,)),
            pltpu.SemaphoreType.DMA((n_row,)),
            pltpu.SemaphoreType.DMA((2,)),
            pltpu.SemaphoreType.DMA((2,)),
            pltpu.SemaphoreType.DMA((2,)),
            VMEM((1, width), jnp.float32),
            VMEM((phases + 1, size, 128), jnp.float32),
            VMEM((phases, size, 128), jnp.float32),
            pltpu.SemaphoreType.DMA((phases,)),
            pltpu.SemaphoreType.DMA((phases,)),
        ]
        + gather_scratch(),
        compiler_params=params(3, 48),
        cost_estimate=cost(75),
    )(parts, x, d_mid, result, gain, give, take, small)


def blocks_start(low, land, s1, r1):
    r, c, t = place()
    copies = []
    for m, f in CROSSED:
        col = 1 - c if f else c
        k = m * 2 + f
        copies.append(
            remote(low.at[block_of(m) + col], land.at[k], s1.at[k], r1.at[k], partner(r, m), col)
        )
        copies[-1].start()
    return copies


def blocks_turn(first, low, land, mine, total, s2, r2, here):
    r, c, t = place()
    own = t * 2 + c
    for copy in first:
        copy.wait_recv()
    summed = low[own].astype(jnp.float32)
    for m, f in CROSSED:
        summed = summed + land[m * 2 + f].astype(jnp.float32)
    mine[...] = summed.astype(jnp.bfloat16)
    copies = [pltpu.make_async_copy(mine, total.at[own], here)]
    for m, f in CROSSED:
        k = m * 2 + f
        copies.append(
            remote(mine, total.at[own], s2.at[k], r2.at[k], partner(r, m), 1 - c if f else c)
        )
    for copy in copies:
        copy.start()
    return copies


def blocks_finish(first, second):
    for copy in first:
        copy.wait_send()
    for copy in second:
        copy.wait()


CROSSED = [(m, f) for m in (3, 1, 2) for f in (0, 1)] + [(0, 1)]


def blocks_scratch(slots):
    dma = pltpu.SemaphoreType.DMA
    return [
        VMEM((GROUP, slots, slots), jnp.bfloat16),
        VMEM((GROUP, slots, slots), jnp.bfloat16),
        VMEM((slots, slots), jnp.bfloat16),
        dma((GROUP,)),
        dma((GROUP,)),
        dma((GROUP,)),
        dma((GROUP,)),
        dma,
    ]


def dot(first_op, second_op, first_dim, second_dim, precision=None):
    return lax.dot_general(
        first_op,
        second_op,
        (((first_dim,), (second_dim,)), ((), ())),
        precision=precision,
        preferred_element_type=jnp.float32,
    )


def block_rows(b, slots):
    return pl.ds(pl.multiple_of(b * slots, slots), slots)


def marks(lens, b, slots):
    row = lax.broadcasted_iota(jnp.int32, (slots, slots), 0)
    col = lax.broadcasted_iota(jnp.int32, (slots, slots), 1)
    row_segment, col_segment, within = jnp.zeros_like(row), jnp.zeros_like(row), row
    end = 0
    for k in range(lens.shape[1] - 1):
        end = end + lens[b, k]
        row_segment = row_segment + (row >= end).astype(jnp.int32)
        col_segment = col_segment + (col >= end).astype(jnp.int32)
        within = jnp.where(row >= end, row - end, within)
    return (row_segment == col_segment) & (row >= col), within


def conv_pre(values, within, weights):
    width = values.shape[1]
    shifted = [values]
    for k in range(1, 4):
        valid = within[:, :1] >= k
        shifted.append(jnp.where(valid, pltpu.roll(values, k, 0), 0.0))
    pre = weights[4:5, :]
    for k in range(4):
        pre = pre + weights[3 - k : 4 - k, :] * shifted[k]
    return pre, shifted


def conv_back(grad, pre, shifted, within, weights):
    slots = grad.shape[0]
    gate = jax.nn.sigmoid(pre)
    e = grad * gate * (1.0 + pre * (1.0 - gate))
    sums = [jnp.sum(e * shifted[3 - i], axis=0, keepdims=True) for i in range(4)]
    sums.append(jnp.sum(e, axis=0, keepdims=True))
    back = weights[3:4, :] * e
    for k in range(1, 4):
        valid = within[:, :1] >= k
        back = back + weights[3 - k : 4 - k, :] * pltpu.roll(jnp.where(valid, e, 0.0), slots - k, 0)
    return back, sums


def softplus(values):
    return jnp.maximum(values, 0.0) + jnp.log1p(jnp.exp(-jnp.abs(values)))


def steps_and_levels(mixed, side, low, count):
    slots, width = mixed.shape
    lane = lax.broadcasted_iota(jnp.int32, (slots, width), 1)
    inside = (lane >= low) & (lane < low + count)
    step = jnp.where(inside, softplus(mixed + side[5:6, :]), 0.0)
    rate = jnp.where(inside, -jnp.exp(side[6:7, :]), 0.0)
    row = lax.broadcasted_iota(jnp.int32, (slots, slots), 0)
    col = lax.broadcasted_iota(jnp.int32, (slots, slots), 1)
    tri = (row >= col).astype(jnp.float32)
    level = dot(tri, step * rate, 1, 0, HIGH)
    return step, rate, level, tri, inside


def halves(first, second):
    lane = lax.broadcasted_iota(jnp.int32, first.shape, 1)
    return jnp.where(lane < first.shape[1] // 2, first, second)


def state_parts(mixed, within, side, sh):
    pre, shifted = conv_pre(mixed, within, side)
    act = pre * jax.nn.sigmoid(pre)
    lane = lax.broadcasted_iota(jnp.int32, act.shape, 1)
    first = jnp.where(lane < sh, act, 0.0).astype(jnp.bfloat16)
    second = jnp.where(lane < sh, pltpu.roll(act, act.shape[1] - sh, 1), 0.0).astype(jnp.bfloat16)
    return first, second, pre, shifted


def turned_pair(values, waves):
    half = values.shape[1] // 2
    return values * waves[:, : 2 * half] + pltpu.roll(values, half, 1) * waves[:, 2 * half :]


def turned_back(values, waves):
    half = values.shape[1] // 2
    return values * waves[:, : 2 * half] - pltpu.roll(values, half, 1) * waves[:, 2 * half :]


def wave_rows(within, table):
    slots = within.shape[0]
    picks = (within == lax.broadcasted_iota(jnp.int32, (slots, slots), 1)).astype(jnp.float32)
    return dot(picks, table[...], 1, 0, HIGH)


def attend(projected, rows, at, lens, table, b, slots):
    allowed, within = marks(lens, b, slots)
    waves = wave_rows(within, table)
    query = turned_pair(projected[rows, at : at + HD], waves).astype(jnp.bfloat16)
    key = turned_pair(projected[rows, at + HD : at + 2 * HD], waves).astype(jnp.bfloat16)
    value = projected[rows, at + 2 * HD : at + 3 * HD].astype(jnp.bfloat16)
    scores = jnp.where(allowed, dot(query, key, 1, 1) * HD ** (-0.5), NEG_LARGE)
    exps = jnp.exp(scores - jnp.max(scores, axis=-1, keepdims=True))
    probs = exps / jnp.sum(exps, axis=-1, keepdims=True)
    return query, key, value, probs, waves


def each_block(first, last, body):
    def step(b, carry):
        body(b)
        return carry

    lax.fori_loop(first, last, step, 0)


def mixer_kernel(
    sh, ph, lens, projected, chan, side, table, branch, scanned, crossed,
    low, land, mine, s1, r1, s2, r2, here, conv,
):
    slots = crossed.shape[1]
    mh = chan.shape[1]
    heads_at = 2 * sh
    greet_group(cross=True)

    def before(b):
        rows = block_rows(b, slots)
        allowed, within = marks(lens, b, slots)
        pre, unused = conv_pre(projected[rows, mh : 2 * mh], within, chan)
        conv[rows, :] = pre * jax.nn.sigmoid(pre)
        mixed = projected[rows, 2 * mh + 3 * HD :]
        first, second, unused, unused = state_parts(mixed, within, side, sh)
        low[b] = dot(second, first, 1, 1).astype(jnp.bfloat16)

    def attention(b):
        rows = block_rows(b, slots)
        query, key, value, probs, waves = attend(projected, rows, 2 * mh, lens, table, b, slots)
        branch[rows, mh:] = dot(probs.astype(jnp.bfloat16), value, 1, 0).astype(jnp.bfloat16)

    def after(b):
        rows = block_rows(b, slots)
        allowed, within = marks(lens, b, slots)
        mixed = projected[rows, 2 * mh + 3 * HD :]
        step, rate, level, tri, inside = steps_and_levels(mixed, side, heads_at, ph)
        step_t, level_t = step.T, level.T
        cross = crossed[b].astype(jnp.float32)
        for pair in range(ph // 2):
            cols = slice(pair * 128, (pair + 1) * 128)
            convs = conv[rows, cols]
            conv_low = convs.astype(jnp.bfloat16)
            outs = []
            for h in (2 * pair, 2 * pair + 1):
                at = heads_at + h
                spread = level[:, at : at + 1] - level_t[at : at + 1, :]
                decay = jnp.exp(jnp.where(allowed, spread, NEG_LARGE))
                mixing = cross * decay * step_t[at : at + 1, :]
                outs.append(dot(mixing.astype(jnp.bfloat16), conv_low, 1, 0))
            total = halves(outs[0], outs[1])
            scanned[rows, cols] = total
            gate = projected[rows, cols]
            gated = (total + chan[5:6, cols] * convs) * (gate * jax.nn.sigmoid(gate))
            branch[rows, cols] = gated.astype(jnp.bfloat16)

    each_block(0, GROUP, before)
    first = blocks_start(low, land, s1, r1)
    each_block(0, GROUP // 2, attention)
    second = blocks_turn(first, low, land, mine, crossed, s2, r2, here)
    each_block(GROUP // 2, GROUP, attention)
    blocks_finish(first, second)
    each_block(0, GROUP, after)


def mixer(lens, projected, chan, side, table, sh, ph):
    tokens = projected.shape[0]
    slots = tokens // GROUP
    mh = chan.shape[1]
    vm = pl.BlockSpec(memory_space=VMEM)
    return pl.pallas_call(
        partial(mixer_kernel, sh, ph),
        name="mixer",
        out_shape=(
            jax.ShapeDtypeStruct((tokens, mh + HD), jnp.bfloat16),
            jax.ShapeDtypeStruct((tokens, mh), jnp.float32),
            jax.ShapeDtypeStruct((GROUP, slots, slots), jnp.bfloat16),
        ),
        in_specs=[pl.BlockSpec(memory_space=pltpu.SMEM)] + [vm] * 4,
        out_specs=(vm,) * 3,
        scratch_shapes=blocks_scratch(slots) + [VMEM((tokens, mh), jnp.float32)],
        compiler_params=params(4, 40),
        cost_estimate=cost(30),
    )(lens, projected, chan, side, table)


def mixer_back_kernel(
    sh, ph, lens, projected, chan, side, table, scanned, crossed, grads, out, chan_sums, side_sums,
    low, land, mine, s1, r1, s2, r2, here, summed, misc,
):
    slots = crossed.shape[1]
    mh = chan.shape[1]
    heads_at = 2 * sh
    bf = jnp.bfloat16
    greet_group(cross=True)
    chan_sums[...] = jnp.zeros_like(chan_sums)
    side_sums[...] = jnp.zeros_like(side_sums)

    def scan(b):
        rows = block_rows(b, slots)
        allowed, within = marks(lens, b, slots)
        mixed = projected[rows, 2 * mh + 3 * HD :]
        step, rate, level, tri, inside = steps_and_levels(mixed, side, heads_at, ph)
        step_t, level_t = step.T, level.T
        cross = crossed[b].astype(jnp.float32)
        lane = lax.broadcasted_iota(jnp.int32, (slots, 128), 1)
        place_row = lax.broadcasted_iota(jnp.int32, (slots, slots), 0)
        grad_cross = jnp.zeros((slots, slots), jnp.float32)
        row_sums = jnp.zeros((slots, slots), jnp.float32)
        col_sums = jnp.zeros((slots, slots), jnp.float32)
        for pair in range(ph // 2):
            cols = slice(pair * 128, (pair + 1) * 128)
            weights = chan[:, cols]
            pre, shifted = conv_pre(
                projected[rows, mh + pair * 128 : mh + (pair + 1) * 128], within, weights
            )
            convs = pre * jax.nn.sigmoid(pre)
            conv_low = convs.astype(bf)
            gate = projected[rows, cols]
            sig = jax.nn.sigmoid(gate)
            grad = grads[rows, cols]
            skip = weights[5:6, :]
            grad_mix = grad * (gate * sig)
            out[rows, cols] = (
                grad * (scanned[rows, cols] + skip * convs) * (sig * (1.0 + gate * (1.0 - sig)))
            ).astype(bf)
            skip_sum = jnp.sum(grad_mix * convs, axis=0, keepdims=True)
            grad_low = grad_mix.astype(bf)
            backs = []
            for f in (0, 1):
                at = heads_at + 2 * pair + f
                mask = lane < 64 if f == 0 else lane >= 64
                spread = level[:, at : at + 1] - level_t[at : at + 1, :]
                decay = jnp.exp(jnp.where(allowed, spread, NEG_LARGE))
                step_row = step_t[at : at + 1, :]
                mixing = cross * decay * step_row
                backs.append(dot(mixing.astype(bf), grad_low, 0, 0))
                grad_mixing = dot(jnp.where(mask, grad_mix, 0.0).astype(bf), conv_low, 1, 1)
                weighted = grad_mixing * decay
                grad_cross = grad_cross + weighted * step_row
                weighted = weighted * cross
                col = jnp.sum(weighted, axis=0, keepdims=True)
                row = jnp.sum(weighted * step_row, axis=1, keepdims=True)
                row_sums = jnp.where(lane == at, row, row_sums)
                col_sums = jnp.where(place_row == at, col, col_sums)
            grad_conv = grad_mix * skip + halves(backs[0], backs[1])
            back, sums = conv_back(grad_conv, pre, shifted, within, weights)
            out[rows, mh + pair * 128 : mh + (pair + 1) * 128] = back.astype(bf)
            for i, part in enumerate(sums + [skip_sum]):
                chan_sums[i : i + 1, cols] += part
        low[b] = grad_cross.astype(bf)
        col_sums = col_sums.T
        grad_level = row_sums - step * col_sums
        grad_rate_step = dot(tri, grad_level, 0, 0, HIGH)
        grad_step = (col_sums + grad_rate_step * rate) * jax.nn.sigmoid(mixed + side[5:6, :])
        grad_step = jnp.where(inside, grad_step, 0.0)
        misc[rows, :] = grad_step
        side_sums[5:6, :] += jnp.sum(grad_step, axis=0, keepdims=True)
        side_sums[6:7, :] += jnp.sum(grad_rate_step * step, axis=0, keepdims=True) * rate[:1, :]

    def attention(b):
        rows = block_rows(b, slots)
        at = 2 * mh
        query, key, value, probs, waves = attend(projected, rows, at, lens, table, b, slots)
        grad = grads[rows, mh:].astype(bf)
        grad_probs = dot(grad, value, 1, 1)
        out[rows, at + 2 * HD : at + 3 * HD] = dot(probs.astype(bf), grad, 0, 0).astype(bf)
        grad_raw = probs * (grad_probs - jnp.sum(grad_probs * probs, axis=-1, keepdims=True))
        grad_raw = (grad_raw * HD ** (-0.5)).astype(bf)
        out[rows, at : at + HD] = turned_back(dot(grad_raw, key, 1, 0), waves).astype(bf)
        out[rows, at + HD : at + 2 * HD] = turned_back(dot(grad_raw, query, 0, 0), waves).astype(bf)

    def state(b):
        rows = block_rows(b, slots)
        allowed, within = marks(lens, b, slots)
        mixed = projected[rows, 2 * mh + 3 * HD :]
        first, second, pre, shifted = state_parts(mixed, within, side, sh)
        lane = lax.broadcasted_iota(jnp.int32, pre.shape, 1)
        grad_first = dot(summed[b], second, 0, 0)
        grad_second = pltpu.roll(dot(summed[b], first, 1, 0), sh, 1)
        grad = jnp.where(lane < sh, grad_first, jnp.where(lane < 2 * sh, grad_second, 0.0))
        back, sums = conv_back(grad, pre, shifted, within, side)
        out[rows, 2 * mh + 3 * HD :] = jnp.where(lane < 2 * sh, back, misc[rows, :]).astype(bf)
        for i, part in enumerate(sums):
            side_sums[i : i + 1, :] += part

    each_block(0, GROUP, scan)
    begun = blocks_start(low, land, s1, r1)
    each_block(0, GROUP // 2, attention)
    done = blocks_turn(begun, low, land, mine, summed, s2, r2, here)
    each_block(GROUP // 2, GROUP, attention)
    blocks_finish(begun, done)
    each_block(0, GROUP, state)


def mixer_back(lens, projected, chan, side, table, scanned, crossed, grads, sh, ph):
    tokens = projected.shape[0]
    slots = tokens // GROUP
    mh = chan.shape[1]
    vm = pl.BlockSpec(memory_space=VMEM)
    return pl.pallas_call(
        partial(mixer_back_kernel, sh, ph),
        name="mixer_back",
        out_shape=(
            jax.ShapeDtypeStruct(projected.shape, jnp.bfloat16),
            jax.ShapeDtypeStruct(chan.shape, jnp.float32),
            jax.ShapeDtypeStruct(side.shape, jnp.float32),
        ),
        in_specs=[pl.BlockSpec(memory_space=pltpu.SMEM)] + [vm] * 7,
        out_specs=(vm,) * 3,
        scratch_shapes=blocks_scratch(slots)
        + [
            VMEM((GROUP, slots, slots), jnp.bfloat16),
            VMEM((tokens, 128), jnp.float32),
        ],
        compiler_params=params(5, 48),
        cost_estimate=cost(50),
    )(lens, projected, chan, side, table, scanned, crossed, grads)


def swiglu(ff_gate, ff_up):
    return jax.nn.silu(ff_gate) * ff_up


def cut(array, parts, axis=1):
    rows, cols = array.shape
    return array.reshape(rows, parts, cols // parts).transpose(1, 0, 2)


def local(
    tokens,
    cotangent,
    deal_order,
    seq_lengths,
    mixer_norm_gain,
    mamba_gate_weight,
    mamba_input_weight,
    state_weight,
    step_weight,
    conv_input,
    conv_input_bias,
    conv_state,
    conv_state_bias,
    step_bias,
    decay_log,
    skip_scale,
    mamba_out_weight,
    query_weight,
    key_weight,
    value_weight,
    attn_out_weight,
    ff_norm_gain,
    gate_weight,
    up_weight,
    down_weight,
):
    n_row = lax.axis_size("row")
    r = lax.axis_index("row")
    c = lax.axis_index("col")
    t = member(r)
    bits = data_bits(n_row)
    n_bits = n_row.bit_length() - 1
    slots, width = tokens.shape[1:]
    bf = jnp.bfloat16
    rows = mamba_gate_weight.shape[0]
    mh = mamba_gate_weight.shape[1] // TP
    qh = query_weight.shape[1] // TP
    kvh = key_weight.shape[1]
    sh = state_weight.shape[1] // (2 * GROUP)
    ph = step_weight.shape[1] // TP
    fh = gate_weight.shape[1] // TP
    used = 2 * mh + qh + 2 * kvh + 2 * sh + ph
    spare = -used % 256

    half = state_weight.shape[1] // 2
    state_in_part = lax.dynamic_slice_in_dim(state_weight[:, :half], c * (half // 2), half // 2, 1)
    state_out_part = lax.dynamic_slice_in_dim(state_weight[:, half:], c * (half // 2), half // 2, 1)
    mixed = jnp.concatenate(
        [
            state_in_part.reshape(rows, TP, sh),
            state_out_part.reshape(rows, TP, sh),
            step_weight.reshape(rows, TP, ph),
            jnp.zeros((rows, TP, spare), bf),
        ],
        axis=2,
    ).reshape(rows, TP * (2 * sh + ph + spare))
    in_weights = (
        mamba_gate_weight, mamba_input_weight, query_weight, key_weight, value_weight, mixed,
        mamba_out_weight.T, attn_out_weight.T,
    )
    ff_weights = (gate_weight, up_weight, down_weight.T)

    def assemble(slab):
        held = [(0, slab)]
        for b in bits:
            held = held + [
                (mask | 1 << b, lax.ppermute(part, "row", flips(n_row, 1 << b))) for mask, part in held
            ]
        return place_slabs(
            [mask for mask, part in held], [part for mask, part in held], n_row
        ).reshape(n_row * rows, slab.shape[2])

    def pick(array, index, axis=0):
        return lax.dynamic_index_in_dim(array, index, axis, keepdims=False)

    by_group = sorted(range(n_row), key=lambda row: [row >> b & 1 for b in bits])
    alike = [
        [row for row in by_group if [row >> b & 1 for b in TP_BITS] == [m & 1, m >> 1]]
        for m in range(TP)
    ]

    def sum_groups(grad, after=None):
        grad = grad.astype(bf)
        if after is not None:
            grad, after = lax.optimization_barrier((grad, after))
        part = lax.psum_scatter(
            grad, "row", scatter_dimension=0, axis_index_groups=alike, tiled=True
        ).reshape(TP, rows, grad.shape[1])
        return part, after

    def disperse(part):
        near = [pick(part, t)] + [
            lax.ppermute(pick(part, member(partner(r, m))), "row", flips(n_row, mask_of(m)))
            for m in (1, 2, 3)
        ]
        low, high = bit(r, TP_BITS[0]), bit(r, TP_BITS[1])

        def of(owner):
            inner = [
                jnp.where(low == owner % 2, near[2 * k], near[2 * k + 1]) for k in range(2)
            ]
            return jnp.where(high == owner // 2, inner[0], inner[1])

        return jnp.stack([of(owner) for owner in range(TP)])

    order = [n_bits - 1 - b for b in bits] + [n_bits - 1 - b for b in reversed(TP_BITS)]

    def regroup(array):
        lead = array.shape[:-1]
        cutup = array.reshape(lead + (2,) * n_bits + (rows,))
        dims = list(range(len(lead))) + [len(lead) + i for i in order] + [len(lead) + n_bits]
        return cutup.transpose(dims).reshape(array.shape)

    def ungroup(array):
        lead = array.shape[:-1]
        cutup = array.reshape(lead + (2,) * n_bits + (rows,))
        back = [order.index(i) for i in range(n_bits)]
        dims = list(range(len(lead))) + [len(lead) + i for i in back] + [len(lead) + n_bits]
        return cutup.transpose(dims).reshape(array.shape)

    mixer_gain = regroup(mixer_norm_gain)[None, :]
    ff_gain = regroup(ff_norm_gain)[None, :]

    meta = jnp.concatenate(
        [
            deal_order,
            jnp.pad(seq_lengths[:, 0, :], ((0, 0), (0, 128 - seq_lengths.shape[2]))),
            jnp.zeros((4, 128), jnp.int32),
        ],
        axis=0,
    )
    meta_all, give, take, x_home, gy_home, normed_one, gy_all, w_mixer, slab_ff = deal(
        meta, regroup(tokens), regroup(cotangent), mixer_gain, in_weights, ff_weights, n_row
    )
    normed_one = normed_one.reshape(GROUP * slots, width)
    gy_all = gy_all.reshape(GROUP * slots, width)
    w_mixer = w_mixer.reshape(width, -1)
    w_in, w_out = w_mixer[:, : used + spare], w_mixer[:, used + spare :]
    w_ff = assemble(slab_ff)
    w_gate_up = w_ff[:, : 2 * fh]
    w_down = w_ff[:, 2 * fh :]

    def across(array):
        return lax.ppermute(array, "col", [(0, 1), (1, 0)])

    base = r - bit(r, TP_BITS[0]) * (1 << TP_BITS[0]) - bit(r, TP_BITS[1]) * (1 << TP_BITS[1])
    group_meta = jnp.stack([pick(meta_all, base + mask_of(m)) for m in range(TP)])
    lengths = group_meta[:, 2:4, : seq_lengths.shape[2]].reshape(GROUP, seq_lengths.shape[2])
    half_dim = HD // 2
    inverse = ROPE_BASE ** (-2.0 * jnp.arange(half_dim, dtype=jnp.float32) / HD)
    angles = jnp.arange(slots, dtype=jnp.float32)[:, None] * inverse[None, :]
    cosine, sine = jnp.cos(angles), jnp.sin(angles)
    table = jnp.concatenate([cosine, cosine, -sine, sine], axis=1)

    def piece(array, size, start):
        return lax.dynamic_slice_in_dim(array, start, size, array.ndim - 1)

    eighth = c * TP + t
    chan = jnp.concatenate(
        [
            piece(conv_input, mh, t * mh),
            piece(conv_input_bias[None], mh, t * mh),
            jnp.repeat(piece(skip_scale[None], ph, t * ph), mh // ph, axis=1),
            jnp.zeros((2, mh), jnp.float32),
        ],
        axis=0,
    )
    states = jnp.concatenate([conv_state, conv_state_bias[None]], axis=0)
    states = jnp.concatenate(
        [piece(states, sh, eighth * sh), piece(states, sh, half + eighth * sh)], axis=1
    )
    heads = jnp.concatenate(
        [piece(step_bias[None], ph, t * ph), piece(decay_log[None], ph, t * ph)], axis=0
    )
    after = 128 - 2 * sh - ph
    side = jnp.concatenate(
        [
            jnp.pad(states, ((0, 0), (0, 128 - 2 * sh))),
            jnp.pad(heads, ((0, 0), (2 * sh, after))),
            jnp.zeros((1, 128), jnp.float32),
        ],
        axis=0,
    )

    projected = matmul(normed_one, w_in)
    edges = [0, mh, 2 * mh, 2 * mh + qh, 2 * mh + qh + kvh, 2 * mh + qh + 2 * kvh]
    edges = edges + [edges[-1] + 2 * sh, edges[-1] + 2 * sh + ph]
    branch_in, scanned, crossed = mixer(lengths, projected, chan, side, table, sh, ph)
    branch_part = matmul_trans(branch_in, w_out).astype(bf).reshape(GROUP, slots, width)
    mid, normed_two = middle(branch_part, x_home, ff_gain)
    normed_two = normed_two.reshape(GROUP * slots, width)

    ff_gate_up = matmul(normed_two, w_gate_up)
    ff_gate, ff_up = ff_gate_up[:, :fh], ff_gate_up[:, fh:]
    ff_hidden = swiglu(ff_gate, ff_up).astype(bf)
    ff_part = matmul_trans(ff_hidden, w_down).astype(bf).reshape(GROUP, slots, width)
    grad_hidden = matmul(gy_all, w_down)
    unused_value, pullback = jax.vjp(swiglu, ff_gate, ff_up)
    grad_gate, grad_up = pullback(grad_hidden)
    grad_gate_up = jnp.concatenate([grad_gate.astype(bf), grad_up.astype(bf)], axis=1)
    normed_two_part = (
        matmul_trans(grad_gate_up, w_gate_up).astype(bf).reshape(GROUP, slots, width)
    )
    grad_ff = jnp.concatenate(
        [matmul_left(normed_two, grad_gate_up).astype(bf), matmul_left(gy_all, ff_hidden).astype(bf)],
        axis=1,
    )
    normed_two_part, grad_ff = lax.optimization_barrier((normed_two_part, grad_ff))
    ff_sums, unused_value = sum_groups(grad_ff)
    d_mid, delta_ff_gain, branch_all = turn(
        normed_two_part, mid, gy_home, ff_gain
    )
    ff_pairs = ff_part.reshape(TP, 2, slots, width)
    ff_sum = (
        pick(ff_pairs, c, 1).astype(jnp.float32)
        + across(pick(ff_pairs, 1 - c, 1)).astype(jnp.float32)
    ).astype(bf)
    result = mid + pick(ff_sum, t).astype(jnp.float32)
    for m in (1, 2, 3):
        result = result + lax.ppermute(
            pick(ff_sum, member(partner(r, m))), "row", flips(n_row, mask_of(m))
        ).astype(jnp.float32)
    result = result.astype(bf)
    branch_all = branch_all.reshape(GROUP * slots, width)

    out_sums, ff_sums = sum_groups(matmul_left(branch_all, branch_in), ff_sums)
    grad_branch_in = matmul(branch_all, w_out)
    grad_projected, chan_sums, side_sums = mixer_back(
        lengths, projected, chan, side, table, scanned, crossed, grad_branch_in, sh, ph
    )
    early = jnp.concatenate([grad_projected[:, :mh], grad_projected[:, 2 * mh : edges[5]]], axis=1)
    early_sums, out_sums = sum_groups(matmul_left(normed_one, early), out_sums)
    grad_late = matmul_left(
        normed_one, jnp.concatenate([grad_projected[:, mh : 2 * mh], grad_projected[:, edges[5] :]], axis=1)
    ).astype(bf)
    grad_projected, grad_late = lax.optimization_barrier((grad_projected, grad_late))
    late_sums, early_sums = sum_groups(grad_late, early_sums)
    normed_one_part = matmul_trans(grad_projected, w_in).astype(bf).reshape(GROUP, slots, width)

    def lanes(array):
        array = array.reshape((-1, array.shape[-1]))
        array = jnp.pad(array, ((0, 0), (0, -array.shape[1] % 128)))
        return array.reshape(-1, 128)

    small_parts = [
        lanes(part)
        for part in (
            chan_sums[:4],
            chan_sums[4:5],
            side_sums[5:6, 2 * sh : 2 * sh + ph],
            side_sums[6:7, 2 * sh : 2 * sh + ph],
            jnp.sum(chan_sums[5].reshape(ph, -1), axis=1)[None],
            side_sums[:4, : 2 * sh],
            side_sums[4:5, : 2 * sh],
            delta_ff_gain,
        )
    ]
    counts = [part.shape[0] for part in small_parts] + [width // 128]
    small_parts.append(jnp.zeros((-sum(counts) % 8, 128), jnp.float32))
    starts = [sum(counts[:i]) for i in range(len(counts))]
    starts[-1] += small_parts[-1].shape[0]
    output, grad_tokens, small_all = send_home(
        normed_one_part, x_home, d_mid, result, mixer_gain, give, take,
        jnp.concatenate(small_parts, axis=0), n_row,
    )
    delta_ff, delta_out, delta_early, delta_late = (
        disperse(part) for part in (ff_sums, out_sums, early_sums, late_sums)
    )
    delta_in = jnp.concatenate(
        [delta_early[:, :, :mh], delta_late[:, :, :mh], delta_early[:, :, mh:], delta_late[:, :, mh:]], axis=2
    )

    def join(stacked):
        return stacked.transpose(1, 0, 2).reshape(stacked.shape[1], -1).astype(jnp.float32)

    pieces = [delta_in[:, :, low:high] for low, high in zip(edges[:-1], edges[1:])]
    state_mine = pieces[5]
    state_other = across(state_mine)
    state_first = jnp.where(c == 0, state_mine, state_other)
    state_second = jnp.where(c == 0, state_other, state_mine)
    delta_state = jnp.concatenate(
        [
            join(state_first[:, :, :sh]),
            join(state_second[:, :, :sh]),
            join(state_first[:, :, sh:]),
            join(state_second[:, :, sh:]),
        ],
        axis=1,
    )
    delta_key = jnp.sum(pieces[3].astype(jnp.float32), axis=0)
    delta_value = jnp.sum(pieces[4].astype(jnp.float32), axis=0)

    small_all = small_all.reshape(TP, 2, -1, 128)
    small_col = pick(small_all, c, 1)

    def taken(array, i):
        return lax.slice_in_dim(array, starts[i], starts[i] + counts[i], axis=array.ndim - 2)

    def along(array, i, size):
        got = taken(array, i).reshape(TP, -1, size + -size % 128)[:, :, :size]
        return got.transpose(1, 0, 2).reshape(got.shape[1], TP * size)

    def state_along(i):
        got = taken(small_all, i)[..., : 2 * sh].reshape(TP, 2, -1, 2, sh)
        return got.transpose(2, 3, 1, 0, 4).reshape(got.shape[2], 2 * half)

    def over_all(i):
        return ungroup(jnp.sum(taken(small_all, i), axis=(0, 1)).reshape(width))

    by_col = [
        along(small_col, 0, mh),
        along(small_col, 1, mh)[0],
        along(small_col, 2, ph)[0],
        along(small_col, 3, ph)[0],
        along(small_col, 4, ph)[0],
    ]
    by_all = [state_along(5), state_along(6)[0], over_all(8), over_all(7)]

    return (
        ungroup(output),
        ungroup(grad_tokens),
        by_all[2],
        join(pieces[0]),
        join(pieces[1]),
        delta_state,
        join(pieces[6]),
        by_col[0],
        by_col[1],
        by_all[0],
        by_all[1],
        by_col[2],
        by_col[3],
        by_col[4],
        join(delta_out[:, :, :mh]).T,
        join(pieces[2]),
        delta_key,
        delta_value,
        join(delta_out[:, :, mh:]).T,
        by_all[3],
        join(delta_ff[:, :, :fh]),
        join(delta_ff[:, :, fh : 2 * fh]),
        join(delta_ff[:, :, 2 * fh :]).T,
    )


def solution(mesh):
    both = P("row", "col")
    turned = P("col", "row")
    in_specs = (
        P(None, "row", None),
        P(None, "row", None),
        P(None, "row"),
        P(None, "row", None),
        P(),
        both,
        both,
        P("row", None),
        both,
        P(None, "col"),
        P("col"),
        P(),
        P(),
        P("col"),
        P("col"),
        P("col"),
        turned,
        both,
        both,
        both,
        turned,
        P(),
        both,
        both,
        turned,
    )
    out_specs = (
        P(None, "row", None),
        P(None, "row", None),
        P(),
        both,
        both,
        P("row", None),
        both,
        P(None, "col"),
        P("col"),
        P(),
        P(),
        P("col"),
        P("col"),
        P("col"),
        turned,
        both,
        both,
        both,
        turned,
        P(),
        both,
        both,
        turned,
    )
    return jax.shard_map(local, mesh=mesh, in_specs=in_specs, out_specs=out_specs, check_vma=False)
```

```python
from functools import partial

import jax
import jax.numpy as jnp
from jax import lax
from jax.experimental import pallas as pl
from jax.experimental.pallas import tpu as pltpu
from jax.sharding import PartitionSpec as P

HD = 128
TP = 4
GROUP = 2 * TP
CHUNK = 16
EPS = 1e-05
NEG_LARGE = -1e30
ROPE_BASE = 100000000000.0
MESH = pl.DeviceIdType.MESH
HIGH = lax.Precision.HIGHEST
VMEM = pltpu.VMEM
ANY = pl.ANY


def matmul(first_op, second_op):
    return jnp.dot(first_op, second_op, preferred_element_type=jnp.float32)


def matmul_trans(first_op, second_op):
    return lax.dot_general(
        first_op, second_op, (((1,), (1,)), ((), ())), preferred_element_type=jnp.float32
    )


def matmul_left(first_op, second_op):
    return lax.dot_general(
        first_op, second_op, (((0,), (0,)), ((), ())), preferred_element_type=jnp.float32
    )


MIX, FFN = (0, 1), (0, 1)


def data_bits(n_row, axes):
    return [b for b in reversed(range(n_row.bit_length() - 1)) if b not in axes]


def bit(row, b):
    return lax.rem(lax.div(row, 1 << b), 2)


def flip(row, b):
    return row + (1 << b) * (1 - 2 * bit(row, b))


def member(row, axes):
    return bit(row, axes[0]) + 2 * bit(row, axes[1])


def partner(row, m, axes):
    if m & 1:
        row = flip(row, axes[0])
    if m & 2:
        row = flip(row, axes[1])
    return row


def turned_row(row, mask):
    for b in range(mask.bit_length()):
        row = flip(row, b) if mask >> b & 1 else row
    return row


def group_of(row, n_row, axes):
    index = 0
    for b in data_bits(n_row, axes):
        index = index * 2 + bit(row, b)
    return index


def flips(n_row, mask):
    return [(row, row ^ mask) for row in range(n_row)]


def mask_of(m, axes):
    return (m & 1) * (1 << axes[0]) + (m // 2) * (1 << axes[1])


def place():
    return lax.axis_index("row"), lax.axis_index("col")


def block_of(m, axes):
    return member(partner(lax.axis_index("row"), m, axes), axes) * 2


def plan_of(axes, slots):
    if axes != (0, 1) or slots % 32:
        return [(0, slots, 2, 1)]
    return [(0, slots // 2, 1, 2), (slots // 2, slots, 2, 1)]


def params(number, megabytes):
    return pltpu.CompilerParams(
        collective_id=number, has_side_effects=True, vmem_limit_bytes=megabytes << 20
    )


def cost(microseconds):
    return pl.CostEstimate(flops=0, transcendentals=0, bytes_accessed=microseconds * 3_400_000)


def remote(src, dst, send, recv, row, col):
    return pltpu.make_async_remote_copy(
        src_ref=src, dst_ref=dst, send_sem=send, recv_sem=recv, device_id=(row, col), device_id_type=MESH
    )


def greet(*groups, cross=False):
    r, c = place()
    barrier = pltpu.get_barrier_semaphore()
    others = [(r, 1 - c)]
    for axes in groups:
        for m in (1, 2, 3) if cross else (1, 2):
            others.append((partner(r, m, axes), c))
            if cross:
                others.append((partner(r, m, axes), 1 - c))
    for other in others:
        pl.semaphore_signal(barrier, inc=1, device_id=other, device_id_type=MESH)
    pl.semaphore_wait(barrier, len(others))


def gather_start(src, out, send, recv, here, axes):
    r, c = place()
    own = member(r, axes) * 2 + c
    copies = [
        pltpu.make_async_copy(src, out.at[own], here),
        remote(src, out.at[own], send.at[0], recv.at[0], r, 1 - c),
    ]
    for p, (low, high, near, far) in enumerate(plan_of(axes, src.shape[0])):
        for k, m in ((1, near), (2, far)):
            copies.append(
                remote(
                    src.at[low:high], out.at[own, low:high], send.at[6 * p + k], recv.at[6 * p + k],
                    partner(r, m, axes), c,
                )
            )
    for copy in copies[2:] + copies[:2]:
        copy.start()
    return copies


def gather_finish(copies, out, send, recv, axes):
    r, c = place()
    plan = plan_of(axes, out.shape[1])
    steps = []

    def pass_on(p, k, m, row, col):
        low, high, near, far = plan[p]
        part = out.at[block_of(m, axes) + c, low:high]
        steps.append(remote(part, part, send.at[6 * p + k], recv.at[6 * p + k], row, col))
        steps[-1].start()

    for p, (low, high, near, far) in enumerate(plan):
        copies[2 + 2 * p].wait_recv()
        pass_on(p, 3, near, partner(r, far, axes), c)
        pass_on(p, 4, near, r, 1 - c)
    for p, (low, high, near, far) in enumerate(plan):
        copies[3 + 2 * p].wait_recv()
        pass_on(p, 5, far, r, 1 - c)
    for p, (low, high, near, far) in enumerate(plan):
        steps[2 * p].wait_recv()
        pass_on(p, 6, 3, r, 1 - c)
    copies[0].wait()
    copies[1].wait()
    for copy in copies[2:] + steps[: 2 * len(plan) : 2]:
        copy.wait_send()
    for i, copy in enumerate(steps):
        if i >= 2 * len(plan) or i % 2:
            copy.wait()


ROWS = 16


def by_rows(count, body, first=0):
    def step(i, carry):
        body(pl.ds(pl.multiple_of(i * ROWS, ROWS), ROWS))
        return carry

    lax.fori_loop(first // ROWS, count // ROWS, step, 0)


def scatter_sum(parts, near, held, far, s1, r1, s2, r2, total, axes):
    r, c = place()
    slots = total.shape[0]
    plan = plan_of(axes, slots)
    pairs = {}
    for m in (3, 1, 2, 0):
        pairs[m] = remote(
            parts.at[block_of(m, axes) + 1 - c], near.at[m], s1.at[m], r1.at[m], r, 1 - c
        )
        pairs[m].start()
    sent = {}

    def pair_sum(m, i, low, high):
        block = block_of(m, axes) + c

        def add(rows):
            held[i, rows, :] = (
                parts[block, rows, :].astype(jnp.float32) + near[m, rows, :].astype(jnp.float32)
            ).astype(jnp.bfloat16)

        by_rows(high, add, low)

    def send(i, p, m):
        low, high = plan[p][:2]
        k = 3 * p + i
        sent[i, p] = remote(
            held.at[i, low:high], far.at[i, low:high], s2.at[k], r2.at[k], partner(r, m, axes), c
        )
        sent[i, p].start()

    pairs[3].wait_recv()
    for p, (low, high, first, then) in enumerate(plan):
        pair_sum(3, 1, low, high)
        send(1, p, then)
    for m in (1, 2):
        pairs[m].wait_recv()
        for p, (low, high, first, then) in enumerate(plan):
            pair_sum(m, 0 if m == then else 2, low, high)
            if m == then:
                send(0, p, then)
    for p, (low, high, first, then) in enumerate(plan):
        sent[1, p].wait_recv()

        def add(rows):
            held[2, rows, :] = (
                held[2, rows, :].astype(jnp.float32) + far[1, rows, :].astype(jnp.float32)
            ).astype(jnp.bfloat16)

        by_rows(high, add, low)
        send(2, p, first)
    pairs[0].wait_recv()
    for p in range(len(plan)):
        sent[0, p].wait_recv()
        sent[2, p].wait_recv()
    own = member(r, axes) * 2 + c

    def fold(rows):
        total[rows, :] = (
            parts[own, rows, :].astype(jnp.float32)
            + near[0, rows, :].astype(jnp.float32)
            + far[0, rows, :].astype(jnp.float32)
            + far[2, rows, :].astype(jnp.float32)
        )

    by_rows(slots, fold)
    for copy in list(pairs.values()) + list(sent.values()):
        copy.wait_send()


def scatter_scratch(slots, width):
    return [
        VMEM((TP, slots, width), jnp.bfloat16),
        VMEM((TP - 1, slots, width), jnp.bfloat16),
        VMEM((TP - 1, slots, width), jnp.bfloat16),
        pltpu.SemaphoreType.DMA((TP,)),
        pltpu.SemaphoreType.DMA((TP,)),
        pltpu.SemaphoreType.DMA((6,)),
        pltpu.SemaphoreType.DMA((6,)),
    ]


def gather_scratch():
    return [
        pltpu.SemaphoreType.DMA((13,)),
        pltpu.SemaphoreType.DMA((13,)),
        pltpu.SemaphoreType.DMA,
    ]


def strips(refs, shared, size):
    found, at = [], 0
    for ref, whole in zip(refs, shared):
        count = ref.shape[1] if whole else ref.shape[1] // TP
        found.append((ref, whole, count, at))
        at += count
    return found


def strip_views(refs, shared, owner, piece):
    for ref, whole, count, at in strips(refs, shared, piece.shape[1]):
        cols = slice(None) if whole else pl.ds(pl.multiple_of(owner * count, 128), count)
        yield ref.at[:, cols], piece.at[:, at : at + count]


def cut_start(refs, shared, place_of, send, recv, here, axes):
    r, c = place()
    for source, target in strip_views(refs, shared, member(r, axes), place_of()):
        pltpu.make_async_copy(source, target, here).start()
    for m in (3, 1, 2):
        other = partner(r, m, axes)
        for source, target in strip_views(refs, shared, member(other, axes), place_of()):
            remote(source, target, send.at[m], recv.at[m], other, c).start()


def piece_done(piece, sem):
    pltpu.make_async_copy(piece, piece, sem).wait()


def weight_orders(n_row, cols):
    bits = data_bits(n_row, MIX)
    half = cols // 256 * 128
    return [(slice(0, half), bits), (slice(half, cols), bits)]


def weight_forward(masks, i, whole, send, recv):
    r, c = place()
    n_row = lax.axis_size("row")
    cols, bits = weight_orders(n_row, whole.shape[2])[i]
    copies = []
    for mask in masks:
        at = whole.at[turned_row(r, mask), :, cols]
        crossed = [k for k, b in enumerate(bits) if mask >> b & 1]
        if crossed:
            piece_done(at, recv.at[i, mask])
        for b in bits[max([-1] + crossed) + 1 :]:
            lands = mask | 1 << b
            copies.append(remote(at, at, send.at[i, lands], recv.at[i, lands], flip(r, b), c))
            copies[-1].start()
    return copies


def weight_rounds(n_row, i, cols):
    held = [mask_of(m, MIX) for m in range(TP)]
    rounds = [held]
    for b in weight_orders(n_row, cols)[i][1]:
        rounds.append([mask | 1 << b for mask in held])
        held = held + rounds[-1]
    return rounds


def place_kernel(masks, n_row, *refs):
    slabs, whole, sems = refs[: len(masks)], refs[-2], refs[-1]
    r, c = place()
    copies = []
    for i, mask in enumerate(masks):
        at = whole.at[group_of(turned_row(r, mask), n_row, FFN)]
        copies.append(pltpu.make_async_copy(slabs[i], at, sems.at[i]))
        copies[-1].start()
    for copy in copies:
        copy.wait()


def place_slabs(masks, slabs, n_row):
    return pl.pallas_call(
        partial(place_kernel, masks, n_row),
        name="place",
        out_shape=jax.ShapeDtypeStruct((len(masks),) + slabs[0].shape, slabs[0].dtype),
        in_specs=[pl.BlockSpec(memory_space=ANY)] * len(masks),
        out_specs=pl.BlockSpec(memory_space=ANY),
        scratch_shapes=[pltpu.SemaphoreType.DMA((len(masks),))],
        compiler_params=pltpu.CompilerParams(vmem_limit_bytes=4 << 20),
        cost_estimate=cost(4),
    )(*slabs)


def exchange_rows(buf, land, send, recv):
    r, c = place()
    n_row = lax.axis_size("row")

    def copy(other):
        return remote(
            buf.at[other], land.at[r], send.at[other], recv.at[r], other, c
        )

    def start(off, carry):
        copy(lax.rem(r + off, n_row)).start()
        return carry

    lax.fori_loop(1, n_row, start, 0)


def finish_rows(buf, land, send, recv):
    r, c = place()
    n_row = lax.axis_size("row")

    def finish(off, carry):
        other = lax.rem(r + off, n_row)
        copy = remote(buf.at[other], land.at[other], send.at[other], recv.at[other], other, c)
        copy.wait_send()
        copy.wait_recv()
        return carry

    lax.fori_loop(1, n_row, finish, 0)


def greet_rows():
    r, c = place()
    n_row = lax.axis_size("row")
    barrier = pltpu.get_barrier_semaphore()

    def greet(off, carry):
        pl.semaphore_signal(
            barrier, inc=1, device_id=(lax.rem(r + off, n_row), c), device_id_type=MESH
        )
        return carry

    lax.fori_loop(1, n_row, greet, 0)
    pl.semaphore_signal(barrier, inc=1, device_id=(r, 1 - c), device_id_type=MESH)
    pl.semaphore_wait(barrier, n_row)


COLS = 512


def permute_out(choice, buf, first, second, slots):
    n_row = buf.shape[0]

    def column(i, carry):
        cols = pl.ds(pl.multiple_of(i * COLS, COLS), COLS)
        picked = matmul(choice[:, :slots], first[:, cols]) + matmul(choice[:, slots:], second[:, cols])
        buf[:, :, cols] = picked.astype(jnp.bfloat16).reshape(n_row, CHUNK, COLS)
        return carry

    lax.fori_loop(0, buf.shape[2] // COLS, column, 0)


def permute_in(choice, land, first, second, slots):
    n_row = land.shape[0]

    def column(i, carry):
        cols = pl.ds(pl.multiple_of(i * COLS, COLS), COLS)
        got = land[:, :, cols].reshape(n_row * CHUNK, COLS)
        first[:, cols] = matmul_left(choice[:, :slots], got).astype(jnp.bfloat16)
        second[:, cols] = matmul_left(choice[:, slots:], got).astype(jnp.bfloat16)
        return carry

    lax.fori_loop(0, land.shape[2] // COLS, column, 0)


def deal_kernel(
    meta, tokens, cotangent, gain, *refs
):
    in_refs, up_refs, down_refs, refs = refs[:8], refs[8:10], refs[10:11], refs[11:]
    meta_all, give, take, x_out, gy_out, normed_all, gy_all, whole, slab_up, slab_down = refs[:10]
    x_mine, g_mine, buf, land, normed = refs[10:15]
    load, msend, mrecv, csend, crecv, nsend, nrecv, nhere, gsend, grecv, ghere = refs[15:26]
    wsend, wrecv, wcut, wcut_recv, whole_here, usend, urecv, uhere, dsend, drecv, dhere = refs[26:]
    r, c = place()
    n_row = lax.axis_size("row")
    f = member(r, FFN)
    slots = x_mine.shape[0]
    per_peer = slots // n_row
    loads = [
        pltpu.make_async_copy(tokens.at[c], x_mine, load.at[0]),
        pltpu.make_async_copy(cotangent.at[c], g_mine, load.at[1]),
    ]
    for copy in loads:
        copy.start()
    greet_rows()
    rounds = [weight_rounds(n_row, i, whole.shape[2]) for i in (0, 1)]
    in_shared = [False, False, False, True, True, False, False, False]

    def in_place():
        return whole.at[r]

    def meta_copy(other, slot):
        return remote(meta, meta_all.at[slot], msend.at[other], mrecv.at[slot], other, c)

    def start(off, carry):
        meta_copy(lax.rem(r + off, n_row), r).start()
        return carry

    lax.fori_loop(1, n_row, start, 0)
    meta_all[r] = meta[...]

    def finish(off, carry):
        other = lax.rem(r + off, n_row)
        copy = meta_copy(other, other)
        copy.wait_send()
        copy.wait_recv()
        return carry

    lax.fori_loop(1, n_row, finish, 0)
    cut_start(in_refs, in_shared, in_place, wcut, wcut_recv, whole_here, MIX)
    piece_done(in_place(), whole_here)
    forwards = []
    for i in (0, 1):
        forwards = forwards + weight_forward([0], i, whole, wsend, wrecv)

    shift = slots.bit_length() - 1
    row_no = lax.broadcasted_iota(jnp.int32, (CHUNK, slots), 0)
    wanted = jnp.where(row_no < per_peer, row_no, row_no - per_peer).astype(jnp.float32)
    early = row_no < per_peer
    late = (row_no >= per_peer) & (row_no < 2 * per_peer)
    tri = (
        lax.broadcasted_iota(jnp.int32, (slots, slots), 0)
        < lax.broadcasted_iota(jnp.int32, (slots, slots), 1)
    ).astype(jnp.float32).astype(jnp.bfloat16)
    places = lax.broadcasted_iota(jnp.int32, (slots, slots), 0)

    def order_of(block):
        picked = jnp.where(c == 0, block[0:1, :], block[1:2, :])
        return lax.shift_right_logical(picked, shift), picked - lax.shift_left(
            lax.shift_right_logical(picked, shift), shift
        )

    own_source, own_local = order_of(meta[...])

    def select(mask):
        wide = jnp.broadcast_to(mask.astype(jnp.float32), (CHUNK, slots)).astype(jnp.bfloat16)
        rank = matmul(wide, tri)
        return jnp.where(
            (rank == wanted) & (wide.astype(jnp.float32) > 0.5), 1.0, 0.0
        )

    def build(d, carry):
        rows = pl.ds(pl.multiple_of(d * CHUNK, CHUNK), CHUNK)
        source, local = order_of(meta_all[d])
        chosen = select(source == r).astype(jnp.bfloat16)
        at_home = (places == local).astype(jnp.float32).astype(jnp.bfloat16)
        picks = matmul_trans(chosen, at_home)
        give[rows, :slots] = jnp.where(early, picks, 0.0).astype(jnp.bfloat16)
        give[rows, slots:] = jnp.where(late, picks, 0.0).astype(jnp.bfloat16)
        kept = select(own_source == d)
        take[rows, :slots] = jnp.where(early, kept, 0.0).astype(jnp.bfloat16)
        take[rows, slots:] = jnp.where(late, kept, 0.0).astype(jnp.bfloat16)
        return carry

    lax.fori_loop(0, n_row, build, 0)
    for copy in loads:
        copy.wait()
    permute_out(give, buf, x_mine, g_mine, slots)
    exchange_rows(buf, land, csend, crecv)
    land[r] = buf[r]
    for m in (1, 2, 3):
        piece_done(in_place(), wcut_recv.at[m])
        for i in (0, 1):
            forwards = forwards + weight_forward([mask_of(m, MIX)], i, whole, wsend, wrecv)
    finish_rows(buf, land, csend, crecv)
    permute_in(take, land, x_out, gy_out, slots)

    def norm(rows):
        values = x_out[rows, :].astype(jnp.float32)
        scale = lax.rsqrt(jnp.mean(values * values, axis=-1, keepdims=True) + EPS)
        normed[rows, :] = (values * scale * gain[...]).astype(jnp.bfloat16)

    by_rows(slots, norm)
    first = gather_start(normed, normed_all, nsend, nrecv, nhere, MIX)
    cut_start(up_refs, [False] * 2, lambda: slab_up.at[f], usend, urecv, uhere, FFN)
    cut_start(down_refs, [False], lambda: slab_down.at[f], dsend, drecv, dhere, FFN)
    second = gather_start(gy_out, gy_all, gsend, grecv, ghere, FFN)
    for k in range(1, len(rounds[0])):
        for i in (0, 1):
            forwards = forwards + weight_forward(rounds[i][k], i, whole, wsend, wrecv)
    gather_finish(first, normed_all, nsend, nrecv, MIX)
    gather_finish(second, gy_all, gsend, grecv, FFN)
    for copy in forwards:
        copy.wait_send()
    for m in (1, 2, 3):
        piece_done(in_place(), wcut.at[m])
    for slab, send, recv, here in ((slab_up, usend, urecv, uhere), (slab_down, dsend, drecv, dhere)):
        piece_done(slab.at[f], here)
        for m in (1, 2, 3):
            piece_done(slab.at[f], send.at[m])
            piece_done(slab.at[f], recv.at[m])


def deal(meta, tokens, cotangent, gain, in_weights, ff_weights, n_row):
    slots, width = tokens.shape[1:]
    bf = jnp.bfloat16
    rows = in_weights[0].shape[0]
    in_cols = sum(
        array.shape[1] // (1 if i in (3, 4) else TP) for i, array in enumerate(in_weights)
    )
    up_cols, down_cols = 2 * ff_weights[0].shape[1] // TP, ff_weights[2].shape[1] // TP
    vm, hb = pl.BlockSpec(memory_space=VMEM), pl.BlockSpec(memory_space=ANY)
    dma = pltpu.SemaphoreType.DMA
    return pl.pallas_call(
        deal_kernel,
        name="deal",
        out_shape=(
            jax.ShapeDtypeStruct((n_row, 8, 128), jnp.int32),
            jax.ShapeDtypeStruct((n_row * CHUNK, 2 * slots), bf),
            jax.ShapeDtypeStruct((n_row * CHUNK, 2 * slots), bf),
            jax.ShapeDtypeStruct((slots, width), bf),
            jax.ShapeDtypeStruct((slots, width), bf),
            jax.ShapeDtypeStruct((GROUP, slots, width), bf),
            jax.ShapeDtypeStruct((GROUP, slots, width), bf),
            jax.ShapeDtypeStruct((n_row, rows, in_cols), bf),
            jax.ShapeDtypeStruct((TP, rows, up_cols), bf),
            jax.ShapeDtypeStruct((TP, rows, down_cols), bf),
        ),
        in_specs=[vm, hb, hb, vm] + [hb] * 11,
        out_specs=(vm,) * 5 + (hb,) * 5,
        scratch_shapes=[
            VMEM((slots, width), bf),
            VMEM((slots, width), bf),
            VMEM((n_row, CHUNK, width), bf),
            VMEM((n_row, CHUNK, width), bf),
            VMEM((slots, width), bf),
            dma((2,)),
            dma((n_row,)),
            dma((n_row,)),
            dma((n_row,)),
            dma((n_row,)),
        ]
        + gather_scratch()
        + gather_scratch()
        + [dma((2, n_row)), dma((2, n_row))]
        + [dma((TP,)), dma((TP,)), dma] * 3,
        compiler_params=params(0, 40),
        cost_estimate=cost(100),
    )(meta, tokens, cotangent, gain, *in_weights, *ff_weights)


def middle_kernel(parts, x, gain, mid, normed_all, near, out2, far, s1, r1, s2, r2, normed, nsend, nrecv, nhere):
    greet(*{MIX, FFN})
    scatter_sum(parts, near, out2, far, s1, r1, s2, r2, mid, MIX)

    def norm(rows):
        values = x[rows, :].astype(jnp.float32) + mid[rows, :]
        mid[rows, :] = values
        scale = lax.rsqrt(jnp.mean(values * values, axis=-1, keepdims=True) + EPS)
        normed[rows, :] = (values * scale * gain[...]).astype(jnp.bfloat16)

    by_rows(mid.shape[0], norm)
    started = gather_start(normed, normed_all, nsend, nrecv, nhere, FFN)
    gather_finish(started, normed_all, nsend, nrecv, FFN)


def middle(parts, x, gain):
    slots, width = x.shape
    return pl.pallas_call(
        middle_kernel,
        name="middle",
        out_shape=(
            jax.ShapeDtypeStruct((slots, width), jnp.float32),
            jax.ShapeDtypeStruct((GROUP, slots, width), jnp.bfloat16),
        ),
        in_specs=[pl.BlockSpec(memory_space=VMEM)] * 3,
        out_specs=(pl.BlockSpec(memory_space=VMEM), pl.BlockSpec(memory_space=ANY)),
        scratch_shapes=scatter_scratch(slots, width)
        + [VMEM((slots, width), jnp.bfloat16)]
        + gather_scratch(),
        compiler_params=params(1, 40),
        cost_estimate=cost(60),
    )(parts, x, gain)


def norm_back(values, gain, grad):
    inverse = lax.rsqrt(jnp.mean(values * values, axis=-1, keepdims=True) + EPS)
    scaled = grad * gain
    back = inverse * scaled - values * (
        inverse * inverse * inverse * jnp.mean(values * scaled, axis=-1, keepdims=True)
    )
    return back, jnp.sum(grad * values * inverse, axis=0, keepdims=True)


def turn_kernel(
    parts, mid, gy, gain, d_mid, d_gain, branch_all,
    near, out2, far, s1, r1, s2, r2, branch, nsend, nrecv, nhere,
):
    greet(*{MIX, FFN})
    scatter_sum(parts, near, out2, far, s1, r1, s2, r2, d_mid, FFN)
    d_gain[...] = jnp.zeros_like(d_gain)

    def back(rows):
        values = mid[rows, :]
        grad, gain_part = norm_back(values, gain[...], d_mid[rows, :])
        grad = gy[rows, :].astype(jnp.float32) + grad
        d_mid[rows, :] = grad
        branch[rows, :] = grad.astype(jnp.bfloat16)
        d_gain[...] += gain_part

    by_rows(mid.shape[0], back)
    started = gather_start(branch, branch_all, nsend, nrecv, nhere, MIX)
    gather_finish(started, branch_all, nsend, nrecv, MIX)


def turn(parts, mid, gy, gain):
    slots, width = mid.shape
    return pl.pallas_call(
        turn_kernel,
        name="turn",
        out_shape=(
            jax.ShapeDtypeStruct((slots, width), jnp.float32),
            jax.ShapeDtypeStruct((1, width), jnp.float32),
            jax.ShapeDtypeStruct((GROUP, slots, width), jnp.bfloat16),
        ),
        in_specs=[pl.BlockSpec(memory_space=VMEM)] * 4,
        out_specs=(pl.BlockSpec(memory_space=VMEM),) * 2 + (pl.BlockSpec(memory_space=ANY),),
        scratch_shapes=scatter_scratch(slots, width)
        + [VMEM((slots, width), jnp.bfloat16)]
        + gather_scratch(),
        compiler_params=params(2, 48),
        cost_estimate=cost(60),
    )(parts, mid, gy, gain)


def home_kernel(
    parts, x, d_mid, result, gain, give, take, small, ff_sums,
    output, gradient, small_all, ff_land,
    near, out2, far, s1, r1, s2, r2, total, first, second, buf, land, csend, crecv, here, osend, orecv,
    d_gain, stages, stage_land, tsend, trecv, gsend, grecv, ghere, *more
):
    r, c = place()
    slots, width = x.shape
    bits = data_bits(lax.axis_size("row"), MIX)
    greet_rows()
    delivered = deliver(ff_sums, ff_land, *more, FFN)
    scatter_sum(parts, near, out2, far, s1, r1, s2, r2, total, MIX)
    d_gain[...] = jnp.zeros_like(d_gain)

    def back(rows):
        values = x[rows, :].astype(jnp.float32)
        grad, gain_part = norm_back(values, gain[...], total[rows, :])
        second[rows, :] = (d_mid[rows, :] + grad).astype(jnp.bfloat16)
        first[rows, :] = result[rows, :].astype(jnp.bfloat16)
        d_gain[...] += gain_part

    by_rows(slots, back)
    head = small.shape[0]
    stages[0, :head, :] = small[...]
    for k in range(width // 128):
        stages[0, head + k : head + k + 1, :] = d_gain[:, k * 128 : (k + 1) * 128]

    def stage_copy(i):
        return remote(
            stages.at[i], stage_land.at[i], tsend.at[i], trecv.at[i], flip(r, bits[i]), c
        )

    stage_copy(0).start()
    permute_out(take, buf, first, second, slots)
    exchange_rows(buf, land, csend, crecv)
    land[r] = buf[r]
    for i in range(len(bits)):
        stage_copy(i).wait()
        stages[i + 1] = stages[i] + stage_land[i]
        if i + 1 < len(bits):
            stage_copy(i + 1).start()
    started = gather_start(stages.at[len(bits)], small_all, gsend, grecv, ghere, MIX)
    finish_rows(buf, land, csend, crecv)
    permute_in(give, land, first, second, slots)
    copies = []
    for i, (mine, out) in enumerate(((first, output), (second, gradient))):
        copies.append(pltpu.make_async_copy(mine, out.at[c], here.at[i]))
        copies.append(remote(mine, out.at[c], osend.at[i], orecv.at[i], r, 1 - c))
    for copy in copies:
        copy.start()
    gather_finish(started, small_all, gsend, grecv, MIX)
    for copy in copies + delivered:
        copy.wait()


def deliver(sums, land, send, recv, here, axes):
    r, c = place()
    own = member(r, axes)
    copies = [pltpu.make_async_copy(sums.at[own], land.at[own], here)]
    for m in (3, 1, 2):
        other = partner(r, m, axes)
        copies.append(
            remote(sums.at[member(other, axes)], land.at[own], send.at[m], recv.at[m], other, c)
        )
    for copy in copies:
        copy.start()
    return copies


def deliver_scratch():
    dma = pltpu.SemaphoreType.DMA
    return [dma((TP,)), dma((TP,)), dma]


def last_kernel(at, sums, land, other, s1, r1, here, send, recv):
    r, c = place()
    barrier = pltpu.get_barrier_semaphore()
    for m in (1, 2, 3):
        pl.semaphore_signal(barrier, inc=1, device_id=(partner(r, m, MIX), c), device_id_type=MESH)
    pl.semaphore_signal(barrier, inc=1, device_id=(r, 1 - c), device_id_type=MESH)
    pl.semaphore_wait(barrier, 4)
    for copy in deliver(sums, land, s1, r1, here, MIX):
        copy.wait()
    across = remote(land.at[:, :, at : at + 128], other, send, recv, r, 1 - c)
    across.start()
    across.wait()


def last(sums, at):
    hb = pl.BlockSpec(memory_space=ANY)
    dma = pltpu.SemaphoreType.DMA
    return pl.pallas_call(
        partial(last_kernel, at),
        name="last",
        out_shape=(
            jax.ShapeDtypeStruct(sums.shape, sums.dtype),
            jax.ShapeDtypeStruct(sums.shape[:2] + (128,), sums.dtype),
        ),
        in_specs=[hb],
        out_specs=(hb,) * 2,
        scratch_shapes=deliver_scratch() + [dma, dma],
        compiler_params=params(6, 4),
        cost_estimate=cost(25),
    )(sums)


def unpack_kernel(
    ff, mixer, gate, up, down, mamba_gate, mamba_input, query, key, value, mamba_out, attn_out
):
    f32 = jnp.float32
    mh = mamba_gate.shape[1] // TP
    fh = gate.shape[1] // TP
    qh = query.shape[1] // TP
    kv = key.shape[1]
    at = 2 * mh + qh
    out = mixer.shape[2] - mh - qh
    for m in range(TP):
        def cols(size):
            return slice(m * size, (m + 1) * size)

        gate[:, cols(fh)] = ff[m, :, :fh].astype(f32)
        up[:, cols(fh)] = ff[m, :, fh : 2 * fh].astype(f32)
        down[cols(fh), :] = ff[m, :, 2 * fh :].astype(f32).T
        mamba_gate[:, cols(mh)] = mixer[m, :, :mh].astype(f32)
        mamba_input[:, cols(mh)] = mixer[m, :, mh : 2 * mh].astype(f32)
        query[:, cols(qh)] = mixer[m, :, 2 * mh : at].astype(f32)
        mamba_out[cols(mh), :] = mixer[m, :, out : out + mh].astype(f32).T
        attn_out[cols(qh), :] = mixer[m, :, out + mh :].astype(f32).T
    key[...] = sum(mixer[m, :, at : at + kv].astype(f32) for m in range(TP))
    value[...] = sum(mixer[m, :, at + kv : at + 2 * kv].astype(f32) for m in range(TP))


def unpack(ff, mixer, mh, qh, kv, fh):
    rows = ff.shape[1]
    vm = pl.BlockSpec(memory_space=VMEM)
    shapes = [(rows, TP * fh)] * 2 + [(TP * fh, rows)] + [(rows, TP * mh)] * 2
    shapes += [(rows, TP * qh), (rows, kv), (rows, kv), (TP * mh, rows), (TP * qh, rows)]
    return pl.pallas_call(
        unpack_kernel,
        name="unpack",
        out_shape=tuple(jax.ShapeDtypeStruct(shape, jnp.float32) for shape in shapes),
        in_specs=[vm] * 2,
        out_specs=(vm,) * len(shapes),
        compiler_params=pltpu.CompilerParams(vmem_limit_bytes=40 << 20),
        cost_estimate=cost(8),
    )(ff, mixer)


def send_home(parts, x, d_mid, result, gain, give, take, small, ff_sums, n_row):
    slots, width = x.shape
    bf = jnp.bfloat16
    size = small.shape[0] + width // 128
    phases = len(data_bits(n_row, MIX))
    return pl.pallas_call(
        home_kernel,
        name="home",
        out_shape=(
            jax.ShapeDtypeStruct((2, slots, width), bf),
            jax.ShapeDtypeStruct((2, slots, width), bf),
            jax.ShapeDtypeStruct((GROUP, size, 128), jnp.float32),
            jax.ShapeDtypeStruct(ff_sums.shape, bf),
        ),
        in_specs=[pl.BlockSpec(memory_space=VMEM)] * 8 + [pl.BlockSpec(memory_space=ANY)],
        out_specs=(pl.BlockSpec(memory_space=ANY),) * 4,
        scratch_shapes=scatter_scratch(slots, width)
        + [
            VMEM((slots, width), jnp.float32),
            VMEM((slots, width), bf),
            VMEM((slots, width), bf),
            VMEM((n_row, CHUNK, width), bf),
            VMEM((n_row, CHUNK, width), bf),
            pltpu.SemaphoreType.DMA((n_row,)),
            pltpu.SemaphoreType.DMA((n_row,)),
            pltpu.SemaphoreType.DMA((2,)),
            pltpu.SemaphoreType.DMA((2,)),
            pltpu.SemaphoreType.DMA((2,)),
            VMEM((1, width), jnp.float32),
            VMEM((phases + 1, size, 128), jnp.float32),
            VMEM((phases, size, 128), jnp.float32),
            pltpu.SemaphoreType.DMA((phases,)),
            pltpu.SemaphoreType.DMA((phases,)),
        ]
        + gather_scratch()
        + deliver_scratch(),
        compiler_params=params(3, 48),
        cost_estimate=cost(75),
    )(parts, x, d_mid, result, gain, give, take, small, ff_sums)


def blocks_start(low, land, s1, r1):
    r, c = place()
    copies = []
    for m, f in CROSSED:
        col = 1 - c if f else c
        k = m * 2 + f
        copies.append(
            remote(low.at[block_of(m, MIX) + col], land.at[k], s1.at[k], r1.at[k], partner(r, m, MIX), col)
        )
        copies[-1].start()
    return copies


def blocks_turn(first, low, land, mine, total, s2, r2, here):
    r, c = place()
    own = member(r, MIX) * 2 + c
    for copy in first:
        copy.wait_recv()
    summed = low[own].astype(jnp.float32)
    for m, f in CROSSED:
        summed = summed + land[m * 2 + f].astype(jnp.float32)
    mine[...] = summed.astype(jnp.bfloat16)
    copies = [pltpu.make_async_copy(mine, total.at[own], here)]
    for m, f in CROSSED:
        k = m * 2 + f
        copies.append(
            remote(mine, total.at[own], s2.at[k], r2.at[k], partner(r, m, MIX), 1 - c if f else c)
        )
    for copy in copies:
        copy.start()
    return copies


def blocks_finish(first, second):
    for copy in first:
        copy.wait_send()
    for copy in second:
        copy.wait()


CROSSED = [(m, f) for m in (3, 1, 2) for f in (0, 1)] + [(0, 1)]


def blocks_scratch(slots):
    dma = pltpu.SemaphoreType.DMA
    return [
        VMEM((GROUP, slots, slots), jnp.bfloat16),
        VMEM((GROUP, slots, slots), jnp.bfloat16),
        VMEM((slots, slots), jnp.bfloat16),
        dma((GROUP,)),
        dma((GROUP,)),
        dma((GROUP,)),
        dma((GROUP,)),
        dma,
    ]


def dot(first_op, second_op, first_dim, second_dim, precision=None):
    return lax.dot_general(
        first_op,
        second_op,
        (((first_dim,), (second_dim,)), ((), ())),
        precision=precision,
        preferred_element_type=jnp.float32,
    )


def block_rows(b, slots):
    return pl.ds(pl.multiple_of(b * slots, slots), slots)


def marks(lens, b, slots):
    row = lax.broadcasted_iota(jnp.int32, (slots, slots), 0)
    col = lax.broadcasted_iota(jnp.int32, (slots, slots), 1)
    row_segment, col_segment, within = jnp.zeros_like(row), jnp.zeros_like(row), row
    end = 0
    for k in range(lens.shape[1] - 1):
        end = end + lens[b, k]
        row_segment = row_segment + (row >= end).astype(jnp.int32)
        col_segment = col_segment + (col >= end).astype(jnp.int32)
        within = jnp.where(row >= end, row - end, within)
    return (row_segment == col_segment) & (row >= col), within


def conv_pre(values, within, weights):
    width = values.shape[1]
    shifted = [values]
    for k in range(1, 4):
        valid = within[:, :1] >= k
        shifted.append(jnp.where(valid, pltpu.roll(values, k, 0), 0.0))
    pre = weights[4:5, :]
    for k in range(4):
        pre = pre + weights[3 - k : 4 - k, :] * shifted[k]
    return pre, shifted


def conv_back(grad, pre, shifted, within, weights):
    slots = grad.shape[0]
    gate = jax.nn.sigmoid(pre)
    e = grad * gate * (1.0 + pre * (1.0 - gate))
    sums = [jnp.sum(e * shifted[3 - i], axis=0, keepdims=True) for i in range(4)]
    sums.append(jnp.sum(e, axis=0, keepdims=True))
    back = weights[3:4, :] * e
    for k in range(1, 4):
        valid = within[:, :1] >= k
        back = back + weights[3 - k : 4 - k, :] * pltpu.roll(jnp.where(valid, e, 0.0), slots - k, 0)
    return back, sums


def softplus(values):
    return jnp.maximum(values, 0.0) + jnp.log1p(jnp.exp(-jnp.abs(values)))


def steps_and_levels(mixed, side, low, count):
    slots, width = mixed.shape
    lane = lax.broadcasted_iota(jnp.int32, (slots, width), 1)
    inside = (lane >= low) & (lane < low + count)
    step = jnp.where(inside, softplus(mixed + side[5:6, :]), 0.0)
    rate = jnp.where(inside, -jnp.exp(side[6:7, :]), 0.0)
    row = lax.broadcasted_iota(jnp.int32, (slots, slots), 0)
    col = lax.broadcasted_iota(jnp.int32, (slots, slots), 1)
    tri = (row >= col).astype(jnp.float32)
    level = dot(tri, step * rate, 1, 0, HIGH)
    return step, rate, level, tri, inside


def halves(first, second):
    lane = lax.broadcasted_iota(jnp.int32, first.shape, 1)
    return jnp.where(lane < first.shape[1] // 2, first, second)


def state_parts(mixed, within, side, sh):
    pre, shifted = conv_pre(mixed, within, side)
    act = pre * jax.nn.sigmoid(pre)
    lane = lax.broadcasted_iota(jnp.int32, act.shape, 1)
    first = jnp.where(lane < sh, act, 0.0).astype(jnp.bfloat16)
    second = jnp.where(lane < sh, pltpu.roll(act, act.shape[1] - sh, 1), 0.0).astype(jnp.bfloat16)
    return first, second, pre, shifted


def turned_pair(values, waves):
    half = values.shape[1] // 2
    return values * waves[:, : 2 * half] + pltpu.roll(values, half, 1) * waves[:, 2 * half :]


def turned_back(values, waves):
    half = values.shape[1] // 2
    return values * waves[:, : 2 * half] - pltpu.roll(values, half, 1) * waves[:, 2 * half :]


def wave_rows(within, table):
    slots = within.shape[0]
    picks = (within == lax.broadcasted_iota(jnp.int32, (slots, slots), 1)).astype(jnp.float32)
    return dot(picks, table[...], 1, 0, HIGH)


def attend(projected, rows, at, lens, table, b, slots):
    allowed, within = marks(lens, b, slots)
    waves = wave_rows(within, table)
    query = turned_pair(projected[rows, at : at + HD], waves).astype(jnp.bfloat16)
    key = turned_pair(projected[rows, at + HD : at + 2 * HD], waves).astype(jnp.bfloat16)
    value = projected[rows, at + 2 * HD : at + 3 * HD].astype(jnp.bfloat16)
    scores = jnp.where(allowed, dot(query, key, 1, 1) * HD ** (-0.5), NEG_LARGE)
    exps = jnp.exp(scores - jnp.max(scores, axis=-1, keepdims=True))
    probs = exps / jnp.sum(exps, axis=-1, keepdims=True)
    return query, key, value, probs, waves


def each_block(first, last, body):
    def step(b, carry):
        body(b)
        return carry

    lax.fori_loop(first, last, step, 0)


def mixer_kernel(
    sh, ph, lens, projected, chan, side, table, branch, scanned, crossed,
    low, land, mine, s1, r1, s2, r2, here, conv,
):
    slots = crossed.shape[1]
    mh = chan.shape[1]
    heads_at = 2 * sh
    greet(MIX, cross=True)

    def before(b):
        rows = block_rows(b, slots)
        allowed, within = marks(lens, b, slots)
        pre, unused = conv_pre(projected[rows, mh : 2 * mh], within, chan)
        conv[rows, :] = pre * jax.nn.sigmoid(pre)
        mixed = projected[rows, 2 * mh + 3 * HD :]
        first, second, unused, unused = state_parts(mixed, within, side, sh)
        low[b] = dot(second, first, 1, 1).astype(jnp.bfloat16)

    def attention(b):
        rows = block_rows(b, slots)
        query, key, value, probs, waves = attend(projected, rows, 2 * mh, lens, table, b, slots)
        branch[rows, mh:] = dot(probs.astype(jnp.bfloat16), value, 1, 0).astype(jnp.bfloat16)

    def after(b):
        rows = block_rows(b, slots)
        allowed, within = marks(lens, b, slots)
        mixed = projected[rows, 2 * mh + 3 * HD :]
        step, rate, level, tri, inside = steps_and_levels(mixed, side, heads_at, ph)
        step_t, level_t = step.T, level.T
        cross = crossed[b].astype(jnp.float32)
        for pair in range(ph // 2):
            cols = slice(pair * 128, (pair + 1) * 128)
            convs = conv[rows, cols]
            conv_low = convs.astype(jnp.bfloat16)
            outs = []
            for h in (2 * pair, 2 * pair + 1):
                at = heads_at + h
                spread = level[:, at : at + 1] - level_t[at : at + 1, :]
                decay = jnp.exp(jnp.where(allowed, spread, NEG_LARGE))
                mixing = cross * decay * step_t[at : at + 1, :]
                outs.append(dot(mixing.astype(jnp.bfloat16), conv_low, 1, 0))
            total = halves(outs[0], outs[1])
            scanned[rows, cols] = total
            gate = projected[rows, cols]
            gated = (total + chan[5:6, cols] * convs) * (gate * jax.nn.sigmoid(gate))
            branch[rows, cols] = gated.astype(jnp.bfloat16)

    each_block(0, GROUP, before)
    first = blocks_start(low, land, s1, r1)
    each_block(0, GROUP // 2, attention)
    second = blocks_turn(first, low, land, mine, crossed, s2, r2, here)
    each_block(GROUP // 2, GROUP, attention)
    blocks_finish(first, second)
    each_block(0, GROUP, after)


def mixer(lens, projected, chan, side, table, sh, ph):
    tokens = projected.shape[0]
    slots = tokens // GROUP
    mh = chan.shape[1]
    vm = pl.BlockSpec(memory_space=VMEM)
    return pl.pallas_call(
        partial(mixer_kernel, sh, ph),
        name="mixer",
        out_shape=(
            jax.ShapeDtypeStruct((tokens, mh + HD), jnp.bfloat16),
            jax.ShapeDtypeStruct((tokens, mh), jnp.float32),
            jax.ShapeDtypeStruct((GROUP, slots, slots), jnp.bfloat16),
        ),
        in_specs=[pl.BlockSpec(memory_space=pltpu.SMEM)] + [vm] * 4,
        out_specs=(vm,) * 3,
        scratch_shapes=blocks_scratch(slots) + [VMEM((tokens, mh), jnp.float32)],
        compiler_params=params(4, 40),
        cost_estimate=cost(30),
    )(lens, projected, chan, side, table)


def mixer_back_kernel(
    sh, ph, lens, projected, chan, side, table, scanned, crossed, grads, out, chan_sums, side_sums,
    low, land, mine, s1, r1, s2, r2, here, summed, misc,
):
    slots = crossed.shape[1]
    mh = chan.shape[1]
    heads_at = 2 * sh
    bf = jnp.bfloat16
    greet(MIX, cross=True)
    chan_sums[...] = jnp.zeros_like(chan_sums)
    side_sums[...] = jnp.zeros_like(side_sums)

    def scan(b):
        rows = block_rows(b, slots)
        allowed, within = marks(lens, b, slots)
        mixed = projected[rows, 2 * mh + 3 * HD :]
        step, rate, level, tri, inside = steps_and_levels(mixed, side, heads_at, ph)
        step_t, level_t = step.T, level.T
        cross = crossed[b].astype(jnp.float32)
        lane = lax.broadcasted_iota(jnp.int32, (slots, 128), 1)
        place_row = lax.broadcasted_iota(jnp.int32, (slots, slots), 0)
        grad_cross = jnp.zeros((slots, slots), jnp.float32)
        row_sums = jnp.zeros((slots, slots), jnp.float32)
        col_sums = jnp.zeros((slots, slots), jnp.float32)
        for pair in range(ph // 2):
            cols = slice(pair * 128, (pair + 1) * 128)
            weights = chan[:, cols]
            pre, shifted = conv_pre(
                projected[rows, mh + pair * 128 : mh + (pair + 1) * 128], within, weights
            )
            convs = pre * jax.nn.sigmoid(pre)
            conv_low = convs.astype(bf)
            gate = projected[rows, cols]
            sig = jax.nn.sigmoid(gate)
            grad = grads[rows, cols]
            skip = weights[5:6, :]
            grad_mix = grad * (gate * sig)
            out[rows, cols] = (
                grad * (scanned[rows, cols] + skip * convs) * (sig * (1.0 + gate * (1.0 - sig)))
            ).astype(bf)
            skip_sum = jnp.sum(grad_mix * convs, axis=0, keepdims=True)
            grad_low = grad_mix.astype(bf)
            backs = []
            for f in (0, 1):
                at = heads_at + 2 * pair + f
                mask = lane < 64 if f == 0 else lane >= 64
                spread = level[:, at : at + 1] - level_t[at : at + 1, :]
                decay = jnp.exp(jnp.where(allowed, spread, NEG_LARGE))
                step_row = step_t[at : at + 1, :]
                mixing = cross * decay * step_row
                backs.append(dot(mixing.astype(bf), grad_low, 0, 0))
                grad_mixing = dot(jnp.where(mask, grad_mix, 0.0).astype(bf), conv_low, 1, 1)
                weighted = grad_mixing * decay
                grad_cross = grad_cross + weighted * step_row
                weighted = weighted * cross
                col = jnp.sum(weighted, axis=0, keepdims=True)
                row = jnp.sum(weighted * step_row, axis=1, keepdims=True)
                row_sums = jnp.where(lane == at, row, row_sums)
                col_sums = jnp.where(place_row == at, col, col_sums)
            grad_conv = grad_mix * skip + halves(backs[0], backs[1])
            back, sums = conv_back(grad_conv, pre, shifted, within, weights)
            out[rows, mh + pair * 128 : mh + (pair + 1) * 128] = back.astype(bf)
            for i, part in enumerate(sums + [skip_sum]):
                chan_sums[i : i + 1, cols] += part
        low[b] = grad_cross.astype(bf)
        col_sums = col_sums.T
        grad_level = row_sums - step * col_sums
        grad_rate_step = dot(tri, grad_level, 0, 0, HIGH)
        grad_step = (col_sums + grad_rate_step * rate) * jax.nn.sigmoid(mixed + side[5:6, :])
        grad_step = jnp.where(inside, grad_step, 0.0)
        misc[rows, :] = grad_step
        side_sums[5:6, :] += jnp.sum(grad_step, axis=0, keepdims=True)
        side_sums[6:7, :] += jnp.sum(grad_rate_step * step, axis=0, keepdims=True) * rate[:1, :]

    def attention(b):
        rows = block_rows(b, slots)
        at = 2 * mh
        query, key, value, probs, waves = attend(projected, rows, at, lens, table, b, slots)
        grad = grads[rows, mh:].astype(bf)
        grad_probs = dot(grad, value, 1, 1)
        out[rows, at + 2 * HD : at + 3 * HD] = dot(probs.astype(bf), grad, 0, 0).astype(bf)
        grad_raw = probs * (grad_probs - jnp.sum(grad_probs * probs, axis=-1, keepdims=True))
        grad_raw = (grad_raw * HD ** (-0.5)).astype(bf)
        out[rows, at : at + HD] = turned_back(dot(grad_raw, key, 1, 0), waves).astype(bf)
        out[rows, at + HD : at + 2 * HD] = turned_back(dot(grad_raw, query, 0, 0), waves).astype(bf)

    def state(b):
        rows = block_rows(b, slots)
        allowed, within = marks(lens, b, slots)
        mixed = projected[rows, 2 * mh + 3 * HD :]
        first, second, pre, shifted = state_parts(mixed, within, side, sh)
        lane = lax.broadcasted_iota(jnp.int32, pre.shape, 1)
        grad_first = dot(summed[b], second, 0, 0)
        grad_second = pltpu.roll(dot(summed[b], first, 1, 0), sh, 1)
        grad = jnp.where(lane < sh, grad_first, jnp.where(lane < 2 * sh, grad_second, 0.0))
        back, sums = conv_back(grad, pre, shifted, within, side)
        out[rows, 2 * mh + 3 * HD :] = jnp.where(lane < 2 * sh, back, misc[rows, :]).astype(bf)
        for i, part in enumerate(sums):
            side_sums[i : i + 1, :] += part

    each_block(0, GROUP, scan)
    begun = blocks_start(low, land, s1, r1)
    each_block(0, GROUP // 2, attention)
    done = blocks_turn(begun, low, land, mine, summed, s2, r2, here)
    each_block(GROUP // 2, GROUP, attention)
    blocks_finish(begun, done)
    each_block(0, GROUP, state)


def mixer_back(lens, projected, chan, side, table, scanned, crossed, grads, sh, ph):
    tokens = projected.shape[0]
    slots = tokens // GROUP
    mh = chan.shape[1]
    vm = pl.BlockSpec(memory_space=VMEM)
    return pl.pallas_call(
        partial(mixer_back_kernel, sh, ph),
        name="mixer_back",
        out_shape=(
            jax.ShapeDtypeStruct(projected.shape, jnp.bfloat16),
            jax.ShapeDtypeStruct(chan.shape, jnp.float32),
            jax.ShapeDtypeStruct(side.shape, jnp.float32),
        ),
        in_specs=[pl.BlockSpec(memory_space=pltpu.SMEM)] + [vm] * 7,
        out_specs=(vm,) * 3,
        scratch_shapes=blocks_scratch(slots)
        + [
            VMEM((GROUP, slots, slots), jnp.bfloat16),
            VMEM((tokens, 128), jnp.float32),
        ],
        compiler_params=params(5, 48),
        cost_estimate=cost(50),
    )(lens, projected, chan, side, table, scanned, crossed, grads)


def swiglu(ff_gate, ff_up):
    return jax.nn.silu(ff_gate) * ff_up


def cut(array, parts, axis=1):
    rows, cols = array.shape
    return array.reshape(rows, parts, cols // parts).transpose(1, 0, 2)


def local(
    tokens,
    cotangent,
    deal_order,
    seq_lengths,
    mixer_norm_gain,
    mamba_gate_weight,
    mamba_input_weight,
    state_weight,
    step_weight,
    conv_input,
    conv_input_bias,
    conv_state,
    conv_state_bias,
    step_bias,
    decay_log,
    skip_scale,
    mamba_out_weight,
    query_weight,
    key_weight,
    value_weight,
    attn_out_weight,
    ff_norm_gain,
    gate_weight,
    up_weight,
    down_weight,
):
    n_row = lax.axis_size("row")
    r = lax.axis_index("row")
    c = lax.axis_index("col")
    t = member(r, MIX)
    n_bits = n_row.bit_length() - 1
    slots, width = tokens.shape[1:]
    bf = jnp.bfloat16
    rows = mamba_gate_weight.shape[0]
    mh = mamba_gate_weight.shape[1] // TP
    qh = query_weight.shape[1] // TP
    kvh = key_weight.shape[1]
    sh = state_weight.shape[1] // (2 * GROUP)
    ph = step_weight.shape[1] // TP
    fh = gate_weight.shape[1] // TP
    used = 2 * mh + qh + 2 * kvh + 2 * sh + ph
    spare = -used % 256

    half = state_weight.shape[1] // 2
    state_in_part = lax.dynamic_slice_in_dim(state_weight[:, :half], c * (half // 2), half // 2, 1)
    state_out_part = lax.dynamic_slice_in_dim(state_weight[:, half:], c * (half // 2), half // 2, 1)
    mixed = jnp.concatenate(
        [
            state_in_part.reshape(rows, TP, sh),
            state_out_part.reshape(rows, TP, sh),
            step_weight.reshape(rows, TP, ph),
            jnp.zeros((rows, TP, spare), bf),
        ],
        axis=2,
    ).reshape(rows, TP * (2 * sh + ph + spare))
    in_weights = (
        mamba_gate_weight, mamba_input_weight, query_weight, key_weight, value_weight, mixed,
        mamba_out_weight.T, attn_out_weight.T,
    )
    ff_weights = (gate_weight, up_weight, down_weight.T)

    def assemble(slab, after):
        held = [(0, slab)]
        for b in data_bits(n_row, FFN):
            next_held = []
            for mask, part in held:
                if mask:
                    part, unused_value = lax.optimization_barrier((part, after))
                next_held.append((mask | 1 << b, lax.ppermute(part, "row", flips(n_row, 1 << b))))
            held = held + next_held
        return place_slabs(
            [mask for mask, part in held], [part for mask, part in held], n_row
        ).reshape(n_row * rows, slab.shape[2])

    def pick(array, index, axis=0):
        return lax.dynamic_index_in_dim(array, index, axis, keepdims=False)

    def sum_groups(grad, axes, after=None):
        grad = grad.astype(bf)
        bits = data_bits(n_row, axes)
        order = [n_bits - 1 - b for b in bits + [axes[1], axes[0]]]
        if order != sorted(order):
            cutup = grad.reshape((2,) * n_bits + (rows, grad.shape[1]))
            grad = cutup.transpose(order + [n_bits, n_bits + 1]).reshape(grad.shape)
        if after is not None:
            grad, after = lax.optimization_barrier((grad, after))
        by_group = sorted(range(n_row), key=lambda row: [row >> b & 1 for b in bits])
        alike = [
            [row for row in by_group if [row >> b & 1 for b in axes] == [m & 1, m >> 1]]
            for m in range(TP)
        ]
        part = lax.psum_scatter(
            grad, "row", scatter_dimension=0, axis_index_groups=alike, tiled=True
        ).reshape(TP, rows, grad.shape[1])
        return part, after

    meta = jnp.concatenate(
        [
            deal_order,
            jnp.pad(seq_lengths[:, 0, :], ((0, 0), (0, 128 - seq_lengths.shape[2]))),
            jnp.zeros((4, 128), jnp.int32),
        ],
        axis=0,
    )
    meta_all, give, take, x_home, gy_home, normed_one, gy_all, w_mixer, slab_up, slab_down = deal(
        meta, tokens, cotangent, mixer_norm_gain[None, :], in_weights, ff_weights, n_row
    )
    normed_one = normed_one.reshape(GROUP * slots, width)
    gy_all = gy_all.reshape(GROUP * slots, width)
    w_mixer = w_mixer.reshape(width, -1)
    w_in, w_out = w_mixer[:, : used + spare], w_mixer[:, used + spare :]

    def across(array):
        return lax.ppermute(array, "col", [(0, 1), (1, 0)])

    base = r - sum(bit(r, b) * (1 << b) for b in MIX)
    group_meta = jnp.stack([pick(meta_all, base + mask_of(m, MIX)) for m in range(TP)])
    lengths = group_meta[:, 2:4, : seq_lengths.shape[2]].reshape(GROUP, seq_lengths.shape[2])
    half_dim = HD // 2
    inverse = ROPE_BASE ** (-2.0 * jnp.arange(half_dim, dtype=jnp.float32) / HD)
    angles = jnp.arange(slots, dtype=jnp.float32)[:, None] * inverse[None, :]
    cosine, sine = jnp.cos(angles), jnp.sin(angles)
    table = jnp.concatenate([cosine, cosine, -sine, sine], axis=1)

    def piece(array, size, start):
        return lax.dynamic_slice_in_dim(array, start, size, array.ndim - 1)

    eighth = c * TP + t
    chan = jnp.concatenate(
        [
            piece(conv_input, mh, t * mh),
            piece(conv_input_bias[None], mh, t * mh),
            jnp.repeat(piece(skip_scale[None], ph, t * ph), mh // ph, axis=1),
            jnp.zeros((2, mh), jnp.float32),
        ],
        axis=0,
    )
    states = jnp.concatenate([conv_state, conv_state_bias[None]], axis=0)
    states = jnp.concatenate(
        [piece(states, sh, eighth * sh), piece(states, sh, half + eighth * sh)], axis=1
    )
    heads = jnp.concatenate(
        [piece(step_bias[None], ph, t * ph), piece(decay_log[None], ph, t * ph)], axis=0
    )
    after = 128 - 2 * sh - ph
    side = jnp.concatenate(
        [
            jnp.pad(states, ((0, 0), (0, 128 - 2 * sh))),
            jnp.pad(heads, ((0, 0), (2 * sh, after))),
            jnp.zeros((1, 128), jnp.float32),
        ],
        axis=0,
    )

    projected = matmul(normed_one, w_in)
    edges = [0, mh, 2 * mh, 2 * mh + qh, 2 * mh + qh + kvh, 2 * mh + qh + 2 * kvh]
    edges = edges + [edges[-1] + 2 * sh, edges[-1] + 2 * sh + ph]
    branch_in, scanned, crossed = mixer(lengths, projected, chan, side, table, sh, ph)
    branch_part = matmul_trans(branch_in, w_out).astype(bf).reshape(GROUP, slots, width)
    ff_gain = ff_norm_gain[None, :]
    mid, normed_two = middle(branch_part, x_home, ff_gain)
    normed_two = normed_two.reshape(GROUP * slots, width)
    w_gate_up = assemble(slab_up, branch_part)
    w_down = assemble(slab_down, normed_two)

    ff_gate_up = matmul(normed_two, w_gate_up)
    ff_gate, ff_up = ff_gate_up[:, :fh], ff_gate_up[:, fh:]
    ff_hidden = swiglu(ff_gate, ff_up).astype(bf)
    ff_part = matmul_trans(ff_hidden, w_down).astype(bf).reshape(GROUP, slots, width)
    grad_hidden = matmul(gy_all, w_down)
    unused_value, pullback = jax.vjp(swiglu, ff_gate, ff_up)
    grad_gate, grad_up = pullback(grad_hidden)
    grad_gate_up = jnp.concatenate([grad_gate.astype(bf), grad_up.astype(bf)], axis=1)
    normed_two_part = (
        matmul_trans(grad_gate_up, w_gate_up).astype(bf).reshape(GROUP, slots, width)
    )
    grad_ff = jnp.concatenate(
        [matmul_left(normed_two, grad_gate_up).astype(bf), matmul_left(gy_all, ff_hidden).astype(bf)],
        axis=1,
    )
    normed_two_part, grad_ff = lax.optimization_barrier((normed_two_part, grad_ff))
    ff_sums, unused_value = sum_groups(grad_ff, FFN)
    d_mid, delta_ff_gain, branch_all = turn(
        normed_two_part, mid, gy_home, ff_gain
    )
    ff_pairs = ff_part.reshape(TP, 2, slots, width)
    ff_sum = (
        pick(ff_pairs, c, 1).astype(jnp.float32)
        + across(pick(ff_pairs, 1 - c, 1)).astype(jnp.float32)
    ).astype(bf)
    result = mid + pick(ff_sum, member(r, FFN)).astype(jnp.float32)
    for m in (1, 2, 3):
        result = result + lax.ppermute(
            pick(ff_sum, member(partner(r, m, FFN), FFN)), "row", flips(n_row, mask_of(m, FFN))
        ).astype(jnp.float32)
    result = result.astype(bf)
    branch_all = branch_all.reshape(GROUP * slots, width)

    grad_branch_in = matmul(branch_all, w_out)
    grad_projected, chan_sums, side_sums = mixer_back(
        lengths, projected, chan, side, table, scanned, crossed, grad_branch_in, sh, ph
    )
    grad_mixer = jnp.concatenate(
        [
            matmul_left(normed_one, grad_projected).astype(bf),
            matmul_left(branch_all, branch_in).astype(bf),
        ],
        axis=1,
    )
    grad_projected, grad_mixer = lax.optimization_barrier((grad_projected, grad_mixer))
    mixer_sums, ff_sums = sum_groups(grad_mixer, MIX, ff_sums)
    normed_one_part = matmul_trans(grad_projected, w_in).astype(bf).reshape(GROUP, slots, width)

    def lanes(array):
        array = array.reshape((-1, array.shape[-1]))
        array = jnp.pad(array, ((0, 0), (0, -array.shape[1] % 128)))
        return array.reshape(-1, 128)

    small_parts = [
        lanes(part)
        for part in (
            chan_sums[:4],
            chan_sums[4:5],
            side_sums[5:6, 2 * sh : 2 * sh + ph],
            side_sums[6:7, 2 * sh : 2 * sh + ph],
            jnp.sum(chan_sums[5].reshape(ph, -1), axis=1)[None],
            side_sums[:4, : 2 * sh],
            side_sums[4:5, : 2 * sh],
            delta_ff_gain,
        )
    ]
    counts = [part.shape[0] for part in small_parts] + [width // 128]
    small_parts.append(jnp.zeros((-sum(counts) % 8, 128), jnp.float32))
    starts = [sum(counts[:i]) for i in range(len(counts))]
    starts[-1] += small_parts[-1].shape[0]
    output, grad_tokens, small_all, ff_land = send_home(
        normed_one_part, x_home, d_mid, result, mixer_norm_gain[None, :], give, take,
        jnp.concatenate(small_parts, axis=0), ff_sums, n_row,
    )
    mixer_land, other_land = last(mixer_sums, edges[5])
    (
        delta_gate, delta_up, delta_down, delta_mamba_gate, delta_mamba_input,
        delta_query, delta_key, delta_value, delta_mamba_out, delta_attn_out,
    ) = unpack(ff_land, mixer_land, mh, qh, kvh, fh)

    def join(stacked):
        return stacked.transpose(1, 0, 2).reshape(stacked.shape[1], -1).astype(jnp.float32)

    mine = mixer_land[:, :, edges[5] : edges[5] + 128]
    state_first = jnp.where(c == 0, mine, other_land)
    state_second = jnp.where(c == 0, other_land, mine)
    delta_state = jnp.concatenate(
        [
            join(state_first[:, :, :sh]),
            join(state_second[:, :, :sh]),
            join(state_first[:, :, sh : 2 * sh]),
            join(state_second[:, :, sh : 2 * sh]),
        ],
        axis=1,
    )
    delta_step = join(mine[:, :, 2 * sh : 2 * sh + ph])

    small_all = small_all.reshape(TP, 2, -1, 128)
    small_col = pick(small_all, c, 1)

    def taken(array, i):
        return lax.slice_in_dim(array, starts[i], starts[i] + counts[i], axis=array.ndim - 2)

    def along(array, i, size):
        got = taken(array, i).reshape(TP, -1, size + -size % 128)[:, :, :size]
        return got.transpose(1, 0, 2).reshape(got.shape[1], TP * size)

    def state_along(i):
        got = taken(small_all, i)[..., : 2 * sh].reshape(TP, 2, -1, 2, sh)
        return got.transpose(2, 3, 1, 0, 4).reshape(got.shape[2], 2 * half)

    def over_all(i):
        return jnp.sum(taken(small_all, i), axis=(0, 1)).reshape(width)

    by_col = [
        along(small_col, 0, mh),
        along(small_col, 1, mh)[0],
        along(small_col, 2, ph)[0],
        along(small_col, 3, ph)[0],
        along(small_col, 4, ph)[0],
    ]
    by_all = [state_along(5), state_along(6)[0], over_all(8), over_all(7)]

    return (
        output,
        grad_tokens,
        by_all[2],
        delta_mamba_gate,
        delta_mamba_input,
        delta_state,
        delta_step,
        by_col[0],
        by_col[1],
        by_all[0],
        by_all[1],
        by_col[2],
        by_col[3],
        by_col[4],
        delta_mamba_out,
        delta_query,
        delta_key,
        delta_value,
        delta_attn_out,
        by_all[3],
        delta_gate,
        delta_up,
        delta_down,
    )


def solution(mesh):
    both = P("row", "col")
    turned = P("col", "row")
    in_specs = (
        P(None, "row", None),
        P(None, "row", None),
        P(None, "row"),
        P(None, "row", None),
        P(),
        both,
        both,
        P("row", None),
        both,
        P(None, "col"),
        P("col"),
        P(),
        P(),
        P("col"),
        P("col"),
        P("col"),
        turned,
        both,
        both,
        both,
        turned,
        P(),
        both,
        both,
        turned,
    )
    out_specs = (
        P(None, "row", None),
        P(None, "row", None),
        P(),
        both,
        both,
        P("row", None),
        both,
        P(None, "col"),
        P("col"),
        P(),
        P(),
        P("col"),
        P("col"),
        P("col"),
        turned,
        both,
        both,
        both,
        turned,
        P(),
        both,
        both,
        turned,
    )
    return jax.shard_map(local, mesh=mesh, in_specs=in_specs, out_specs=out_specs, check_vma=False)
```

```python
from functools import partial

import jax
import jax.numpy as jnp
from jax import lax
from jax.experimental import pallas as pl
from jax.experimental.pallas import tpu as pltpu
from jax.sharding import PartitionSpec as P

HD = 128
TP = 4
GROUP = 2 * TP
CHUNK = 16
EPS = 1e-05
NEG_LARGE = -1e30
ROPE_BASE = 100000000000.0
MESH = pl.DeviceIdType.MESH
HIGH = lax.Precision.HIGHEST
VMEM = pltpu.VMEM
ANY = pltpu.HBM


def matmul(first_op, second_op):
    return jnp.dot(first_op, second_op, preferred_element_type=jnp.float32)


def matmul_trans(first_op, second_op):
    return lax.dot_general(
        first_op, second_op, (((1,), (1,)), ((), ())), preferred_element_type=jnp.float32
    )


def matmul_left(first_op, second_op):
    return lax.dot_general(
        first_op, second_op, (((0,), (0,)), ((), ())), preferred_element_type=jnp.float32
    )


MIX, FFN = (0, 1), (0, 1)


def data_bits(n_row, axes):
    return [b for b in reversed(range(n_row.bit_length() - 1)) if b not in axes]


def bit(row, b):
    return lax.rem(lax.div(row, 1 << b), 2)


def flip(row, b):
    return row + (1 << b) * (1 - 2 * bit(row, b))


def member(row, axes):
    return bit(row, axes[0]) + 2 * bit(row, axes[1])


def partner(row, m, axes):
    if m & 1:
        row = flip(row, axes[0])
    if m & 2:
        row = flip(row, axes[1])
    return row


def turned_row(row, mask):
    for b in range(mask.bit_length()):
        row = flip(row, b) if mask >> b & 1 else row
    return row


def group_of(row, n_row, axes):
    index = 0
    for b in data_bits(n_row, axes):
        index = index * 2 + bit(row, b)
    return index


def flips(n_row, mask):
    return [(row, row ^ mask) for row in range(n_row)]


def mask_of(m, axes):
    return (m & 1) * (1 << axes[0]) + (m // 2) * (1 << axes[1])


def place():
    return lax.axis_index("row"), lax.axis_index("col")


def block_of(m, axes):
    return member(partner(lax.axis_index("row"), m, axes), axes) * 2


def plan_of(axes, slots):
    if axes != (0, 1) or slots % 32:
        return [(0, slots, 2, 1)]
    return [(0, slots // 2, 1, 2), (slots // 2, slots, 2, 1)]


def params(number, megabytes):
    return pltpu.CompilerParams(
        collective_id=number, has_side_effects=True, vmem_limit_bytes=megabytes << 20
    )


def cost(microseconds):
    return pl.CostEstimate(flops=0, transcendentals=0, bytes_accessed=microseconds * 3_400_000)


def remote(src, dst, send, recv, row, col):
    return pltpu.make_async_remote_copy(
        src_ref=src, dst_ref=dst, send_sem=send, recv_sem=recv, device_id=(row, col), device_id_type=MESH
    )


def greet(*groups, cross=False):
    r, c = place()
    barrier = pltpu.get_barrier_semaphore()
    others = [(r, 1 - c)]
    for axes in groups:
        for m in (1, 2, 3) if cross else (1, 2):
            others.append((partner(r, m, axes), c))
            if cross:
                others.append((partner(r, m, axes), 1 - c))
    for other in others:
        pl.semaphore_signal(barrier, inc=1, device_id=other, device_id_type=MESH)
    pl.semaphore_wait(barrier, len(others))


def gather_start(src, out, send, recv, here, axes):
    r, c = place()
    own = member(r, axes) * 2 + c
    copies = [
        pltpu.make_async_copy(src, out.at[own], here),
        remote(src, out.at[own], send.at[0], recv.at[0], r, 1 - c),
    ]
    for p, (low, high, near, far) in enumerate(plan_of(axes, src.shape[0])):
        for k, m in ((1, near), (2, far)):
            copies.append(
                remote(
                    src.at[low:high], out.at[own, low:high], send.at[6 * p + k], recv.at[6 * p + k],
                    partner(r, m, axes), c,
                )
            )
    for copy in copies[2:] + copies[:2]:
        copy.start()
    return copies


def gather_pass(steps, p, k, m, row, col, out, send, recv, axes):
    r, c = place()
    low, high = plan_of(axes, out.shape[1])[p][:2]
    part = out.at[block_of(m, axes) + c, low:high]
    steps.append(remote(part, part, send.at[6 * p + k], recv.at[6 * p + k], row, col))
    steps[-1].start()


def gather_turn(copies, out, send, recv, axes):
    r, c = place()
    steps = []
    for p, (low, high, near, far) in enumerate(plan_of(axes, out.shape[1])):
        copies[2 + 2 * p].wait_recv()
        gather_pass(steps, p, 3, near, partner(r, far, axes), c, out, send, recv, axes)
        gather_pass(steps, p, 4, near, r, 1 - c, out, send, recv, axes)
    return steps


def gather_finish(copies, steps, out, send, recv, axes):
    r, c = place()
    plan = plan_of(axes, out.shape[1])
    for p, (low, high, near, far) in enumerate(plan):
        copies[3 + 2 * p].wait_recv()
        gather_pass(steps, p, 5, far, r, 1 - c, out, send, recv, axes)
    for p in range(len(plan)):
        steps[2 * p].wait_recv()
        gather_pass(steps, p, 6, 3, r, 1 - c, out, send, recv, axes)
    copies[0].wait()
    copies[1].wait()
    for copy in copies[2:] + steps[: 2 * len(plan) : 2]:
        copy.wait_send()
    for i, copy in enumerate(steps):
        if i >= 2 * len(plan) or i % 2:
            copy.wait()


def gather(src, out, send, recv, here, axes):
    copies = gather_start(src, out, send, recv, here, axes)
    gather_finish(copies, gather_turn(copies, out, send, recv, axes), out, send, recv, axes)


ROWS = 16


def by_rows(count, body, first=0):
    def step(i, carry):
        body(pl.ds(pl.multiple_of(i * ROWS, ROWS), ROWS))
        return carry

    lax.fori_loop(first // ROWS, count // ROWS, step, 0)


def scatter_steps(parts, near, held, far, s1, r1, s2, r2, total, axes):
    r, c = place()
    slots = total.shape[0]
    plan = plan_of(axes, slots)
    pairs = {}
    for m in (3, 1, 2, 0):
        pairs[m] = remote(
            parts.at[block_of(m, axes) + 1 - c], near.at[m], s1.at[m], r1.at[m], r, 1 - c
        )
        pairs[m].start()
    sent = {}

    def pair_sum(m, i, low, high):
        block = block_of(m, axes) + c

        def add(rows):
            held[i, rows, :] = (
                parts[block, rows, :].astype(jnp.float32) + near[m, rows, :].astype(jnp.float32)
            ).astype(jnp.bfloat16)

        by_rows(high, add, low)

    def send(i, p, m):
        low, high = plan[p][:2]
        k = 3 * p + i
        sent[i, p] = remote(
            held.at[i, low:high], far.at[i, low:high], s2.at[k], r2.at[k], partner(r, m, axes), c
        )
        sent[i, p].start()

    yield
    pairs[3].wait_recv()
    for p, (low, high, first, then) in enumerate(plan):
        pair_sum(3, 1, low, high)
        send(1, p, then)
    for m in (1, 2):
        pairs[m].wait_recv()
        for p, (low, high, first, then) in enumerate(plan):
            pair_sum(m, 0 if m == then else 2, low, high)
            if m == then:
                send(0, p, then)
    yield
    for p, (low, high, first, then) in enumerate(plan):
        sent[1, p].wait_recv()

        def add(rows):
            held[2, rows, :] = (
                held[2, rows, :].astype(jnp.float32) + far[1, rows, :].astype(jnp.float32)
            ).astype(jnp.bfloat16)

        by_rows(high, add, low)
        send(2, p, first)
    yield
    pairs[0].wait_recv()
    for p in range(len(plan)):
        sent[0, p].wait_recv()
        sent[2, p].wait_recv()
    own = member(r, axes) * 2 + c

    def fold(rows):
        total[rows, :] = (
            parts[own, rows, :].astype(jnp.float32)
            + near[0, rows, :].astype(jnp.float32)
            + far[0, rows, :].astype(jnp.float32)
            + far[2, rows, :].astype(jnp.float32)
        )

    by_rows(slots, fold)
    for copy in list(pairs.values()) + list(sent.values()):
        copy.wait_send()
    yield


def scatter_sum(*args):
    for step in scatter_steps(*args):
        pass


def scatter_scratch(slots, width):
    return [
        VMEM((TP, slots, width), jnp.bfloat16),
        VMEM((TP - 1, slots, width), jnp.bfloat16),
        VMEM((TP - 1, slots, width), jnp.bfloat16),
        pltpu.SemaphoreType.DMA((TP,)),
        pltpu.SemaphoreType.DMA((TP,)),
        pltpu.SemaphoreType.DMA((6,)),
        pltpu.SemaphoreType.DMA((6,)),
    ]


def gather_scratch():
    return [
        pltpu.SemaphoreType.DMA((13,)),
        pltpu.SemaphoreType.DMA((13,)),
        pltpu.SemaphoreType.DMA,
    ]


def strip_views(refs, owner, piece):
    at = 0
    for ref in refs:
        count = ref.shape[1] // TP
        yield ref.at[:, pl.ds(pl.multiple_of(owner * count, 128), count)], piece.at[:, at : at + count]
        at += count


def cut_start(refs, piece, send, recv, here, axes):
    r, c = place()
    for source, target in strip_views(refs, member(r, axes), piece):
        pltpu.make_async_copy(source, target, here).start()
    for m in (3, 1, 2):
        other = partner(r, m, axes)
        for source, target in strip_views(refs, member(other, axes), piece):
            remote(source, target, send.at[m], recv.at[m], other, c).start()


def piece_done(piece, sem):
    pltpu.make_async_copy(piece, piece, sem).wait()


def weight_forward(masks, whole, cols, send, recv):
    r, c = place()
    n_row = lax.axis_size("row")
    bits = data_bits(n_row, MIX)
    copies = []
    for mask in masks:
        at = whole.at[turned_row(r, mask), :, cols]
        crossed = [k for k, b in enumerate(bits) if mask >> b & 1]
        if crossed:
            piece_done(at, recv.at[mask])
        for b in bits[max([-1] + crossed) + 1 :]:
            lands = mask | 1 << b
            copies.append(remote(at, at, send.at[lands], recv.at[lands], flip(r, b), c))
            copies[-1].start()
    return copies


def weight_rounds(n_row, held):
    rounds = []
    for b in data_bits(n_row, MIX):
        rounds.append([mask | 1 << b for mask in held])
        held = held + rounds[-1]
    return rounds


def spread(masks, whole, cols, send, recv):
    r, c = place()
    copies = []
    for mask in masks:
        at = whole.at[turned_row(r, mask), :, cols]
        for m in (3, 1, 2):
            lands = mask | mask_of(m, MIX)
            copies.append(remote(at, at, send.at[lands], recv.at[lands], partner(r, m, MIX), c))
            copies[-1].start()
    return copies


def place_kernel(masks, n_row, *refs):
    slabs, whole, sems = refs[: len(masks)], refs[-2], refs[-1]
    r, c = place()
    copies = []
    for i, mask in enumerate(masks):
        at = whole.at[group_of(turned_row(r, mask), n_row, FFN)]
        copies.append(pltpu.make_async_copy(slabs[i], at, sems.at[i]))
        copies[-1].start()
    for copy in copies:
        copy.wait()


def place_slabs(masks, slabs, n_row):
    return pl.pallas_call(
        partial(place_kernel, masks, n_row),
        name="place",
        out_shape=jax.ShapeDtypeStruct((len(masks),) + slabs[0].shape, slabs[0].dtype),
        in_specs=[pl.BlockSpec(memory_space=ANY)] * len(masks),
        out_specs=pl.BlockSpec(memory_space=ANY),
        scratch_shapes=[pltpu.SemaphoreType.DMA((len(masks),))],
        compiler_params=pltpu.CompilerParams(vmem_limit_bytes=4 << 20),
        cost_estimate=cost(4),
    )(*slabs)


def exchange_rows(buf, land, send, recv):
    r, c = place()
    n_row = lax.axis_size("row")

    def copy(other):
        return remote(
            buf.at[other], land.at[r], send.at[other], recv.at[r], other, c
        )

    def start(off, carry):
        copy(lax.rem(r + off, n_row)).start()
        return carry

    lax.fori_loop(1, n_row, start, 0)


def finish_rows(buf, land, send, recv):
    r, c = place()
    n_row = lax.axis_size("row")

    def finish(off, carry):
        other = lax.rem(r + off, n_row)
        copy = remote(buf.at[other], land.at[other], send.at[other], recv.at[other], other, c)
        copy.wait_send()
        copy.wait_recv()
        return carry

    lax.fori_loop(1, n_row, finish, 0)


def greet_rows():
    r, c = place()
    n_row = lax.axis_size("row")
    barrier = pltpu.get_barrier_semaphore()

    def greet(off, carry):
        pl.semaphore_signal(
            barrier, inc=1, device_id=(lax.rem(r + off, n_row), c), device_id_type=MESH
        )
        return carry

    lax.fori_loop(1, n_row, greet, 0)
    pl.semaphore_signal(barrier, inc=1, device_id=(r, 1 - c), device_id_type=MESH)
    pl.semaphore_wait(barrier, n_row)


COLS = 512


def permute_out(choice, buf, first, second, slots):
    n_row = buf.shape[0]

    def column(i, carry):
        cols = pl.ds(pl.multiple_of(i * COLS, COLS), COLS)
        picked = matmul(choice[:, :slots], first[:, cols]) + matmul(choice[:, slots:], second[:, cols])
        buf[:, :, cols] = picked.astype(jnp.bfloat16).reshape(n_row, CHUNK, COLS)
        return carry

    lax.fori_loop(0, buf.shape[2] // COLS, column, 0)


def permute_in(choice, land, first, second, slots):
    n_row = land.shape[0]

    def column(i, carry):
        cols = pl.ds(pl.multiple_of(i * COLS, COLS), COLS)
        got = land[:, :, cols].reshape(n_row * CHUNK, COLS)
        first[:, cols] = matmul_left(choice[:, :slots], got).astype(jnp.bfloat16)
        second[:, cols] = matmul_left(choice[:, slots:], got).astype(jnp.bfloat16)
        return carry

    lax.fori_loop(0, land.shape[2] // COLS, column, 0)


def deal_kernel(
    meta, tokens, cotangent, gain, *refs
):
    kv_refs, first_refs, second_refs, refs = refs[:2], refs[2:5], refs[5:8], refs[8:]
    up_refs, down_refs, refs = refs[:2], refs[2:3], refs[3:]
    meta_all, give, take, x_out, gy_out, normed_all, gy_all, whole, slab_up, slab_down = refs[:10]
    x_mine, g_mine, buf, land, normed = refs[10:15]
    load, msend, mrecv, csend, crecv, nsend, nrecv, nhere, gsend, grecv, ghere = refs[15:26]
    wsend, wrecv, acut, arecv, ahere, bcut, brecv, bhere, usend, urecv, uhere, dsend, drecv, dhere, kv_here = refs[26:]
    r, c = place()
    n_row = lax.axis_size("row")
    f = member(r, FFN)
    slots = x_mine.shape[0]
    per_peer = slots // n_row
    loads = [
        pltpu.make_async_copy(tokens.at[c], x_mine, load.at[0]),
        pltpu.make_async_copy(cotangent.at[c], g_mine, load.at[1]),
    ]
    for copy in loads:
        copy.start()
    greet_rows()
    group = [mask_of(m, MIX) for m in range(TP)]
    first_cols = sum(ref.shape[1] for ref in first_refs) // TP
    kv_cols = first_cols + sum(ref.shape[1] for ref in kv_refs)
    cuts = (
        (slice(0, first_cols), first_refs, acut, arecv, ahere),
        (slice(kv_cols, whole.shape[2]), second_refs, bcut, brecv, bhere),
    )
    kv = slice(first_cols, kv_cols)

    def meta_copy(other, slot):
        return remote(meta, meta_all.at[slot], msend.at[other], mrecv.at[slot], other, c)

    def start(off, carry):
        meta_copy(lax.rem(r + off, n_row), r).start()
        return carry

    lax.fori_loop(1, n_row, start, 0)
    meta_all[r] = meta[...]
    at = first_cols
    for ref in kv_refs:
        pltpu.make_async_copy(ref, whole.at[r, :, at : at + ref.shape[1]], kv_here).start()
        at += ref.shape[1]
    for cols, refs_of, send, recv, here in cuts:
        cut_start(refs_of, whole.at[r, :, cols], send, recv, here, MIX)
    forwards = []
    for i, (cols, refs_of, send, recv, here) in enumerate(cuts):
        piece_done(whole.at[r, :, cols], here)
        forwards = forwards + weight_forward([0], whole, cols, wsend.at[i], wrecv.at[i])
    piece_done(whole.at[r, :, kv], kv_here)
    forwards = forwards + weight_forward([0], whole, kv, wsend.at[2], wrecv.at[2])

    def finish(off, carry):
        other = lax.rem(r + off, n_row)
        copy = meta_copy(other, other)
        copy.wait_send()
        copy.wait_recv()
        return carry

    lax.fori_loop(1, n_row, finish, 0)

    shift = slots.bit_length() - 1
    row_no = lax.broadcasted_iota(jnp.int32, (CHUNK, slots), 0)
    wanted = jnp.where(row_no < per_peer, row_no, row_no - per_peer).astype(jnp.float32)
    early = row_no < per_peer
    late = (row_no >= per_peer) & (row_no < 2 * per_peer)
    tri = (
        lax.broadcasted_iota(jnp.int32, (slots, slots), 0)
        < lax.broadcasted_iota(jnp.int32, (slots, slots), 1)
    ).astype(jnp.float32).astype(jnp.bfloat16)
    places = lax.broadcasted_iota(jnp.int32, (slots, slots), 0)

    def order_of(block):
        picked = jnp.where(c == 0, block[0:1, :], block[1:2, :])
        return lax.shift_right_logical(picked, shift), picked - lax.shift_left(
            lax.shift_right_logical(picked, shift), shift
        )

    own_source, own_local = order_of(meta[...])

    def select(mask):
        wide = jnp.broadcast_to(mask.astype(jnp.float32), (CHUNK, slots)).astype(jnp.bfloat16)
        rank = matmul(wide, tri)
        return jnp.where(
            (rank == wanted) & (wide.astype(jnp.float32) > 0.5), 1.0, 0.0
        )

    def build(d, carry):
        rows = pl.ds(pl.multiple_of(d * CHUNK, CHUNK), CHUNK)
        source, local = order_of(meta_all[d])
        chosen = select(source == r).astype(jnp.bfloat16)
        at_home = (places == local).astype(jnp.float32).astype(jnp.bfloat16)
        picks = matmul_trans(chosen, at_home)
        give[rows, :slots] = jnp.where(early, picks, 0.0).astype(jnp.bfloat16)
        give[rows, slots:] = jnp.where(late, picks, 0.0).astype(jnp.bfloat16)
        kept = select(own_source == d)
        take[rows, :slots] = jnp.where(early, kept, 0.0).astype(jnp.bfloat16)
        take[rows, slots:] = jnp.where(late, kept, 0.0).astype(jnp.bfloat16)
        return carry

    lax.fori_loop(0, n_row, build, 0)
    for copy in loads:
        copy.wait()
    permute_out(give, buf, x_mine, g_mine, slots)
    exchange_rows(buf, land, csend, crecv)
    land[r] = buf[r]
    for i, (cols, refs_of, send, recv, here) in enumerate(cuts):
        for m in (1, 2, 3):
            piece_done(whole.at[r, :, cols], recv.at[m])
            forwards = forwards + weight_forward([group[m]], whole, cols, wsend.at[i], wrecv.at[i])
    finish_rows(buf, land, csend, crecv)
    permute_in(take, land, x_out, gy_out, slots)

    def norm(rows):
        values = x_out[rows, :].astype(jnp.float32)
        scale = lax.rsqrt(jnp.mean(values * values, axis=-1, keepdims=True) + EPS)
        normed[rows, :] = (values * scale * gain[...]).astype(jnp.bfloat16)

    by_rows(slots, norm)
    first = gather_start(normed, normed_all, nsend, nrecv, nhere, MIX)
    cut_start(up_refs, slab_up.at[f], usend, urecv, uhere, FFN)
    cut_start(down_refs, slab_down.at[f], dsend, drecv, dhere, FFN)
    second = gather_start(gy_out, gy_all, gsend, grecv, ghere, FFN)
    kv_rounds = weight_rounds(n_row, [0])
    steps = []
    for k, masks in enumerate(weight_rounds(n_row, group)):
        forwards = forwards + weight_forward(kv_rounds[k], whole, kv, wsend.at[2], wrecv.at[2])
        for i in (0, 1):
            forwards = forwards + weight_forward(masks, whole, cuts[i][0], wsend.at[i], wrecv.at[i])
            if k == 0 and i == 0:
                steps.append(gather_turn(first, normed_all, nsend, nrecv, MIX))
            if k == 0 and i == 1:
                steps.append(gather_turn(second, gy_all, gsend, grecv, FFN))
        if k == len(kv_rounds) - 1:
            kv_held = [0] + [mask for masks in kv_rounds for mask in masks]
            spreads = spread(kv_held, whole, kv, wsend.at[2], wrecv.at[2])
    gather_finish(first, steps[0], normed_all, nsend, nrecv, MIX)
    gather_finish(second, steps[1], gy_all, gsend, grecv, FFN)
    for copy in forwards:
        copy.wait_send()
    for cols, refs_of, send, recv, here in cuts:
        for m in (1, 2, 3):
            piece_done(whole.at[r, :, cols], send.at[m])
    for copy in spreads:
        copy.wait()
    for slab, send, recv, here in ((slab_up, usend, urecv, uhere), (slab_down, dsend, drecv, dhere)):
        piece_done(slab.at[f], here)
        for m in (1, 2, 3):
            piece_done(slab.at[f], send.at[m])
            piece_done(slab.at[f], recv.at[m])


def deal(meta, tokens, cotangent, gain, in_weights, ff_weights, n_row):
    slots, width = tokens.shape[1:]
    bf = jnp.bfloat16
    rows = in_weights[0].shape[0]
    in_cols = sum(
        array.shape[1] // (1 if i < 2 else TP) for i, array in enumerate(in_weights)
    )
    up_cols, down_cols = 2 * ff_weights[0].shape[1] // TP, ff_weights[2].shape[1] // TP
    vm, hb = pl.BlockSpec(memory_space=VMEM), pl.BlockSpec(memory_space=ANY)
    dma = pltpu.SemaphoreType.DMA
    return pl.pallas_call(
        deal_kernel,
        name="deal",
        out_shape=(
            jax.ShapeDtypeStruct((n_row, 8, 128), jnp.int32),
            jax.ShapeDtypeStruct((n_row * CHUNK, 2 * slots), bf),
            jax.ShapeDtypeStruct((n_row * CHUNK, 2 * slots), bf),
            jax.ShapeDtypeStruct((slots, width), bf),
            jax.ShapeDtypeStruct((slots, width), bf),
            jax.ShapeDtypeStruct((GROUP, slots, width), bf),
            jax.ShapeDtypeStruct((GROUP, slots, width), bf),
            jax.ShapeDtypeStruct((n_row, rows, in_cols), bf),
            jax.ShapeDtypeStruct((TP, rows, up_cols), bf),
            jax.ShapeDtypeStruct((TP, rows, down_cols), bf),
        ),
        in_specs=[vm, hb, hb, vm] + [hb] * 11,
        out_specs=(vm,) * 5 + (hb,) * 5,
        scratch_shapes=[
            VMEM((slots, width), bf),
            VMEM((slots, width), bf),
            VMEM((n_row, CHUNK, width), bf),
            VMEM((n_row, CHUNK, width), bf),
            VMEM((slots, width), bf),
            dma((2,)),
            dma((n_row,)),
            dma((n_row,)),
            dma((n_row,)),
            dma((n_row,)),
        ]
        + gather_scratch()
        + gather_scratch()
        + [dma((3, n_row)), dma((3, n_row))]
        + [dma((TP,)), dma((TP,)), dma] * 4
        + [dma],
        compiler_params=params(0, 58),
        cost_estimate=cost(100),
    )(meta, tokens, cotangent, gain, *in_weights, *ff_weights)


def middle_kernel(parts, x, gain, mid, normed_all, near, out2, far, s1, r1, s2, r2, normed, nsend, nrecv, nhere):
    greet(*{MIX, FFN})
    scatter_sum(parts, near, out2, far, s1, r1, s2, r2, mid, MIX)

    def norm(rows):
        values = x[rows, :].astype(jnp.float32) + mid[rows, :]
        mid[rows, :] = values
        scale = lax.rsqrt(jnp.mean(values * values, axis=-1, keepdims=True) + EPS)
        normed[rows, :] = (values * scale * gain[...]).astype(jnp.bfloat16)

    by_rows(mid.shape[0], norm)
    gather(normed, normed_all, nsend, nrecv, nhere, FFN)


def middle(parts, x, gain):
    slots, width = x.shape
    return pl.pallas_call(
        middle_kernel,
        name="middle",
        out_shape=(
            jax.ShapeDtypeStruct((slots, width), jnp.float32),
            jax.ShapeDtypeStruct((GROUP, slots, width), jnp.bfloat16),
        ),
        in_specs=[pl.BlockSpec(memory_space=VMEM)] * 3,
        out_specs=(pl.BlockSpec(memory_space=VMEM), pl.BlockSpec(memory_space=ANY)),
        scratch_shapes=scatter_scratch(slots, width)
        + [VMEM((slots, width), jnp.bfloat16)]
        + gather_scratch(),
        compiler_params=params(1, 40),
        cost_estimate=cost(60),
    )(parts, x, gain)


def norm_back(values, gain, grad):
    inverse = lax.rsqrt(jnp.mean(values * values, axis=-1, keepdims=True) + EPS)
    scaled = grad * gain
    back = inverse * scaled - values * (
        inverse * inverse * inverse * jnp.mean(values * scaled, axis=-1, keepdims=True)
    )
    return back, jnp.sum(grad * values * inverse, axis=0, keepdims=True)


def turn_kernel(
    parts, mid, gy, gain, d_mid, d_gain, branch_all,
    near, out2, far, s1, r1, s2, r2, branch, nsend, nrecv, nhere,
):
    greet(*{MIX, FFN})
    scatter_sum(parts, near, out2, far, s1, r1, s2, r2, d_mid, FFN)
    d_gain[...] = jnp.zeros_like(d_gain)

    def back(rows):
        values = mid[rows, :]
        grad, gain_part = norm_back(values, gain[...], d_mid[rows, :])
        grad = gy[rows, :].astype(jnp.float32) + grad
        d_mid[rows, :] = grad
        branch[rows, :] = grad.astype(jnp.bfloat16)
        d_gain[...] += gain_part

    by_rows(mid.shape[0], back)
    gather(branch, branch_all, nsend, nrecv, nhere, MIX)


def turn(parts, mid, gy, gain):
    slots, width = mid.shape
    return pl.pallas_call(
        turn_kernel,
        name="turn",
        out_shape=(
            jax.ShapeDtypeStruct((slots, width), jnp.float32),
            jax.ShapeDtypeStruct((1, width), jnp.float32),
            jax.ShapeDtypeStruct((GROUP, slots, width), jnp.bfloat16),
        ),
        in_specs=[pl.BlockSpec(memory_space=VMEM)] * 4,
        out_specs=(pl.BlockSpec(memory_space=VMEM),) * 2 + (pl.BlockSpec(memory_space=ANY),),
        scratch_shapes=scatter_scratch(slots, width)
        + [VMEM((slots, width), jnp.bfloat16)]
        + gather_scratch(),
        compiler_params=params(2, 48),
        cost_estimate=cost(60),
    )(parts, mid, gy, gain)


def home_kernel(
    parts, x, d_mid, result, gain, give, take, small, kv_parts, ff_sums,
    output, gradient, small_all, kv_sums, ff_land,
    near, out2, far, s1, r1, s2, r2, total, first, second, buf, land, csend, crecv, here, osend, orecv,
    d_gain, stages, stage_land, tsend, trecv, gsend, grecv, ghere, *more
):
    r, c = place()
    slots, width = x.shape
    bits = data_bits(lax.axis_size("row"), MIX)
    greet_rows()
    kv_near, kv_held, kv_far, kv_s1, kv_r1, kv_s2, kv_r2 = more[3:]
    delivered = deliver(ff_sums, ff_land, *more[:3], FFN)
    scatter_sum(parts, near, out2, far, s1, r1, s2, r2, total, MIX)
    d_gain[...] = jnp.zeros_like(d_gain)

    def back(rows):
        values = x[rows, :].astype(jnp.float32)
        grad, gain_part = norm_back(values, gain[...], total[rows, :])
        second[rows, :] = (d_mid[rows, :] + grad).astype(jnp.bfloat16)
        first[rows, :] = result[rows, :].astype(jnp.bfloat16)
        d_gain[...] += gain_part

    by_rows(slots, back)
    head = small.shape[0]
    stages[0, :head, :] = small[...]
    for k in range(width // 128):
        stages[0, head + k : head + k + 1, :] = d_gain[:, k * 128 : (k + 1) * 128]

    def stage_copy(i):
        return remote(
            stages.at[i], stage_land.at[i], tsend.at[i], trecv.at[i], flip(r, bits[i]), c
        )

    stage_copy(0).start()
    permute_out(take, buf, first, second, slots)
    exchange_rows(buf, land, csend, crecv)
    land[r] = buf[r]
    own = member(r, MIX)
    groups = kv_parts.shape[0]
    kv_sent = []
    for m in (3, 1, 2):
        other = partner(r, m, MIX)
        kv_sent.append(
            remote(kv_parts.at[:, member(other, MIX)], kv_near.at[m], kv_s1.at[m], kv_r1.at[m], other, c)
        )
        kv_sent[-1].start()
    for i in range(len(bits)):
        stage_copy(i).wait()
        stages[i + 1] = stages[i] + stage_land[i]
        if i + 1 < len(bits):
            stage_copy(i + 1).start()
    started = gather_start(stages.at[len(bits)], small_all, gsend, grecv, ghere, MIX)
    for copy in kv_sent:
        copy.wait()
    passed = gather_turn(started, small_all, gsend, grecv, MIX)

    def kv_pair(g):
        kv_held[g] = (
            kv_parts[g, own].astype(jnp.float32)
            + kv_near[1, g].astype(jnp.float32)
            + kv_near[2, g].astype(jnp.float32)
            + kv_near[3, g].astype(jnp.float32)
        ).astype(jnp.bfloat16)

    each_block(0, groups, kv_pair)
    kv_far_sent = []
    for k in range(1, groups):
        other = turned_row(r, sum((1 << b) * (k >> i & 1) for i, b in enumerate(bits)))
        kv_far_sent.append(
            remote(
                kv_held.at[group_of(other, lax.axis_size("row"), MIX)],
                kv_far.at[k], kv_s2.at[k], kv_r2.at[k], other, c,
            )
        )
        kv_far_sent[-1].start()
    finish_rows(buf, land, csend, crecv)
    permute_in(give, land, first, second, slots)
    copies = []
    for i, (mine, out) in enumerate(((first, output), (second, gradient))):
        copies.append(pltpu.make_async_copy(mine, out.at[c], here.at[i]))
        copies.append(remote(mine, out.at[c], osend.at[i], orecv.at[i], r, 1 - c))
    for copy in copies:
        copy.start()
    gather_finish(started, passed, small_all, gsend, grecv, MIX)
    for copy in kv_far_sent:
        copy.wait()
    kv_total = kv_held[group_of(r, lax.axis_size("row"), MIX)].astype(jnp.float32)
    for k in range(1, groups):
        kv_total = kv_total + kv_far[k].astype(jnp.float32)
    kv_sums[...] = kv_total
    for copy in copies + delivered:
        copy.wait()


def deliver(sums, land, send, recv, here, axes):
    r, c = place()
    own = member(r, axes)
    copies = [pltpu.make_async_copy(sums.at[own], land.at[own], here)]
    for m in (3, 1, 2):
        other = partner(r, m, axes)
        copies.append(
            remote(sums.at[member(other, axes)], land.at[own], send.at[m], recv.at[m], other, c)
        )
    for copy in copies:
        copy.start()
    return copies


def deliver_scratch():
    dma = pltpu.SemaphoreType.DMA
    return [dma((TP,)), dma((TP,)), dma]


def last_kernel(at, sums, land, other, s1, r1, here, send, recv):
    r, c = place()
    barrier = pltpu.get_barrier_semaphore()
    for m in (1, 2, 3):
        pl.semaphore_signal(barrier, inc=1, device_id=(partner(r, m, MIX), c), device_id_type=MESH)
    pl.semaphore_signal(barrier, inc=1, device_id=(r, 1 - c), device_id_type=MESH)
    pl.semaphore_wait(barrier, 4)
    for copy in deliver(sums, land, s1, r1, here, MIX):
        copy.wait()
    across = remote(land.at[:, :, at : at + 128], other, send, recv, r, 1 - c)
    across.start()
    across.wait()


def last(sums, at):
    hb = pl.BlockSpec(memory_space=ANY)
    dma = pltpu.SemaphoreType.DMA
    return pl.pallas_call(
        partial(last_kernel, at),
        name="last",
        out_shape=(
            jax.ShapeDtypeStruct(sums.shape, sums.dtype),
            jax.ShapeDtypeStruct(sums.shape[:2] + (128,), sums.dtype),
        ),
        in_specs=[hb],
        out_specs=(hb,) * 2,
        scratch_shapes=deliver_scratch() + [dma, dma],
        compiler_params=params(6, 4),
        cost_estimate=cost(25),
    )(sums)


def products_kernel(parts, *refs):
    pairs = len(refs) - len(parts)
    for part, out in zip(parts, refs[pairs:]):
        at = 0
        for i, low, high in part:
            left, right = refs[2 * i], refs[2 * i + 1]
            out[:, at : at + high - low] = dot(left[...], right[:, low:high], 0, 0).astype(out.dtype)
            at += high - low


def products(pairs, *parts):
    tokens, width = pairs[0][0].shape
    tile = 256
    specs = []
    for left, right in pairs:
        specs.append(pl.BlockSpec((tokens, tile), lambda i: (0, i)))
        specs.append(pl.BlockSpec(right.shape, lambda i: (0, 0)))
    totals = [sum(high - low for i, low, high in part) for part in parts]
    return pl.pallas_call(
        partial(products_kernel, parts),
        name="products",
        grid=(width // tile,),
        out_shape=tuple(jax.ShapeDtypeStruct((width, total), jnp.bfloat16) for total in totals),
        in_specs=specs,
        out_specs=tuple(pl.BlockSpec((tile, total), lambda i: (i, 0)) for total in totals),
        compiler_params=pltpu.CompilerParams(vmem_limit_bytes=40 << 20),
        cost_estimate=cost(10),
    )(*[array for pair in pairs for array in pair])


def unpack_kernel(
    ff, mixer, gate, up, down, mamba_gate, mamba_input, query, mamba_out, attn_out
):
    f32 = jnp.float32
    mh = mamba_gate.shape[1] // TP
    fh = gate.shape[1] // TP
    qh = query.shape[1] // TP
    at = 2 * mh + qh
    out = mixer.shape[2] - mh - qh
    for m in range(TP):
        def cols(size):
            return slice(m * size, (m + 1) * size)

        gate[:, cols(fh)] = ff[m, :, :fh].astype(f32)
        up[:, cols(fh)] = ff[m, :, fh : 2 * fh].astype(f32)
        down[cols(fh), :] = ff[m, :, 2 * fh :].astype(f32).T
        mamba_gate[:, cols(mh)] = mixer[m, :, :mh].astype(f32)
        mamba_input[:, cols(mh)] = mixer[m, :, mh : 2 * mh].astype(f32)
        query[:, cols(qh)] = mixer[m, :, 2 * mh : at].astype(f32)
        mamba_out[cols(mh), :] = mixer[m, :, out : out + mh].astype(f32).T
        attn_out[cols(qh), :] = mixer[m, :, out + mh :].astype(f32).T


def unpack(ff, mixer, mh, qh, fh):
    rows = ff.shape[1]
    vm = pl.BlockSpec(memory_space=VMEM)
    shapes = [(rows, TP * fh)] * 2 + [(TP * fh, rows)] + [(rows, TP * mh)] * 2
    shapes += [(rows, TP * qh), (TP * mh, rows), (TP * qh, rows)]
    return pl.pallas_call(
        unpack_kernel,
        name="unpack",
        out_shape=tuple(jax.ShapeDtypeStruct(shape, jnp.float32) for shape in shapes),
        in_specs=[vm] * 2,
        out_specs=(vm,) * len(shapes),
        compiler_params=pltpu.CompilerParams(vmem_limit_bytes=40 << 20),
        cost_estimate=cost(8),
    )(ff, mixer)


def send_home(parts, x, d_mid, result, gain, give, take, small, kv_parts, ff_sums, n_row):
    slots, width = x.shape
    bf = jnp.bfloat16
    size = small.shape[0] + width // 128
    phases = len(data_bits(n_row, MIX))
    return pl.pallas_call(
        home_kernel,
        name="home",
        out_shape=(
            jax.ShapeDtypeStruct((2, slots, width), bf),
            jax.ShapeDtypeStruct((2, slots, width), bf),
            jax.ShapeDtypeStruct((GROUP, size, 128), jnp.float32),
            jax.ShapeDtypeStruct(kv_parts.shape[2:], jnp.float32),
            jax.ShapeDtypeStruct(ff_sums.shape, bf),
        ),
        in_specs=[pl.BlockSpec(memory_space=VMEM)] * 9 + [pl.BlockSpec(memory_space=ANY)],
        out_specs=(
            (pl.BlockSpec(memory_space=ANY),) * 3
            + (pl.BlockSpec(memory_space=VMEM), pl.BlockSpec(memory_space=ANY))
        ),
        scratch_shapes=scatter_scratch(slots, width)
        + [
            VMEM((slots, width), jnp.float32),
            VMEM((slots, width), bf),
            VMEM((slots, width), bf),
            VMEM((n_row, CHUNK, width), bf),
            VMEM((n_row, CHUNK, width), bf),
            pltpu.SemaphoreType.DMA((n_row,)),
            pltpu.SemaphoreType.DMA((n_row,)),
            pltpu.SemaphoreType.DMA((2,)),
            pltpu.SemaphoreType.DMA((2,)),
            pltpu.SemaphoreType.DMA((2,)),
            VMEM((1, width), jnp.float32),
            VMEM((phases + 1, size, 128), jnp.float32),
            VMEM((phases, size, 128), jnp.float32),
            pltpu.SemaphoreType.DMA((phases,)),
            pltpu.SemaphoreType.DMA((phases,)),
        ]
        + gather_scratch()
        + deliver_scratch()
        + [
            VMEM((TP, kv_parts.shape[0]) + kv_parts.shape[2:], bf),
            VMEM((kv_parts.shape[0],) + kv_parts.shape[2:], bf),
            VMEM((kv_parts.shape[0],) + kv_parts.shape[2:], bf),
            pltpu.SemaphoreType.DMA((TP,)),
            pltpu.SemaphoreType.DMA((TP,)),
            pltpu.SemaphoreType.DMA((kv_parts.shape[0],)),
            pltpu.SemaphoreType.DMA((kv_parts.shape[0],)),
        ],
        compiler_params=params(3, 48),
        cost_estimate=cost(75),
    )(parts, x, d_mid, result, gain, give, take, small, kv_parts, ff_sums)


def blocks_start(low, land, s1, r1):
    r, c = place()
    copies = []
    for m, f in CROSSED:
        col = 1 - c if f else c
        k = m * 2 + f
        copies.append(
            remote(low.at[block_of(m, MIX) + col], land.at[k], s1.at[k], r1.at[k], partner(r, m, MIX), col)
        )
        copies[-1].start()
    return copies


def blocks_turn(first, low, land, mine, total, s2, r2, here):
    r, c = place()
    own = member(r, MIX) * 2 + c
    for copy in first:
        copy.wait_recv()
    summed = low[own].astype(jnp.float32)
    for m, f in CROSSED:
        summed = summed + land[m * 2 + f].astype(jnp.float32)
    mine[...] = summed.astype(jnp.bfloat16)
    copies = [pltpu.make_async_copy(mine, total.at[own], here)]
    for m, f in CROSSED:
        k = m * 2 + f
        copies.append(
            remote(mine, total.at[own], s2.at[k], r2.at[k], partner(r, m, MIX), 1 - c if f else c)
        )
    for copy in copies:
        copy.start()
    return copies


def blocks_finish(first, second):
    for copy in first:
        copy.wait_send()
    for copy in second:
        copy.wait()


CROSSED = [(m, f) for m in (3, 1, 2) for f in (0, 1)] + [(0, 1)]


def blocks_scratch(slots):
    dma = pltpu.SemaphoreType.DMA
    return [
        VMEM((GROUP, slots, slots), jnp.bfloat16),
        VMEM((GROUP, slots, slots), jnp.bfloat16),
        VMEM((slots, slots), jnp.bfloat16),
        dma((GROUP,)),
        dma((GROUP,)),
        dma((GROUP,)),
        dma((GROUP,)),
        dma,
    ]


def dot(first_op, second_op, first_dim, second_dim, precision=None):
    return lax.dot_general(
        first_op,
        second_op,
        (((first_dim,), (second_dim,)), ((), ())),
        precision=precision,
        preferred_element_type=jnp.float32,
    )


def block_rows(b, slots):
    return pl.ds(pl.multiple_of(b * slots, slots), slots)


def marks(lens, b, slots):
    row = lax.broadcasted_iota(jnp.int32, (slots, slots), 0)
    col = lax.broadcasted_iota(jnp.int32, (slots, slots), 1)
    row_segment, col_segment, within = jnp.zeros_like(row), jnp.zeros_like(row), row
    end = 0
    for k in range(lens.shape[1] - 1):
        end = end + lens[b, k]
        row_segment = row_segment + (row >= end).astype(jnp.int32)
        col_segment = col_segment + (col >= end).astype(jnp.int32)
        within = jnp.where(row >= end, row - end, within)
    return (row_segment == col_segment) & (row >= col), within


def conv_pre(values, within, weights):
    width = values.shape[1]
    shifted = [values]
    for k in range(1, 4):
        valid = within[:, :1] >= k
        shifted.append(jnp.where(valid, pltpu.roll(values, k, 0), 0.0))
    pre = weights[4:5, :]
    for k in range(4):
        pre = pre + weights[3 - k : 4 - k, :] * shifted[k]
    return pre, shifted


def conv_back(grad, pre, shifted, within, weights):
    slots = grad.shape[0]
    gate = jax.nn.sigmoid(pre)
    e = grad * gate * (1.0 + pre * (1.0 - gate))
    sums = [jnp.sum(e * shifted[3 - i], axis=0, keepdims=True) for i in range(4)]
    sums.append(jnp.sum(e, axis=0, keepdims=True))
    back = weights[3:4, :] * e
    for k in range(1, 4):
        valid = within[:, :1] >= k
        back = back + weights[3 - k : 4 - k, :] * pltpu.roll(jnp.where(valid, e, 0.0), slots - k, 0)
    return back, sums


def softplus(values):
    return jnp.maximum(values, 0.0) + jnp.log1p(jnp.exp(-jnp.abs(values)))


def steps_and_levels(mixed, side, low, count):
    slots, width = mixed.shape
    lane = lax.broadcasted_iota(jnp.int32, (slots, width), 1)
    inside = (lane >= low) & (lane < low + count)
    step = jnp.where(inside, softplus(mixed + side[5:6, :]), 0.0)
    rate = jnp.where(inside, -jnp.exp(side[6:7, :]), 0.0)
    row = lax.broadcasted_iota(jnp.int32, (slots, slots), 0)
    col = lax.broadcasted_iota(jnp.int32, (slots, slots), 1)
    tri = (row >= col).astype(jnp.float32)
    level = dot(tri, step * rate, 1, 0, HIGH)
    return step, rate, level, tri, inside


def halves(first, second):
    lane = lax.broadcasted_iota(jnp.int32, first.shape, 1)
    return jnp.where(lane < first.shape[1] // 2, first, second)


def state_parts(mixed, within, side, sh):
    pre, shifted = conv_pre(mixed, within, side)
    act = pre * jax.nn.sigmoid(pre)
    lane = lax.broadcasted_iota(jnp.int32, act.shape, 1)
    first = jnp.where(lane < sh, act, 0.0).astype(jnp.bfloat16)
    second = jnp.where(lane < sh, pltpu.roll(act, act.shape[1] - sh, 1), 0.0).astype(jnp.bfloat16)
    return first, second, pre, shifted


def turned_pair(values, waves):
    half = values.shape[1] // 2
    return values * waves[:, : 2 * half] + pltpu.roll(values, half, 1) * waves[:, 2 * half :]


def turned_back(values, waves):
    half = values.shape[1] // 2
    return values * waves[:, : 2 * half] - pltpu.roll(values, half, 1) * waves[:, 2 * half :]


def wave_rows(within, table):
    slots = within.shape[0]
    picks = (within == lax.broadcasted_iota(jnp.int32, (slots, slots), 1)).astype(jnp.float32)
    return dot(picks, table[...], 1, 0, HIGH)


def attend(projected, rows, at, lens, table, b, slots):
    allowed, within = marks(lens, b, slots)
    waves = wave_rows(within, table)
    query = turned_pair(projected[rows, at : at + HD], waves).astype(jnp.bfloat16)
    key = turned_pair(projected[rows, at + HD : at + 2 * HD], waves).astype(jnp.bfloat16)
    value = projected[rows, at + 2 * HD : at + 3 * HD].astype(jnp.bfloat16)
    scores = jnp.where(allowed, dot(query, key, 1, 1) * HD ** (-0.5), NEG_LARGE)
    exps = jnp.exp(scores - jnp.max(scores, axis=-1, keepdims=True))
    probs = exps / jnp.sum(exps, axis=-1, keepdims=True)
    return query, key, value, probs, waves


def each_block(first, last, body):
    def step(b, carry):
        body(b)
        return carry

    lax.fori_loop(first, last, step, 0)


def mixer_kernel(
    sh, ph, lens, projected, chan, side, table, branch, scanned, crossed,
    low, land, mine, s1, r1, s2, r2, here, conv,
):
    slots = crossed.shape[1]
    mh = chan.shape[1]
    heads_at = 2 * sh
    greet(MIX, cross=True)

    def before(b):
        rows = block_rows(b, slots)
        allowed, within = marks(lens, b, slots)
        pre, unused = conv_pre(projected[rows, mh : 2 * mh], within, chan)
        conv[rows, :] = pre * jax.nn.sigmoid(pre)
        mixed = projected[rows, 2 * mh + 3 * HD :]
        first, second, unused, unused = state_parts(mixed, within, side, sh)
        low[b] = dot(second, first, 1, 1).astype(jnp.bfloat16)

    def attention(b):
        rows = block_rows(b, slots)
        query, key, value, probs, waves = attend(projected, rows, 2 * mh, lens, table, b, slots)
        branch[rows, mh:] = dot(probs.astype(jnp.bfloat16), value, 1, 0).astype(jnp.bfloat16)

    def after(b):
        rows = block_rows(b, slots)
        allowed, within = marks(lens, b, slots)
        mixed = projected[rows, 2 * mh + 3 * HD :]
        step, rate, level, tri, inside = steps_and_levels(mixed, side, heads_at, ph)
        step_t, level_t = step.T, level.T
        cross = crossed[b].astype(jnp.float32)
        for pair in range(ph // 2):
            cols = slice(pair * 128, (pair + 1) * 128)
            convs = conv[rows, cols]
            conv_low = convs.astype(jnp.bfloat16)
            outs = []
            for h in (2 * pair, 2 * pair + 1):
                at = heads_at + h
                spread = level[:, at : at + 1] - level_t[at : at + 1, :]
                decay = jnp.exp(jnp.where(allowed, spread, NEG_LARGE))
                mixing = cross * decay * step_t[at : at + 1, :]
                outs.append(dot(mixing.astype(jnp.bfloat16), conv_low, 1, 0))
            total = halves(outs[0], outs[1])
            scanned[rows, cols] = total
            gate = projected[rows, cols]
            gated = (total + chan[5:6, cols] * convs) * (gate * jax.nn.sigmoid(gate))
            branch[rows, cols] = gated.astype(jnp.bfloat16)

    each_block(0, GROUP, before)
    first = blocks_start(low, land, s1, r1)
    each_block(0, GROUP // 2, attention)
    second = blocks_turn(first, low, land, mine, crossed, s2, r2, here)
    each_block(GROUP // 2, GROUP, attention)
    blocks_finish(first, second)
    each_block(0, GROUP, after)


def mixer(lens, projected, chan, side, table, sh, ph):
    tokens = projected.shape[0]
    slots = tokens // GROUP
    mh = chan.shape[1]
    vm = pl.BlockSpec(memory_space=VMEM)
    return pl.pallas_call(
        partial(mixer_kernel, sh, ph),
        name="mixer",
        out_shape=(
            jax.ShapeDtypeStruct((tokens, mh + HD), jnp.bfloat16),
            jax.ShapeDtypeStruct((tokens, mh), jnp.float32),
            jax.ShapeDtypeStruct((GROUP, slots, slots), jnp.bfloat16),
        ),
        in_specs=[pl.BlockSpec(memory_space=pltpu.SMEM)] + [vm] * 4,
        out_specs=(vm,) * 3,
        scratch_shapes=blocks_scratch(slots) + [VMEM((tokens, mh), jnp.float32)],
        compiler_params=params(4, 40),
        cost_estimate=cost(30),
    )(lens, projected, chan, side, table)


def mixer_back_kernel(
    sh, ph, lens, projected, chan, side, table, scanned, crossed, grads, ff_parts, mid,
    out, chan_sums, side_sums, result,
    low, land, mine, s1, r1, s2, r2, here, summed, misc, total, near, held, far, t1, u1, t2, u2,
):
    slots = crossed.shape[1]
    mh = chan.shape[1]
    heads_at = 2 * sh
    bf = jnp.bfloat16
    greet(MIX, cross=True)
    assert MIX == FFN
    steps = scatter_steps(ff_parts, near, held, far, t1, u1, t2, u2, total, FFN)
    next(steps)
    chan_sums[...] = jnp.zeros_like(chan_sums)
    side_sums[...] = jnp.zeros_like(side_sums)

    def scan(b):
        rows = block_rows(b, slots)
        allowed, within = marks(lens, b, slots)
        mixed = projected[rows, 2 * mh + 3 * HD :]
        step, rate, level, tri, inside = steps_and_levels(mixed, side, heads_at, ph)
        step_t, level_t = step.T, level.T
        cross = crossed[b].astype(jnp.float32)
        lane = lax.broadcasted_iota(jnp.int32, (slots, 128), 1)
        place_row = lax.broadcasted_iota(jnp.int32, (slots, slots), 0)
        grad_cross = jnp.zeros((slots, slots), jnp.float32)
        row_sums = jnp.zeros((slots, slots), jnp.float32)
        col_sums = jnp.zeros((slots, slots), jnp.float32)
        for pair in range(ph // 2):
            cols = slice(pair * 128, (pair + 1) * 128)
            weights = chan[:, cols]
            pre, shifted = conv_pre(
                projected[rows, mh + pair * 128 : mh + (pair + 1) * 128], within, weights
            )
            convs = pre * jax.nn.sigmoid(pre)
            conv_low = convs.astype(bf)
            gate = projected[rows, cols]
            sig = jax.nn.sigmoid(gate)
            grad = grads[rows, cols]
            skip = weights[5:6, :]
            grad_mix = grad * (gate * sig)
            out[rows, cols] = (
                grad * (scanned[rows, cols] + skip * convs) * (sig * (1.0 + gate * (1.0 - sig)))
            ).astype(bf)
            skip_sum = jnp.sum(grad_mix * convs, axis=0, keepdims=True)
            grad_low = grad_mix.astype(bf)
            backs = []
            for f in (0, 1):
                at = heads_at + 2 * pair + f
                mask = lane < 64 if f == 0 else lane >= 64
                spread = level[:, at : at + 1] - level_t[at : at + 1, :]
                decay = jnp.exp(jnp.where(allowed, spread, NEG_LARGE))
                step_row = step_t[at : at + 1, :]
                mixing = cross * decay * step_row
                backs.append(dot(mixing.astype(bf), grad_low, 0, 0))
                grad_mixing = dot(jnp.where(mask, grad_mix, 0.0).astype(bf), conv_low, 1, 1)
                weighted = grad_mixing * decay
                grad_cross = grad_cross + weighted * step_row
                weighted = weighted * cross
                col = jnp.sum(weighted, axis=0, keepdims=True)
                row = jnp.sum(weighted * step_row, axis=1, keepdims=True)
                row_sums = jnp.where(lane == at, row, row_sums)
                col_sums = jnp.where(place_row == at, col, col_sums)
            grad_conv = grad_mix * skip + halves(backs[0], backs[1])
            back, sums = conv_back(grad_conv, pre, shifted, within, weights)
            out[rows, mh + pair * 128 : mh + (pair + 1) * 128] = back.astype(bf)
            for i, part in enumerate(sums + [skip_sum]):
                chan_sums[i : i + 1, cols] += part
        low[b] = grad_cross.astype(bf)
        col_sums = col_sums.T
        grad_level = row_sums - step * col_sums
        grad_rate_step = dot(tri, grad_level, 0, 0, HIGH)
        grad_step = (col_sums + grad_rate_step * rate) * jax.nn.sigmoid(mixed + side[5:6, :])
        grad_step = jnp.where(inside, grad_step, 0.0)
        misc[rows, :] = grad_step
        side_sums[5:6, :] += jnp.sum(grad_step, axis=0, keepdims=True)
        side_sums[6:7, :] += jnp.sum(grad_rate_step * step, axis=0, keepdims=True) * rate[:1, :]

    def attention(b):
        rows = block_rows(b, slots)
        at = 2 * mh
        query, key, value, probs, waves = attend(projected, rows, at, lens, table, b, slots)
        grad = grads[rows, mh:].astype(bf)
        grad_probs = dot(grad, value, 1, 1)
        out[rows, at + 2 * HD : at + 3 * HD] = dot(probs.astype(bf), grad, 0, 0).astype(bf)
        grad_raw = probs * (grad_probs - jnp.sum(grad_probs * probs, axis=-1, keepdims=True))
        grad_raw = (grad_raw * HD ** (-0.5)).astype(bf)
        out[rows, at : at + HD] = turned_back(dot(grad_raw, key, 1, 0), waves).astype(bf)
        out[rows, at + HD : at + 2 * HD] = turned_back(dot(grad_raw, query, 0, 0), waves).astype(bf)

    def state(b):
        rows = block_rows(b, slots)
        allowed, within = marks(lens, b, slots)
        mixed = projected[rows, 2 * mh + 3 * HD :]
        first, second, pre, shifted = state_parts(mixed, within, side, sh)
        lane = lax.broadcasted_iota(jnp.int32, pre.shape, 1)
        grad_first = dot(summed[b], second, 0, 0)
        grad_second = pltpu.roll(dot(summed[b], first, 1, 0), sh, 1)
        grad = jnp.where(lane < sh, grad_first, jnp.where(lane < 2 * sh, grad_second, 0.0))
        back, sums = conv_back(grad, pre, shifted, within, side)
        out[rows, 2 * mh + 3 * HD :] = jnp.where(lane < 2 * sh, back, misc[rows, :]).astype(bf)
        for i, part in enumerate(sums):
            side_sums[i : i + 1, :] += part

    each_block(0, GROUP // 2, scan)
    next(steps)
    each_block(GROUP // 2, GROUP, scan)
    begun = blocks_start(low, land, s1, r1)
    next(steps)
    each_block(0, GROUP // 2, attention)
    done = blocks_turn(begun, low, land, mine, summed, s2, r2, here)
    each_block(GROUP // 2, GROUP, attention)
    blocks_finish(begun, done)
    each_block(0, GROUP, state)
    next(steps)

    def finish(rows):
        result[rows, :] = (total[rows, :] + mid[rows, :]).astype(bf)

    by_rows(slots, finish)


def mixer_back(lens, projected, chan, side, table, scanned, crossed, grads, ff_parts, mid, sh, ph):
    tokens = projected.shape[0]
    slots = tokens // GROUP
    mh = chan.shape[1]
    vm = pl.BlockSpec(memory_space=VMEM)
    return pl.pallas_call(
        partial(mixer_back_kernel, sh, ph),
        name="mixer_back",
        out_shape=(
            jax.ShapeDtypeStruct(projected.shape, jnp.bfloat16),
            jax.ShapeDtypeStruct(chan.shape, jnp.float32),
            jax.ShapeDtypeStruct(side.shape, jnp.float32),
            jax.ShapeDtypeStruct(mid.shape, jnp.bfloat16),
        ),
        in_specs=[pl.BlockSpec(memory_space=pltpu.SMEM)] + [vm] * 9,
        out_specs=(vm,) * 4,
        scratch_shapes=blocks_scratch(slots)
        + [
            VMEM((GROUP, slots, slots), jnp.bfloat16),
            VMEM((tokens, 128), jnp.float32),
            VMEM(mid.shape, jnp.float32),
        ]
        + scatter_scratch(*mid.shape),
        compiler_params=params(5, 56),
        cost_estimate=cost(50),
    )(lens, projected, chan, side, table, scanned, crossed, grads, ff_parts, mid)


def swiglu(ff_gate, ff_up):
    return jax.nn.silu(ff_gate) * ff_up


def cut(array, parts, axis=1):
    rows, cols = array.shape
    return array.reshape(rows, parts, cols // parts).transpose(1, 0, 2)


def local(
    tokens,
    cotangent,
    deal_order,
    seq_lengths,
    mixer_norm_gain,
    mamba_gate_weight,
    mamba_input_weight,
    state_weight,
    step_weight,
    conv_input,
    conv_input_bias,
    conv_state,
    conv_state_bias,
    step_bias,
    decay_log,
    skip_scale,
    mamba_out_weight,
    query_weight,
    key_weight,
    value_weight,
    attn_out_weight,
    ff_norm_gain,
    gate_weight,
    up_weight,
    down_weight,
):
    n_row = lax.axis_size("row")
    r = lax.axis_index("row")
    c = lax.axis_index("col")
    t = member(r, MIX)
    n_bits = n_row.bit_length() - 1
    slots, width = tokens.shape[1:]
    bf = jnp.bfloat16
    rows = mamba_gate_weight.shape[0]
    mh = mamba_gate_weight.shape[1] // TP
    qh = query_weight.shape[1] // TP
    kvh = key_weight.shape[1]
    sh = state_weight.shape[1] // (2 * GROUP)
    ph = step_weight.shape[1] // TP
    fh = gate_weight.shape[1] // TP
    used = 2 * mh + qh + 2 * kvh + 2 * sh + ph
    spare = -used % 256

    half = state_weight.shape[1] // 2
    state_in_part = lax.dynamic_slice_in_dim(state_weight[:, :half], c * (half // 2), half // 2, 1)
    state_out_part = lax.dynamic_slice_in_dim(state_weight[:, half:], c * (half // 2), half // 2, 1)
    mixed = jnp.concatenate(
        [
            state_in_part.reshape(rows, TP, sh),
            state_out_part.reshape(rows, TP, sh),
            step_weight.reshape(rows, TP, ph),
            jnp.zeros((rows, TP, spare), bf),
        ],
        axis=2,
    ).reshape(rows, TP * (2 * sh + ph + spare))
    in_weights = (
        key_weight, value_weight,
        mamba_gate_weight, mamba_input_weight, query_weight,
        mixed, mamba_out_weight.T, attn_out_weight.T,
    )
    ff_weights = (gate_weight, up_weight, down_weight.T)

    def assemble(slab, after):
        held = [(0, slab)]
        for b in data_bits(n_row, FFN):
            next_held = []
            for mask, part in held:
                if mask:
                    part, unused_value = lax.optimization_barrier((part, after))
                next_held.append((mask | 1 << b, lax.ppermute(part, "row", flips(n_row, 1 << b))))
            held = held + next_held
        return place_slabs(
            [mask for mask, part in held], [part for mask, part in held], n_row
        ).reshape(n_row * rows, slab.shape[2])

    def pick(array, index, axis=0):
        return lax.dynamic_index_in_dim(array, index, axis, keepdims=False)

    def sum_groups(grad, axes, after=None):
        grad = grad.astype(bf)
        bits = data_bits(n_row, axes)
        order = [n_bits - 1 - b for b in bits + [axes[1], axes[0]]]
        if order != sorted(order):
            cutup = grad.reshape((2,) * n_bits + (rows, grad.shape[1]))
            grad = cutup.transpose(order + [n_bits, n_bits + 1]).reshape(grad.shape)
        if after is not None:
            grad, after = lax.optimization_barrier((grad, after))
        by_group = sorted(range(n_row), key=lambda row: [row >> b & 1 for b in bits])
        alike = [
            [row for row in by_group if [row >> b & 1 for b in axes] == [m & 1, m >> 1]]
            for m in range(TP)
        ]
        part = lax.psum_scatter(
            grad, "row", scatter_dimension=0, axis_index_groups=alike, tiled=True
        ).reshape(TP, rows, grad.shape[1])
        return part, after

    meta = jnp.concatenate(
        [
            deal_order,
            jnp.pad(seq_lengths[:, 0, :], ((0, 0), (0, 128 - seq_lengths.shape[2]))),
            jnp.zeros((4, 128), jnp.int32),
        ],
        axis=0,
    )
    meta_all, give, take, x_home, gy_home, normed_one, gy_all, w_mixer, slab_up, slab_down = deal(
        meta, tokens, cotangent, mixer_norm_gain[None, :], in_weights, ff_weights, n_row
    )
    normed_one = normed_one.reshape(GROUP * slots, width)
    gy_all = gy_all.reshape(GROUP * slots, width)
    w_mixer = w_mixer.reshape(width, -1)
    w_in, w_out = w_mixer[:, : used + spare], w_mixer[:, used + spare :]

    base = r - sum(bit(r, b) * (1 << b) for b in MIX)
    group_meta = jnp.stack([pick(meta_all, base + mask_of(m, MIX)) for m in range(TP)])
    lengths = group_meta[:, 2:4, : seq_lengths.shape[2]].reshape(GROUP, seq_lengths.shape[2])
    half_dim = HD // 2
    inverse = ROPE_BASE ** (-2.0 * jnp.arange(half_dim, dtype=jnp.float32) / HD)
    angles = jnp.arange(slots, dtype=jnp.float32)[:, None] * inverse[None, :]
    cosine, sine = jnp.cos(angles), jnp.sin(angles)
    table = jnp.concatenate([cosine, cosine, -sine, sine], axis=1)

    def piece(array, size, start):
        return lax.dynamic_slice_in_dim(array, start, size, array.ndim - 1)

    eighth = c * TP + t
    chan = jnp.concatenate(
        [
            piece(conv_input, mh, t * mh),
            piece(conv_input_bias[None], mh, t * mh),
            jnp.repeat(piece(skip_scale[None], ph, t * ph), mh // ph, axis=1),
            jnp.zeros((2, mh), jnp.float32),
        ],
        axis=0,
    )
    states = jnp.concatenate([conv_state, conv_state_bias[None]], axis=0)
    states = jnp.concatenate(
        [piece(states, sh, eighth * sh), piece(states, sh, half + eighth * sh)], axis=1
    )
    heads = jnp.concatenate(
        [piece(step_bias[None], ph, t * ph), piece(decay_log[None], ph, t * ph)], axis=0
    )
    after = 128 - 2 * sh - ph
    side = jnp.concatenate(
        [
            jnp.pad(states, ((0, 0), (0, 128 - 2 * sh))),
            jnp.pad(heads, ((0, 0), (2 * sh, after))),
            jnp.zeros((1, 128), jnp.float32),
        ],
        axis=0,
    )

    projected = matmul(normed_one, w_in)
    edges = [0, mh, 2 * mh, 2 * mh + qh, 2 * mh + qh + kvh, 2 * mh + qh + 2 * kvh]
    edges = edges + [edges[-1] + 2 * sh, edges[-1] + 2 * sh + ph]
    branch_in, scanned, crossed = mixer(lengths, projected, chan, side, table, sh, ph)
    branch_part = matmul_trans(branch_in, w_out).astype(bf).reshape(GROUP, slots, width)
    ff_gain = ff_norm_gain[None, :]
    mid, normed_two = middle(branch_part, x_home, ff_gain)
    normed_two = normed_two.reshape(GROUP * slots, width)
    w_gate_up = assemble(slab_up, branch_part)
    w_down = assemble(slab_down, normed_two)

    ff_gate_up = matmul(normed_two, w_gate_up)
    ff_gate, ff_up = ff_gate_up[:, :fh], ff_gate_up[:, fh:]
    ff_hidden = swiglu(ff_gate, ff_up).astype(bf)
    ff_part = matmul_trans(ff_hidden, w_down).astype(bf).reshape(GROUP, slots, width)
    grad_hidden = matmul(gy_all, w_down)
    unused_value, pullback = jax.vjp(swiglu, ff_gate, ff_up)
    grad_gate, grad_up = pullback(grad_hidden)
    grad_gate_up = jnp.concatenate([grad_gate.astype(bf), grad_up.astype(bf)], axis=1)
    (grad_ff,) = products(
        [(normed_two, grad_gate_up), (gy_all, ff_hidden)], [(0, 0, 2 * fh), (1, 0, fh)]
    )
    grad_gate_up, grad_ff = lax.optimization_barrier((grad_gate_up, grad_ff))
    ff_sums, unused_value = sum_groups(grad_ff, FFN)
    normed_two_part = (
        matmul_trans(grad_gate_up, w_gate_up).astype(bf).reshape(GROUP, slots, width)
    )
    d_mid, delta_ff_gain, branch_all = turn(
        normed_two_part, mid, gy_home, ff_gain
    )
    branch_all = branch_all.reshape(GROUP * slots, width)

    grad_branch_in = matmul(branch_all, w_out)
    grad_projected, chan_sums, side_sums, result = mixer_back(
        lengths, projected, chan, side, table, scanned, crossed, grad_branch_in, ff_part, mid, sh, ph
    )
    grad_mixer, grad_kv = products(
        [(normed_one, grad_projected), (branch_all, branch_in)],
        [(0, 0, edges[3]), (0, edges[5], used + spare), (1, 0, mh + qh)],
        [(0, edges[3], edges[5])],
    )
    grad_projected, grad_mixer = lax.optimization_barrier((grad_projected, grad_mixer))
    mixer_sums, ff_sums = sum_groups(grad_mixer, MIX, ff_sums)
    normed_one_part = matmul_trans(grad_projected, w_in).astype(bf).reshape(GROUP, slots, width)

    def lanes(array):
        array = array.reshape((-1, array.shape[-1]))
        array = jnp.pad(array, ((0, 0), (0, -array.shape[1] % 128)))
        return array.reshape(-1, 128)

    small_parts = [
        lanes(part)
        for part in (
            chan_sums[:4],
            chan_sums[4:5],
            side_sums[5:6, 2 * sh : 2 * sh + ph],
            side_sums[6:7, 2 * sh : 2 * sh + ph],
            jnp.sum(chan_sums[5].reshape(ph, -1), axis=1)[None],
            side_sums[:4, : 2 * sh],
            side_sums[4:5, : 2 * sh],
            delta_ff_gain,
        )
    ]
    counts = [part.shape[0] for part in small_parts] + [width // 128]
    small_parts.append(jnp.zeros((-sum(counts) % 8, 128), jnp.float32))
    starts = [sum(counts[:i]) for i in range(len(counts))]
    starts[-1] += small_parts[-1].shape[0]
    output, grad_tokens, small_all, delta_kv, ff_land = send_home(
        normed_one_part, x_home, d_mid, result, mixer_norm_gain[None, :], give, take,
        jnp.concatenate(small_parts, axis=0),
        grad_kv.reshape(n_row // TP, TP, rows, 2 * kvh), ff_sums, n_row,
    )
    mixer_land, other_land = last(mixer_sums, edges[3])
    (
        delta_gate, delta_up, delta_down, delta_mamba_gate, delta_mamba_input,
        delta_query, delta_mamba_out, delta_attn_out,
    ) = unpack(ff_land, mixer_land, mh, qh, fh)
    delta_key, delta_value = delta_kv[:, :kvh], delta_kv[:, kvh:]

    def join(stacked):
        return stacked.transpose(1, 0, 2).reshape(stacked.shape[1], -1).astype(jnp.float32)

    mine = mixer_land[:, :, edges[3] : edges[3] + 128]
    state_first = jnp.where(c == 0, mine, other_land)
    state_second = jnp.where(c == 0, other_land, mine)
    delta_state = jnp.concatenate(
        [
            join(state_first[:, :, :sh]),
            join(state_second[:, :, :sh]),
            join(state_first[:, :, sh : 2 * sh]),
            join(state_second[:, :, sh : 2 * sh]),
        ],
        axis=1,
    )
    delta_step = join(mine[:, :, 2 * sh : 2 * sh + ph])

    small_all = small_all.reshape(TP, 2, -1, 128)
    small_col = pick(small_all, c, 1)

    def taken(array, i):
        return lax.slice_in_dim(array, starts[i], starts[i] + counts[i], axis=array.ndim - 2)

    def along(array, i, size):
        got = taken(array, i).reshape(TP, -1, size + -size % 128)[:, :, :size]
        return got.transpose(1, 0, 2).reshape(got.shape[1], TP * size)

    def state_along(i):
        got = taken(small_all, i)[..., : 2 * sh].reshape(TP, 2, -1, 2, sh)
        return got.transpose(2, 3, 1, 0, 4).reshape(got.shape[2], 2 * half)

    def over_all(i):
        return jnp.sum(taken(small_all, i), axis=(0, 1)).reshape(width)

    by_col = [
        along(small_col, 0, mh),
        along(small_col, 1, mh)[0],
        along(small_col, 2, ph)[0],
        along(small_col, 3, ph)[0],
        along(small_col, 4, ph)[0],
    ]
    by_all = [state_along(5), state_along(6)[0], over_all(8), over_all(7)]

    return (
        output,
        grad_tokens,
        by_all[2],
        delta_mamba_gate,
        delta_mamba_input,
        delta_state,
        delta_step,
        by_col[0],
        by_col[1],
        by_all[0],
        by_all[1],
        by_col[2],
        by_col[3],
        by_col[4],
        delta_mamba_out,
        delta_query,
        delta_key,
        delta_value,
        delta_attn_out,
        by_all[3],
        delta_gate,
        delta_up,
        delta_down,
    )


def solution(mesh):
    both = P("row", "col")
    turned = P("col", "row")
    in_specs = (
        P(None, "row", None),
        P(None, "row", None),
        P(None, "row"),
        P(None, "row", None),
        P(),
        both,
        both,
        P("row", None),
        both,
        P(None, "col"),
        P("col"),
        P(),
        P(),
        P("col"),
        P("col"),
        P("col"),
        turned,
        both,
        both,
        both,
        turned,
        P(),
        both,
        both,
        turned,
    )
    out_specs = (
        P(None, "row", None),
        P(None, "row", None),
        P(),
        both,
        both,
        P("row", None),
        both,
        P(None, "col"),
        P("col"),
        P(),
        P(),
        P("col"),
        P("col"),
        P("col"),
        turned,
        both,
        both,
        both,
        turned,
        P(),
        both,
        both,
        turned,
    )
    return jax.shard_map(local, mesh=mesh, in_specs=in_specs, out_specs=out_specs, check_vma=False)
```

```python
from functools import partial

import jax
import jax.numpy as jnp
from jax import lax
from jax.experimental import pallas as pl
from jax.experimental.pallas import tpu as pltpu
from jax.sharding import PartitionSpec as P

HD = 128
TP = 4
GROUP = 2 * TP
CHUNK = 16
EPS = 1e-05
NEG_LARGE = -1e30
ROPE_BASE = 100000000000.0
MESH = pl.DeviceIdType.MESH
HIGH = lax.Precision.HIGHEST
VMEM = pltpu.VMEM
ANY = pltpu.HBM


def matmul(first_op, second_op):
    return jnp.dot(first_op, second_op, preferred_element_type=jnp.float32)


def matmul_trans(first_op, second_op):
    return lax.dot_general(
        first_op, second_op, (((1,), (1,)), ((), ())), preferred_element_type=jnp.float32
    )


def matmul_left(first_op, second_op):
    return lax.dot_general(
        first_op, second_op, (((0,), (0,)), ((), ())), preferred_element_type=jnp.float32
    )


MIX, FFN = (0, 1), (0, 1)


def data_bits(n_row, axes):
    return [b for b in reversed(range(n_row.bit_length() - 1)) if b not in axes]


def bit(row, b):
    return lax.rem(lax.div(row, 1 << b), 2)


def flip(row, b):
    return row + (1 << b) * (1 - 2 * bit(row, b))


def member(row, axes):
    return bit(row, axes[0]) + 2 * bit(row, axes[1])


def partner(row, m, axes):
    if m & 1:
        row = flip(row, axes[0])
    if m & 2:
        row = flip(row, axes[1])
    return row


def turned_row(row, mask):
    for b in range(mask.bit_length()):
        row = flip(row, b) if mask >> b & 1 else row
    return row


def group_of(row, n_row, axes):
    index = 0
    for b in data_bits(n_row, axes):
        index = index * 2 + bit(row, b)
    return index


def flips(n_row, mask):
    return [(row, row ^ mask) for row in range(n_row)]


def mask_of(m, axes):
    return (m & 1) * (1 << axes[0]) + (m // 2) * (1 << axes[1])


def place():
    return lax.axis_index("row"), lax.axis_index("col")


def block_of(m, axes):
    return member(partner(lax.axis_index("row"), m, axes), axes) * 2


def plan_of(axes, slots):
    if axes != (0, 1) or slots % 32:
        return [(0, slots, 2, 1)]
    return [(0, slots // 2, 1, 2), (slots // 2, slots, 2, 1)]


def params(number, megabytes):
    return pltpu.CompilerParams(
        collective_id=number, has_side_effects=True, vmem_limit_bytes=megabytes << 20
    )


def cost(microseconds):
    return pl.CostEstimate(flops=0, transcendentals=0, bytes_accessed=microseconds * 3_400_000)


def remote(src, dst, send, recv, row, col):
    return pltpu.make_async_remote_copy(
        src_ref=src, dst_ref=dst, send_sem=send, recv_sem=recv, device_id=(row, col), device_id_type=MESH
    )


def greet(*groups, cross=False, beyond=()):
    r, c = place()
    barrier = pltpu.get_barrier_semaphore()
    others = [(r, 1 - c)]
    for axes in groups:
        for m in (1, 2, 3) if cross else (1, 2):
            others.append((partner(r, m, axes), c))
            if cross:
                others.append((partner(r, m, axes), 1 - c))
    others = others + [(flip(r, b), c) for b in beyond]
    for other in others:
        pl.semaphore_signal(barrier, inc=1, device_id=other, device_id_type=MESH)
    pl.semaphore_wait(barrier, len(others))


def gather_start(src, out, send, recv, here, axes):
    r, c = place()
    own = member(r, axes) * 2 + c
    copies = [
        pltpu.make_async_copy(src, out.at[own], here),
        remote(src, out.at[own], send.at[0], recv.at[0], r, 1 - c),
    ]
    for p, (low, high, near, far) in enumerate(plan_of(axes, src.shape[0])):
        for k, m in ((1, near), (2, far)):
            copies.append(
                remote(
                    src.at[low:high], out.at[own, low:high], send.at[6 * p + k], recv.at[6 * p + k],
                    partner(r, m, axes), c,
                )
            )
    for copy in copies[2:] + copies[:2]:
        copy.start()
    return copies


def gather_pass(steps, p, k, m, row, col, out, send, recv, axes):
    r, c = place()
    low, high = plan_of(axes, out.shape[1])[p][:2]
    part = out.at[block_of(m, axes) + c, low:high]
    steps.append(remote(part, part, send.at[6 * p + k], recv.at[6 * p + k], row, col))
    steps[-1].start()


def gather_turn(copies, out, send, recv, axes):
    r, c = place()
    steps = []
    for p, (low, high, near, far) in enumerate(plan_of(axes, out.shape[1])):
        copies[2 + 2 * p].wait_recv()
        gather_pass(steps, p, 3, near, partner(r, far, axes), c, out, send, recv, axes)
        gather_pass(steps, p, 4, near, r, 1 - c, out, send, recv, axes)
    return steps


def gather_finish(copies, steps, out, send, recv, axes):
    r, c = place()
    plan = plan_of(axes, out.shape[1])
    for p, (low, high, near, far) in enumerate(plan):
        copies[3 + 2 * p].wait_recv()
        gather_pass(steps, p, 5, far, r, 1 - c, out, send, recv, axes)
    for p in range(len(plan)):
        steps[2 * p].wait_recv()
        gather_pass(steps, p, 6, 3, r, 1 - c, out, send, recv, axes)
    copies[0].wait()
    copies[1].wait()
    for copy in copies[2:] + steps[: 2 * len(plan) : 2]:
        copy.wait_send()
    for i, copy in enumerate(steps):
        if i >= 2 * len(plan) or i % 2:
            copy.wait()


def gather(src, out, send, recv, here, axes):
    copies = gather_start(src, out, send, recv, here, axes)
    gather_finish(copies, gather_turn(copies, out, send, recv, axes), out, send, recv, axes)


ROWS = 16


def by_rows(count, body, first=0):
    def step(i, carry):
        body(pl.ds(pl.multiple_of(i * ROWS, ROWS), ROWS))
        return carry

    lax.fori_loop(first // ROWS, count // ROWS, step, 0)


def scatter_steps(parts, near, held, far, s1, r1, s2, r2, total, axes):
    r, c = place()
    slots = total.shape[0]
    plan = plan_of(axes, slots)
    pairs = {}
    for m in (3, 1, 2, 0):
        pairs[m] = remote(
            parts.at[block_of(m, axes) + 1 - c], near.at[m], s1.at[m], r1.at[m], r, 1 - c
        )
        pairs[m].start()
    sent = {}

    def pair_sum(m, i, low, high):
        block = block_of(m, axes) + c

        def add(rows):
            held[i, rows, :] = (
                parts[block, rows, :].astype(jnp.float32) + near[m, rows, :].astype(jnp.float32)
            ).astype(jnp.bfloat16)

        by_rows(high, add, low)

    def send(i, p, m):
        low, high = plan[p][:2]
        k = 3 * p + i
        sent[i, p] = remote(
            held.at[i, low:high], far.at[i, low:high], s2.at[k], r2.at[k], partner(r, m, axes), c
        )
        sent[i, p].start()

    yield
    pairs[3].wait_recv()
    for p, (low, high, first, then) in enumerate(plan):
        pair_sum(3, 1, low, high)
        send(1, p, then)
    for m in (1, 2):
        pairs[m].wait_recv()
        for p, (low, high, first, then) in enumerate(plan):
            pair_sum(m, 0 if m == then else 2, low, high)
            if m == then:
                send(0, p, then)
    yield
    for p, (low, high, first, then) in enumerate(plan):
        sent[1, p].wait_recv()

        def add(rows):
            held[2, rows, :] = (
                held[2, rows, :].astype(jnp.float32) + far[1, rows, :].astype(jnp.float32)
            ).astype(jnp.bfloat16)

        by_rows(high, add, low)
        send(2, p, first)
    yield
    pairs[0].wait_recv()
    for p in range(len(plan)):
        sent[0, p].wait_recv()
        sent[2, p].wait_recv()
    own = member(r, axes) * 2 + c

    def fold(rows):
        total[rows, :] = (
            parts[own, rows, :].astype(jnp.float32)
            + near[0, rows, :].astype(jnp.float32)
            + far[0, rows, :].astype(jnp.float32)
            + far[2, rows, :].astype(jnp.float32)
        )

    by_rows(slots, fold)
    for copy in list(pairs.values()) + list(sent.values()):
        copy.wait_send()
    yield


def scatter_sum(*args):
    for step in scatter_steps(*args):
        pass


def scatter_scratch(slots, width):
    return [
        VMEM((TP, slots, width), jnp.bfloat16),
        VMEM((TP - 1, slots, width), jnp.bfloat16),
        VMEM((TP - 1, slots, width), jnp.bfloat16),
        pltpu.SemaphoreType.DMA((TP,)),
        pltpu.SemaphoreType.DMA((TP,)),
        pltpu.SemaphoreType.DMA((6,)),
        pltpu.SemaphoreType.DMA((6,)),
    ]


def gather_scratch():
    return [
        pltpu.SemaphoreType.DMA((13,)),
        pltpu.SemaphoreType.DMA((13,)),
        pltpu.SemaphoreType.DMA,
    ]


def strip_views(refs, owner, piece):
    at = 0
    for ref in refs:
        count = ref.shape[1] // TP
        yield ref.at[:, pl.ds(pl.multiple_of(owner * count, 128), count)], piece.at[:, at : at + count]
        at += count


def cut_start(refs, piece, send, recv, here, axes):
    r, c = place()
    for source, target in strip_views(refs, member(r, axes), piece):
        pltpu.make_async_copy(source, target, here).start()
    for m in (3, 1, 2):
        other = partner(r, m, axes)
        for source, target in strip_views(refs, member(other, axes), piece):
            remote(source, target, send.at[m], recv.at[m], other, c).start()


def piece_done(piece, sem):
    pltpu.make_async_copy(piece, piece, sem).wait()


def weight_forward(masks, whole, cols, send, recv):
    r, c = place()
    n_row = lax.axis_size("row")
    bits = data_bits(n_row, MIX)
    copies = []
    for mask in masks:
        at = whole.at[turned_row(r, mask), :, cols]
        crossed = [k for k, b in enumerate(bits) if mask >> b & 1]
        if crossed:
            piece_done(at, recv.at[mask])
        for b in bits[max([-1] + crossed) + 1 :]:
            lands = mask | 1 << b
            copies.append(remote(at, at, send.at[lands], recv.at[lands], flip(r, b), c))
            copies[-1].start()
    return copies


def weight_rounds(n_row, held):
    rounds = []
    for b in data_bits(n_row, MIX):
        rounds.append([mask | 1 << b for mask in held])
        held = held + rounds[-1]
    return rounds


def spread(masks, whole, cols, send, recv):
    r, c = place()
    copies = []
    for mask in masks:
        at = whole.at[turned_row(r, mask), :, cols]
        for m in (3, 1, 2):
            lands = mask | mask_of(m, MIX)
            copies.append(remote(at, at, send.at[lands], recv.at[lands], partner(r, m, MIX), c))
            copies[-1].start()
    return copies


def place_kernel(masks, n_row, *refs):
    slabs, whole, sems = refs[: len(masks)], refs[-2], refs[-1]
    r, c = place()
    copies = []
    for i, mask in enumerate(masks):
        at = whole.at[group_of(turned_row(r, mask), n_row, FFN)]
        copies.append(pltpu.make_async_copy(slabs[i], at, sems.at[i]))
        copies[-1].start()
    for copy in copies:
        copy.wait()


def place_slabs(masks, slabs, n_row):
    return pl.pallas_call(
        partial(place_kernel, masks, n_row),
        name="place",
        out_shape=jax.ShapeDtypeStruct((len(masks),) + slabs[0].shape, slabs[0].dtype),
        in_specs=[pl.BlockSpec(memory_space=ANY)] * len(masks),
        out_specs=pl.BlockSpec(memory_space=ANY),
        scratch_shapes=[pltpu.SemaphoreType.DMA((len(masks),))],
        compiler_params=pltpu.CompilerParams(vmem_limit_bytes=4 << 20),
        cost_estimate=cost(4),
    )(*slabs)


def exchange_rows(buf, land, send, recv):
    r, c = place()
    n_row = lax.axis_size("row")

    def copy(other):
        return remote(
            buf.at[other], land.at[r], send.at[other], recv.at[r], other, c
        )

    def start(off, carry):
        copy(lax.rem(r + off, n_row)).start()
        return carry

    lax.fori_loop(1, n_row, start, 0)


def finish_rows(buf, land, send, recv):
    r, c = place()
    n_row = lax.axis_size("row")

    def finish(off, carry):
        other = lax.rem(r + off, n_row)
        copy = remote(buf.at[other], land.at[other], send.at[other], recv.at[other], other, c)
        copy.wait_send()
        copy.wait_recv()
        return carry

    lax.fori_loop(1, n_row, finish, 0)


def greet_rows(meanwhile=None):
    r, c = place()
    n_row = lax.axis_size("row")
    barrier = pltpu.get_barrier_semaphore()

    def greet(off, carry):
        pl.semaphore_signal(
            barrier, inc=1, device_id=(lax.rem(r + off, n_row), c), device_id_type=MESH
        )
        return carry

    lax.fori_loop(1, n_row, greet, 0)
    pl.semaphore_signal(barrier, inc=1, device_id=(r, 1 - c), device_id_type=MESH)
    if meanwhile is not None:
        meanwhile()
    pl.semaphore_wait(barrier, n_row)


COLS = 512


def permute_out(choice, buf, first, second, slots):
    n_row = buf.shape[0]

    def column(i, carry):
        cols = pl.ds(pl.multiple_of(i * COLS, COLS), COLS)
        picked = matmul(choice[:, :slots], first[:, cols]) + matmul(choice[:, slots:], second[:, cols])
        buf[:, :, cols] = picked.astype(jnp.bfloat16).reshape(n_row, CHUNK, COLS)
        return carry

    lax.fori_loop(0, buf.shape[2] // COLS, column, 0)


def permute_in(choice, land, first, second, slots):
    n_row = land.shape[0]

    def column(i, carry):
        cols = pl.ds(pl.multiple_of(i * COLS, COLS), COLS)
        got = land[:, :, cols].reshape(n_row * CHUNK, COLS)
        first[:, cols] = matmul_left(choice[:, :slots], got).astype(jnp.bfloat16)
        second[:, cols] = matmul_left(choice[:, slots:], got).astype(jnp.bfloat16)
        return carry

    lax.fori_loop(0, land.shape[2] // COLS, column, 0)


def deal_kernel(
    order, lengths, tokens, cotangent, gain, *refs
):
    kv_refs, first_refs, refs = refs[:2], refs[2:5], refs[5:]
    states, steps_in, mamba_out, attn_out, refs = *refs[:4], refs[4:]
    up_refs, down, refs = refs[:2], refs[2], refs[3:]
    meta_all, give, take, x_out, gy_out, normed_all, gy_all, whole, slab_up, slab_down = refs[:10]
    x_mine, g_mine, buf, land, normed = refs[10:15]
    load, msend, mrecv, csend, crecv, nsend, nrecv, nhere, gsend, grecv, ghere = refs[15:26]
    wsend, wrecv, acut, arecv, ahere, bcut, brecv, bhere, usend, urecv, uhere, dsend, drecv, dhere, kv_here = refs[26:41]
    meta, mixed, mamba_turned, attn_turned, down_turned = refs[41:]
    second_refs, down_refs = (mixed, mamba_turned, attn_turned), (down_turned,)
    r, c = place()
    n_row = lax.axis_size("row")
    f = member(r, FFN)
    slots = x_mine.shape[0]
    per_peer = slots // n_row
    loads = [
        pltpu.make_async_copy(tokens.at[c], x_mine, load.at[0]),
        pltpu.make_async_copy(cotangent.at[c], g_mine, load.at[1]),
    ]
    for copy in loads:
        copy.start()
    bf = jnp.bfloat16

    def turn_weight(source, target):
        target[...] = source[...].astype(jnp.float32).T.astype(bf)

    def prepare():
        count = lengths.shape[2]
        meta[...] = jnp.zeros_like(meta)
        meta[0:2, :] = order[...]
        for i in range(2):
            meta[2 + i : 3 + i, 0:count] = lengths[i]
        part = states.shape[1] // 4
        values = states[...].astype(jnp.float32)
        first = jnp.where(c == 0, values[:, :part], values[:, part : 2 * part])
        second = jnp.where(c == 0, values[:, 2 * part : 3 * part], values[:, 3 * part :])
        step_values = steps_in[...].astype(jnp.float32)
        sh, ph = part // TP, step_values.shape[1] // TP
        width = mixed.shape[1] // TP
        for k in range(TP):
            cols = slice(k * sh, (k + 1) * sh)
            strip = [first[:, cols], second[:, cols], step_values[:, k * ph : (k + 1) * ph]]
            strip.append(jnp.zeros((values.shape[0], width - 2 * sh - ph), jnp.float32))
            mixed[:, k * width : (k + 1) * width] = jnp.concatenate(strip, axis=1).astype(bf)
        turn_weight(mamba_out, mamba_turned)
        turn_weight(attn_out, attn_turned)

    greet_rows(prepare)
    group = [mask_of(m, MIX) for m in range(TP)]
    first_cols = sum(ref.shape[1] for ref in first_refs) // TP
    kv_cols = first_cols + sum(ref.shape[1] for ref in kv_refs)
    cuts = (
        (slice(0, first_cols), first_refs, acut, arecv, ahere),
        (slice(kv_cols, whole.shape[2]), second_refs, bcut, brecv, bhere),
    )
    kv = slice(first_cols, kv_cols)

    def meta_copy(other, slot):
        return remote(meta, meta_all.at[slot], msend.at[other], mrecv.at[slot], other, c)

    def start(off, carry):
        meta_copy(lax.rem(r + off, n_row), r).start()
        return carry

    lax.fori_loop(1, n_row, start, 0)
    meta_all[r] = meta[...]
    at = first_cols
    for ref in kv_refs:
        pltpu.make_async_copy(ref, whole.at[r, :, at : at + ref.shape[1]], kv_here).start()
        at += ref.shape[1]
    for cols, refs_of, send, recv, here in cuts:
        cut_start(refs_of, whole.at[r, :, cols], send, recv, here, MIX)
    forwards = []
    for i, (cols, refs_of, send, recv, here) in enumerate(cuts):
        piece_done(whole.at[r, :, cols], here)
        forwards = forwards + weight_forward([0], whole, cols, wsend.at[i], wrecv.at[i])
    piece_done(whole.at[r, :, kv], kv_here)
    forwards = forwards + weight_forward([0], whole, kv, wsend.at[2], wrecv.at[2])

    def finish(off, carry):
        other = lax.rem(r + off, n_row)
        copy = meta_copy(other, other)
        copy.wait_send()
        copy.wait_recv()
        return carry

    lax.fori_loop(1, n_row, finish, 0)

    shift = slots.bit_length() - 1
    row_no = lax.broadcasted_iota(jnp.int32, (CHUNK, slots), 0)
    wanted = jnp.where(row_no < per_peer, row_no, row_no - per_peer).astype(jnp.float32)
    early = row_no < per_peer
    late = (row_no >= per_peer) & (row_no < 2 * per_peer)
    tri = (
        lax.broadcasted_iota(jnp.int32, (slots, slots), 0)
        < lax.broadcasted_iota(jnp.int32, (slots, slots), 1)
    ).astype(jnp.float32).astype(jnp.bfloat16)
    places = lax.broadcasted_iota(jnp.int32, (slots, slots), 0)

    def order_of(block):
        picked = jnp.where(c == 0, block[0:1, :], block[1:2, :])
        return lax.shift_right_logical(picked, shift), picked - lax.shift_left(
            lax.shift_right_logical(picked, shift), shift
        )

    own_source, own_local = order_of(meta[...])

    def select(mask):
        wide = jnp.broadcast_to(mask.astype(jnp.float32), (CHUNK, slots)).astype(jnp.bfloat16)
        rank = matmul(wide, tri)
        return jnp.where(
            (rank == wanted) & (wide.astype(jnp.float32) > 0.5), 1.0, 0.0
        )

    def build(d, carry):
        rows = pl.ds(pl.multiple_of(d * CHUNK, CHUNK), CHUNK)
        source, local = order_of(meta_all[d])
        chosen = select(source == r).astype(jnp.bfloat16)
        at_home = (places == local).astype(jnp.float32).astype(jnp.bfloat16)
        picks = matmul_trans(chosen, at_home)
        give[rows, :slots] = jnp.where(early, picks, 0.0).astype(jnp.bfloat16)
        give[rows, slots:] = jnp.where(late, picks, 0.0).astype(jnp.bfloat16)
        kept = select(own_source == d)
        take[rows, :slots] = jnp.where(early, kept, 0.0).astype(jnp.bfloat16)
        take[rows, slots:] = jnp.where(late, kept, 0.0).astype(jnp.bfloat16)
        return carry

    lax.fori_loop(0, n_row, build, 0)
    for copy in loads:
        copy.wait()
    permute_out(give, buf, x_mine, g_mine, slots)
    exchange_rows(buf, land, csend, crecv)
    land[r] = buf[r]
    for i, (cols, refs_of, send, recv, here) in enumerate(cuts):
        for m in (1, 2, 3):
            piece_done(whole.at[r, :, cols], recv.at[m])
            forwards = forwards + weight_forward([group[m]], whole, cols, wsend.at[i], wrecv.at[i])
    turn_weight(down, down_turned)
    finish_rows(buf, land, csend, crecv)
    permute_in(take, land, x_out, gy_out, slots)

    def norm(rows):
        values = x_out[rows, :].astype(jnp.float32)
        scale = lax.rsqrt(jnp.mean(values * values, axis=-1, keepdims=True) + EPS)
        normed[rows, :] = (values * scale * gain[...]).astype(jnp.bfloat16)

    by_rows(slots, norm)
    first = gather_start(normed, normed_all, nsend, nrecv, nhere, MIX)
    cut_start(up_refs, slab_up.at[f], usend, urecv, uhere, FFN)
    cut_start(down_refs, slab_down.at[f], dsend, drecv, dhere, FFN)
    second = gather_start(gy_out, gy_all, gsend, grecv, ghere, FFN)
    kv_rounds = weight_rounds(n_row, [0])
    steps = []
    for k, masks in enumerate(weight_rounds(n_row, group)):
        forwards = forwards + weight_forward(kv_rounds[k], whole, kv, wsend.at[2], wrecv.at[2])
        for i in (0, 1):
            forwards = forwards + weight_forward(masks, whole, cuts[i][0], wsend.at[i], wrecv.at[i])
            if k == 0 and i == 0:
                steps.append(gather_turn(first, normed_all, nsend, nrecv, MIX))
            if k == 0 and i == 1:
                steps.append(gather_turn(second, gy_all, gsend, grecv, FFN))
        if k == len(kv_rounds) - 1:
            kv_held = [0] + [mask for masks in kv_rounds for mask in masks]
            spreads = spread(kv_held, whole, kv, wsend.at[2], wrecv.at[2])
    gather_finish(first, steps[0], normed_all, nsend, nrecv, MIX)
    gather_finish(second, steps[1], gy_all, gsend, grecv, FFN)
    for copy in forwards:
        copy.wait_send()
    for cols, refs_of, send, recv, here in cuts:
        for m in (1, 2, 3):
            piece_done(whole.at[r, :, cols], send.at[m])
    for copy in spreads:
        copy.wait()
    for slab, send, recv, here in ((slab_up, usend, urecv, uhere), (slab_down, dsend, drecv, dhere)):
        piece_done(slab.at[f], here)
        for m in (1, 2, 3):
            piece_done(slab.at[f], send.at[m])
            piece_done(slab.at[f], recv.at[m])


def deal(order, lengths, tokens, cotangent, gain, kv, first, second, ff, strip, n_row):
    slots, width = tokens.shape[1:]
    bf = jnp.bfloat16
    rows = first[0].shape[0]
    states, steps_in, mamba_out, attn_out = second
    in_cols = sum(array.shape[1] for array in kv) + sum(array.shape[1] for array in first) // TP
    in_cols += strip + (mamba_out.shape[0] + attn_out.shape[0]) // TP
    up_cols, down_cols = 2 * ff[0].shape[1] // TP, ff[2].shape[0] // TP
    vm, hb = pl.BlockSpec(memory_space=VMEM), pl.BlockSpec(memory_space=ANY)
    dma = pltpu.SemaphoreType.DMA
    return pl.pallas_call(
        deal_kernel,
        name="deal",
        out_shape=(
            jax.ShapeDtypeStruct((n_row, 8, 128), jnp.int32),
            jax.ShapeDtypeStruct((n_row * CHUNK, 2 * slots), bf),
            jax.ShapeDtypeStruct((n_row * CHUNK, 2 * slots), bf),
            jax.ShapeDtypeStruct((slots, width), bf),
            jax.ShapeDtypeStruct((slots, width), bf),
            jax.ShapeDtypeStruct((GROUP, slots, width), bf),
            jax.ShapeDtypeStruct((GROUP, slots, width), bf),
            jax.ShapeDtypeStruct((n_row, rows, in_cols), bf),
            jax.ShapeDtypeStruct((TP, rows, up_cols), bf),
            jax.ShapeDtypeStruct((TP, rows, down_cols), bf),
        ),
        in_specs=[vm, vm, hb, hb, vm] + [hb] * 5 + [vm] * 4 + [hb, hb, vm],
        out_specs=(vm,) * 5 + (hb,) * 5,
        scratch_shapes=[
            VMEM((slots, width), bf),
            VMEM((slots, width), bf),
            VMEM((n_row, CHUNK, width), bf),
            VMEM((n_row, CHUNK, width), bf),
            VMEM((slots, width), bf),
            dma((2,)),
            dma((n_row,)),
            dma((n_row,)),
            dma((n_row,)),
            dma((n_row,)),
        ]
        + gather_scratch()
        + gather_scratch()
        + [dma((3, n_row)), dma((3, n_row))]
        + [dma((TP,)), dma((TP,)), dma] * 4
        + [dma]
        + [
            VMEM((8, 128), jnp.int32),
            VMEM((rows, TP * strip), bf),
            VMEM((rows, mamba_out.shape[0]), bf),
            VMEM((rows, attn_out.shape[0]), bf),
            VMEM((rows, ff[2].shape[0]), bf),
        ],
        compiler_params=params(0, 58),
        cost_estimate=cost(100),
    )(order, lengths, tokens, cotangent, gain, *kv, *first, *second, *ff)


def slab_copy(slab, whole, mask, b, send, recv):
    r, c = place()
    n_row = lax.axis_size("row")
    at = whole.at[group_of(turned_row(r, mask), n_row, FFN)]
    lands = mask | 1 << b
    k = group_index(lands, n_row)
    return remote(at if mask else slab, at, send.at[k], recv.at[k], flip(r, b), c)


def group_index(mask, n_row):
    return sum((mask >> b & 1) << i for i, b in enumerate(data_bits(n_row, FFN)))


def middle_kernel(
    parts, x, gain, slab, mid, normed_all, whole,
    near, out2, far, s1, r1, s2, r2, normed, nsend, nrecv, nhere, wsend, wrecv, where,
):
    r, c = place()
    n_row = lax.axis_size("row")
    bits = data_bits(n_row, FFN)
    greet(*{MIX, FFN}, beyond=bits)
    own = pltpu.make_async_copy(slab, whole.at[group_of(r, n_row, FFN)], where)
    own.start()
    copies = {1 << b: slab_copy(slab, whole, 0, b, wsend, wrecv) for b in bits}
    for copy in copies.values():
        copy.start()
    scatter_sum(parts, near, out2, far, s1, r1, s2, r2, mid, MIX)

    def norm(rows):
        values = x[rows, :].astype(jnp.float32) + mid[rows, :]
        mid[rows, :] = values
        scale = lax.rsqrt(jnp.mean(values * values, axis=-1, keepdims=True) + EPS)
        normed[rows, :] = (values * scale * gain[...]).astype(jnp.bfloat16)

    by_rows(mid.shape[0], norm)
    started = gather_start(normed, normed_all, nsend, nrecv, nhere, FFN)
    passed = gather_turn(started, normed_all, nsend, nrecv, FFN)
    for i, b in enumerate(bits):
        for mask in [mask for mask in copies if mask >> b & 1]:
            copies[mask].wait_recv()
            for later in bits[i + 1 :]:
                lands = mask | 1 << later
                copies[lands] = slab_copy(slab, whole, mask, later, wsend, wrecv)
                copies[lands].start()
    gather_finish(started, passed, normed_all, nsend, nrecv, FFN)
    own.wait()
    for copy in copies.values():
        copy.wait_send()


def middle(parts, x, gain, slab, n_row):
    slots, width = x.shape
    groups = n_row // TP
    vm, hb = pl.BlockSpec(memory_space=VMEM), pl.BlockSpec(memory_space=ANY)
    return pl.pallas_call(
        middle_kernel,
        name="middle",
        out_shape=(
            jax.ShapeDtypeStruct((slots, width), jnp.float32),
            jax.ShapeDtypeStruct((GROUP, slots, width), jnp.bfloat16),
            jax.ShapeDtypeStruct((groups,) + slab.shape, slab.dtype),
        ),
        in_specs=[vm] * 3 + [hb],
        out_specs=(vm, hb, hb),
        scratch_shapes=scatter_scratch(slots, width)
        + [VMEM((slots, width), jnp.bfloat16)]
        + gather_scratch()
        + [
            pltpu.SemaphoreType.DMA((groups,)),
            pltpu.SemaphoreType.DMA((groups,)),
            pltpu.SemaphoreType.DMA,
        ],
        compiler_params=params(1, 40),
        cost_estimate=cost(60),
    )(parts, x, gain, slab)


def norm_back(values, gain, grad):
    inverse = lax.rsqrt(jnp.mean(values * values, axis=-1, keepdims=True) + EPS)
    scaled = grad * gain
    back = inverse * scaled - values * (
        inverse * inverse * inverse * jnp.mean(values * scaled, axis=-1, keepdims=True)
    )
    return back, jnp.sum(grad * values * inverse, axis=0, keepdims=True)


def turn_kernel(
    parts, mid, gy, gain, d_mid, d_gain, branch_all,
    near, out2, far, s1, r1, s2, r2, branch, nsend, nrecv, nhere,
):
    greet(*{MIX, FFN})
    scatter_sum(parts, near, out2, far, s1, r1, s2, r2, d_mid, FFN)
    d_gain[...] = jnp.zeros_like(d_gain)

    def back(rows):
        values = mid[rows, :]
        grad, gain_part = norm_back(values, gain[...], d_mid[rows, :])
        grad = gy[rows, :].astype(jnp.float32) + grad
        d_mid[rows, :] = grad
        branch[rows, :] = grad.astype(jnp.bfloat16)
        d_gain[...] += gain_part

    by_rows(mid.shape[0], back)
    gather(branch, branch_all, nsend, nrecv, nhere, MIX)


def turn(parts, mid, gy, gain):
    slots, width = mid.shape
    return pl.pallas_call(
        turn_kernel,
        name="turn",
        out_shape=(
            jax.ShapeDtypeStruct((slots, width), jnp.float32),
            jax.ShapeDtypeStruct((1, width), jnp.float32),
            jax.ShapeDtypeStruct((GROUP, slots, width), jnp.bfloat16),
        ),
        in_specs=[pl.BlockSpec(memory_space=VMEM)] * 4,
        out_specs=(pl.BlockSpec(memory_space=VMEM),) * 2 + (pl.BlockSpec(memory_space=ANY),),
        scratch_shapes=scatter_scratch(slots, width)
        + [VMEM((slots, width), jnp.bfloat16)]
        + gather_scratch(),
        compiler_params=params(2, 48),
        cost_estimate=cost(60),
    )(parts, mid, gy, gain)


def home_kernel(
    parts, x, d_mid, ff_parts, mid, gain, give, take, chan_sums, side_sums, ff_gain_sums, kv_parts, ff_sums,
    output, gradient, small_all, kv_sums, ff_land,
    near, out2, far, s1, r1, s2, r2, total, first, second, buf, land, csend, crecv, here, osend, orecv,
    d_gain, stages, stage_land, tsend, trecv, gsend, grecv, ghere, *more
):
    r, c = place()
    slots, width = x.shape
    bits = data_bits(lax.axis_size("row"), MIX)
    greet_rows()
    kv_near, kv_held, kv_far, kv_s1, kv_r1, kv_s2, kv_r2 = more[3:10]
    ff_total = more[10]
    delivered = deliver(ff_sums, ff_land, *more[:3], FFN)
    steps = scatter_steps(parts, near, out2, far, s1, r1, s2, r2, total, MIX)
    ff_steps = scatter_steps(ff_parts, *more[11:], ff_total, FFN)
    for pair in zip(steps, ff_steps):
        pass
    d_gain[...] = jnp.zeros_like(d_gain)

    def back(rows):
        values = x[rows, :].astype(jnp.float32)
        grad, gain_part = norm_back(values, gain[...], total[rows, :])
        second[rows, :] = (d_mid[rows, :] + grad).astype(jnp.bfloat16)
        first[rows, :] = (ff_total[rows, :] + mid[rows, :]).astype(jnp.bfloat16)
        d_gain[...] += gain_part

    by_rows(slots, back)
    at = 0
    for sums in (chan_sums, side_sums, ff_gain_sums, d_gain):
        for i in range(sums.shape[0]):
            for k in range(sums.shape[1] // 128):
                stages[0, at : at + 1, :] = sums[i : i + 1, k * 128 : (k + 1) * 128]
                at += 1

    def stage_copy(i):
        return remote(
            stages.at[i], stage_land.at[i], tsend.at[i], trecv.at[i], flip(r, bits[i]), c
        )

    stage_copy(0).start()
    permute_out(take, buf, first, second, slots)
    exchange_rows(buf, land, csend, crecv)
    land[r] = buf[r]
    own = member(r, MIX)
    groups = kv_parts.shape[0]
    kv_sent = []
    for m in (3, 1, 2):
        other = partner(r, m, MIX)
        kv_sent.append(
            remote(kv_parts.at[:, member(other, MIX)], kv_near.at[m], kv_s1.at[m], kv_r1.at[m], other, c)
        )
        kv_sent[-1].start()
    for i in range(len(bits)):
        stage_copy(i).wait()
        stages[i + 1] = stages[i] + stage_land[i]
        if i + 1 < len(bits):
            stage_copy(i + 1).start()
    started = gather_start(stages.at[len(bits)], small_all, gsend, grecv, ghere, MIX)
    for copy in kv_sent:
        copy.wait()
    passed = gather_turn(started, small_all, gsend, grecv, MIX)

    def kv_pair(g):
        kv_held[g] = (
            kv_parts[g, own].astype(jnp.float32)
            + kv_near[1, g].astype(jnp.float32)
            + kv_near[2, g].astype(jnp.float32)
            + kv_near[3, g].astype(jnp.float32)
        ).astype(jnp.bfloat16)

    each_block(0, groups, kv_pair)
    kv_far_sent = []
    for k in range(1, groups):
        other = turned_row(r, sum((1 << b) * (k >> i & 1) for i, b in enumerate(bits)))
        kv_far_sent.append(
            remote(
                kv_held.at[group_of(other, lax.axis_size("row"), MIX)],
                kv_far.at[k], kv_s2.at[k], kv_r2.at[k], other, c,
            )
        )
        kv_far_sent[-1].start()
    finish_rows(buf, land, csend, crecv)
    permute_in(give, land, first, second, slots)
    copies = []
    for i, (mine, out) in enumerate(((first, output), (second, gradient))):
        copies.append(pltpu.make_async_copy(mine, out.at[c], here.at[i]))
        copies.append(remote(mine, out.at[c], osend.at[i], orecv.at[i], r, 1 - c))
    for copy in copies:
        copy.start()
    gather_finish(started, passed, small_all, gsend, grecv, MIX)
    for copy in kv_far_sent:
        copy.wait()
    kv_total = kv_held[group_of(r, lax.axis_size("row"), MIX)].astype(jnp.float32)
    for k in range(1, groups):
        kv_total = kv_total + kv_far[k].astype(jnp.float32)
    kv_sums[...] = kv_total
    for copy in copies + delivered:
        copy.wait()


def deliver(sums, land, send, recv, here, axes):
    r, c = place()
    own = member(r, axes)
    copies = [pltpu.make_async_copy(sums.at[own], land.at[own], here)]
    for m in (3, 1, 2):
        other = partner(r, m, axes)
        copies.append(
            remote(sums.at[member(other, axes)], land.at[own], send.at[m], recv.at[m], other, c)
        )
    for copy in copies:
        copy.start()
    return copies


def deliver_scratch():
    dma = pltpu.SemaphoreType.DMA
    return [dma((TP,)), dma((TP,)), dma]


def last_kernel(at, sums, land, other, s1, r1, here, send, recv):
    r, c = place()
    barrier = pltpu.get_barrier_semaphore()
    for m in (1, 2, 3):
        pl.semaphore_signal(barrier, inc=1, device_id=(partner(r, m, MIX), c), device_id_type=MESH)
    pl.semaphore_signal(barrier, inc=1, device_id=(r, 1 - c), device_id_type=MESH)
    pl.semaphore_wait(barrier, 4)
    for copy in deliver(sums, land, s1, r1, here, MIX):
        copy.wait()
    across = remote(land.at[:, :, at : at + 128], other, send, recv, r, 1 - c)
    across.start()
    across.wait()


def last(sums, at):
    hb = pl.BlockSpec(memory_space=ANY)
    dma = pltpu.SemaphoreType.DMA
    return pl.pallas_call(
        partial(last_kernel, at),
        name="last",
        out_shape=(
            jax.ShapeDtypeStruct(sums.shape, sums.dtype),
            jax.ShapeDtypeStruct(sums.shape[:2] + (128,), sums.dtype),
        ),
        in_specs=[hb],
        out_specs=(hb,) * 2,
        scratch_shapes=deliver_scratch() + [dma, dma],
        compiler_params=params(6, 4),
        cost_estimate=cost(25),
    )(sums)


def products_kernel(parts, *refs):
    pairs = len(refs) - len(parts)
    for part, out in zip(parts, refs[pairs:]):
        at = 0
        for i, low, high in part:
            left, right = refs[2 * i], refs[2 * i + 1]
            out[:, at : at + high - low] = dot(left[...], right[:, low:high], 0, 0).astype(out.dtype)
            at += high - low


def products(pairs, *parts):
    tokens, width = pairs[0][0].shape
    tile = min(512, width)
    specs = []
    for left, right in pairs:
        specs.append(pl.BlockSpec((tokens, tile), lambda i: (0, i)))
        specs.append(pl.BlockSpec(right.shape, lambda i: (0, 0)))
    totals = [sum(high - low for i, low, high in part) for part in parts]
    return pl.pallas_call(
        partial(products_kernel, parts),
        name="products",
        grid=(width // tile,),
        out_shape=tuple(jax.ShapeDtypeStruct((width, total), jnp.bfloat16) for total in totals),
        in_specs=specs,
        out_specs=tuple(pl.BlockSpec((tile, total), lambda i: (i, 0)) for total in totals),
        compiler_params=pltpu.CompilerParams(vmem_limit_bytes=40 << 20),
        cost_estimate=cost(10),
    )(*[array for pair in pairs for array in pair])


def unpack_kernel(
    sh, ph, ff, mixer, misc, small, kv, home_out, home_grad,
    output, gradient, mixer_gain, mamba_gate, mamba_input, state, step, conv_k, conv_b, state_k, state_b,
    step_bias, decay, skip, mamba_out, query, key, value, attn_out, ff_gain, gate, up, down, sems,
):
    c = lax.axis_index("col")
    f32 = jnp.float32
    copies = [
        pltpu.make_async_copy(home_out, output, sems.at[0]),
        pltpu.make_async_copy(home_grad, gradient, sems.at[1]),
    ]
    for copy in copies:
        copy.start()
    mh = mamba_gate.shape[1] // TP
    fh = gate.shape[1] // TP
    qh = query.shape[1] // TP
    kvh = key.shape[1]
    at = 2 * mh + qh
    out = mixer.shape[2] - mh - qh
    for m in range(TP):
        def cols(size):
            return slice(m * size, (m + 1) * size)

        gate[:, cols(fh)] = ff[m, :, :fh].astype(f32)
        up[:, cols(fh)] = ff[m, :, fh : 2 * fh].astype(f32)
        down[cols(fh), :] = ff[m, :, 2 * fh :].astype(f32).T
        mamba_gate[:, cols(mh)] = mixer[m, :, :mh].astype(f32)
        mamba_input[:, cols(mh)] = mixer[m, :, mh : 2 * mh].astype(f32)
        query[:, cols(qh)] = mixer[m, :, 2 * mh : at].astype(f32)
        mamba_out[cols(mh), :] = mixer[m, :, out : out + mh].astype(f32).T
        attn_out[cols(qh), :] = mixer[m, :, out + mh :].astype(f32).T
    key[...] = kv[:, :kvh]
    value[...] = kv[:, kvh:]

    mine = [mixer[m, :, at : at + 128].astype(f32) for m in range(TP)]
    other = [misc[m].astype(f32) for m in range(TP)]
    by_col = [
        [jnp.where(c == col, mine[m], other[m]) for m in range(TP)] for col in range(2)
    ]
    state[...] = jnp.concatenate(
        [
            by_col[col][m][:, part * sh : (part + 1) * sh]
            for part in range(2)
            for col in range(2)
            for m in range(TP)
        ],
        axis=1,
    )
    step[...] = jnp.concatenate([part[:, 2 * sh : 2 * sh + ph] for part in mine], axis=1)

    lanes = mh // 128
    channels = [
        jnp.concatenate(
            [
                small[2 * m + c, i * lanes + k : i * lanes + k + 1, :]
                for m in range(TP)
                for k in range(lanes)
            ],
            axis=1,
        )
        for i in range(6)
    ]
    for i in range(4):
        conv_k[i : i + 1, :] = channels[i]
    conv_b[...] = channels[4]
    per_head = mh // ph
    shape = (TP * mh, TP * ph)
    heads = lax.broadcasted_iota(jnp.int32, shape, 1) * per_head
    channel = lax.broadcasted_iota(jnp.int32, shape, 0)
    picks = ((channel >= heads) & (channel < heads + per_head)).astype(f32)
    skip[...] = dot(jnp.broadcast_to(channels[5], (8, TP * mh)), picks, 1, 0, HIGH)[:1, :]
    start = 8 * lanes
    sides = [[small[2 * m + col, start : start + 8, :] for m in range(TP)] for col in range(2)]
    states = jnp.concatenate(
        [
            sides[col][m][:, part * sh : (part + 1) * sh]
            for part in range(2)
            for col in range(2)
            for m in range(TP)
        ],
        axis=1,
    )
    state_k[...] = states[:4, :]
    state_b[...] = states[4:5, :]
    own_heads = jnp.concatenate(
        [jnp.where(c == 0, sides[0][m], sides[1][m])[:, 2 * sh : 2 * sh + ph] for m in range(TP)], axis=1
    )
    step_bias[...] = own_heads[5:6, :]
    decay[...] = own_heads[6:7, :]
    start = start + 8
    for gain in (ff_gain, mixer_gain):
        count = gain.shape[1] // 128
        total = sum(small[i, start : start + count, :] for i in range(GROUP))
        for k in range(count):
            gain[:, k * 128 : (k + 1) * 128] = total[k : k + 1, :]
        start = start + count
    for copy in copies:
        copy.wait()


def unpack(ff, mixer, misc, small, kv, output, gradient, mh, qh, fh, sh, ph):
    rows, width = ff.shape[1], output.shape[2]
    kvh = kv.shape[1] // 2
    vm, hb = pl.BlockSpec(memory_space=VMEM), pl.BlockSpec(memory_space=ANY)
    f32 = jnp.float32
    shapes = [
        (1, width),
        (rows, TP * mh),
        (rows, TP * mh),
        (rows, 2 * GROUP * sh),
        (rows, TP * ph),
        (4, TP * mh),
        (1, TP * mh),
        (4, 2 * GROUP * sh),
        (1, 2 * GROUP * sh),
        (1, TP * ph),
        (1, TP * ph),
        (1, TP * ph),
        (TP * mh, rows),
        (rows, TP * qh),
        (rows, kvh),
        (rows, kvh),
        (TP * qh, rows),
        (1, width),
        (rows, TP * fh),
        (rows, TP * fh),
        (TP * fh, rows),
    ]
    return pl.pallas_call(
        partial(unpack_kernel, sh, ph),
        name="unpack",
        out_shape=tuple(jax.ShapeDtypeStruct(a.shape, a.dtype) for a in (output, gradient))
        + tuple(jax.ShapeDtypeStruct(shape, f32) for shape in shapes),
        in_specs=[vm] * 5 + [hb] * 2,
        out_specs=(hb,) * 2 + (vm,) * len(shapes),
        scratch_shapes=[pltpu.SemaphoreType.DMA((2,))],
        compiler_params=pltpu.CompilerParams(vmem_limit_bytes=40 << 20),
        cost_estimate=cost(8),
    )(ff, mixer, misc, small, kv, output, gradient)


def send_home(parts, x, d_mid, ff_parts, mid, gain, give, take, small, kv_parts, ff_sums, n_row):
    slots, width = x.shape
    bf = jnp.bfloat16
    size = sum(part.size for part in small) // 128 + width // 128
    phases = len(data_bits(n_row, MIX))
    return pl.pallas_call(
        home_kernel,
        name="home",
        out_shape=(
            jax.ShapeDtypeStruct((2, slots, width), bf),
            jax.ShapeDtypeStruct((2, slots, width), bf),
            jax.ShapeDtypeStruct((GROUP, size, 128), jnp.float32),
            jax.ShapeDtypeStruct(kv_parts.shape[2:], jnp.float32),
            jax.ShapeDtypeStruct(ff_sums.shape, bf),
        ),
        in_specs=[pl.BlockSpec(memory_space=VMEM)] * 12 + [pl.BlockSpec(memory_space=ANY)],
        out_specs=(
            (pl.BlockSpec(memory_space=ANY),) * 3
            + (pl.BlockSpec(memory_space=VMEM), pl.BlockSpec(memory_space=ANY))
        ),
        scratch_shapes=scatter_scratch(slots, width)
        + [
            VMEM((slots, width), jnp.float32),
            VMEM((slots, width), bf),
            VMEM((slots, width), bf),
            VMEM((n_row, CHUNK, width), bf),
            VMEM((n_row, CHUNK, width), bf),
            pltpu.SemaphoreType.DMA((n_row,)),
            pltpu.SemaphoreType.DMA((n_row,)),
            pltpu.SemaphoreType.DMA((2,)),
            pltpu.SemaphoreType.DMA((2,)),
            pltpu.SemaphoreType.DMA((2,)),
            VMEM((1, width), jnp.float32),
            VMEM((phases + 1, size, 128), jnp.float32),
            VMEM((phases, size, 128), jnp.float32),
            pltpu.SemaphoreType.DMA((phases,)),
            pltpu.SemaphoreType.DMA((phases,)),
        ]
        + gather_scratch()
        + deliver_scratch()
        + [
            VMEM((TP, kv_parts.shape[0]) + kv_parts.shape[2:], bf),
            VMEM((kv_parts.shape[0],) + kv_parts.shape[2:], bf),
            VMEM((kv_parts.shape[0],) + kv_parts.shape[2:], bf),
            pltpu.SemaphoreType.DMA((TP,)),
            pltpu.SemaphoreType.DMA((TP,)),
            pltpu.SemaphoreType.DMA((kv_parts.shape[0],)),
            pltpu.SemaphoreType.DMA((kv_parts.shape[0],)),
            VMEM((slots, width), jnp.float32),
        ]
        + scatter_scratch(slots, width),
        compiler_params=params(3, 56),
        cost_estimate=cost(75),
    )(parts, x, d_mid, ff_parts, mid, gain, give, take, *small, kv_parts, ff_sums)


def blocks_start(low, land, s1, r1):
    r, c = place()
    copies = []
    for m, f in CROSSED:
        col = 1 - c if f else c
        k = m * 2 + f
        copies.append(
            remote(low.at[block_of(m, MIX) + col], land.at[k], s1.at[k], r1.at[k], partner(r, m, MIX), col)
        )
        copies[-1].start()
    return copies


def blocks_turn(first, low, land, mine, total, s2, r2, here):
    r, c = place()
    own = member(r, MIX) * 2 + c
    for copy in first:
        copy.wait_recv()
    summed = low[own].astype(jnp.float32)
    for m, f in CROSSED:
        summed = summed + land[m * 2 + f].astype(jnp.float32)
    mine[...] = summed.astype(jnp.bfloat16)
    copies = [pltpu.make_async_copy(mine, total.at[own], here)]
    for m, f in CROSSED:
        k = m * 2 + f
        copies.append(
            remote(mine, total.at[own], s2.at[k], r2.at[k], partner(r, m, MIX), 1 - c if f else c)
        )
    for copy in copies:
        copy.start()
    return copies


def blocks_finish(first, second):
    for copy in first:
        copy.wait_send()
    for copy in second:
        copy.wait()


CROSSED = [(m, f) for m in (3, 1, 2) for f in (0, 1)] + [(0, 1)]


def blocks_scratch(slots):
    dma = pltpu.SemaphoreType.DMA
    return [
        VMEM((GROUP, slots, slots), jnp.bfloat16),
        VMEM((GROUP, slots, slots), jnp.bfloat16),
        VMEM((slots, slots), jnp.bfloat16),
        dma((GROUP,)),
        dma((GROUP,)),
        dma((GROUP,)),
        dma((GROUP,)),
        dma,
    ]


def dot(first_op, second_op, first_dim, second_dim, precision=None):
    return lax.dot_general(
        first_op,
        second_op,
        (((first_dim,), (second_dim,)), ((), ())),
        precision=precision,
        preferred_element_type=jnp.float32,
    )


def block_rows(b, slots):
    return pl.ds(pl.multiple_of(b * slots, slots), slots)


def marks(lens, b, slots):
    row = lax.broadcasted_iota(jnp.int32, (slots, slots), 0)
    col = lax.broadcasted_iota(jnp.int32, (slots, slots), 1)
    row_segment, col_segment, within = jnp.zeros_like(row), jnp.zeros_like(row), row
    end = 0
    for k in range(lens.shape[1] - 1):
        end = end + lens[b, k]
        row_segment = row_segment + (row >= end).astype(jnp.int32)
        col_segment = col_segment + (col >= end).astype(jnp.int32)
        within = jnp.where(row >= end, row - end, within)
    return (row_segment == col_segment) & (row >= col), within


def conv_pre(values, within, weights):
    width = values.shape[1]
    shifted = [values]
    for k in range(1, 4):
        valid = within[:, :1] >= k
        shifted.append(jnp.where(valid, pltpu.roll(values, k, 0), 0.0))
    pre = weights[4:5, :]
    for k in range(4):
        pre = pre + weights[3 - k : 4 - k, :] * shifted[k]
    return pre, shifted


def conv_back(grad, pre, shifted, within, weights):
    slots = grad.shape[0]
    gate = jax.nn.sigmoid(pre)
    e = grad * gate * (1.0 + pre * (1.0 - gate))
    sums = [jnp.sum(e * shifted[3 - i], axis=0, keepdims=True) for i in range(4)]
    sums.append(jnp.sum(e, axis=0, keepdims=True))
    back = weights[3:4, :] * e
    for k in range(1, 4):
        valid = within[:, :1] >= k
        back = back + weights[3 - k : 4 - k, :] * pltpu.roll(jnp.where(valid, e, 0.0), slots - k, 0)
    return back, sums


def softplus(values):
    return jnp.maximum(values, 0.0) + jnp.log1p(jnp.exp(-jnp.abs(values)))


def steps_and_levels(mixed, side, low, count):
    slots, width = mixed.shape
    lane = lax.broadcasted_iota(jnp.int32, (slots, width), 1)
    inside = (lane >= low) & (lane < low + count)
    step = jnp.where(inside, softplus(mixed + side[5:6, :]), 0.0)
    rate = jnp.where(inside, -jnp.exp(side[6:7, :]), 0.0)
    row = lax.broadcasted_iota(jnp.int32, (slots, slots), 0)
    col = lax.broadcasted_iota(jnp.int32, (slots, slots), 1)
    tri = (row >= col).astype(jnp.float32)
    level = dot(tri, step * rate, 1, 0, HIGH)
    return step, rate, level, tri, inside


def halves(first, second):
    lane = lax.broadcasted_iota(jnp.int32, first.shape, 1)
    return jnp.where(lane < first.shape[1] // 2, first, second)


def state_parts(mixed, within, side, sh):
    pre, shifted = conv_pre(mixed, within, side)
    act = pre * jax.nn.sigmoid(pre)
    lane = lax.broadcasted_iota(jnp.int32, act.shape, 1)
    first = jnp.where(lane < sh, act, 0.0).astype(jnp.bfloat16)
    second = jnp.where(lane < sh, pltpu.roll(act, act.shape[1] - sh, 1), 0.0).astype(jnp.bfloat16)
    return first, second, pre, shifted


def turned_pair(values, waves):
    half = values.shape[1] // 2
    return values * waves[:, : 2 * half] + pltpu.roll(values, half, 1) * waves[:, 2 * half :]


def turned_back(values, waves):
    half = values.shape[1] // 2
    return values * waves[:, : 2 * half] - pltpu.roll(values, half, 1) * waves[:, 2 * half :]


def wave_rows(within, table):
    slots = within.shape[0]
    picks = (within == lax.broadcasted_iota(jnp.int32, (slots, slots), 1)).astype(jnp.float32)
    return dot(picks, table[...], 1, 0, HIGH)


def attend(projected, rows, at, lens, table, b, slots):
    allowed, within = marks(lens, b, slots)
    waves = wave_rows(within, table)
    query = turned_pair(projected[rows, at : at + HD], waves).astype(jnp.bfloat16)
    key = turned_pair(projected[rows, at + HD : at + 2 * HD], waves).astype(jnp.bfloat16)
    value = projected[rows, at + 2 * HD : at + 3 * HD].astype(jnp.bfloat16)
    scores = jnp.where(allowed, dot(query, key, 1, 1) * HD ** (-0.5), NEG_LARGE)
    exps = jnp.exp(scores - jnp.max(scores, axis=-1, keepdims=True))
    probs = exps / jnp.sum(exps, axis=-1, keepdims=True)
    return query, key, value, probs, waves


def each_block(first, last, body):
    def step(b, carry):
        body(b)
        return carry

    lax.fori_loop(first, last, step, 0)


def mixer_kernel(
    sh, ph, lens, projected, chan, side, table, branch, scanned, crossed,
    low, land, mine, s1, r1, s2, r2, here, conv,
):
    slots = crossed.shape[1]
    mh = chan.shape[1]
    heads_at = 2 * sh
    greet(MIX, cross=True)

    def before(b):
        rows = block_rows(b, slots)
        allowed, within = marks(lens, b, slots)
        pre, unused = conv_pre(projected[rows, mh : 2 * mh], within, chan)
        conv[rows, :] = pre * jax.nn.sigmoid(pre)
        mixed = projected[rows, 2 * mh + 3 * HD :]
        first, second, unused, unused = state_parts(mixed, within, side, sh)
        low[b] = dot(second, first, 1, 1).astype(jnp.bfloat16)

    def attention(b):
        rows = block_rows(b, slots)
        query, key, value, probs, waves = attend(projected, rows, 2 * mh, lens, table, b, slots)
        branch[rows, mh:] = dot(probs.astype(jnp.bfloat16), value, 1, 0).astype(jnp.bfloat16)

    def after(b):
        rows = block_rows(b, slots)
        allowed, within = marks(lens, b, slots)
        mixed = projected[rows, 2 * mh + 3 * HD :]
        step, rate, level, tri, inside = steps_and_levels(mixed, side, heads_at, ph)
        step_t, level_t = step.T, level.T
        cross = crossed[b].astype(jnp.float32)
        for pair in range(ph // 2):
            cols = slice(pair * 128, (pair + 1) * 128)
            convs = conv[rows, cols]
            conv_low = convs.astype(jnp.bfloat16)
            outs = []
            for h in (2 * pair, 2 * pair + 1):
                at = heads_at + h
                spread = level[:, at : at + 1] - level_t[at : at + 1, :]
                decay = jnp.exp(jnp.where(allowed, spread, NEG_LARGE))
                mixing = cross * decay * step_t[at : at + 1, :]
                outs.append(dot(mixing.astype(jnp.bfloat16), conv_low, 1, 0))
            total = halves(outs[0], outs[1])
            scanned[rows, cols] = total
            gate = projected[rows, cols]
            gated = (total + chan[5:6, cols] * convs) * (gate * jax.nn.sigmoid(gate))
            branch[rows, cols] = gated.astype(jnp.bfloat16)

    each_block(0, GROUP, before)
    first = blocks_start(low, land, s1, r1)
    each_block(0, GROUP // 2, attention)
    second = blocks_turn(first, low, land, mine, crossed, s2, r2, here)
    each_block(GROUP // 2, GROUP, attention)
    blocks_finish(first, second)
    each_block(0, GROUP, after)


def mixer(lens, projected, chan, side, table, sh, ph):
    tokens = projected.shape[0]
    slots = tokens // GROUP
    mh = chan.shape[1]
    vm = pl.BlockSpec(memory_space=VMEM)
    return pl.pallas_call(
        partial(mixer_kernel, sh, ph),
        name="mixer",
        out_shape=(
            jax.ShapeDtypeStruct((tokens, mh + HD), jnp.bfloat16),
            jax.ShapeDtypeStruct((tokens, mh), jnp.float32),
            jax.ShapeDtypeStruct((GROUP, slots, slots), jnp.bfloat16),
        ),
        in_specs=[pl.BlockSpec(memory_space=pltpu.SMEM)] + [vm] * 4,
        out_specs=(vm,) * 3,
        scratch_shapes=blocks_scratch(slots) + [VMEM((tokens, mh), jnp.float32)],
        compiler_params=params(4, 40),
        cost_estimate=cost(30),
    )(lens, projected, chan, side, table)


def mixer_back_kernel(
    sh, ph, lens, projected, chan, side, table, scanned, crossed, grads,
    out, chan_sums, side_sums,
    low, land, mine, s1, r1, s2, r2, here, summed, misc,
):
    slots = crossed.shape[1]
    mh = chan.shape[1]
    heads_at = 2 * sh
    bf = jnp.bfloat16
    greet(MIX, cross=True)
    chan_sums[...] = jnp.zeros_like(chan_sums)
    side_sums[...] = jnp.zeros_like(side_sums)

    def scan(b):
        rows = block_rows(b, slots)
        allowed, within = marks(lens, b, slots)
        mixed = projected[rows, 2 * mh + 3 * HD :]
        step, rate, level, tri, inside = steps_and_levels(mixed, side, heads_at, ph)
        step_t, level_t = step.T, level.T
        cross = crossed[b].astype(jnp.float32)
        lane = lax.broadcasted_iota(jnp.int32, (slots, 128), 1)
        place_row = lax.broadcasted_iota(jnp.int32, (slots, slots), 0)
        grad_cross = jnp.zeros((slots, slots), jnp.float32)
        row_sums = jnp.zeros((slots, slots), jnp.float32)
        col_sums = jnp.zeros((slots, slots), jnp.float32)
        for pair in range(ph // 2):
            cols = slice(pair * 128, (pair + 1) * 128)
            weights = chan[:, cols]
            pre, shifted = conv_pre(
                projected[rows, mh + pair * 128 : mh + (pair + 1) * 128], within, weights
            )
            convs = pre * jax.nn.sigmoid(pre)
            conv_low = convs.astype(bf)
            gate = projected[rows, cols]
            sig = jax.nn.sigmoid(gate)
            grad = grads[rows, cols]
            skip = weights[5:6, :]
            grad_mix = grad * (gate * sig)
            out[rows, cols] = (
                grad * (scanned[rows, cols] + skip * convs) * (sig * (1.0 + gate * (1.0 - sig)))
            ).astype(bf)
            skip_sum = jnp.sum(grad_mix * convs, axis=0, keepdims=True)
            grad_low = grad_mix.astype(bf)
            backs = []
            for f in (0, 1):
                at = heads_at + 2 * pair + f
                mask = lane < 64 if f == 0 else lane >= 64
                spread = level[:, at : at + 1] - level_t[at : at + 1, :]
                decay = jnp.exp(jnp.where(allowed, spread, NEG_LARGE))
                step_row = step_t[at : at + 1, :]
                mixing = cross * decay * step_row
                backs.append(dot(mixing.astype(bf), grad_low, 0, 0))
                grad_mixing = dot(jnp.where(mask, grad_mix, 0.0).astype(bf), conv_low, 1, 1)
                weighted = grad_mixing * decay
                grad_cross = grad_cross + weighted * step_row
                weighted = weighted * cross
                col = jnp.sum(weighted, axis=0, keepdims=True)
                row = jnp.sum(weighted * step_row, axis=1, keepdims=True)
                row_sums = jnp.where(lane == at, row, row_sums)
                col_sums = jnp.where(place_row == at, col, col_sums)
            grad_conv = grad_mix * skip + halves(backs[0], backs[1])
            back, sums = conv_back(grad_conv, pre, shifted, within, weights)
            out[rows, mh + pair * 128 : mh + (pair + 1) * 128] = back.astype(bf)
            for i, part in enumerate(sums + [skip_sum]):
                chan_sums[i : i + 1, cols] += part
        low[b] = grad_cross.astype(bf)
        col_sums = col_sums.T
        grad_level = row_sums - step * col_sums
        grad_rate_step = dot(tri, grad_level, 0, 0, HIGH)
        grad_step = (col_sums + grad_rate_step * rate) * jax.nn.sigmoid(mixed + side[5:6, :])
        grad_step = jnp.where(inside, grad_step, 0.0)
        misc[rows, :] = grad_step
        side_sums[5:6, :] += jnp.sum(grad_step, axis=0, keepdims=True)
        side_sums[6:7, :] += jnp.sum(grad_rate_step * step, axis=0, keepdims=True) * rate[:1, :]

    def attention(b):
        rows = block_rows(b, slots)
        at = 2 * mh
        query, key, value, probs, waves = attend(projected, rows, at, lens, table, b, slots)
        grad = grads[rows, mh:].astype(bf)
        grad_probs = dot(grad, value, 1, 1)
        out[rows, at + 2 * HD : at + 3 * HD] = dot(probs.astype(bf), grad, 0, 0).astype(bf)
        grad_raw = probs * (grad_probs - jnp.sum(grad_probs * probs, axis=-1, keepdims=True))
        grad_raw = (grad_raw * HD ** (-0.5)).astype(bf)
        out[rows, at : at + HD] = turned_back(dot(grad_raw, key, 1, 0), waves).astype(bf)
        out[rows, at + HD : at + 2 * HD] = turned_back(dot(grad_raw, query, 0, 0), waves).astype(bf)

    def state(b):
        rows = block_rows(b, slots)
        allowed, within = marks(lens, b, slots)
        mixed = projected[rows, 2 * mh + 3 * HD :]
        first, second, pre, shifted = state_parts(mixed, within, side, sh)
        lane = lax.broadcasted_iota(jnp.int32, pre.shape, 1)
        grad_first = dot(summed[b], second, 0, 0)
        grad_second = pltpu.roll(dot(summed[b], first, 1, 0), sh, 1)
        grad = jnp.where(lane < sh, grad_first, jnp.where(lane < 2 * sh, grad_second, 0.0))
        back, sums = conv_back(grad, pre, shifted, within, side)
        out[rows, 2 * mh + 3 * HD :] = jnp.where(lane < 2 * sh, back, misc[rows, :]).astype(bf)
        for i, part in enumerate(sums):
            side_sums[i : i + 1, :] += part

    each_block(0, GROUP, scan)
    begun = blocks_start(low, land, s1, r1)
    each_block(0, GROUP // 2, attention)
    done = blocks_turn(begun, low, land, mine, summed, s2, r2, here)
    each_block(GROUP // 2, GROUP, attention)
    blocks_finish(begun, done)
    each_block(0, GROUP, state)


def mixer_back(lens, projected, chan, side, table, scanned, crossed, grads, sh, ph):
    tokens = projected.shape[0]
    slots = tokens // GROUP
    mh = chan.shape[1]
    vm = pl.BlockSpec(memory_space=VMEM)
    return pl.pallas_call(
        partial(mixer_back_kernel, sh, ph),
        name="mixer_back",
        out_shape=(
            jax.ShapeDtypeStruct(projected.shape, jnp.bfloat16),
            jax.ShapeDtypeStruct(chan.shape, jnp.float32),
            jax.ShapeDtypeStruct(side.shape, jnp.float32),
        ),
        in_specs=[pl.BlockSpec(memory_space=pltpu.SMEM)] + [vm] * 7,
        out_specs=(vm,) * 3,
        scratch_shapes=blocks_scratch(slots)
        + [
            VMEM((GROUP, slots, slots), jnp.bfloat16),
            VMEM((tokens, 128), jnp.float32),
        ],
        compiler_params=params(5, 48),
        cost_estimate=cost(50),
    )(lens, projected, chan, side, table, scanned, crossed, grads)


def swiglu(ff_gate, ff_up):
    return jax.nn.silu(ff_gate) * ff_up


def cut(array, parts, axis=1):
    rows, cols = array.shape
    return array.reshape(rows, parts, cols // parts).transpose(1, 0, 2)


def local(
    tokens,
    cotangent,
    deal_order,
    seq_lengths,
    mixer_norm_gain,
    mamba_gate_weight,
    mamba_input_weight,
    state_weight,
    step_weight,
    conv_input,
    conv_input_bias,
    conv_state,
    conv_state_bias,
    step_bias,
    decay_log,
    skip_scale,
    mamba_out_weight,
    query_weight,
    key_weight,
    value_weight,
    attn_out_weight,
    ff_norm_gain,
    gate_weight,
    up_weight,
    down_weight,
):
    n_row = lax.axis_size("row")
    r = lax.axis_index("row")
    c = lax.axis_index("col")
    t = member(r, MIX)
    n_bits = n_row.bit_length() - 1
    slots, width = tokens.shape[1:]
    bf = jnp.bfloat16
    rows = mamba_gate_weight.shape[0]
    mh = mamba_gate_weight.shape[1] // TP
    qh = query_weight.shape[1] // TP
    kvh = key_weight.shape[1]
    sh = state_weight.shape[1] // (2 * GROUP)
    ph = step_weight.shape[1] // TP
    fh = gate_weight.shape[1] // TP
    used = 2 * mh + qh + 2 * kvh + 2 * sh + ph
    spare = -used % 256

    half = state_weight.shape[1] // 2
    def assemble(slab, after):
        held = [(0, slab)]
        for b in data_bits(n_row, FFN):
            next_held = []
            for mask, part in held:
                if mask:
                    part, unused_value = lax.optimization_barrier((part, after))
                next_held.append((mask | 1 << b, lax.ppermute(part, "row", flips(n_row, 1 << b))))
            held = held + next_held
        return place_slabs(
            [mask for mask, part in held], [part for mask, part in held], n_row
        ).reshape(n_row * rows, slab.shape[2])

    def pick(array, index, axis=0):
        return lax.dynamic_index_in_dim(array, index, axis, keepdims=False)

    def sum_groups(grad, axes, after=None):
        grad = grad.astype(bf)
        bits = data_bits(n_row, axes)
        order = [n_bits - 1 - b for b in bits + [axes[1], axes[0]]]
        if order != sorted(order):
            cutup = grad.reshape((2,) * n_bits + (rows, grad.shape[1]))
            grad = cutup.transpose(order + [n_bits, n_bits + 1]).reshape(grad.shape)
        if after is not None:
            grad, after = lax.optimization_barrier((grad, after))
        by_group = sorted(range(n_row), key=lambda row: [row >> b & 1 for b in bits])
        alike = [
            [row for row in by_group if [row >> b & 1 for b in axes] == [m & 1, m >> 1]]
            for m in range(TP)
        ]
        part = lax.psum_scatter(
            grad, "row", scatter_dimension=0, axis_index_groups=alike, tiled=True
        ).reshape(TP, rows, grad.shape[1])
        return part, after

    meta_all, give, take, x_home, gy_home, normed_one, gy_all, w_mixer, slab_up, slab_down = deal(
        deal_order,
        seq_lengths,
        tokens,
        cotangent,
        mixer_norm_gain[None, :],
        (key_weight, value_weight),
        (mamba_gate_weight, mamba_input_weight, query_weight),
        (state_weight, step_weight, mamba_out_weight, attn_out_weight),
        (gate_weight, up_weight, down_weight),
        2 * sh + ph + spare,
        n_row,
    )
    normed_one = normed_one.reshape(GROUP * slots, width)
    gy_all = gy_all.reshape(GROUP * slots, width)
    w_mixer = w_mixer.reshape(width, -1)
    w_in, w_out = w_mixer[:, : used + spare], w_mixer[:, used + spare :]

    base = r - sum(bit(r, b) * (1 << b) for b in MIX)
    group_meta = jnp.stack([pick(meta_all, base + mask_of(m, MIX)) for m in range(TP)])
    lengths = group_meta[:, 2:4, : seq_lengths.shape[2]].reshape(GROUP, seq_lengths.shape[2])
    half_dim = HD // 2
    inverse = ROPE_BASE ** (-2.0 * jnp.arange(half_dim, dtype=jnp.float32) / HD)
    angles = jnp.arange(slots, dtype=jnp.float32)[:, None] * inverse[None, :]
    cosine, sine = jnp.cos(angles), jnp.sin(angles)
    table = jnp.concatenate([cosine, cosine, -sine, sine], axis=1)

    def piece(array, size, start):
        return lax.dynamic_slice_in_dim(array, start, size, array.ndim - 1)

    eighth = c * TP + t
    chan = jnp.concatenate(
        [
            piece(conv_input, mh, t * mh),
            piece(conv_input_bias[None], mh, t * mh),
            jnp.repeat(piece(skip_scale[None], ph, t * ph), mh // ph, axis=1),
            jnp.zeros((2, mh), jnp.float32),
        ],
        axis=0,
    )
    states = jnp.concatenate([conv_state, conv_state_bias[None]], axis=0)
    states = jnp.concatenate(
        [piece(states, sh, eighth * sh), piece(states, sh, half + eighth * sh)], axis=1
    )
    heads = jnp.concatenate(
        [piece(step_bias[None], ph, t * ph), piece(decay_log[None], ph, t * ph)], axis=0
    )
    after = 128 - 2 * sh - ph
    side = jnp.concatenate(
        [
            jnp.pad(states, ((0, 0), (0, 128 - 2 * sh))),
            jnp.pad(heads, ((0, 0), (2 * sh, after))),
            jnp.zeros((1, 128), jnp.float32),
        ],
        axis=0,
    )

    projected = matmul(normed_one, w_in)
    edges = [0, mh, 2 * mh, 2 * mh + qh, 2 * mh + qh + kvh, 2 * mh + qh + 2 * kvh]
    edges = edges + [edges[-1] + 2 * sh, edges[-1] + 2 * sh + ph]
    branch_in, scanned, crossed = mixer(lengths, projected, chan, side, table, sh, ph)
    branch_part = matmul_trans(branch_in, w_out).astype(bf).reshape(GROUP, slots, width)
    ff_gain = ff_norm_gain[None, :]
    mid, normed_two, w_down = middle(branch_part, x_home, ff_gain, slab_down, n_row)
    normed_two = normed_two.reshape(GROUP * slots, width)
    w_gate_up = assemble(slab_up, branch_part)
    w_down = w_down.reshape(n_row * rows, -1)

    ff_gate_up = matmul(normed_two, w_gate_up)
    ff_gate, ff_up = ff_gate_up[:, :fh], ff_gate_up[:, fh:]
    ff_hidden = swiglu(ff_gate, ff_up).astype(bf)
    grad_hidden = matmul(gy_all, w_down)
    unused_value, pullback = jax.vjp(swiglu, ff_gate, ff_up)
    grad_gate, grad_up = pullback(grad_hidden)
    grad_gate_up = jnp.concatenate([grad_gate.astype(bf), grad_up.astype(bf)], axis=1)
    (grad_ff,) = products(
        [(normed_two, grad_gate_up), (gy_all, ff_hidden)], [(0, 0, 2 * fh), (1, 0, fh)]
    )
    grad_gate_up, grad_ff = lax.optimization_barrier((grad_gate_up, grad_ff))
    ff_sums, unused_value = sum_groups(grad_ff, FFN)
    normed_two_part = (
        matmul_trans(grad_gate_up, w_gate_up).astype(bf).reshape(GROUP, slots, width)
    )
    d_mid, delta_ff_gain, branch_all = turn(
        normed_two_part, mid, gy_home, ff_gain
    )
    branch_all = branch_all.reshape(GROUP * slots, width)

    grad_branch_in = matmul(branch_all, w_out)
    grad_projected, chan_sums, side_sums = mixer_back(
        lengths, projected, chan, side, table, scanned, crossed, grad_branch_in, sh, ph
    )
    grad_mixer, grad_kv = products(
        [(normed_one, grad_projected), (branch_all, branch_in)],
        [(0, 0, edges[3]), (0, edges[5], used + spare), (1, 0, mh + qh)],
        [(0, edges[3], edges[5])],
    )
    grad_projected, grad_mixer, ff_hidden = lax.optimization_barrier(
        (grad_projected, grad_mixer, ff_hidden)
    )
    ff_part = matmul_trans(ff_hidden, w_down).astype(bf).reshape(GROUP, slots, width)
    mixer_sums, ff_sums = sum_groups(grad_mixer, MIX, ff_sums)
    normed_one_part = matmul_trans(grad_projected, w_in).astype(bf).reshape(GROUP, slots, width)

    output, grad_tokens, small_all, delta_kv, ff_land = send_home(
        normed_one_part, x_home, d_mid, ff_part, mid, mixer_norm_gain[None, :], give, take,
        (chan_sums, side_sums, delta_ff_gain),
        grad_kv.reshape(n_row // TP, TP, rows, 2 * kvh), ff_sums, n_row,
    )
    mixer_land, other_land = last(mixer_sums, edges[3])
    results = unpack(
        ff_land, mixer_land, other_land, small_all, delta_kv, output, grad_tokens, mh, qh, fh, sh, ph
    )
    flat = (2, 8, 10, 11, 12, 13, 19)
    return tuple(
        array.reshape(array.shape[1]) if i in flat else array for i, array in enumerate(results)
    )


def solution(mesh):
    both = P("row", "col")
    turned = P("col", "row")
    in_specs = (
        P(None, "row", None),
        P(None, "row", None),
        P(None, "row"),
        P(None, "row", None),
        P(),
        both,
        both,
        P("row", None),
        both,
        P(None, "col"),
        P("col"),
        P(),
        P(),
        P("col"),
        P("col"),
        P("col"),
        turned,
        both,
        both,
        both,
        turned,
        P(),
        both,
        both,
        turned,
    )
    out_specs = (
        P(None, "row", None),
        P(None, "row", None),
        P(),
        both,
        both,
        P("row", None),
        both,
        P(None, "col"),
        P("col"),
        P(),
        P(),
        P("col"),
        P("col"),
        P("col"),
        turned,
        both,
        both,
        both,
        turned,
        P(),
        both,
        both,
        turned,
    )
    return jax.shard_map(local, mesh=mesh, in_specs=in_specs, out_specs=out_specs, check_vma=False)
```

```python
from functools import partial

import jax
import jax.numpy as jnp
from jax import lax
from jax.experimental import pallas as pl
from jax.experimental.pallas import tpu as pltpu
from jax.sharding import PartitionSpec as P

HD = 128
TP = 4
GROUP = 2 * TP
CHUNK = 16
EPS = 1e-05
NEG_LARGE = -1e30
ROPE_BASE = 100000000000.0
MESH = pl.DeviceIdType.MESH
HIGH = lax.Precision.HIGHEST
VMEM = pltpu.VMEM
ANY = pltpu.HBM


def matmul(first_op, second_op):
    return jnp.dot(first_op, second_op, preferred_element_type=jnp.float32)


def matmul_trans(first_op, second_op):
    return lax.dot_general(
        first_op, second_op, (((1,), (1,)), ((), ())), preferred_element_type=jnp.float32
    )


def matmul_left(first_op, second_op):
    return lax.dot_general(
        first_op, second_op, (((0,), (0,)), ((), ())), preferred_element_type=jnp.float32
    )


MIX, FFN = (0, 1), (0, 1)


def data_bits(n_row, axes):
    return [b for b in reversed(range(n_row.bit_length() - 1)) if b not in axes]


def bit(row, b):
    return lax.rem(lax.div(row, 1 << b), 2)


def flip(row, b):
    return row + (1 << b) * (1 - 2 * bit(row, b))


def member(row, axes):
    return bit(row, axes[0]) + 2 * bit(row, axes[1])


def partner(row, m, axes):
    if m & 1:
        row = flip(row, axes[0])
    if m & 2:
        row = flip(row, axes[1])
    return row


def turned_row(row, mask):
    for b in range(mask.bit_length()):
        row = flip(row, b) if mask >> b & 1 else row
    return row


def group_of(row, n_row, axes):
    index = 0
    for b in data_bits(n_row, axes):
        index = index * 2 + bit(row, b)
    return index


def flips(n_row, mask):
    return [(row, row ^ mask) for row in range(n_row)]


def mask_of(m, axes):
    return (m & 1) * (1 << axes[0]) + (m // 2) * (1 << axes[1])


def place():
    return lax.axis_index("row"), lax.axis_index("col")


def block_of(m, axes):
    return member(partner(lax.axis_index("row"), m, axes), axes) * 2


def plan_of(axes, slots):
    if axes != (0, 1) or slots % 32:
        return [(0, slots, 2, 1)]
    return [(0, slots // 2, 1, 2), (slots // 2, slots, 2, 1)]


def params(number, megabytes):
    return pltpu.CompilerParams(
        collective_id=number, has_side_effects=True, vmem_limit_bytes=megabytes << 20
    )


def cost(microseconds):
    return pl.CostEstimate(flops=0, transcendentals=0, bytes_accessed=microseconds * 3_400_000)


def remote(src, dst, send, recv, row, col):
    return pltpu.make_async_remote_copy(
        src_ref=src, dst_ref=dst, send_sem=send, recv_sem=recv, device_id=(row, col), device_id_type=MESH
    )


def greet(*groups, cross=False, beyond=()):
    r, c = place()
    barrier = pltpu.get_barrier_semaphore()
    others = [(r, 1 - c)]
    for axes in groups:
        for m in (1, 2, 3) if cross else (1, 2):
            others.append((partner(r, m, axes), c))
            if cross:
                others.append((partner(r, m, axes), 1 - c))
    others = others + [(flip(r, b), c) for b in beyond]
    for other in others:
        pl.semaphore_signal(barrier, inc=1, device_id=other, device_id_type=MESH)
    pl.semaphore_wait(barrier, len(others))


def gather_start(src, out, send, recv, here, axes):
    r, c = place()
    own = member(r, axes) * 2 + c
    copies = [
        pltpu.make_async_copy(src, out.at[own], here),
        remote(src, out.at[own], send.at[0], recv.at[0], r, 1 - c),
    ]
    for p, (low, high, near, far) in enumerate(plan_of(axes, src.shape[0])):
        for k, m in ((1, near), (2, far)):
            copies.append(
                remote(
                    src.at[low:high], out.at[own, low:high], send.at[6 * p + k], recv.at[6 * p + k],
                    partner(r, m, axes), c,
                )
            )
    for copy in copies[2:] + copies[:2]:
        copy.start()
    return copies


def gather_pass(steps, p, k, m, row, col, out, send, recv, axes):
    r, c = place()
    low, high = plan_of(axes, out.shape[1])[p][:2]
    part = out.at[block_of(m, axes) + c, low:high]
    steps.append(remote(part, part, send.at[6 * p + k], recv.at[6 * p + k], row, col))
    steps[-1].start()


def gather_turn(copies, out, send, recv, axes):
    r, c = place()
    steps = []
    for p, (low, high, near, far) in enumerate(plan_of(axes, out.shape[1])):
        copies[2 + 2 * p].wait_recv()
        gather_pass(steps, p, 3, near, partner(r, far, axes), c, out, send, recv, axes)
        gather_pass(steps, p, 4, near, r, 1 - c, out, send, recv, axes)
    return steps


def gather_finish(copies, steps, out, send, recv, axes):
    r, c = place()
    plan = plan_of(axes, out.shape[1])
    for p, (low, high, near, far) in enumerate(plan):
        copies[3 + 2 * p].wait_recv()
        gather_pass(steps, p, 5, far, r, 1 - c, out, send, recv, axes)
    for p in range(len(plan)):
        steps[2 * p].wait_recv()
        gather_pass(steps, p, 6, 3, r, 1 - c, out, send, recv, axes)
    copies[0].wait()
    copies[1].wait()
    for copy in copies[2:] + steps[: 2 * len(plan) : 2]:
        copy.wait_send()
    for i, copy in enumerate(steps):
        if i >= 2 * len(plan) or i % 2:
            copy.wait()


def gather(src, out, send, recv, here, axes):
    copies = gather_start(src, out, send, recv, here, axes)
    gather_finish(copies, gather_turn(copies, out, send, recv, axes), out, send, recv, axes)


ROWS = 16


def by_rows(count, body, first=0):
    def step(i, carry):
        body(pl.ds(pl.multiple_of(i * ROWS, ROWS), ROWS))
        return carry

    lax.fori_loop(first // ROWS, count // ROWS, step, 0)


def scatter_steps(parts, near, held, far, s1, r1, s2, r2, total, axes):
    r, c = place()
    slots = total.shape[0]
    plan = plan_of(axes, slots)
    pairs = {}
    for m in (3, 1, 2, 0):
        pairs[m] = remote(
            parts.at[block_of(m, axes) + 1 - c], near.at[m], s1.at[m], r1.at[m], r, 1 - c
        )
        pairs[m].start()
    sent = {}

    def pair_sum(m, i, low, high):
        block = block_of(m, axes) + c

        def add(rows):
            held[i, rows, :] = (
                parts[block, rows, :].astype(jnp.float32) + near[m, rows, :].astype(jnp.float32)
            ).astype(jnp.bfloat16)

        by_rows(high, add, low)

    def send(i, p, m):
        low, high = plan[p][:2]
        k = 3 * p + i
        sent[i, p] = remote(
            held.at[i, low:high], far.at[i, low:high], s2.at[k], r2.at[k], partner(r, m, axes), c
        )
        sent[i, p].start()

    yield
    pairs[3].wait_recv()
    for p, (low, high, first, then) in enumerate(plan):
        pair_sum(3, 1, low, high)
        send(1, p, then)
    for m in (1, 2):
        pairs[m].wait_recv()
        for p, (low, high, first, then) in enumerate(plan):
            pair_sum(m, 0 if m == then else 2, low, high)
            if m == then:
                send(0, p, then)
    yield
    for p, (low, high, first, then) in enumerate(plan):
        sent[1, p].wait_recv()

        def add(rows):
            held[2, rows, :] = (
                held[2, rows, :].astype(jnp.float32) + far[1, rows, :].astype(jnp.float32)
            ).astype(jnp.bfloat16)

        by_rows(high, add, low)
        send(2, p, first)
    yield
    pairs[0].wait_recv()
    for p in range(len(plan)):
        sent[0, p].wait_recv()
        sent[2, p].wait_recv()
    own = member(r, axes) * 2 + c

    def fold(rows):
        total[rows, :] = (
            parts[own, rows, :].astype(jnp.float32)
            + near[0, rows, :].astype(jnp.float32)
            + far[0, rows, :].astype(jnp.float32)
            + far[2, rows, :].astype(jnp.float32)
        )

    by_rows(slots, fold)
    for copy in list(pairs.values()) + list(sent.values()):
        copy.wait_send()
    yield


def scatter_sum(*args):
    for step in scatter_steps(*args):
        pass


def scatter_scratch(slots, width):
    return [
        VMEM((TP, slots, width), jnp.bfloat16),
        VMEM((TP - 1, slots, width), jnp.bfloat16),
        VMEM((TP - 1, slots, width), jnp.bfloat16),
        pltpu.SemaphoreType.DMA((TP,)),
        pltpu.SemaphoreType.DMA((TP,)),
        pltpu.SemaphoreType.DMA((6,)),
        pltpu.SemaphoreType.DMA((6,)),
    ]


def gather_scratch():
    return [
        pltpu.SemaphoreType.DMA((13,)),
        pltpu.SemaphoreType.DMA((13,)),
        pltpu.SemaphoreType.DMA,
    ]


def strip_views(refs, owner, piece):
    at = 0
    for ref in refs:
        count = ref.shape[1] // TP
        yield ref.at[:, pl.ds(pl.multiple_of(owner * count, 128), count)], piece.at[:, at : at + count]
        at += count


def cut_start(refs, piece, send, recv, here, axes):
    r, c = place()
    for source, target in strip_views(refs, member(r, axes), piece):
        pltpu.make_async_copy(source, target, here).start()
    for m in (3, 1, 2):
        other = partner(r, m, axes)
        for source, target in strip_views(refs, member(other, axes), piece):
            remote(source, target, send.at[m], recv.at[m], other, c).start()


def piece_done(piece, sem):
    pltpu.make_async_copy(piece, piece, sem).wait()


def weight_forward(masks, whole, cols, send, recv):
    r, c = place()
    n_row = lax.axis_size("row")
    bits = data_bits(n_row, MIX)
    copies = []
    for mask in masks:
        at = whole.at[turned_row(r, mask), :, cols]
        crossed = [k for k, b in enumerate(bits) if mask >> b & 1]
        if crossed:
            piece_done(at, recv.at[mask])
        for b in bits[max([-1] + crossed) + 1 :]:
            lands = mask | 1 << b
            copies.append(remote(at, at, send.at[lands], recv.at[lands], flip(r, b), c))
            copies[-1].start()
    return copies


def weight_rounds(n_row, held):
    rounds = []
    for b in data_bits(n_row, MIX):
        rounds.append([mask | 1 << b for mask in held])
        held = held + rounds[-1]
    return rounds


def spread(masks, whole, cols, send, recv):
    r, c = place()
    copies = []
    for mask in masks:
        at = whole.at[turned_row(r, mask), :, cols]
        for m in (3, 1, 2):
            lands = mask | mask_of(m, MIX)
            copies.append(remote(at, at, send.at[lands], recv.at[lands], partner(r, m, MIX), c))
            copies[-1].start()
    return copies


def place_kernel(masks, n_row, *refs):
    slabs, whole, sems = refs[: len(masks)], refs[-2], refs[-1]
    r, c = place()
    copies = []
    for i, mask in enumerate(masks):
        at = whole.at[group_of(turned_row(r, mask), n_row, FFN)]
        copies.append(pltpu.make_async_copy(slabs[i], at, sems.at[i]))
        copies[-1].start()
    for copy in copies:
        copy.wait()


def place_slabs(masks, slabs, n_row):
    return pl.pallas_call(
        partial(place_kernel, masks, n_row),
        name="place",
        out_shape=jax.ShapeDtypeStruct((len(masks),) + slabs[0].shape, slabs[0].dtype),
        in_specs=[pl.BlockSpec(memory_space=ANY)] * len(masks),
        out_specs=pl.BlockSpec(memory_space=ANY),
        scratch_shapes=[pltpu.SemaphoreType.DMA((len(masks),))],
        compiler_params=pltpu.CompilerParams(vmem_limit_bytes=4 << 20),
        cost_estimate=cost(4),
    )(*slabs)


def exchange_rows(buf, land, send, recv):
    r, c = place()
    n_row = lax.axis_size("row")

    def copy(other):
        return remote(
            buf.at[other], land.at[r], send.at[other], recv.at[r], other, c
        )

    def start(off, carry):
        copy(lax.rem(r + off, n_row)).start()
        return carry

    lax.fori_loop(1, n_row, start, 0)


def finish_rows(buf, land, send, recv):
    r, c = place()
    n_row = lax.axis_size("row")

    def finish(off, carry):
        other = lax.rem(r + off, n_row)
        copy = remote(buf.at[other], land.at[other], send.at[other], recv.at[other], other, c)
        copy.wait_send()
        copy.wait_recv()
        return carry

    lax.fori_loop(1, n_row, finish, 0)


def greet_rows(meanwhile=None):
    r, c = place()
    n_row = lax.axis_size("row")
    barrier = pltpu.get_barrier_semaphore()

    def greet(off, carry):
        pl.semaphore_signal(
            barrier, inc=1, device_id=(lax.rem(r + off, n_row), c), device_id_type=MESH
        )
        return carry

    lax.fori_loop(1, n_row, greet, 0)
    pl.semaphore_signal(barrier, inc=1, device_id=(r, 1 - c), device_id_type=MESH)
    if meanwhile is not None:
        meanwhile()
    pl.semaphore_wait(barrier, n_row)


COLS = 512


def permute_out(choice, buf, first, second, slots):
    n_row = buf.shape[0]

    def column(i, carry):
        cols = pl.ds(pl.multiple_of(i * COLS, COLS), COLS)
        picked = matmul(choice[:, :slots], first[:, cols]) + matmul(choice[:, slots:], second[:, cols])
        buf[:, :, cols] = picked.astype(jnp.bfloat16).reshape(n_row, CHUNK, COLS)
        return carry

    lax.fori_loop(0, buf.shape[2] // COLS, column, 0)


def permute_in(choice, land, first, second, slots):
    n_row = land.shape[0]

    def column(i, carry):
        cols = pl.ds(pl.multiple_of(i * COLS, COLS), COLS)
        got = land[:, :, cols].reshape(n_row * CHUNK, COLS)
        first[:, cols] = matmul_left(choice[:, :slots], got).astype(jnp.bfloat16)
        second[:, cols] = matmul_left(choice[:, slots:], got).astype(jnp.bfloat16)
        return carry

    lax.fori_loop(0, land.shape[2] // COLS, column, 0)


def deal_kernel(
    order, lengths, tokens, cotangent, gain, *refs
):
    kv_refs, first_refs, refs = refs[:2], refs[2:5], refs[5:]
    states, steps_in, mamba_out, attn_out, refs = *refs[:4], refs[4:]
    up_refs, down, refs = refs[:2], refs[2], refs[3:]
    meta_all, give, take, x_out, gy_out, normed_all, gy_all, whole, slab_up, slab_down = refs[:10]
    x_mine, g_mine, buf, land, normed = refs[10:15]
    load, msend, mrecv, csend, crecv, nsend, nrecv, nhere, gsend, grecv, ghere = refs[15:26]
    wsend, wrecv, acut, arecv, ahere, bcut, brecv, bhere, usend, urecv, uhere, dsend, drecv, dhere, kv_here = refs[26:41]
    meta, mixed, mamba_turned, attn_turned, down_turned = refs[41:]
    second_refs, down_refs = (mixed, mamba_turned, attn_turned), (down_turned,)
    r, c = place()
    n_row = lax.axis_size("row")
    f = member(r, FFN)
    slots = x_mine.shape[0]
    per_peer = slots // n_row
    loads = [
        pltpu.make_async_copy(tokens.at[c], x_mine, load.at[0]),
        pltpu.make_async_copy(cotangent.at[c], g_mine, load.at[1]),
    ]
    for copy in loads:
        copy.start()
    bf = jnp.bfloat16

    def turn_weight(source, target):
        target[...] = source[...].astype(jnp.float32).T.astype(bf)

    def prepare():
        count = lengths.shape[2]
        meta[...] = jnp.zeros_like(meta)
        meta[0:2, :] = order[...]
        for i in range(2):
            meta[2 + i : 3 + i, 0:count] = lengths[i]
        part = states.shape[1] // 4
        values = states[...].astype(jnp.float32)
        first = jnp.where(c == 0, values[:, :part], values[:, part : 2 * part])
        second = jnp.where(c == 0, values[:, 2 * part : 3 * part], values[:, 3 * part :])
        step_values = steps_in[...].astype(jnp.float32)
        sh, ph = part // TP, step_values.shape[1] // TP
        width = mixed.shape[1] // TP
        for k in range(TP):
            cols = slice(k * sh, (k + 1) * sh)
            strip = [first[:, cols], second[:, cols], step_values[:, k * ph : (k + 1) * ph]]
            strip.append(jnp.zeros((values.shape[0], width - 2 * sh - ph), jnp.float32))
            mixed[:, k * width : (k + 1) * width] = jnp.concatenate(strip, axis=1).astype(bf)
        turn_weight(mamba_out, mamba_turned)
        turn_weight(attn_out, attn_turned)

    greet_rows(prepare)
    group = [mask_of(m, MIX) for m in range(TP)]
    first_cols = sum(ref.shape[1] for ref in first_refs) // TP
    kv_cols = first_cols + sum(ref.shape[1] for ref in kv_refs)
    cuts = (
        (slice(0, first_cols), first_refs, acut, arecv, ahere),
        (slice(kv_cols, whole.shape[2]), second_refs, bcut, brecv, bhere),
    )
    kv = slice(first_cols, kv_cols)

    def meta_copy(other, slot):
        return remote(meta, meta_all.at[slot], msend.at[other], mrecv.at[slot], other, c)

    def start(off, carry):
        meta_copy(lax.rem(r + off, n_row), r).start()
        return carry

    lax.fori_loop(1, n_row, start, 0)
    meta_all[r] = meta[...]
    at = first_cols
    for ref in kv_refs:
        pltpu.make_async_copy(ref, whole.at[r, :, at : at + ref.shape[1]], kv_here).start()
        at += ref.shape[1]
    for cols, refs_of, send, recv, here in cuts:
        cut_start(refs_of, whole.at[r, :, cols], send, recv, here, MIX)
    forwards = []
    for i, (cols, refs_of, send, recv, here) in enumerate(cuts):
        piece_done(whole.at[r, :, cols], here)
        forwards = forwards + weight_forward([0], whole, cols, wsend.at[i], wrecv.at[i])
    piece_done(whole.at[r, :, kv], kv_here)
    forwards = forwards + weight_forward([0], whole, kv, wsend.at[2], wrecv.at[2])

    def finish(off, carry):
        other = lax.rem(r + off, n_row)
        copy = meta_copy(other, other)
        copy.wait_send()
        copy.wait_recv()
        return carry

    lax.fori_loop(1, n_row, finish, 0)

    shift = slots.bit_length() - 1
    row_no = lax.broadcasted_iota(jnp.int32, (CHUNK, slots), 0)
    wanted = jnp.where(row_no < per_peer, row_no, row_no - per_peer).astype(jnp.float32)
    early = row_no < per_peer
    late = (row_no >= per_peer) & (row_no < 2 * per_peer)
    tri = (
        lax.broadcasted_iota(jnp.int32, (slots, slots), 0)
        < lax.broadcasted_iota(jnp.int32, (slots, slots), 1)
    ).astype(jnp.float32).astype(jnp.bfloat16)
    places = lax.broadcasted_iota(jnp.int32, (slots, slots), 0)

    def order_of(block):
        picked = jnp.where(c == 0, block[0:1, :], block[1:2, :])
        return lax.shift_right_logical(picked, shift), picked - lax.shift_left(
            lax.shift_right_logical(picked, shift), shift
        )

    own_source, own_local = order_of(meta[...])

    def select(mask):
        wide = jnp.broadcast_to(mask.astype(jnp.float32), (CHUNK, slots)).astype(jnp.bfloat16)
        rank = matmul(wide, tri)
        return jnp.where(
            (rank == wanted) & (wide.astype(jnp.float32) > 0.5), 1.0, 0.0
        )

    def build(d, carry):
        rows = pl.ds(pl.multiple_of(d * CHUNK, CHUNK), CHUNK)
        source, local = order_of(meta_all[d])
        chosen = select(source == r).astype(jnp.bfloat16)
        at_home = (places == local).astype(jnp.float32).astype(jnp.bfloat16)
        picks = matmul_trans(chosen, at_home)
        give[rows, :slots] = jnp.where(early, picks, 0.0).astype(jnp.bfloat16)
        give[rows, slots:] = jnp.where(late, picks, 0.0).astype(jnp.bfloat16)
        kept = select(own_source == d)
        take[rows, :slots] = jnp.where(early, kept, 0.0).astype(jnp.bfloat16)
        take[rows, slots:] = jnp.where(late, kept, 0.0).astype(jnp.bfloat16)
        return carry

    lax.fori_loop(0, n_row, build, 0)
    for copy in loads:
        copy.wait()
    permute_out(give, buf, x_mine, g_mine, slots)
    exchange_rows(buf, land, csend, crecv)
    land[r] = buf[r]
    for i, (cols, refs_of, send, recv, here) in enumerate(cuts):
        for m in (1, 2, 3):
            piece_done(whole.at[r, :, cols], recv.at[m])
            forwards = forwards + weight_forward([group[m]], whole, cols, wsend.at[i], wrecv.at[i])
    turn_weight(down, down_turned)
    finish_rows(buf, land, csend, crecv)
    permute_in(take, land, x_out, gy_out, slots)

    def norm(rows):
        values = x_out[rows, :].astype(jnp.float32)
        scale = lax.rsqrt(jnp.mean(values * values, axis=-1, keepdims=True) + EPS)
        normed[rows, :] = (values * scale * gain[...]).astype(jnp.bfloat16)

    by_rows(slots, norm)
    first = gather_start(normed, normed_all, nsend, nrecv, nhere, MIX)
    cut_start(up_refs, slab_up.at[f], usend, urecv, uhere, FFN)
    cut_start(down_refs, slab_down.at[f], dsend, drecv, dhere, FFN)
    second = gather_start(gy_out, gy_all, gsend, grecv, ghere, FFN)
    kv_rounds = weight_rounds(n_row, [0])
    steps = []
    for k, masks in enumerate(weight_rounds(n_row, group)):
        forwards = forwards + weight_forward(kv_rounds[k], whole, kv, wsend.at[2], wrecv.at[2])
        for i in (0, 1):
            forwards = forwards + weight_forward(masks, whole, cuts[i][0], wsend.at[i], wrecv.at[i])
            if k == 0 and i == 0:
                steps.append(gather_turn(first, normed_all, nsend, nrecv, MIX))
            if k == 0 and i == 1:
                steps.append(gather_turn(second, gy_all, gsend, grecv, FFN))
        if k == len(kv_rounds) - 1:
            kv_held = [0] + [mask for masks in kv_rounds for mask in masks]
            spreads = spread(kv_held, whole, kv, wsend.at[2], wrecv.at[2])
    gather_finish(first, steps[0], normed_all, nsend, nrecv, MIX)
    gather_finish(second, steps[1], gy_all, gsend, grecv, FFN)
    for copy in forwards:
        copy.wait_send()
    for cols, refs_of, send, recv, here in cuts:
        for m in (1, 2, 3):
            piece_done(whole.at[r, :, cols], send.at[m])
    for copy in spreads:
        copy.wait()
    for slab, send, recv, here in ((slab_up, usend, urecv, uhere), (slab_down, dsend, drecv, dhere)):
        piece_done(slab.at[f], here)
        for m in (1, 2, 3):
            piece_done(slab.at[f], send.at[m])
            piece_done(slab.at[f], recv.at[m])


def deal(order, lengths, tokens, cotangent, gain, kv, first, second, ff, strip, n_row):
    slots, width = tokens.shape[1:]
    bf = jnp.bfloat16
    rows = first[0].shape[0]
    states, steps_in, mamba_out, attn_out = second
    in_cols = sum(array.shape[1] for array in kv) + sum(array.shape[1] for array in first) // TP
    in_cols += strip + (mamba_out.shape[0] + attn_out.shape[0]) // TP
    up_cols, down_cols = 2 * ff[0].shape[1] // TP, ff[2].shape[0] // TP
    vm, hb = pl.BlockSpec(memory_space=VMEM), pl.BlockSpec(memory_space=ANY)
    dma = pltpu.SemaphoreType.DMA
    return pl.pallas_call(
        deal_kernel,
        name="deal",
        out_shape=(
            jax.ShapeDtypeStruct((n_row, 8, 128), jnp.int32),
            jax.ShapeDtypeStruct((n_row * CHUNK, 2 * slots), bf),
            jax.ShapeDtypeStruct((n_row * CHUNK, 2 * slots), bf),
            jax.ShapeDtypeStruct((slots, width), bf),
            jax.ShapeDtypeStruct((slots, width), bf),
            jax.ShapeDtypeStruct((GROUP, slots, width), bf),
            jax.ShapeDtypeStruct((GROUP, slots, width), bf),
            jax.ShapeDtypeStruct((n_row, rows, in_cols), bf),
            jax.ShapeDtypeStruct((TP, rows, up_cols), bf),
            jax.ShapeDtypeStruct((TP, rows, down_cols), bf),
        ),
        in_specs=[vm, vm, hb, hb, vm] + [vm] * 12,
        out_specs=(vm,) * 5 + (hb,) * 5,
        scratch_shapes=[
            VMEM((slots, width), bf),
            VMEM((slots, width), bf),
            VMEM((n_row, CHUNK, width), bf),
            VMEM((n_row, CHUNK, width), bf),
            VMEM((slots, width), bf),
            dma((2,)),
            dma((n_row,)),
            dma((n_row,)),
            dma((n_row,)),
            dma((n_row,)),
        ]
        + gather_scratch()
        + gather_scratch()
        + [dma((3, n_row)), dma((3, n_row))]
        + [dma((TP,)), dma((TP,)), dma] * 4
        + [dma]
        + [
            VMEM((8, 128), jnp.int32),
            VMEM((rows, TP * strip), bf),
            VMEM((rows, mamba_out.shape[0]), bf),
            VMEM((rows, attn_out.shape[0]), bf),
            VMEM((rows, ff[2].shape[0]), bf),
        ],
        compiler_params=params(0, 58),
        cost_estimate=cost(100),
    )(order, lengths, tokens, cotangent, gain, *kv, *first, *second, *ff)


def slab_copy(slab, whole, mask, b, send, recv):
    r, c = place()
    n_row = lax.axis_size("row")
    at = whole.at[group_of(turned_row(r, mask), n_row, FFN)]
    lands = mask | 1 << b
    k = group_index(lands, n_row)
    return remote(at if mask else slab, at, send.at[k], recv.at[k], flip(r, b), c)


def group_index(mask, n_row):
    return sum((mask >> b & 1) << i for i, b in enumerate(data_bits(n_row, FFN)))


def middle_kernel(
    parts, x, gain, slab, mid, normed_all, whole,
    near, out2, far, s1, r1, s2, r2, normed, nsend, nrecv, nhere, wsend, wrecv, where,
):
    r, c = place()
    n_row = lax.axis_size("row")
    bits = data_bits(n_row, FFN)
    greet(*{MIX, FFN}, beyond=bits)
    own = pltpu.make_async_copy(slab, whole.at[group_of(r, n_row, FFN)], where)
    own.start()
    copies = {1 << b: slab_copy(slab, whole, 0, b, wsend, wrecv) for b in bits}
    for copy in copies.values():
        copy.start()
    scatter_sum(parts, near, out2, far, s1, r1, s2, r2, mid, MIX)

    def norm(rows):
        values = x[rows, :].astype(jnp.float32) + mid[rows, :]
        mid[rows, :] = values
        scale = lax.rsqrt(jnp.mean(values * values, axis=-1, keepdims=True) + EPS)
        normed[rows, :] = (values * scale * gain[...]).astype(jnp.bfloat16)

    by_rows(mid.shape[0], norm)
    started = gather_start(normed, normed_all, nsend, nrecv, nhere, FFN)
    passed = gather_turn(started, normed_all, nsend, nrecv, FFN)
    for i, b in enumerate(bits):
        for mask in [mask for mask in copies if mask >> b & 1]:
            copies[mask].wait_recv()
            for later in bits[i + 1 :]:
                lands = mask | 1 << later
                copies[lands] = slab_copy(slab, whole, mask, later, wsend, wrecv)
                copies[lands].start()
    gather_finish(started, passed, normed_all, nsend, nrecv, FFN)
    own.wait()
    for copy in copies.values():
        copy.wait_send()


def middle(parts, x, gain, slab, n_row):
    slots, width = x.shape
    groups = n_row // TP
    vm, hb = pl.BlockSpec(memory_space=VMEM), pl.BlockSpec(memory_space=ANY)
    return pl.pallas_call(
        middle_kernel,
        name="middle",
        out_shape=(
            jax.ShapeDtypeStruct((slots, width), jnp.float32),
            jax.ShapeDtypeStruct((GROUP, slots, width), jnp.bfloat16),
            jax.ShapeDtypeStruct((groups,) + slab.shape, slab.dtype),
        ),
        in_specs=[vm] * 3 + [hb],
        out_specs=(vm, hb, hb),
        scratch_shapes=scatter_scratch(slots, width)
        + [VMEM((slots, width), jnp.bfloat16)]
        + gather_scratch()
        + [
            pltpu.SemaphoreType.DMA((groups,)),
            pltpu.SemaphoreType.DMA((groups,)),
            pltpu.SemaphoreType.DMA,
        ],
        compiler_params=params(1, 30),
        cost_estimate=cost(60),
    )(parts, x, gain, slab)


def norm_back(values, gain, grad):
    inverse = lax.rsqrt(jnp.mean(values * values, axis=-1, keepdims=True) + EPS)
    scaled = grad * gain
    back = inverse * scaled - values * (
        inverse * inverse * inverse * jnp.mean(values * scaled, axis=-1, keepdims=True)
    )
    return back, jnp.sum(grad * values * inverse, axis=0, keepdims=True)


def turn_kernel(
    parts, mid, gy, gain, d_mid, d_gain, branch_all,
    near, out2, far, s1, r1, s2, r2, branch, nsend, nrecv, nhere,
):
    greet(*{MIX, FFN})
    scatter_sum(parts, near, out2, far, s1, r1, s2, r2, d_mid, FFN)
    d_gain[...] = jnp.zeros_like(d_gain)

    def back(rows):
        values = mid[rows, :]
        grad, gain_part = norm_back(values, gain[...], d_mid[rows, :])
        grad = gy[rows, :].astype(jnp.float32) + grad
        d_mid[rows, :] = grad
        branch[rows, :] = grad.astype(jnp.bfloat16)
        d_gain[...] += gain_part

    by_rows(mid.shape[0], back)
    gather(branch, branch_all, nsend, nrecv, nhere, MIX)


def turn(parts, mid, gy, gain):
    slots, width = mid.shape
    return pl.pallas_call(
        turn_kernel,
        name="turn",
        out_shape=(
            jax.ShapeDtypeStruct((slots, width), jnp.float32),
            jax.ShapeDtypeStruct((1, width), jnp.float32),
            jax.ShapeDtypeStruct((GROUP, slots, width), jnp.bfloat16),
        ),
        in_specs=[pl.BlockSpec(memory_space=VMEM)] * 4,
        out_specs=(pl.BlockSpec(memory_space=VMEM),) * 2 + (pl.BlockSpec(memory_space=ANY),),
        scratch_shapes=scatter_scratch(slots, width)
        + [VMEM((slots, width), jnp.bfloat16)]
        + gather_scratch(),
        compiler_params=params(2, 30),
        cost_estimate=cost(60),
    )(parts, mid, gy, gain)


def home_kernel(
    parts, x, d_mid, ff_parts, mid, gain, take, chan_sums, side_sums, ff_gain_sums, kv_parts, ff_sums,
    buf, small_all, kv_sums, ff_land,
    near, out2, far, s1, r1, s2, r2, total, first, second, d_gain, stages, stage_land, tsend, trecv, gsend, grecv, ghere, *more
):
    r, c = place()
    slots, width = x.shape
    bits = data_bits(lax.axis_size("row"), MIX)
    greet_rows()
    kv_near, kv_held, kv_far, kv_s1, kv_r1, kv_s2, kv_r2 = more[3:10]
    ff_total = more[10]
    delivered = deliver(ff_sums, ff_land, *more[:3], FFN)
    steps = scatter_steps(parts, near, out2, far, s1, r1, s2, r2, total, MIX)
    ff_steps = scatter_steps(ff_parts, *more[11:], ff_total, FFN)
    for pair in zip(steps, ff_steps):
        pass
    d_gain[...] = jnp.zeros_like(d_gain)

    def back(rows):
        values = x[rows, :].astype(jnp.float32)
        grad, gain_part = norm_back(values, gain[...], total[rows, :])
        second[rows, :] = (d_mid[rows, :] + grad).astype(jnp.bfloat16)
        first[rows, :] = (ff_total[rows, :] + mid[rows, :]).astype(jnp.bfloat16)
        d_gain[...] += gain_part

    by_rows(slots, back)
    at = 0
    for sums in (chan_sums, side_sums, ff_gain_sums, d_gain):
        for i in range(sums.shape[0]):
            for k in range(sums.shape[1] // 128):
                stages[0, at : at + 1, :] = sums[i : i + 1, k * 128 : (k + 1) * 128]
                at += 1

    def stage_copy(i):
        return remote(
            stages.at[i], stage_land.at[i], tsend.at[i], trecv.at[i], flip(r, bits[i]), c
        )

    stage_copy(0).start()
    permute_out(take, buf, first, second, slots)
    own = member(r, MIX)
    groups = kv_parts.shape[0]
    kv_sent = []
    for m in (3, 1, 2):
        other = partner(r, m, MIX)
        kv_sent.append(
            remote(kv_parts.at[:, member(other, MIX)], kv_near.at[m], kv_s1.at[m], kv_r1.at[m], other, c)
        )
        kv_sent[-1].start()
    for i in range(len(bits)):
        stage_copy(i).wait()
        stages[i + 1] = stages[i] + stage_land[i]
        if i + 1 < len(bits):
            stage_copy(i + 1).start()
    started = gather_start(stages.at[len(bits)], small_all, gsend, grecv, ghere, MIX)
    for copy in kv_sent:
        copy.wait()
    passed = gather_turn(started, small_all, gsend, grecv, MIX)

    def kv_pair(g):
        kv_held[g] = (
            kv_parts[g, own].astype(jnp.float32)
            + kv_near[1, g].astype(jnp.float32)
            + kv_near[2, g].astype(jnp.float32)
            + kv_near[3, g].astype(jnp.float32)
        ).astype(jnp.bfloat16)

    each_block(0, groups, kv_pair)
    kv_far_sent = []
    for k in range(1, groups):
        other = turned_row(r, sum((1 << b) * (k >> i & 1) for i, b in enumerate(bits)))
        kv_far_sent.append(
            remote(
                kv_held.at[group_of(other, lax.axis_size("row"), MIX)],
                kv_far.at[k], kv_s2.at[k], kv_r2.at[k], other, c,
            )
        )
        kv_far_sent[-1].start()
    gather_finish(started, passed, small_all, gsend, grecv, MIX)
    for copy in kv_far_sent:
        copy.wait()
    kv_total = kv_held[group_of(r, lax.axis_size("row"), MIX)].astype(jnp.float32)
    for k in range(1, groups):
        kv_total = kv_total + kv_far[k].astype(jnp.float32)
    kv_sums[...] = kv_total
    for copy in delivered:
        copy.wait()


def deliver(sums, land, send, recv, here, axes):
    r, c = place()
    own = member(r, axes)
    copies = [pltpu.make_async_copy(sums.at[own], land.at[own], here)]
    for m in (3, 1, 2):
        other = partner(r, m, axes)
        copies.append(
            remote(sums.at[member(other, axes)], land.at[own], send.at[m], recv.at[m], other, c)
        )
    for copy in copies:
        copy.start()
    return copies


def deliver_scratch():
    dma = pltpu.SemaphoreType.DMA
    return [dma((TP,)), dma((TP,)), dma]


def last_kernel(
    at, buf, give, sums, output, gradient, sums_land, other,
    land, first, second, csend, crecv, here, osend, orecv, s1, r1, h1, send, recv,
):
    r, c = place()
    greet_rows()
    exchange_rows(buf, land, csend, crecv)
    delivered = deliver(sums, sums_land, s1, r1, h1, MIX)
    land[r] = buf[r]
    for copy in delivered:
        copy.wait()
    across = remote(sums_land.at[:, :, at : at + 128], other, send, recv, r, 1 - c)
    across.start()
    finish_rows(buf, land, csend, crecv)
    permute_in(give, land, first, second, first.shape[0])
    copies = [across]
    for i, (mine, out) in enumerate(((first, output), (second, gradient))):
        copies.append(pltpu.make_async_copy(mine, out.at[c], here.at[i]))
        copies.append(remote(mine, out.at[c], osend.at[i], orecv.at[i], r, 1 - c))
    for copy in copies[1:]:
        copy.start()
    for copy in copies:
        copy.wait()


def last(buf, give, sums, at):
    n_row, chunk, width = buf.shape
    slots = give.shape[1] // 2
    vm, hb = pl.BlockSpec(memory_space=VMEM), pl.BlockSpec(memory_space=ANY)
    dma = pltpu.SemaphoreType.DMA
    bf = jnp.bfloat16
    return pl.pallas_call(
        partial(last_kernel, at),
        name="last",
        out_shape=(
            jax.ShapeDtypeStruct((2, slots, width), bf),
            jax.ShapeDtypeStruct((2, slots, width), bf),
            jax.ShapeDtypeStruct(sums.shape, sums.dtype),
            jax.ShapeDtypeStruct(sums.shape[:2] + (128,), sums.dtype),
        ),
        in_specs=[vm, vm, hb],
        out_specs=(hb,) * 4,
        scratch_shapes=[
            VMEM(buf.shape, bf),
            VMEM((slots, width), bf),
            VMEM((slots, width), bf),
            dma((n_row,)),
            dma((n_row,)),
            dma((2,)),
            dma((2,)),
            dma((2,)),
        ]
        + deliver_scratch()
        + [dma, dma],
        compiler_params=params(6, 32),
        cost_estimate=cost(35),
    )(buf, give, sums)


def products_kernel(parts, *refs):
    pairs = len(refs) - len(parts)
    for part, out in zip(parts, refs[pairs:]):
        at = 0
        for i, low, high in part:
            left, right = refs[2 * i], refs[2 * i + 1]
            out[:, at : at + high - low] = dot(left[...], right[:, low:high], 0, 0).astype(out.dtype)
            at += high - low


def products(pairs, *parts):
    tokens, width = pairs[0][0].shape
    tile = min(512, width)
    specs = []
    for left, right in pairs:
        specs.append(pl.BlockSpec((tokens, tile), lambda i: (0, i)))
        specs.append(pl.BlockSpec(right.shape, lambda i: (0, 0)))
    totals = [sum(high - low for i, low, high in part) for part in parts]
    return pl.pallas_call(
        partial(products_kernel, parts),
        name="products",
        grid=(width // tile,),
        out_shape=tuple(jax.ShapeDtypeStruct((width, total), jnp.bfloat16) for total in totals),
        in_specs=specs,
        out_specs=tuple(pl.BlockSpec((tile, total), lambda i: (i, 0)) for total in totals),
        compiler_params=pltpu.CompilerParams(vmem_limit_bytes=30 << 20),
        cost_estimate=cost(10),
    )(*[array for pair in pairs for array in pair])


def unpack_kernel(
    sh, ph, ff, mixer, misc, small, kv, home_out, home_grad,
    output, gradient, mixer_gain, mamba_gate, mamba_input, state, step, conv_k, conv_b, state_k, state_b,
    step_bias, decay, skip, mamba_out, query, key, value, attn_out, ff_gain, gate, up, down, sems,
):
    c = lax.axis_index("col")
    f32 = jnp.float32
    copies = [
        pltpu.make_async_copy(home_out, output, sems.at[0]),
        pltpu.make_async_copy(home_grad, gradient, sems.at[1]),
    ]
    for copy in copies:
        copy.start()
    mh = mamba_gate.shape[1] // TP
    fh = gate.shape[1] // TP
    qh = query.shape[1] // TP
    kvh = key.shape[1]
    at = 2 * mh + qh
    out = mixer.shape[2] - mh - qh
    for m in range(TP):
        def cols(size):
            return slice(m * size, (m + 1) * size)

        gate[:, cols(fh)] = ff[m, :, :fh].astype(f32)
        up[:, cols(fh)] = ff[m, :, fh : 2 * fh].astype(f32)
        down[cols(fh), :] = ff[m, :, 2 * fh :].astype(f32).T
        mamba_gate[:, cols(mh)] = mixer[m, :, :mh].astype(f32)
        mamba_input[:, cols(mh)] = mixer[m, :, mh : 2 * mh].astype(f32)
        query[:, cols(qh)] = mixer[m, :, 2 * mh : at].astype(f32)
        mamba_out[cols(mh), :] = mixer[m, :, out : out + mh].astype(f32).T
        attn_out[cols(qh), :] = mixer[m, :, out + mh :].astype(f32).T
    key[...] = kv[:, :kvh]
    value[...] = kv[:, kvh:]

    mine = [mixer[m, :, at : at + 128].astype(f32) for m in range(TP)]
    other = [misc[m].astype(f32) for m in range(TP)]
    by_col = [
        [jnp.where(c == col, mine[m], other[m]) for m in range(TP)] for col in range(2)
    ]
    state[...] = jnp.concatenate(
        [
            by_col[col][m][:, part * sh : (part + 1) * sh]
            for part in range(2)
            for col in range(2)
            for m in range(TP)
        ],
        axis=1,
    )
    step[...] = jnp.concatenate([part[:, 2 * sh : 2 * sh + ph] for part in mine], axis=1)

    lanes = mh // 128
    channels = [
        jnp.concatenate(
            [
                small[2 * m + c, i * lanes + k : i * lanes + k + 1, :]
                for m in range(TP)
                for k in range(lanes)
            ],
            axis=1,
        )
        for i in range(6)
    ]
    for i in range(4):
        conv_k[i : i + 1, :] = channels[i]
    conv_b[...] = channels[4]
    per_head = mh // ph
    shape = (TP * mh, TP * ph)
    heads = lax.broadcasted_iota(jnp.int32, shape, 1) * per_head
    channel = lax.broadcasted_iota(jnp.int32, shape, 0)
    picks = ((channel >= heads) & (channel < heads + per_head)).astype(f32)
    skip[...] = dot(jnp.broadcast_to(channels[5], (8, TP * mh)), picks, 1, 0, HIGH)[:1, :]
    start = 8 * lanes
    sides = [[small[2 * m + col, start : start + 8, :] for m in range(TP)] for col in range(2)]
    states = jnp.concatenate(
        [
            sides[col][m][:, part * sh : (part + 1) * sh]
            for part in range(2)
            for col in range(2)
            for m in range(TP)
        ],
        axis=1,
    )
    state_k[...] = states[:4, :]
    state_b[...] = states[4:5, :]
    own_heads = jnp.concatenate(
        [jnp.where(c == 0, sides[0][m], sides[1][m])[:, 2 * sh : 2 * sh + ph] for m in range(TP)], axis=1
    )
    step_bias[...] = own_heads[5:6, :]
    decay[...] = own_heads[6:7, :]
    start = start + 8
    for gain in (ff_gain, mixer_gain):
        count = gain.shape[1] // 128
        total = sum(small[i, start : start + count, :] for i in range(GROUP))
        for k in range(count):
            gain[:, k * 128 : (k + 1) * 128] = total[k : k + 1, :]
        start = start + count
    for copy in copies:
        copy.wait()


def unpack(ff, mixer, misc, small, kv, output, gradient, mh, qh, fh, sh, ph):
    rows, width = ff.shape[1], output.shape[2]
    kvh = kv.shape[1] // 2
    vm, hb = pl.BlockSpec(memory_space=VMEM), pl.BlockSpec(memory_space=ANY)
    f32 = jnp.float32
    shapes = [
        (1, width),
        (rows, TP * mh),
        (rows, TP * mh),
        (rows, 2 * GROUP * sh),
        (rows, TP * ph),
        (4, TP * mh),
        (1, TP * mh),
        (4, 2 * GROUP * sh),
        (1, 2 * GROUP * sh),
        (1, TP * ph),
        (1, TP * ph),
        (1, TP * ph),
        (TP * mh, rows),
        (rows, TP * qh),
        (rows, kvh),
        (rows, kvh),
        (TP * qh, rows),
        (1, width),
        (rows, TP * fh),
        (rows, TP * fh),
        (TP * fh, rows),
    ]
    return pl.pallas_call(
        partial(unpack_kernel, sh, ph),
        name="unpack",
        out_shape=tuple(jax.ShapeDtypeStruct(a.shape, a.dtype) for a in (output, gradient))
        + tuple(jax.ShapeDtypeStruct(shape, f32) for shape in shapes),
        in_specs=[vm] * 5 + [hb] * 2,
        out_specs=(hb,) * 2 + (vm,) * len(shapes),
        scratch_shapes=[pltpu.SemaphoreType.DMA((2,))],
        compiler_params=pltpu.CompilerParams(vmem_limit_bytes=40 << 20),
        cost_estimate=cost(8),
    )(ff, mixer, misc, small, kv, output, gradient)


def send_home(parts, x, d_mid, ff_parts, mid, gain, take, small, kv_parts, ff_sums, n_row):
    slots, width = x.shape
    bf = jnp.bfloat16
    size = sum(part.size for part in small) // 128 + width // 128
    phases = len(data_bits(n_row, MIX))
    return pl.pallas_call(
        home_kernel,
        name="home",
        out_shape=(
            jax.ShapeDtypeStruct((n_row, CHUNK, width), bf),
            jax.ShapeDtypeStruct((GROUP, size, 128), jnp.float32),
            jax.ShapeDtypeStruct(kv_parts.shape[2:], jnp.float32),
            jax.ShapeDtypeStruct(ff_sums.shape, bf),
        ),
        in_specs=[pl.BlockSpec(memory_space=VMEM)] * 11 + [pl.BlockSpec(memory_space=ANY)],
        out_specs=(
            pl.BlockSpec(memory_space=VMEM),
            pl.BlockSpec(memory_space=ANY),
            pl.BlockSpec(memory_space=VMEM),
            pl.BlockSpec(memory_space=ANY),
        ),
        scratch_shapes=scatter_scratch(slots, width)
        + [
            VMEM((slots, width), jnp.float32),
            VMEM((slots, width), bf),
            VMEM((slots, width), bf),
            VMEM((1, width), jnp.float32),
            VMEM((phases + 1, size, 128), jnp.float32),
            VMEM((phases, size, 128), jnp.float32),
            pltpu.SemaphoreType.DMA((phases,)),
            pltpu.SemaphoreType.DMA((phases,)),
        ]
        + gather_scratch()
        + deliver_scratch()
        + [
            VMEM((TP, kv_parts.shape[0]) + kv_parts.shape[2:], bf),
            VMEM((kv_parts.shape[0],) + kv_parts.shape[2:], bf),
            VMEM((kv_parts.shape[0],) + kv_parts.shape[2:], bf),
            pltpu.SemaphoreType.DMA((TP,)),
            pltpu.SemaphoreType.DMA((TP,)),
            pltpu.SemaphoreType.DMA((kv_parts.shape[0],)),
            pltpu.SemaphoreType.DMA((kv_parts.shape[0],)),
            VMEM((slots, width), jnp.float32),
        ]
        + scatter_scratch(slots, width),
        compiler_params=params(3, 40),
        cost_estimate=cost(75),
    )(parts, x, d_mid, ff_parts, mid, gain, take, *small, kv_parts, ff_sums)


def blocks_start(low, land, s1, r1):
    r, c = place()
    copies = []
    for m, f in CROSSED:
        col = 1 - c if f else c
        k = m * 2 + f
        copies.append(
            remote(low.at[block_of(m, MIX) + col], land.at[k], s1.at[k], r1.at[k], partner(r, m, MIX), col)
        )
        copies[-1].start()
    return copies


def blocks_turn(first, low, land, mine, total, s2, r2, here):
    r, c = place()
    own = member(r, MIX) * 2 + c
    for copy in first:
        copy.wait_recv()
    summed = low[own].astype(jnp.float32)
    for m, f in CROSSED:
        summed = summed + land[m * 2 + f].astype(jnp.float32)
    mine[...] = summed.astype(jnp.bfloat16)
    copies = [pltpu.make_async_copy(mine, total.at[own], here)]
    for m, f in CROSSED:
        k = m * 2 + f
        copies.append(
            remote(mine, total.at[own], s2.at[k], r2.at[k], partner(r, m, MIX), 1 - c if f else c)
        )
    for copy in copies:
        copy.start()
    return copies


def blocks_finish(first, second):
    for copy in first:
        copy.wait_send()
    for copy in second:
        copy.wait()


CROSSED = [(m, f) for m in (3, 1, 2) for f in (0, 1)] + [(0, 1)]


def blocks_scratch(slots):
    dma = pltpu.SemaphoreType.DMA
    return [
        VMEM((GROUP, slots, slots), jnp.bfloat16),
        VMEM((GROUP, slots, slots), jnp.bfloat16),
        VMEM((slots, slots), jnp.bfloat16),
        dma((GROUP,)),
        dma((GROUP,)),
        dma((GROUP,)),
        dma((GROUP,)),
        dma,
    ]


def dot(first_op, second_op, first_dim, second_dim, precision=None):
    return lax.dot_general(
        first_op,
        second_op,
        (((first_dim,), (second_dim,)), ((), ())),
        precision=precision,
        preferred_element_type=jnp.float32,
    )


def block_rows(b, slots):
    return pl.ds(pl.multiple_of(b * slots, slots), slots)


def marks(lens, b, slots):
    row = lax.broadcasted_iota(jnp.int32, (slots, slots), 0)
    col = lax.broadcasted_iota(jnp.int32, (slots, slots), 1)
    row_segment, col_segment, within = jnp.zeros_like(row), jnp.zeros_like(row), row
    end = 0
    for k in range(lens.shape[1] - 1):
        end = end + lens[b, k]
        row_segment = row_segment + (row >= end).astype(jnp.int32)
        col_segment = col_segment + (col >= end).astype(jnp.int32)
        within = jnp.where(row >= end, row - end, within)
    return (row_segment == col_segment) & (row >= col), within


def conv_pre(values, within, weights):
    width = values.shape[1]
    shifted = [values]
    for k in range(1, 4):
        valid = within[:, :1] >= k
        shifted.append(jnp.where(valid, pltpu.roll(values, k, 0), 0.0))
    pre = weights[4:5, :]
    for k in range(4):
        pre = pre + weights[3 - k : 4 - k, :] * shifted[k]
    return pre, shifted


def conv_back(grad, pre, shifted, within, weights):
    slots = grad.shape[0]
    gate = jax.nn.sigmoid(pre)
    e = grad * gate * (1.0 + pre * (1.0 - gate))
    sums = [jnp.sum(e * shifted[3 - i], axis=0, keepdims=True) for i in range(4)]
    sums.append(jnp.sum(e, axis=0, keepdims=True))
    back = weights[3:4, :] * e
    for k in range(1, 4):
        valid = within[:, :1] >= k
        back = back + weights[3 - k : 4 - k, :] * pltpu.roll(jnp.where(valid, e, 0.0), slots - k, 0)
    return back, sums


def softplus(values):
    return jnp.maximum(values, 0.0) + jnp.log1p(jnp.exp(-jnp.abs(values)))


def steps_and_levels(mixed, side, low, count):
    slots, width = mixed.shape
    lane = lax.broadcasted_iota(jnp.int32, (slots, width), 1)
    inside = (lane >= low) & (lane < low + count)
    step = jnp.where(inside, softplus(mixed + side[5:6, :]), 0.0)
    rate = jnp.where(inside, -jnp.exp(side[6:7, :]), 0.0)
    row = lax.broadcasted_iota(jnp.int32, (slots, slots), 0)
    col = lax.broadcasted_iota(jnp.int32, (slots, slots), 1)
    tri = (row >= col).astype(jnp.float32)
    level = dot(tri, step * rate, 1, 0, HIGH)
    return step, rate, level, tri, inside


def halves(first, second):
    lane = lax.broadcasted_iota(jnp.int32, first.shape, 1)
    return jnp.where(lane < first.shape[1] // 2, first, second)


def state_parts(mixed, within, side, sh):
    pre, shifted = conv_pre(mixed, within, side)
    act = pre * jax.nn.sigmoid(pre)
    lane = lax.broadcasted_iota(jnp.int32, act.shape, 1)
    first = jnp.where(lane < sh, act, 0.0).astype(jnp.bfloat16)
    second = jnp.where(lane < sh, pltpu.roll(act, act.shape[1] - sh, 1), 0.0).astype(jnp.bfloat16)
    return first, second, pre, shifted


def turned_pair(values, waves):
    half = values.shape[1] // 2
    return values * waves[:, : 2 * half] + pltpu.roll(values, half, 1) * waves[:, 2 * half :]


def turned_back(values, waves):
    half = values.shape[1] // 2
    return values * waves[:, : 2 * half] - pltpu.roll(values, half, 1) * waves[:, 2 * half :]


def wave_rows(within, table):
    slots = within.shape[0]
    picks = (within == lax.broadcasted_iota(jnp.int32, (slots, slots), 1)).astype(jnp.float32)
    return dot(picks, table[...], 1, 0, HIGH)


def attend(projected, rows, at, lens, table, b, slots):
    allowed, within = marks(lens, b, slots)
    waves = wave_rows(within, table)
    query = turned_pair(projected[rows, at : at + HD], waves).astype(jnp.bfloat16)
    key = turned_pair(projected[rows, at + HD : at + 2 * HD], waves).astype(jnp.bfloat16)
    value = projected[rows, at + 2 * HD : at + 3 * HD].astype(jnp.bfloat16)
    scores = jnp.where(allowed, dot(query, key, 1, 1) * HD ** (-0.5), NEG_LARGE)
    exps = jnp.exp(scores - jnp.max(scores, axis=-1, keepdims=True))
    probs = exps / jnp.sum(exps, axis=-1, keepdims=True)
    return query, key, value, probs, waves


def each_block(first, last, body):
    def step(b, carry):
        body(b)
        return carry

    lax.fori_loop(first, last, step, 0)


def mixer_kernel(
    sh, ph, lens, projected, chan, side, table, branch, scanned, crossed,
    low, land, mine, s1, r1, s2, r2, here, conv,
):
    slots = crossed.shape[1]
    mh = chan.shape[1]
    heads_at = 2 * sh
    greet(MIX, cross=True)

    def before(b):
        rows = block_rows(b, slots)
        allowed, within = marks(lens, b, slots)
        pre, unused = conv_pre(projected[rows, mh : 2 * mh], within, chan)
        conv[rows, :] = pre * jax.nn.sigmoid(pre)
        mixed = projected[rows, 2 * mh + 3 * HD :]
        first, second, unused, unused = state_parts(mixed, within, side, sh)
        low[b] = dot(second, first, 1, 1).astype(jnp.bfloat16)

    def attention(b):
        rows = block_rows(b, slots)
        query, key, value, probs, waves = attend(projected, rows, 2 * mh, lens, table, b, slots)
        branch[rows, mh:] = dot(probs.astype(jnp.bfloat16), value, 1, 0).astype(jnp.bfloat16)

    def after(b):
        rows = block_rows(b, slots)
        allowed, within = marks(lens, b, slots)
        mixed = projected[rows, 2 * mh + 3 * HD :]
        step, rate, level, tri, inside = steps_and_levels(mixed, side, heads_at, ph)
        step_t, level_t = step.T, level.T
        cross = crossed[b].astype(jnp.float32)
        for pair in range(ph // 2):
            cols = slice(pair * 128, (pair + 1) * 128)
            convs = conv[rows, cols]
            conv_low = convs.astype(jnp.bfloat16)
            outs = []
            for h in (2 * pair, 2 * pair + 1):
                at = heads_at + h
                spread = level[:, at : at + 1] - level_t[at : at + 1, :]
                decay = jnp.exp(jnp.where(allowed, spread, NEG_LARGE))
                mixing = cross * decay * step_t[at : at + 1, :]
                outs.append(dot(mixing.astype(jnp.bfloat16), conv_low, 1, 0))
            total = halves(outs[0], outs[1])
            scanned[rows, cols] = total
            gate = projected[rows, cols]
            gated = (total + chan[5:6, cols] * convs) * (gate * jax.nn.sigmoid(gate))
            branch[rows, cols] = gated.astype(jnp.bfloat16)

    each_block(0, GROUP, before)
    first = blocks_start(low, land, s1, r1)
    each_block(0, GROUP // 2, attention)
    second = blocks_turn(first, low, land, mine, crossed, s2, r2, here)
    each_block(GROUP // 2, GROUP, attention)
    blocks_finish(first, second)
    each_block(0, GROUP, after)


def mixer(lens, projected, chan, side, table, sh, ph):
    tokens = projected.shape[0]
    slots = tokens // GROUP
    mh = chan.shape[1]
    vm = pl.BlockSpec(memory_space=VMEM)
    return pl.pallas_call(
        partial(mixer_kernel, sh, ph),
        name="mixer",
        out_shape=(
            jax.ShapeDtypeStruct((tokens, mh + HD), jnp.bfloat16),
            jax.ShapeDtypeStruct((tokens, mh), jnp.float32),
            jax.ShapeDtypeStruct((GROUP, slots, slots), jnp.bfloat16),
        ),
        in_specs=[pl.BlockSpec(memory_space=pltpu.SMEM)] + [vm] * 4,
        out_specs=(vm,) * 3,
        scratch_shapes=blocks_scratch(slots) + [VMEM((tokens, mh), jnp.float32)],
        compiler_params=params(4, 40),
        cost_estimate=cost(30),
    )(lens, projected, chan, side, table)


def mixer_back_kernel(
    sh, ph, lens, projected, chan, side, table, scanned, crossed, grads,
    out, chan_sums, side_sums,
    low, land, mine, s1, r1, s2, r2, here, summed, misc,
):
    slots = crossed.shape[1]
    mh = chan.shape[1]
    heads_at = 2 * sh
    bf = jnp.bfloat16
    greet(MIX, cross=True)
    chan_sums[...] = jnp.zeros_like(chan_sums)
    side_sums[...] = jnp.zeros_like(side_sums)

    def scan(b):
        rows = block_rows(b, slots)
        allowed, within = marks(lens, b, slots)
        mixed = projected[rows, 2 * mh + 3 * HD :]
        step, rate, level, tri, inside = steps_and_levels(mixed, side, heads_at, ph)
        step_t, level_t = step.T, level.T
        cross = crossed[b].astype(jnp.float32)
        lane = lax.broadcasted_iota(jnp.int32, (slots, 128), 1)
        place_row = lax.broadcasted_iota(jnp.int32, (slots, slots), 0)
        grad_cross = jnp.zeros((slots, slots), jnp.float32)
        row_sums = jnp.zeros((slots, slots), jnp.float32)
        col_sums = jnp.zeros((slots, slots), jnp.float32)
        for pair in range(ph // 2):
            cols = slice(pair * 128, (pair + 1) * 128)
            weights = chan[:, cols]
            pre, shifted = conv_pre(
                projected[rows, mh + pair * 128 : mh + (pair + 1) * 128], within, weights
            )
            convs = pre * jax.nn.sigmoid(pre)
            conv_low = convs.astype(bf)
            gate = projected[rows, cols]
            sig = jax.nn.sigmoid(gate)
            grad = grads[rows, cols]
            skip = weights[5:6, :]
            grad_mix = grad * (gate * sig)
            out[rows, cols] = (
                grad * (scanned[rows, cols] + skip * convs) * (sig * (1.0 + gate * (1.0 - sig)))
            ).astype(bf)
            skip_sum = jnp.sum(grad_mix * convs, axis=0, keepdims=True)
            grad_low = grad_mix.astype(bf)
            backs = []
            for f in (0, 1):
                at = heads_at + 2 * pair + f
                mask = lane < 64 if f == 0 else lane >= 64
                spread = level[:, at : at + 1] - level_t[at : at + 1, :]
                decay = jnp.exp(jnp.where(allowed, spread, NEG_LARGE))
                step_row = step_t[at : at + 1, :]
                mixing = cross * decay * step_row
                backs.append(dot(mixing.astype(bf), grad_low, 0, 0))
                grad_mixing = dot(jnp.where(mask, grad_mix, 0.0).astype(bf), conv_low, 1, 1)
                weighted = grad_mixing * decay
                grad_cross = grad_cross + weighted * step_row
                weighted = weighted * cross
                col = jnp.sum(weighted, axis=0, keepdims=True)
                row = jnp.sum(weighted * step_row, axis=1, keepdims=True)
                row_sums = jnp.where(lane == at, row, row_sums)
                col_sums = jnp.where(place_row == at, col, col_sums)
            grad_conv = grad_mix * skip + halves(backs[0], backs[1])
            back, sums = conv_back(grad_conv, pre, shifted, within, weights)
            out[rows, mh + pair * 128 : mh + (pair + 1) * 128] = back.astype(bf)
            for i, part in enumerate(sums + [skip_sum]):
                chan_sums[i : i + 1, cols] += part
        low[b] = grad_cross.astype(bf)
        col_sums = col_sums.T
        grad_level = row_sums - step * col_sums
        grad_rate_step = dot(tri, grad_level, 0, 0, HIGH)
        grad_step = (col_sums + grad_rate_step * rate) * jax.nn.sigmoid(mixed + side[5:6, :])
        grad_step = jnp.where(inside, grad_step, 0.0)
        misc[rows, :] = grad_step
        side_sums[5:6, :] += jnp.sum(grad_step, axis=0, keepdims=True)
        side_sums[6:7, :] += jnp.sum(grad_rate_step * step, axis=0, keepdims=True) * rate[:1, :]

    def attention(b):
        rows = block_rows(b, slots)
        at = 2 * mh
        query, key, value, probs, waves = attend(projected, rows, at, lens, table, b, slots)
        grad = grads[rows, mh:].astype(bf)
        grad_probs = dot(grad, value, 1, 1)
        out[rows, at + 2 * HD : at + 3 * HD] = dot(probs.astype(bf), grad, 0, 0).astype(bf)
        grad_raw = probs * (grad_probs - jnp.sum(grad_probs * probs, axis=-1, keepdims=True))
        grad_raw = (grad_raw * HD ** (-0.5)).astype(bf)
        out[rows, at : at + HD] = turned_back(dot(grad_raw, key, 1, 0), waves).astype(bf)
        out[rows, at + HD : at + 2 * HD] = turned_back(dot(grad_raw, query, 0, 0), waves).astype(bf)

    def state(b):
        rows = block_rows(b, slots)
        allowed, within = marks(lens, b, slots)
        mixed = projected[rows, 2 * mh + 3 * HD :]
        first, second, pre, shifted = state_parts(mixed, within, side, sh)
        lane = lax.broadcasted_iota(jnp.int32, pre.shape, 1)
        grad_first = dot(summed[b], second, 0, 0)
        grad_second = pltpu.roll(dot(summed[b], first, 1, 0), sh, 1)
        grad = jnp.where(lane < sh, grad_first, jnp.where(lane < 2 * sh, grad_second, 0.0))
        back, sums = conv_back(grad, pre, shifted, within, side)
        out[rows, 2 * mh + 3 * HD :] = jnp.where(lane < 2 * sh, back, misc[rows, :]).astype(bf)
        for i, part in enumerate(sums):
            side_sums[i : i + 1, :] += part

    each_block(0, GROUP, scan)
    begun = blocks_start(low, land, s1, r1)
    each_block(0, GROUP // 2, attention)
    done = blocks_turn(begun, low, land, mine, summed, s2, r2, here)
    each_block(GROUP // 2, GROUP, attention)
    blocks_finish(begun, done)
    each_block(0, GROUP, state)


def mixer_back(lens, projected, chan, side, table, scanned, crossed, grads, sh, ph):
    tokens = projected.shape[0]
    slots = tokens // GROUP
    mh = chan.shape[1]
    vm = pl.BlockSpec(memory_space=VMEM)
    return pl.pallas_call(
        partial(mixer_back_kernel, sh, ph),
        name="mixer_back",
        out_shape=(
            jax.ShapeDtypeStruct(projected.shape, jnp.bfloat16),
            jax.ShapeDtypeStruct(chan.shape, jnp.float32),
            jax.ShapeDtypeStruct(side.shape, jnp.float32),
        ),
        in_specs=[pl.BlockSpec(memory_space=pltpu.SMEM)] + [vm] * 7,
        out_specs=(vm,) * 3,
        scratch_shapes=blocks_scratch(slots)
        + [
            VMEM((GROUP, slots, slots), jnp.bfloat16),
            VMEM((tokens, 128), jnp.float32),
        ],
        compiler_params=params(5, 48),
        cost_estimate=cost(50),
    )(lens, projected, chan, side, table, scanned, crossed, grads)


def swiglu(ff_gate, ff_up):
    return jax.nn.silu(ff_gate) * ff_up


def cut(array, parts, axis=1):
    rows, cols = array.shape
    return array.reshape(rows, parts, cols // parts).transpose(1, 0, 2)


def local(
    tokens,
    cotangent,
    deal_order,
    seq_lengths,
    mixer_norm_gain,
    mamba_gate_weight,
    mamba_input_weight,
    state_weight,
    step_weight,
    conv_input,
    conv_input_bias,
    conv_state,
    conv_state_bias,
    step_bias,
    decay_log,
    skip_scale,
    mamba_out_weight,
    query_weight,
    key_weight,
    value_weight,
    attn_out_weight,
    ff_norm_gain,
    gate_weight,
    up_weight,
    down_weight,
):
    n_row = lax.axis_size("row")
    r = lax.axis_index("row")
    c = lax.axis_index("col")
    t = member(r, MIX)
    n_bits = n_row.bit_length() - 1
    slots, width = tokens.shape[1:]
    bf = jnp.bfloat16
    rows = mamba_gate_weight.shape[0]
    mh = mamba_gate_weight.shape[1] // TP
    qh = query_weight.shape[1] // TP
    kvh = key_weight.shape[1]
    sh = state_weight.shape[1] // (2 * GROUP)
    ph = step_weight.shape[1] // TP
    fh = gate_weight.shape[1] // TP
    used = 2 * mh + qh + 2 * kvh + 2 * sh + ph
    spare = -used % 256

    half = state_weight.shape[1] // 2
    def assemble(slab, after):
        held = [(0, slab)]
        for b in data_bits(n_row, FFN):
            next_held = []
            for mask, part in held:
                if mask:
                    part, unused_value = lax.optimization_barrier((part, after))
                next_held.append((mask | 1 << b, lax.ppermute(part, "row", flips(n_row, 1 << b))))
            held = held + next_held
        return place_slabs(
            [mask for mask, part in held], [part for mask, part in held], n_row
        ).reshape(n_row * rows, slab.shape[2])

    def pick(array, index, axis=0):
        return lax.dynamic_index_in_dim(array, index, axis, keepdims=False)

    def sum_groups(grad, axes, after=None):
        grad = grad.astype(bf)
        bits = data_bits(n_row, axes)
        order = [n_bits - 1 - b for b in bits + [axes[1], axes[0]]]
        if order != sorted(order):
            cutup = grad.reshape((2,) * n_bits + (rows, grad.shape[1]))
            grad = cutup.transpose(order + [n_bits, n_bits + 1]).reshape(grad.shape)
        if after is not None:
            grad, after = lax.optimization_barrier((grad, after))
        by_group = sorted(range(n_row), key=lambda row: [row >> b & 1 for b in bits])
        alike = [
            [row for row in by_group if [row >> b & 1 for b in axes] == [m & 1, m >> 1]]
            for m in range(TP)
        ]
        part = lax.psum_scatter(
            grad, "row", scatter_dimension=0, axis_index_groups=alike, tiled=True
        ).reshape(TP, rows, grad.shape[1])
        return part, after

    meta_all, give, take, x_home, gy_home, normed_one, gy_all, w_mixer, slab_up, slab_down = deal(
        deal_order,
        seq_lengths,
        tokens,
        cotangent,
        mixer_norm_gain[None, :],
        (key_weight, value_weight),
        (mamba_gate_weight, mamba_input_weight, query_weight),
        (state_weight, step_weight, mamba_out_weight, attn_out_weight),
        (gate_weight, up_weight, down_weight),
        2 * sh + ph + spare,
        n_row,
    )
    normed_one = normed_one.reshape(GROUP * slots, width)
    gy_all = gy_all.reshape(GROUP * slots, width)
    w_mixer = w_mixer.reshape(width, -1)
    w_in, w_out = w_mixer[:, : used + spare], w_mixer[:, used + spare :]

    base = r - sum(bit(r, b) * (1 << b) for b in MIX)
    group_meta = jnp.stack([pick(meta_all, base + mask_of(m, MIX)) for m in range(TP)])
    lengths = group_meta[:, 2:4, : seq_lengths.shape[2]].reshape(GROUP, seq_lengths.shape[2])
    half_dim = HD // 2
    inverse = ROPE_BASE ** (-2.0 * jnp.arange(half_dim, dtype=jnp.float32) / HD)
    angles = jnp.arange(slots, dtype=jnp.float32)[:, None] * inverse[None, :]
    cosine, sine = jnp.cos(angles), jnp.sin(angles)
    table = jnp.concatenate([cosine, cosine, -sine, sine], axis=1)

    def piece(array, size, start):
        return lax.dynamic_slice_in_dim(array, start, size, array.ndim - 1)

    eighth = c * TP + t
    chan = jnp.concatenate(
        [
            piece(conv_input, mh, t * mh),
            piece(conv_input_bias[None], mh, t * mh),
            jnp.repeat(piece(skip_scale[None], ph, t * ph), mh // ph, axis=1),
            jnp.zeros((2, mh), jnp.float32),
        ],
        axis=0,
    )
    states = jnp.concatenate([conv_state, conv_state_bias[None]], axis=0)
    states = jnp.concatenate(
        [piece(states, sh, eighth * sh), piece(states, sh, half + eighth * sh)], axis=1
    )
    heads = jnp.concatenate(
        [piece(step_bias[None], ph, t * ph), piece(decay_log[None], ph, t * ph)], axis=0
    )
    after = 128 - 2 * sh - ph
    side = jnp.concatenate(
        [
            jnp.pad(states, ((0, 0), (0, 128 - 2 * sh))),
            jnp.pad(heads, ((0, 0), (2 * sh, after))),
            jnp.zeros((1, 128), jnp.float32),
        ],
        axis=0,
    )

    projected = matmul(normed_one, w_in)
    edges = [0, mh, 2 * mh, 2 * mh + qh, 2 * mh + qh + kvh, 2 * mh + qh + 2 * kvh]
    edges = edges + [edges[-1] + 2 * sh, edges[-1] + 2 * sh + ph]
    branch_in, scanned, crossed = mixer(lengths, projected, chan, side, table, sh, ph)
    branch_part = matmul_trans(branch_in, w_out).astype(bf).reshape(GROUP, slots, width)
    ff_gain = ff_norm_gain[None, :]
    mid, normed_two, w_down = middle(branch_part, x_home, ff_gain, slab_down, n_row)
    normed_two = normed_two.reshape(GROUP * slots, width)
    w_gate_up = assemble(slab_up, branch_part)
    w_down = w_down.reshape(n_row * rows, -1)

    ff_gate_up = matmul(normed_two, w_gate_up)
    ff_gate, ff_up = ff_gate_up[:, :fh], ff_gate_up[:, fh:]
    ff_hidden = swiglu(ff_gate, ff_up).astype(bf)
    grad_hidden = matmul(gy_all, w_down)
    unused_value, pullback = jax.vjp(swiglu, ff_gate, ff_up)
    grad_gate, grad_up = pullback(grad_hidden)
    grad_gate_up = jnp.concatenate([grad_gate.astype(bf), grad_up.astype(bf)], axis=1)
    (grad_ff,) = products(
        [(normed_two, grad_gate_up), (gy_all, ff_hidden)], [(0, 0, 2 * fh), (1, 0, fh)]
    )
    grad_gate_up, grad_ff = lax.optimization_barrier((grad_gate_up, grad_ff))
    ff_sums, unused_value = sum_groups(grad_ff, FFN)
    normed_two_part = (
        matmul_trans(grad_gate_up, w_gate_up).astype(bf).reshape(GROUP, slots, width)
    )
    d_mid, delta_ff_gain, branch_all = turn(
        normed_two_part, mid, gy_home, ff_gain
    )
    branch_all = branch_all.reshape(GROUP * slots, width)

    grad_branch_in = matmul(branch_all, w_out)
    grad_projected, chan_sums, side_sums = mixer_back(
        lengths, projected, chan, side, table, scanned, crossed, grad_branch_in, sh, ph
    )
    grad_mixer, grad_kv = products(
        [(normed_one, grad_projected), (branch_all, branch_in)],
        [(0, 0, edges[3]), (0, edges[5], used + spare), (1, 0, mh + qh)],
        [(0, edges[3], edges[5])],
    )
    grad_projected, grad_mixer, ff_hidden = lax.optimization_barrier(
        (grad_projected, grad_mixer, ff_hidden)
    )
    ff_part = matmul_trans(ff_hidden, w_down).astype(bf).reshape(GROUP, slots, width)
    mixer_sums, ff_sums = sum_groups(grad_mixer, MIX, ff_sums)
    normed_one_part = matmul_trans(grad_projected, w_in).astype(bf).reshape(GROUP, slots, width)

    buf, small_all, delta_kv, ff_land = send_home(
        normed_one_part, x_home, d_mid, ff_part, mid, mixer_norm_gain[None, :], take,
        (chan_sums, side_sums, delta_ff_gain),
        grad_kv.reshape(n_row // TP, TP, rows, 2 * kvh), ff_sums, n_row,
    )
    output, grad_tokens, mixer_land, other_land = last(buf, give, mixer_sums, edges[3])
    results = unpack(
        ff_land, mixer_land, other_land, small_all, delta_kv, output, grad_tokens, mh, qh, fh, sh, ph
    )
    flat = (2, 8, 10, 11, 12, 13, 19)
    return tuple(
        array.reshape(array.shape[1]) if i in flat else array for i, array in enumerate(results)
    )


def solution(mesh):
    both = P("row", "col")
    turned = P("col", "row")
    in_specs = (
        P(None, "row", None),
        P(None, "row", None),
        P(None, "row"),
        P(None, "row", None),
        P(),
        both,
        both,
        P("row", None),
        both,
        P(None, "col"),
        P("col"),
        P(),
        P(),
        P("col"),
        P("col"),
        P("col"),
        turned,
        both,
        both,
        both,
        turned,
        P(),
        both,
        both,
        turned,
    )
    out_specs = (
        P(None, "row", None),
        P(None, "row", None),
        P(),
        both,
        both,
        P("row", None),
        both,
        P(None, "col"),
        P("col"),
        P(),
        P(),
        P("col"),
        P("col"),
        P("col"),
        turned,
        both,
        both,
        both,
        turned,
        P(),
        both,
        both,
        turned,
    )
    return jax.shard_map(local, mesh=mesh, in_specs=in_specs, out_specs=out_specs, check_vma=False)
```

```python
from functools import partial

import jax
import jax.numpy as jnp
from jax import lax
from jax.experimental import pallas as pl
from jax.experimental.pallas import tpu as pltpu
from jax.sharding import PartitionSpec as P

HD = 128
TP = 4
GROUP = 2 * TP
CHUNK = 16
EPS = 1e-05
NEG_LARGE = -1e30
ROPE_BASE = 100000000000.0
MESH = pl.DeviceIdType.MESH
HIGH = lax.Precision.HIGHEST
VMEM = pltpu.VMEM
ANY = pltpu.HBM


def matmul(first_op, second_op):
    return jnp.dot(first_op, second_op, preferred_element_type=jnp.float32)


def matmul_trans(first_op, second_op):
    return lax.dot_general(
        first_op, second_op, (((1,), (1,)), ((), ())), preferred_element_type=jnp.float32
    )


def matmul_left(first_op, second_op):
    return lax.dot_general(
        first_op, second_op, (((0,), (0,)), ((), ())), preferred_element_type=jnp.float32
    )


MIX, FFN = (0, 1), (0, 1)


def data_bits(n_row, axes):
    return [b for b in reversed(range(n_row.bit_length() - 1)) if b not in axes]


def bit(row, b):
    return lax.rem(lax.div(row, 1 << b), 2)


def flip(row, b):
    return row + (1 << b) * (1 - 2 * bit(row, b))


def member(row, axes):
    return bit(row, axes[0]) + 2 * bit(row, axes[1])


def partner(row, m, axes):
    if m & 1:
        row = flip(row, axes[0])
    if m & 2:
        row = flip(row, axes[1])
    return row


def turned_row(row, mask):
    for b in range(mask.bit_length()):
        row = flip(row, b) if mask >> b & 1 else row
    return row


def group_of(row, n_row, axes):
    index = 0
    for b in data_bits(n_row, axes):
        index = index * 2 + bit(row, b)
    return index


def flips(n_row, mask):
    return [(row, row ^ mask) for row in range(n_row)]


def mask_of(m, axes):
    return (m & 1) * (1 << axes[0]) + (m // 2) * (1 << axes[1])


def place():
    return lax.axis_index("row"), lax.axis_index("col")


def block_of(m, axes):
    return member(partner(lax.axis_index("row"), m, axes), axes) * 2


def plan_of(axes, slots):
    if axes != (0, 1) or slots % 32:
        return [(0, slots, 2, 1)]
    return [(0, slots // 2, 1, 2), (slots // 2, slots, 2, 1)]


def params(number, megabytes):
    return pltpu.CompilerParams(
        collective_id=number, has_side_effects=True, vmem_limit_bytes=megabytes << 20
    )


def cost(microseconds):
    return pl.CostEstimate(flops=0, transcendentals=0, bytes_accessed=microseconds * 3_400_000)


def remote(src, dst, send, recv, row, col):
    return pltpu.make_async_remote_copy(
        src_ref=src, dst_ref=dst, send_sem=send, recv_sem=recv, device_id=(row, col), device_id_type=MESH
    )


def greet(*groups, cross=False, beyond=()):
    r, c = place()
    barrier = pltpu.get_barrier_semaphore()
    others = [(r, 1 - c)]
    for axes in groups:
        for m in (1, 2, 3) if cross else (1, 2):
            others.append((partner(r, m, axes), c))
            if cross:
                others.append((partner(r, m, axes), 1 - c))
    others = others + [(flip(r, b), c) for b in beyond]
    for other in others:
        pl.semaphore_signal(barrier, inc=1, device_id=other, device_id_type=MESH)
    pl.semaphore_wait(barrier, len(others))


def gather_start(src, out, send, recv, here, axes):
    r, c = place()
    own = member(r, axes) * 2 + c
    copies = [
        pltpu.make_async_copy(src, out.at[own], here),
        remote(src, out.at[own], send.at[0], recv.at[0], r, 1 - c),
    ]
    for p, (low, high, near, far) in enumerate(plan_of(axes, src.shape[0])):
        for k, m in ((1, near), (2, far)):
            copies.append(
                remote(
                    src.at[low:high], out.at[own, low:high], send.at[6 * p + k], recv.at[6 * p + k],
                    partner(r, m, axes), c,
                )
            )
    for copy in copies[2:] + copies[:2]:
        copy.start()
    return copies


def gather_pass(steps, p, k, m, row, col, out, send, recv, axes):
    r, c = place()
    low, high = plan_of(axes, out.shape[1])[p][:2]
    part = out.at[block_of(m, axes) + c, low:high]
    steps.append(remote(part, part, send.at[6 * p + k], recv.at[6 * p + k], row, col))
    steps[-1].start()


def gather_turn(copies, out, send, recv, axes):
    r, c = place()
    steps = []
    for p, (low, high, near, far) in enumerate(plan_of(axes, out.shape[1])):
        copies[2 + 2 * p].wait_recv()
        gather_pass(steps, p, 3, near, partner(r, far, axes), c, out, send, recv, axes)
        gather_pass(steps, p, 4, near, r, 1 - c, out, send, recv, axes)
    return steps


def gather_finish(copies, steps, out, send, recv, axes):
    r, c = place()
    plan = plan_of(axes, out.shape[1])
    for p, (low, high, near, far) in enumerate(plan):
        copies[3 + 2 * p].wait_recv()
        gather_pass(steps, p, 5, far, r, 1 - c, out, send, recv, axes)
    for p in range(len(plan)):
        steps[2 * p].wait_recv()
        gather_pass(steps, p, 6, 3, r, 1 - c, out, send, recv, axes)
    copies[0].wait()
    copies[1].wait()
    for copy in copies[2:] + steps[: 2 * len(plan) : 2]:
        copy.wait_send()
    for i, copy in enumerate(steps):
        if i >= 2 * len(plan) or i % 2:
            copy.wait()


def gather(src, out, send, recv, here, axes):
    copies = gather_start(src, out, send, recv, here, axes)
    gather_finish(copies, gather_turn(copies, out, send, recv, axes), out, send, recv, axes)


ROWS = 16


def by_rows(count, body, first=0):
    def step(i, carry):
        body(pl.ds(pl.multiple_of(i * ROWS, ROWS), ROWS))
        return carry

    lax.fori_loop(first // ROWS, count // ROWS, step, 0)


def scatter_steps(parts, near, held, far, s1, r1, s2, r2, total, axes):
    r, c = place()
    slots = total.shape[0]
    plan = plan_of(axes, slots)
    pairs = {}
    for m in (3, 1, 2, 0):
        pairs[m] = remote(
            parts.at[block_of(m, axes) + 1 - c], near.at[m], s1.at[m], r1.at[m], r, 1 - c
        )
        pairs[m].start()
    sent = {}

    def pair_sum(m, i, low, high):
        block = block_of(m, axes) + c

        def add(rows):
            held[i, rows, :] = (
                parts[block, rows, :].astype(jnp.float32) + near[m, rows, :].astype(jnp.float32)
            ).astype(jnp.bfloat16)

        by_rows(high, add, low)

    def send(i, p, m):
        low, high = plan[p][:2]
        k = 3 * p + i
        sent[i, p] = remote(
            held.at[i, low:high], far.at[i, low:high], s2.at[k], r2.at[k], partner(r, m, axes), c
        )
        sent[i, p].start()

    yield
    pairs[3].wait_recv()
    for p, (low, high, first, then) in enumerate(plan):
        pair_sum(3, 1, low, high)
        send(1, p, then)
    for m in (1, 2):
        pairs[m].wait_recv()
        for p, (low, high, first, then) in enumerate(plan):
            pair_sum(m, 0 if m == then else 2, low, high)
            if m == then:
                send(0, p, then)
    yield
    for p, (low, high, first, then) in enumerate(plan):
        sent[1, p].wait_recv()

        def add(rows):
            held[2, rows, :] = (
                held[2, rows, :].astype(jnp.float32) + far[1, rows, :].astype(jnp.float32)
            ).astype(jnp.bfloat16)

        by_rows(high, add, low)
        send(2, p, first)
    yield
    pairs[0].wait_recv()
    for p in range(len(plan)):
        sent[0, p].wait_recv()
        sent[2, p].wait_recv()
    own = member(r, axes) * 2 + c

    def fold(rows):
        total[rows, :] = (
            parts[own, rows, :].astype(jnp.float32)
            + near[0, rows, :].astype(jnp.float32)
            + far[0, rows, :].astype(jnp.float32)
            + far[2, rows, :].astype(jnp.float32)
        )

    by_rows(slots, fold)
    for copy in list(pairs.values()) + list(sent.values()):
        copy.wait_send()
    yield


def scatter_sum(*args):
    for step in scatter_steps(*args):
        pass


def scatter_scratch(slots, width):
    return [
        VMEM((TP, slots, width), jnp.bfloat16),
        VMEM((TP - 1, slots, width), jnp.bfloat16),
        VMEM((TP - 1, slots, width), jnp.bfloat16),
        pltpu.SemaphoreType.DMA((TP,)),
        pltpu.SemaphoreType.DMA((TP,)),
        pltpu.SemaphoreType.DMA((6,)),
        pltpu.SemaphoreType.DMA((6,)),
    ]


def gather_scratch():
    return [
        pltpu.SemaphoreType.DMA((13,)),
        pltpu.SemaphoreType.DMA((13,)),
        pltpu.SemaphoreType.DMA,
    ]


def strip_views(refs, owner, piece):
    at = 0
    for ref in refs:
        count = ref.shape[1] // TP
        yield ref.at[:, pl.ds(pl.multiple_of(owner * count, 128), count)], piece.at[:, at : at + count]
        at += count


def cut_start(refs, piece, send, recv, here, axes):
    r, c = place()
    for source, target in strip_views(refs, member(r, axes), piece):
        pltpu.make_async_copy(source, target, here).start()
    for m in (3, 1, 2):
        other = partner(r, m, axes)
        for source, target in strip_views(refs, member(other, axes), piece):
            remote(source, target, send.at[m], recv.at[m], other, c).start()


def piece_done(piece, sem):
    pltpu.make_async_copy(piece, piece, sem).wait()


def weight_forward(masks, whole, cols, send, recv):
    r, c = place()
    n_row = lax.axis_size("row")
    bits = data_bits(n_row, MIX)
    copies = []
    for mask in masks:
        at = whole.at[turned_row(r, mask), :, cols]
        crossed = [k for k, b in enumerate(bits) if mask >> b & 1]
        if crossed:
            piece_done(at, recv.at[mask])
        for b in bits[max([-1] + crossed) + 1 :]:
            lands = mask | 1 << b
            copies.append(remote(at, at, send.at[lands], recv.at[lands], flip(r, b), c))
            copies[-1].start()
    return copies


def weight_rounds(n_row, held):
    rounds = []
    for b in data_bits(n_row, MIX):
        rounds.append([mask | 1 << b for mask in held])
        held = held + rounds[-1]
    return rounds


def spread(masks, whole, cols, send, recv):
    r, c = place()
    copies = []
    for mask in masks:
        at = whole.at[turned_row(r, mask), :, cols]
        for m in (3, 1, 2):
            lands = mask | mask_of(m, MIX)
            copies.append(remote(at, at, send.at[lands], recv.at[lands], partner(r, m, MIX), c))
            copies[-1].start()
    return copies


def place_kernel(masks, n_row, *refs):
    slabs, whole, sems = refs[: len(masks)], refs[-2], refs[-1]
    r, c = place()
    copies = []
    for i, mask in enumerate(masks):
        at = whole.at[group_of(turned_row(r, mask), n_row, FFN)]
        copies.append(pltpu.make_async_copy(slabs[i], at, sems.at[i]))
        copies[-1].start()
    for copy in copies:
        copy.wait()


def place_slabs(masks, slabs, n_row):
    return pl.pallas_call(
        partial(place_kernel, masks, n_row),
        name="place",
        out_shape=jax.ShapeDtypeStruct((len(masks),) + slabs[0].shape, slabs[0].dtype),
        in_specs=[pl.BlockSpec(memory_space=ANY)] * len(masks),
        out_specs=pl.BlockSpec(memory_space=ANY),
        scratch_shapes=[pltpu.SemaphoreType.DMA((len(masks),))],
        compiler_params=pltpu.CompilerParams(vmem_limit_bytes=4 << 20),
        cost_estimate=cost(4),
    )(*slabs)


def exchange_rows(buf, land, send, recv):
    r, c = place()
    n_row = lax.axis_size("row")

    def copy(other):
        return remote(
            buf.at[other], land.at[r], send.at[other], recv.at[r], other, c
        )

    def start(off, carry):
        copy(lax.rem(r + off, n_row)).start()
        return carry

    lax.fori_loop(1, n_row, start, 0)


def finish_rows(buf, land, send, recv):
    r, c = place()
    n_row = lax.axis_size("row")

    def finish(off, carry):
        other = lax.rem(r + off, n_row)
        copy = remote(buf.at[other], land.at[other], send.at[other], recv.at[other], other, c)
        copy.wait_send()
        copy.wait_recv()
        return carry

    lax.fori_loop(1, n_row, finish, 0)


def greet_rows(meanwhile=None):
    r, c = place()
    n_row = lax.axis_size("row")
    barrier = pltpu.get_barrier_semaphore()

    def greet(off, carry):
        pl.semaphore_signal(
            barrier, inc=1, device_id=(lax.rem(r + off, n_row), c), device_id_type=MESH
        )
        return carry

    lax.fori_loop(1, n_row, greet, 0)
    pl.semaphore_signal(barrier, inc=1, device_id=(r, 1 - c), device_id_type=MESH)
    if meanwhile is not None:
        meanwhile()
    pl.semaphore_wait(barrier, n_row)


COLS = 512


def permute_out(choice, buf, first, second, slots):
    n_row = buf.shape[0]

    def column(i, carry):
        cols = pl.ds(pl.multiple_of(i * COLS, COLS), COLS)
        picked = matmul(choice[:, :slots], first[:, cols]) + matmul(choice[:, slots:], second[:, cols])
        buf[:, :, cols] = picked.astype(jnp.bfloat16).reshape(n_row, CHUNK, COLS)
        return carry

    lax.fori_loop(0, buf.shape[2] // COLS, column, 0)


def permute_in(choice, land, first, second, slots, then=None):
    n_row = land.shape[0]

    def column(i, carry):
        cols = pl.ds(pl.multiple_of(i * COLS, COLS), COLS)
        got = land[:, :, cols].reshape(n_row * CHUNK, COLS)
        first[:, cols] = matmul_left(choice[:, :slots], got).astype(jnp.bfloat16)
        second[:, cols] = matmul_left(choice[:, slots:], got).astype(jnp.bfloat16)
        if then is not None:
            then(i, cols)
        return carry

    lax.fori_loop(0, land.shape[2] // COLS, column, 0)


def deal_kernel(
    order, lengths, tokens, cotangent, gain, *refs
):
    kv_refs, first_refs, refs = refs[:2], refs[2:5], refs[5:]
    states, steps_in, mamba_out, attn_out, refs = *refs[:4], refs[4:]
    up_refs, down, refs = refs[:2], refs[2], refs[3:]
    meta_all, give, take, x_out, gy_out, normed_all, gy_all, whole, slab_up, slab_down = refs[:10]
    x_mine, g_mine, buf, land, normed = refs[10:15]
    load, msend, mrecv, csend, crecv, nsend, nrecv, nhere, gsend, grecv, ghere = refs[15:26]
    wsend, wrecv, acut, arecv, ahere, bcut, brecv, bhere, usend, urecv, uhere, dsend, drecv, dhere, kv_here = refs[26:41]
    meta, mixed, mamba_turned, attn_turned, down_turned = refs[41:]
    second_refs, down_refs = (mixed, mamba_turned, attn_turned), (down_turned,)
    r, c = place()
    n_row = lax.axis_size("row")
    f = member(r, FFN)
    slots = x_mine.shape[0]
    per_peer = slots // n_row
    loads = [
        pltpu.make_async_copy(tokens.at[c], x_mine, load.at[0]),
        pltpu.make_async_copy(cotangent.at[c], g_mine, load.at[1]),
    ]
    for copy in loads:
        copy.start()
    bf = jnp.bfloat16

    def turn_weight(source, target):
        target[...] = source[...].astype(jnp.float32).T.astype(bf)

    def prepare():
        count = lengths.shape[2]
        meta[...] = jnp.zeros_like(meta)
        meta[0:2, :] = order[...]
        for i in range(2):
            meta[2 + i : 3 + i, 0:count] = lengths[i]
        part = states.shape[1] // 4
        values = states[...].astype(jnp.float32)
        first = jnp.where(c == 0, values[:, :part], values[:, part : 2 * part])
        second = jnp.where(c == 0, values[:, 2 * part : 3 * part], values[:, 3 * part :])
        step_values = steps_in[...].astype(jnp.float32)
        sh, ph = part // TP, step_values.shape[1] // TP
        width = mixed.shape[1] // TP
        for k in range(TP):
            cols = slice(k * sh, (k + 1) * sh)
            strip = [first[:, cols], second[:, cols], step_values[:, k * ph : (k + 1) * ph]]
            strip.append(jnp.zeros((values.shape[0], width - 2 * sh - ph), jnp.float32))
            mixed[:, k * width : (k + 1) * width] = jnp.concatenate(strip, axis=1).astype(bf)
        turn_weight(mamba_out, mamba_turned)
        turn_weight(attn_out, attn_turned)

    greet_rows(prepare)
    group = [mask_of(m, MIX) for m in range(TP)]
    first_cols = sum(ref.shape[1] for ref in first_refs) // TP
    kv_cols = first_cols + sum(ref.shape[1] for ref in kv_refs)
    cuts = (
        (slice(0, first_cols), first_refs, acut, arecv, ahere),
        (slice(kv_cols, whole.shape[2]), second_refs, bcut, brecv, bhere),
    )
    kv = slice(first_cols, kv_cols)

    def meta_copy(other, slot):
        return remote(meta, meta_all.at[slot], msend.at[other], mrecv.at[slot], other, c)

    def start(off, carry):
        meta_copy(lax.rem(r + off, n_row), r).start()
        return carry

    lax.fori_loop(1, n_row, start, 0)
    meta_all[r] = meta[...]
    at = first_cols
    for ref in kv_refs:
        pltpu.make_async_copy(ref, whole.at[r, :, at : at + ref.shape[1]], kv_here).start()
        at += ref.shape[1]
    for cols, refs_of, send, recv, here in cuts:
        cut_start(refs_of, whole.at[r, :, cols], send, recv, here, MIX)
    forwards = []
    for i, (cols, refs_of, send, recv, here) in enumerate(cuts):
        piece_done(whole.at[r, :, cols], here)
        forwards = forwards + weight_forward([0], whole, cols, wsend.at[i], wrecv.at[i])
    piece_done(whole.at[r, :, kv], kv_here)
    forwards = forwards + weight_forward([0], whole, kv, wsend.at[2], wrecv.at[2])

    def finish(off, carry):
        other = lax.rem(r + off, n_row)
        copy = meta_copy(other, other)
        copy.wait_send()
        copy.wait_recv()
        return carry

    lax.fori_loop(1, n_row, finish, 0)

    shift = slots.bit_length() - 1
    row_no = lax.broadcasted_iota(jnp.int32, (CHUNK, slots), 0)
    wanted = jnp.where(row_no < per_peer, row_no, row_no - per_peer).astype(jnp.float32)
    early = row_no < per_peer
    late = (row_no >= per_peer) & (row_no < 2 * per_peer)
    tri = (
        lax.broadcasted_iota(jnp.int32, (slots, slots), 0)
        < lax.broadcasted_iota(jnp.int32, (slots, slots), 1)
    ).astype(jnp.float32).astype(jnp.bfloat16)
    places = lax.broadcasted_iota(jnp.int32, (slots, slots), 0)

    def order_of(block):
        picked = jnp.where(c == 0, block[0:1, :], block[1:2, :])
        return lax.shift_right_logical(picked, shift), picked - lax.shift_left(
            lax.shift_right_logical(picked, shift), shift
        )

    own_source, own_local = order_of(meta[...])

    def select(mask):
        wide = jnp.broadcast_to(mask.astype(jnp.float32), (CHUNK, slots)).astype(jnp.bfloat16)
        rank = matmul(wide, tri)
        return jnp.where(
            (rank == wanted) & (wide.astype(jnp.float32) > 0.5), 1.0, 0.0
        )

    def build(d, carry):
        rows = pl.ds(pl.multiple_of(d * CHUNK, CHUNK), CHUNK)
        source, local = order_of(meta_all[d])
        chosen = select(source == r).astype(jnp.bfloat16)
        at_home = (places == local).astype(jnp.float32).astype(jnp.bfloat16)
        picks = matmul_trans(chosen, at_home)
        give[rows, :slots] = jnp.where(early, picks, 0.0).astype(jnp.bfloat16)
        give[rows, slots:] = jnp.where(late, picks, 0.0).astype(jnp.bfloat16)
        kept = select(own_source == d)
        take[rows, :slots] = jnp.where(early, kept, 0.0).astype(jnp.bfloat16)
        take[rows, slots:] = jnp.where(late, kept, 0.0).astype(jnp.bfloat16)
        return carry

    lax.fori_loop(0, n_row, build, 0)
    for copy in loads:
        copy.wait()
    permute_out(give, buf, x_mine, g_mine, slots)
    exchange_rows(buf, land, csend, crecv)
    land[r] = buf[r]
    for i, (cols, refs_of, send, recv, here) in enumerate(cuts):
        for m in (1, 2, 3):
            piece_done(whole.at[r, :, cols], recv.at[m])
            forwards = forwards + weight_forward([group[m]], whole, cols, wsend.at[i], wrecv.at[i])
    turn_weight(down, down_turned)
    finish_rows(buf, land, csend, crecv)
    permute_in(take, land, x_out, gy_out, slots)

    def norm(rows):
        values = x_out[rows, :].astype(jnp.float32)
        scale = lax.rsqrt(jnp.mean(values * values, axis=-1, keepdims=True) + EPS)
        normed[rows, :] = (values * scale * gain[...]).astype(jnp.bfloat16)

    by_rows(slots, norm)
    first = gather_start(normed, normed_all, nsend, nrecv, nhere, MIX)
    cut_start(up_refs, slab_up.at[f], usend, urecv, uhere, FFN)
    cut_start(down_refs, slab_down.at[f], dsend, drecv, dhere, FFN)
    second = gather_start(gy_out, gy_all, gsend, grecv, ghere, FFN)
    kv_rounds = weight_rounds(n_row, [0])
    steps = []
    for k, masks in enumerate(weight_rounds(n_row, group)):
        forwards = forwards + weight_forward(kv_rounds[k], whole, kv, wsend.at[2], wrecv.at[2])
        for i in (0, 1):
            forwards = forwards + weight_forward(masks, whole, cuts[i][0], wsend.at[i], wrecv.at[i])
            if k == 0 and i == 0:
                steps.append(gather_turn(first, normed_all, nsend, nrecv, MIX))
            if k == 0 and i == 1:
                steps.append(gather_turn(second, gy_all, gsend, grecv, FFN))
        if k == len(kv_rounds) - 1:
            kv_held = [0] + [mask for masks in kv_rounds for mask in masks]
            spreads = spread(kv_held, whole, kv, wsend.at[2], wrecv.at[2])
    gather_finish(first, steps[0], normed_all, nsend, nrecv, MIX)
    gather_finish(second, steps[1], gy_all, gsend, grecv, FFN)
    for copy in forwards:
        copy.wait_send()
    for cols, refs_of, send, recv, here in cuts:
        for m in (1, 2, 3):
            piece_done(whole.at[r, :, cols], send.at[m])
    for copy in spreads:
        copy.wait()
    for slab, send, recv, here in ((slab_up, usend, urecv, uhere), (slab_down, dsend, drecv, dhere)):
        piece_done(slab.at[f], here)
        for m in (1, 2, 3):
            piece_done(slab.at[f], send.at[m])
            piece_done(slab.at[f], recv.at[m])


def deal(order, lengths, tokens, cotangent, gain, kv, first, second, ff, strip, n_row):
    slots, width = tokens.shape[1:]
    bf = jnp.bfloat16
    rows = first[0].shape[0]
    states, steps_in, mamba_out, attn_out = second
    in_cols = sum(array.shape[1] for array in kv) + sum(array.shape[1] for array in first) // TP
    in_cols += strip + (mamba_out.shape[0] + attn_out.shape[0]) // TP
    up_cols, down_cols = 2 * ff[0].shape[1] // TP, ff[2].shape[0] // TP
    vm, hb = pl.BlockSpec(memory_space=VMEM), pl.BlockSpec(memory_space=ANY)
    dma = pltpu.SemaphoreType.DMA
    return pl.pallas_call(
        deal_kernel,
        name="deal",
        out_shape=(
            jax.ShapeDtypeStruct((n_row, 8, 128), jnp.int32),
            jax.ShapeDtypeStruct((n_row * CHUNK, 2 * slots), bf),
            jax.ShapeDtypeStruct((n_row * CHUNK, 2 * slots), bf),
            jax.ShapeDtypeStruct((slots, width), bf),
            jax.ShapeDtypeStruct((slots, width), bf),
            jax.ShapeDtypeStruct((GROUP, slots, width), bf),
            jax.ShapeDtypeStruct((GROUP, slots, width), bf),
            jax.ShapeDtypeStruct((n_row, rows, in_cols), bf),
            jax.ShapeDtypeStruct((TP, rows, up_cols), bf),
            jax.ShapeDtypeStruct((TP, rows, down_cols), bf),
        ),
        in_specs=[vm, vm, hb, hb, vm] + [vm] * 12,
        out_specs=(vm,) * 5 + (hb,) * 5,
        scratch_shapes=[
            VMEM((slots, width), bf),
            VMEM((slots, width), bf),
            VMEM((n_row, CHUNK, width), bf),
            VMEM((n_row, CHUNK, width), bf),
            VMEM((slots, width), bf),
            dma((2,)),
            dma((n_row,)),
            dma((n_row,)),
            dma((n_row,)),
            dma((n_row,)),
        ]
        + gather_scratch()
        + gather_scratch()
        + [dma((3, n_row)), dma((3, n_row))]
        + [dma((TP,)), dma((TP,)), dma] * 4
        + [dma]
        + [
            VMEM((8, 128), jnp.int32),
            VMEM((rows, TP * strip), bf),
            VMEM((rows, mamba_out.shape[0]), bf),
            VMEM((rows, attn_out.shape[0]), bf),
            VMEM((rows, ff[2].shape[0]), bf),
        ],
        compiler_params=params(0, 58),
        cost_estimate=cost(100),
    )(order, lengths, tokens, cotangent, gain, *kv, *first, *second, *ff)


def slab_copy(slab, whole, mask, b, send, recv):
    r, c = place()
    n_row = lax.axis_size("row")
    at = whole.at[group_of(turned_row(r, mask), n_row, FFN)]
    lands = mask | 1 << b
    k = group_index(lands, n_row)
    return remote(at if mask else slab, at, send.at[k], recv.at[k], flip(r, b), c)


def group_index(mask, n_row):
    return sum((mask >> b & 1) << i for i, b in enumerate(data_bits(n_row, FFN)))


def middle_kernel(
    parts, x, gain, slab, mid, normed_all, whole,
    near, out2, far, s1, r1, s2, r2, normed, nsend, nrecv, nhere, wsend, wrecv, where,
):
    r, c = place()
    n_row = lax.axis_size("row")
    bits = data_bits(n_row, FFN)
    greet(*{MIX, FFN}, beyond=bits)
    own = pltpu.make_async_copy(slab, whole.at[group_of(r, n_row, FFN)], where)
    own.start()
    copies = {1 << b: slab_copy(slab, whole, 0, b, wsend, wrecv) for b in bits}
    for copy in copies.values():
        copy.start()
    scatter_sum(parts, near, out2, far, s1, r1, s2, r2, mid, MIX)

    def norm(rows):
        values = x[rows, :].astype(jnp.float32) + mid[rows, :]
        mid[rows, :] = values
        scale = lax.rsqrt(jnp.mean(values * values, axis=-1, keepdims=True) + EPS)
        normed[rows, :] = (values * scale * gain[...]).astype(jnp.bfloat16)

    by_rows(mid.shape[0], norm)
    started = gather_start(normed, normed_all, nsend, nrecv, nhere, FFN)
    passed = gather_turn(started, normed_all, nsend, nrecv, FFN)
    for i, b in enumerate(bits):
        for mask in [mask for mask in copies if mask >> b & 1]:
            copies[mask].wait_recv()
            for later in bits[i + 1 :]:
                lands = mask | 1 << later
                copies[lands] = slab_copy(slab, whole, mask, later, wsend, wrecv)
                copies[lands].start()
    gather_finish(started, passed, normed_all, nsend, nrecv, FFN)
    own.wait()
    for copy in copies.values():
        copy.wait_send()


def middle(parts, x, gain, slab, n_row):
    slots, width = x.shape
    groups = n_row // TP
    vm, hb = pl.BlockSpec(memory_space=VMEM), pl.BlockSpec(memory_space=ANY)
    return pl.pallas_call(
        middle_kernel,
        name="middle",
        out_shape=(
            jax.ShapeDtypeStruct((slots, width), jnp.float32),
            jax.ShapeDtypeStruct((GROUP, slots, width), jnp.bfloat16),
            jax.ShapeDtypeStruct((groups,) + slab.shape, slab.dtype),
        ),
        in_specs=[vm] * 3 + [hb],
        out_specs=(vm, hb, hb),
        scratch_shapes=scatter_scratch(slots, width)
        + [VMEM((slots, width), jnp.bfloat16)]
        + gather_scratch()
        + [
            pltpu.SemaphoreType.DMA((groups,)),
            pltpu.SemaphoreType.DMA((groups,)),
            pltpu.SemaphoreType.DMA,
        ],
        compiler_params=params(1, 30),
        cost_estimate=cost(60),
    )(parts, x, gain, slab)


def norm_back(values, gain, grad):
    inverse = lax.rsqrt(jnp.mean(values * values, axis=-1, keepdims=True) + EPS)
    scaled = grad * gain
    back = inverse * scaled - values * (
        inverse * inverse * inverse * jnp.mean(values * scaled, axis=-1, keepdims=True)
    )
    return back, jnp.sum(grad * values * inverse, axis=0, keepdims=True)


def turn_kernel(
    parts, mid, gy, gain, d_mid, d_gain, branch_all,
    near, out2, far, s1, r1, s2, r2, branch, nsend, nrecv, nhere,
):
    greet(*{MIX, FFN})
    scatter_sum(parts, near, out2, far, s1, r1, s2, r2, d_mid, FFN)
    d_gain[...] = jnp.zeros_like(d_gain)

    def back(rows):
        values = mid[rows, :]
        grad, gain_part = norm_back(values, gain[...], d_mid[rows, :])
        grad = gy[rows, :].astype(jnp.float32) + grad
        d_mid[rows, :] = grad
        branch[rows, :] = grad.astype(jnp.bfloat16)
        d_gain[...] += gain_part

    by_rows(mid.shape[0], back)
    gather(branch, branch_all, nsend, nrecv, nhere, MIX)


def turn(parts, mid, gy, gain):
    slots, width = mid.shape
    return pl.pallas_call(
        turn_kernel,
        name="turn",
        out_shape=(
            jax.ShapeDtypeStruct((slots, width), jnp.float32),
            jax.ShapeDtypeStruct((1, width), jnp.float32),
            jax.ShapeDtypeStruct((GROUP, slots, width), jnp.bfloat16),
        ),
        in_specs=[pl.BlockSpec(memory_space=VMEM)] * 4,
        out_specs=(pl.BlockSpec(memory_space=VMEM),) * 2 + (pl.BlockSpec(memory_space=ANY),),
        scratch_shapes=scatter_scratch(slots, width)
        + [VMEM((slots, width), jnp.bfloat16)]
        + gather_scratch(),
        compiler_params=params(2, 30),
        cost_estimate=cost(60),
    )(parts, mid, gy, gain)


def home_kernel(
    parts, x, d_mid, ff_parts, mid, gain, take, chan_sums, side_sums, ff_gain_sums, kv_parts, ff_sums,
    buf, small_all, kv_sums, ff_land,
    near, out2, far, s1, r1, s2, r2, total, first, second, d_gain, stages, stage_land, tsend, trecv, gsend, grecv, ghere, *more
):
    r, c = place()
    slots, width = x.shape
    bits = data_bits(lax.axis_size("row"), MIX)
    greet_rows()
    kv_near, kv_held, kv_far, kv_s1, kv_r1, kv_s2, kv_r2 = more[3:10]
    ff_total = more[10]
    delivered = deliver(ff_sums, ff_land, *more[:3], FFN)
    steps = scatter_steps(parts, near, out2, far, s1, r1, s2, r2, total, MIX)
    ff_steps = scatter_steps(ff_parts, *more[11:], ff_total, FFN)
    for pair in zip(steps, ff_steps):
        pass
    d_gain[...] = jnp.zeros_like(d_gain)

    def back(rows):
        values = x[rows, :].astype(jnp.float32)
        grad, gain_part = norm_back(values, gain[...], total[rows, :])
        second[rows, :] = (d_mid[rows, :] + grad).astype(jnp.bfloat16)
        first[rows, :] = (ff_total[rows, :] + mid[rows, :]).astype(jnp.bfloat16)
        d_gain[...] += gain_part

    by_rows(slots, back)
    at = 0
    for sums in (chan_sums, side_sums, ff_gain_sums, d_gain):
        for i in range(sums.shape[0]):
            for k in range(sums.shape[1] // 128):
                stages[0, at : at + 1, :] = sums[i : i + 1, k * 128 : (k + 1) * 128]
                at += 1

    def stage_copy(i):
        return remote(
            stages.at[i], stage_land.at[i], tsend.at[i], trecv.at[i], flip(r, bits[i]), c
        )

    stage_copy(0).start()
    permute_out(take, buf, first, second, slots)
    own = member(r, MIX)
    groups = kv_parts.shape[0]
    kv_sent = []
    for m in (3, 1, 2):
        other = partner(r, m, MIX)
        kv_sent.append(
            remote(kv_parts.at[:, member(other, MIX)], kv_near.at[m], kv_s1.at[m], kv_r1.at[m], other, c)
        )
        kv_sent[-1].start()
    for i in range(len(bits)):
        stage_copy(i).wait()
        stages[i + 1] = stages[i] + stage_land[i]
        if i + 1 < len(bits):
            stage_copy(i + 1).start()
    started = gather_start(stages.at[len(bits)], small_all, gsend, grecv, ghere, MIX)
    for copy in kv_sent:
        copy.wait()
    passed = gather_turn(started, small_all, gsend, grecv, MIX)

    def kv_pair(g):
        kv_held[g] = (
            kv_parts[g, own].astype(jnp.float32)
            + kv_near[1, g].astype(jnp.float32)
            + kv_near[2, g].astype(jnp.float32)
            + kv_near[3, g].astype(jnp.float32)
        ).astype(jnp.bfloat16)

    each_block(0, groups, kv_pair)
    kv_far_sent = []
    for k in range(1, groups):
        other = turned_row(r, sum((1 << b) * (k >> i & 1) for i, b in enumerate(bits)))
        kv_far_sent.append(
            remote(
                kv_held.at[group_of(other, lax.axis_size("row"), MIX)],
                kv_far.at[k], kv_s2.at[k], kv_r2.at[k], other, c,
            )
        )
        kv_far_sent[-1].start()
    gather_finish(started, passed, small_all, gsend, grecv, MIX)
    for copy in kv_far_sent:
        copy.wait()
    kv_total = kv_held[group_of(r, lax.axis_size("row"), MIX)].astype(jnp.float32)
    for k in range(1, groups):
        kv_total = kv_total + kv_far[k].astype(jnp.float32)
    kv_sums[...] = kv_total
    for copy in delivered:
        copy.wait()


def deliver(sums, land, send, recv, here, axes):
    r, c = place()
    own = member(r, axes)
    copies = [pltpu.make_async_copy(sums.at[own], land.at[own], here)]
    for m in (3, 1, 2):
        other = partner(r, m, axes)
        copies.append(
            remote(sums.at[member(other, axes)], land.at[own], send.at[m], recv.at[m], other, c)
        )
    for copy in copies:
        copy.start()
    return copies


def deliver_scratch():
    dma = pltpu.SemaphoreType.DMA
    return [dma((TP,)), dma((TP,)), dma]


def last_kernel(
    at, buf, give, sums, output, gradient, sums_land, other,
    land, first, second, csend, crecv, here, osend, orecv, s1, r1, h1, send, recv,
):
    r, c = place()
    greet_rows()
    exchange_rows(buf, land, csend, crecv)
    delivered = deliver(sums, sums_land, s1, r1, h1, MIX)
    land[r] = buf[r]
    for copy in delivered:
        copy.wait()
    across = remote(sums_land.at[:, :, at : at + 128], other, send, recv, r, 1 - c)
    across.start()
    finish_rows(buf, land, csend, crecv)

    def home_copies(i, cols):
        copies = []
        for k, (mine, out) in enumerate(((first, output), (second, gradient))):
            source, target = mine.at[:, cols], out.at[c, :, cols]
            copies.append(pltpu.make_async_copy(source, target, here.at[k, i]))
            copies.append(remote(source, target, osend.at[k, i], orecv.at[k, i], r, 1 - c))
        return copies

    def send_column(i, cols):
        for copy in home_copies(i, cols):
            copy.start()

    permute_in(give, land, first, second, first.shape[0], send_column)

    def finish(i, carry):
        for copy in home_copies(i, pl.ds(pl.multiple_of(i * COLS, COLS), COLS)):
            copy.wait()
        return carry

    lax.fori_loop(0, first.shape[1] // COLS, finish, 0)
    across.wait()


def last(buf, give, sums, at):
    n_row, chunk, width = buf.shape
    slots = give.shape[1] // 2
    vm, hb = pl.BlockSpec(memory_space=VMEM), pl.BlockSpec(memory_space=ANY)
    dma = pltpu.SemaphoreType.DMA
    bf = jnp.bfloat16
    return pl.pallas_call(
        partial(last_kernel, at),
        name="last",
        out_shape=(
            jax.ShapeDtypeStruct((2, slots, width), bf),
            jax.ShapeDtypeStruct((2, slots, width), bf),
            jax.ShapeDtypeStruct(sums.shape, sums.dtype),
            jax.ShapeDtypeStruct(sums.shape[:2] + (128,), sums.dtype),
        ),
        in_specs=[vm, vm, hb],
        out_specs=(hb,) * 4,
        scratch_shapes=[
            VMEM(buf.shape, bf),
            VMEM((slots, width), bf),
            VMEM((slots, width), bf),
            dma((n_row,)),
            dma((n_row,)),
        ]
        + [dma((2, width // COLS))] * 3
        + deliver_scratch()
        + [dma, dma],
        compiler_params=params(6, 48),
        cost_estimate=cost(35),
    )(buf, give, sums)


def products_kernel(parts, *refs):
    pairs = len(refs) - len(parts)
    for part, out in zip(parts, refs[pairs:]):
        at = 0
        for i, low, high in part:
            left, right = refs[2 * i], refs[2 * i + 1]
            out[:, at : at + high - low] = dot(left[...], right[:, low:high], 0, 0).astype(out.dtype)
            at += high - low


def products(pairs, *parts):
    tokens, width = pairs[0][0].shape
    tile = min(512, width)
    specs = []
    for left, right in pairs:
        specs.append(pl.BlockSpec((tokens, tile), lambda i: (0, i)))
        specs.append(pl.BlockSpec(right.shape, lambda i: (0, 0)))
    totals = [sum(high - low for i, low, high in part) for part in parts]
    return pl.pallas_call(
        partial(products_kernel, parts),
        name="products",
        grid=(width // tile,),
        out_shape=tuple(jax.ShapeDtypeStruct((width, total), jnp.bfloat16) for total in totals),
        in_specs=specs,
        out_specs=tuple(pl.BlockSpec((tile, total), lambda i: (i, 0)) for total in totals),
        compiler_params=pltpu.CompilerParams(vmem_limit_bytes=40 << 20),
        cost_estimate=cost(10),
    )(*[array for pair in pairs for array in pair])


def unpack_kernel(
    sh, ph, ff, mixer, misc, small, kv, home_out, home_grad,
    output, gradient, mixer_gain, mamba_gate, mamba_input, state, step, conv_k, conv_b, state_k, state_b,
    step_bias, decay, skip, mamba_out, query, key, value, attn_out, ff_gain, gate, up, down, sems,
):
    c = lax.axis_index("col")
    f32 = jnp.float32
    copies = [
        pltpu.make_async_copy(home_out, output, sems.at[0]),
        pltpu.make_async_copy(home_grad, gradient, sems.at[1]),
    ]
    for copy in copies:
        copy.start()
    mh = mamba_gate.shape[1] // TP
    fh = gate.shape[1] // TP
    qh = query.shape[1] // TP
    kvh = key.shape[1]
    at = 2 * mh + qh
    out = mixer.shape[2] - mh - qh
    for m in range(TP):
        def cols(size):
            return slice(m * size, (m + 1) * size)

        gate[:, cols(fh)] = ff[m, :, :fh].astype(f32)
        up[:, cols(fh)] = ff[m, :, fh : 2 * fh].astype(f32)
        down[cols(fh), :] = ff[m, :, 2 * fh :].astype(f32).T
        mamba_gate[:, cols(mh)] = mixer[m, :, :mh].astype(f32)
        mamba_input[:, cols(mh)] = mixer[m, :, mh : 2 * mh].astype(f32)
        query[:, cols(qh)] = mixer[m, :, 2 * mh : at].astype(f32)
        mamba_out[cols(mh), :] = mixer[m, :, out : out + mh].astype(f32).T
        attn_out[cols(qh), :] = mixer[m, :, out + mh :].astype(f32).T
    key[...] = kv[:, :kvh]
    value[...] = kv[:, kvh:]

    mine = [mixer[m, :, at : at + 128].astype(f32) for m in range(TP)]
    other = [misc[m].astype(f32) for m in range(TP)]
    by_col = [
        [jnp.where(c == col, mine[m], other[m]) for m in range(TP)] for col in range(2)
    ]
    state[...] = jnp.concatenate(
        [
            by_col[col][m][:, part * sh : (part + 1) * sh]
            for part in range(2)
            for col in range(2)
            for m in range(TP)
        ],
        axis=1,
    )
    step[...] = jnp.concatenate([part[:, 2 * sh : 2 * sh + ph] for part in mine], axis=1)

    lanes = mh // 128
    channels = [
        jnp.concatenate(
            [
                small[2 * m + c, i * lanes + k : i * lanes + k + 1, :]
                for m in range(TP)
                for k in range(lanes)
            ],
            axis=1,
        )
        for i in range(6)
    ]
    for i in range(4):
        conv_k[i : i + 1, :] = channels[i]
    conv_b[...] = channels[4]
    per_head = mh // ph
    shape = (TP * mh, TP * ph)
    heads = lax.broadcasted_iota(jnp.int32, shape, 1) * per_head
    channel = lax.broadcasted_iota(jnp.int32, shape, 0)
    picks = ((channel >= heads) & (channel < heads + per_head)).astype(f32)
    skip[...] = dot(jnp.broadcast_to(channels[5], (8, TP * mh)), picks, 1, 0, HIGH)[:1, :]
    start = 8 * lanes
    sides = [[small[2 * m + col, start : start + 8, :] for m in range(TP)] for col in range(2)]
    states = jnp.concatenate(
        [
            sides[col][m][:, part * sh : (part + 1) * sh]
            for part in range(2)
            for col in range(2)
            for m in range(TP)
        ],
        axis=1,
    )
    state_k[...] = states[:4, :]
    state_b[...] = states[4:5, :]
    own_heads = jnp.concatenate(
        [jnp.where(c == 0, sides[0][m], sides[1][m])[:, 2 * sh : 2 * sh + ph] for m in range(TP)], axis=1
    )
    step_bias[...] = own_heads[5:6, :]
    decay[...] = own_heads[6:7, :]
    start = start + 8
    for gain in (ff_gain, mixer_gain):
        count = gain.shape[1] // 128
        total = sum(small[i, start : start + count, :] for i in range(GROUP))
        for k in range(count):
            gain[:, k * 128 : (k + 1) * 128] = total[k : k + 1, :]
        start = start + count
    for copy in copies:
        copy.wait()


def unpack(ff, mixer, misc, small, kv, output, gradient, mh, qh, fh, sh, ph):
    rows, width = ff.shape[1], output.shape[2]
    kvh = kv.shape[1] // 2
    vm, hb = pl.BlockSpec(memory_space=VMEM), pl.BlockSpec(memory_space=ANY)
    f32 = jnp.float32
    shapes = [
        (1, width),
        (rows, TP * mh),
        (rows, TP * mh),
        (rows, 2 * GROUP * sh),
        (rows, TP * ph),
        (4, TP * mh),
        (1, TP * mh),
        (4, 2 * GROUP * sh),
        (1, 2 * GROUP * sh),
        (1, TP * ph),
        (1, TP * ph),
        (1, TP * ph),
        (TP * mh, rows),
        (rows, TP * qh),
        (rows, kvh),
        (rows, kvh),
        (TP * qh, rows),
        (1, width),
        (rows, TP * fh),
        (rows, TP * fh),
        (TP * fh, rows),
    ]
    return pl.pallas_call(
        partial(unpack_kernel, sh, ph),
        name="unpack",
        out_shape=tuple(jax.ShapeDtypeStruct(a.shape, a.dtype) for a in (output, gradient))
        + tuple(jax.ShapeDtypeStruct(shape, f32) for shape in shapes),
        in_specs=[vm] * 5 + [hb] * 2,
        out_specs=(hb,) * 2 + (vm,) * len(shapes),
        scratch_shapes=[pltpu.SemaphoreType.DMA((2,))],
        compiler_params=pltpu.CompilerParams(vmem_limit_bytes=40 << 20),
        cost_estimate=cost(8),
    )(ff, mixer, misc, small, kv, output, gradient)


def send_home(parts, x, d_mid, ff_parts, mid, gain, take, small, kv_parts, ff_sums, n_row):
    slots, width = x.shape
    bf = jnp.bfloat16
    size = sum(part.size for part in small) // 128 + width // 128
    phases = len(data_bits(n_row, MIX))
    return pl.pallas_call(
        home_kernel,
        name="home",
        out_shape=(
            jax.ShapeDtypeStruct((n_row, CHUNK, width), bf),
            jax.ShapeDtypeStruct((GROUP, size, 128), jnp.float32),
            jax.ShapeDtypeStruct(kv_parts.shape[2:], jnp.float32),
            jax.ShapeDtypeStruct(ff_sums.shape, bf),
        ),
        in_specs=[pl.BlockSpec(memory_space=VMEM)] * 11 + [pl.BlockSpec(memory_space=ANY)],
        out_specs=(
            pl.BlockSpec(memory_space=VMEM),
            pl.BlockSpec(memory_space=ANY),
            pl.BlockSpec(memory_space=VMEM),
            pl.BlockSpec(memory_space=ANY),
        ),
        scratch_shapes=scatter_scratch(slots, width)
        + [
            VMEM((slots, width), jnp.float32),
            VMEM((slots, width), bf),
            VMEM((slots, width), bf),
            VMEM((1, width), jnp.float32),
            VMEM((phases + 1, size, 128), jnp.float32),
            VMEM((phases, size, 128), jnp.float32),
            pltpu.SemaphoreType.DMA((phases,)),
            pltpu.SemaphoreType.DMA((phases,)),
        ]
        + gather_scratch()
        + deliver_scratch()
        + [
            VMEM((TP, kv_parts.shape[0]) + kv_parts.shape[2:], bf),
            VMEM((kv_parts.shape[0],) + kv_parts.shape[2:], bf),
            VMEM((kv_parts.shape[0],) + kv_parts.shape[2:], bf),
            pltpu.SemaphoreType.DMA((TP,)),
            pltpu.SemaphoreType.DMA((TP,)),
            pltpu.SemaphoreType.DMA((kv_parts.shape[0],)),
            pltpu.SemaphoreType.DMA((kv_parts.shape[0],)),
            VMEM((slots, width), jnp.float32),
        ]
        + scatter_scratch(slots, width),
        compiler_params=params(3, 48),
        cost_estimate=cost(75),
    )(parts, x, d_mid, ff_parts, mid, gain, take, *small, kv_parts, ff_sums)


def blocks_start(low, land, s1, r1):
    r, c = place()
    copies = []
    for m, f in CROSSED:
        col = 1 - c if f else c
        k = m * 2 + f
        copies.append(
            remote(low.at[block_of(m, MIX) + col], land.at[k], s1.at[k], r1.at[k], partner(r, m, MIX), col)
        )
        copies[-1].start()
    return copies


def blocks_turn(first, low, land, mine, total, s2, r2, here):
    r, c = place()
    own = member(r, MIX) * 2 + c
    for copy in first:
        copy.wait_recv()
    summed = low[own].astype(jnp.float32)
    for m, f in CROSSED:
        summed = summed + land[m * 2 + f].astype(jnp.float32)
    mine[...] = summed.astype(jnp.bfloat16)
    copies = [pltpu.make_async_copy(mine, total.at[own], here)]
    for m, f in CROSSED:
        k = m * 2 + f
        copies.append(
            remote(mine, total.at[own], s2.at[k], r2.at[k], partner(r, m, MIX), 1 - c if f else c)
        )
    for copy in copies:
        copy.start()
    return copies


def blocks_finish(first, second):
    for copy in first:
        copy.wait_send()
    for copy in second:
        copy.wait()


CROSSED = [(m, f) for m in (3, 1, 2) for f in (0, 1)] + [(0, 1)]


def blocks_scratch(slots):
    dma = pltpu.SemaphoreType.DMA
    return [
        VMEM((GROUP, slots, slots), jnp.bfloat16),
        VMEM((GROUP, slots, slots), jnp.bfloat16),
        VMEM((slots, slots), jnp.bfloat16),
        dma((GROUP,)),
        dma((GROUP,)),
        dma((GROUP,)),
        dma((GROUP,)),
        dma,
    ]


def dot(first_op, second_op, first_dim, second_dim, precision=None):
    return lax.dot_general(
        first_op,
        second_op,
        (((first_dim,), (second_dim,)), ((), ())),
        precision=precision,
        preferred_element_type=jnp.float32,
    )


def block_rows(b, slots):
    return pl.ds(pl.multiple_of(b * slots, slots), slots)


def marks(lens, b, slots):
    row = lax.broadcasted_iota(jnp.int32, (slots, slots), 0)
    col = lax.broadcasted_iota(jnp.int32, (slots, slots), 1)
    row_segment, col_segment, within = jnp.zeros_like(row), jnp.zeros_like(row), row
    end = 0
    for k in range(lens.shape[1] - 1):
        end = end + lens[b, k]
        row_segment = row_segment + (row >= end).astype(jnp.int32)
        col_segment = col_segment + (col >= end).astype(jnp.int32)
        within = jnp.where(row >= end, row - end, within)
    return (row_segment == col_segment) & (row >= col), within


def conv_pre(values, within, weights):
    width = values.shape[1]
    shifted = [values]
    for k in range(1, 4):
        valid = within[:, :1] >= k
        shifted.append(jnp.where(valid, pltpu.roll(values, k, 0), 0.0))
    pre = weights[4:5, :]
    for k in range(4):
        pre = pre + weights[3 - k : 4 - k, :] * shifted[k]
    return pre, shifted


def conv_back(grad, pre, shifted, within, weights):
    slots = grad.shape[0]
    gate = jax.nn.sigmoid(pre)
    e = grad * gate * (1.0 + pre * (1.0 - gate))
    sums = [jnp.sum(e * shifted[3 - i], axis=0, keepdims=True) for i in range(4)]
    sums.append(jnp.sum(e, axis=0, keepdims=True))
    back = weights[3:4, :] * e
    for k in range(1, 4):
        valid = within[:, :1] >= k
        back = back + weights[3 - k : 4 - k, :] * pltpu.roll(jnp.where(valid, e, 0.0), slots - k, 0)
    return back, sums


def softplus(values):
    return jnp.maximum(values, 0.0) + jnp.log1p(jnp.exp(-jnp.abs(values)))


def steps_and_levels(mixed, side, low, count):
    slots, width = mixed.shape
    lane = lax.broadcasted_iota(jnp.int32, (slots, width), 1)
    inside = (lane >= low) & (lane < low + count)
    step = jnp.where(inside, softplus(mixed + side[5:6, :]), 0.0)
    rate = jnp.where(inside, -jnp.exp(side[6:7, :]), 0.0)
    row = lax.broadcasted_iota(jnp.int32, (slots, slots), 0)
    col = lax.broadcasted_iota(jnp.int32, (slots, slots), 1)
    tri = (row >= col).astype(jnp.float32)
    level = dot(tri, step * rate, 1, 0, HIGH)
    return step, rate, level, tri, inside


def halves(first, second):
    lane = lax.broadcasted_iota(jnp.int32, first.shape, 1)
    return jnp.where(lane < first.shape[1] // 2, first, second)


def state_parts(mixed, within, side, sh):
    pre, shifted = conv_pre(mixed, within, side)
    act = pre * jax.nn.sigmoid(pre)
    lane = lax.broadcasted_iota(jnp.int32, act.shape, 1)
    first = jnp.where(lane < sh, act, 0.0).astype(jnp.bfloat16)
    second = jnp.where(lane < sh, pltpu.roll(act, act.shape[1] - sh, 1), 0.0).astype(jnp.bfloat16)
    return first, second, pre, shifted


def turned_pair(values, waves):
    half = values.shape[1] // 2
    return values * waves[:, : 2 * half] + pltpu.roll(values, half, 1) * waves[:, 2 * half :]


def turned_back(values, waves):
    half = values.shape[1] // 2
    return values * waves[:, : 2 * half] - pltpu.roll(values, half, 1) * waves[:, 2 * half :]


def wave_rows(within, table):
    slots = within.shape[0]
    picks = (within == lax.broadcasted_iota(jnp.int32, (slots, slots), 1)).astype(jnp.float32)
    return dot(picks, table[...], 1, 0, HIGH)


def attend(projected, rows, at, lens, table, b, slots):
    allowed, within = marks(lens, b, slots)
    waves = wave_rows(within, table)
    query = turned_pair(projected[rows, at : at + HD], waves).astype(jnp.bfloat16)
    key = turned_pair(projected[rows, at + HD : at + 2 * HD], waves).astype(jnp.bfloat16)
    value = projected[rows, at + 2 * HD : at + 3 * HD].astype(jnp.bfloat16)
    scores = jnp.where(allowed, dot(query, key, 1, 1) * HD ** (-0.5), NEG_LARGE)
    exps = jnp.exp(scores - jnp.max(scores, axis=-1, keepdims=True))
    probs = exps / jnp.sum(exps, axis=-1, keepdims=True)
    return query, key, value, probs, waves


def each_block(first, last, body):
    def step(b, carry):
        body(b)
        return carry

    lax.fori_loop(first, last, step, 0)


def mixer_kernel(
    sh, ph, lens, projected, chan, side, table, branch, scanned, crossed,
    low, land, mine, s1, r1, s2, r2, here, conv,
):
    slots = crossed.shape[1]
    mh = chan.shape[1]
    heads_at = 2 * sh
    greet(MIX, cross=True)

    def before(b):
        rows = block_rows(b, slots)
        allowed, within = marks(lens, b, slots)
        pre, unused = conv_pre(projected[rows, mh : 2 * mh], within, chan)
        conv[rows, :] = pre * jax.nn.sigmoid(pre)
        mixed = projected[rows, 2 * mh + 3 * HD :]
        first, second, unused, unused = state_parts(mixed, within, side, sh)
        low[b] = dot(second, first, 1, 1).astype(jnp.bfloat16)

    def attention(b):
        rows = block_rows(b, slots)
        query, key, value, probs, waves = attend(projected, rows, 2 * mh, lens, table, b, slots)
        branch[rows, mh:] = dot(probs.astype(jnp.bfloat16), value, 1, 0).astype(jnp.bfloat16)

    def after(b):
        rows = block_rows(b, slots)
        allowed, within = marks(lens, b, slots)
        mixed = projected[rows, 2 * mh + 3 * HD :]
        step, rate, level, tri, inside = steps_and_levels(mixed, side, heads_at, ph)
        step_t, level_t = step.T, level.T
        cross = crossed[b].astype(jnp.float32)
        for pair in range(ph // 2):
            cols = slice(pair * 128, (pair + 1) * 128)
            convs = conv[rows, cols]
            conv_low = convs.astype(jnp.bfloat16)
            outs = []
            for h in (2 * pair, 2 * pair + 1):
                at = heads_at + h
                spread = level[:, at : at + 1] - level_t[at : at + 1, :]
                decay = jnp.exp(jnp.where(allowed, spread, NEG_LARGE))
                mixing = cross * decay * step_t[at : at + 1, :]
                outs.append(dot(mixing.astype(jnp.bfloat16), conv_low, 1, 0))
            total = halves(outs[0], outs[1])
            scanned[rows, cols] = total
            gate = projected[rows, cols]
            gated = (total + chan[5:6, cols] * convs) * (gate * jax.nn.sigmoid(gate))
            branch[rows, cols] = gated.astype(jnp.bfloat16)

    each_block(0, GROUP, before)
    first = blocks_start(low, land, s1, r1)
    each_block(0, GROUP // 2, attention)
    second = blocks_turn(first, low, land, mine, crossed, s2, r2, here)
    each_block(GROUP // 2, GROUP, attention)
    blocks_finish(first, second)
    each_block(0, GROUP, after)


def mixer(lens, projected, chan, side, table, sh, ph):
    tokens = projected.shape[0]
    slots = tokens // GROUP
    mh = chan.shape[1]
    vm = pl.BlockSpec(memory_space=VMEM)
    return pl.pallas_call(
        partial(mixer_kernel, sh, ph),
        name="mixer",
        out_shape=(
            jax.ShapeDtypeStruct((tokens, mh + HD), jnp.bfloat16),
            jax.ShapeDtypeStruct((tokens, mh), jnp.float32),
            jax.ShapeDtypeStruct((GROUP, slots, slots), jnp.bfloat16),
        ),
        in_specs=[pl.BlockSpec(memory_space=pltpu.SMEM)] + [vm] * 4,
        out_specs=(vm,) * 3,
        scratch_shapes=blocks_scratch(slots) + [VMEM((tokens, mh), jnp.float32)],
        compiler_params=params(4, 40),
        cost_estimate=cost(30),
    )(lens, projected, chan, side, table)


def mixer_back_kernel(
    sh, ph, lens, projected, chan, side, table, scanned, crossed, grads,
    out, chan_sums, side_sums,
    low, land, mine, s1, r1, s2, r2, here, summed, misc,
):
    slots = crossed.shape[1]
    mh = chan.shape[1]
    heads_at = 2 * sh
    bf = jnp.bfloat16
    greet(MIX, cross=True)
    chan_sums[...] = jnp.zeros_like(chan_sums)
    side_sums[...] = jnp.zeros_like(side_sums)

    def scan(b):
        rows = block_rows(b, slots)
        allowed, within = marks(lens, b, slots)
        mixed = projected[rows, 2 * mh + 3 * HD :]
        step, rate, level, tri, inside = steps_and_levels(mixed, side, heads_at, ph)
        step_t, level_t = step.T, level.T
        cross = crossed[b].astype(jnp.float32)
        lane = lax.broadcasted_iota(jnp.int32, (slots, 128), 1)
        place_row = lax.broadcasted_iota(jnp.int32, (slots, slots), 0)
        grad_cross = jnp.zeros((slots, slots), jnp.float32)
        row_sums = jnp.zeros((slots, slots), jnp.float32)
        col_sums = jnp.zeros((slots, slots), jnp.float32)
        for pair in range(ph // 2):
            cols = slice(pair * 128, (pair + 1) * 128)
            weights = chan[:, cols]
            pre, shifted = conv_pre(
                projected[rows, mh + pair * 128 : mh + (pair + 1) * 128], within, weights
            )
            convs = pre * jax.nn.sigmoid(pre)
            conv_low = convs.astype(bf)
            gate = projected[rows, cols]
            sig = jax.nn.sigmoid(gate)
            grad = grads[rows, cols]
            skip = weights[5:6, :]
            grad_mix = grad * (gate * sig)
            out[rows, cols] = (
                grad * (scanned[rows, cols] + skip * convs) * (sig * (1.0 + gate * (1.0 - sig)))
            ).astype(bf)
            skip_sum = jnp.sum(grad_mix * convs, axis=0, keepdims=True)
            grad_low = grad_mix.astype(bf)
            backs = []
            for f in (0, 1):
                at = heads_at + 2 * pair + f
                mask = lane < 64 if f == 0 else lane >= 64
                spread = level[:, at : at + 1] - level_t[at : at + 1, :]
                decay = jnp.exp(jnp.where(allowed, spread, NEG_LARGE))
                step_row = step_t[at : at + 1, :]
                mixing = cross * decay * step_row
                backs.append(dot(mixing.astype(bf), grad_low, 0, 0))
                grad_mixing = dot(jnp.where(mask, grad_mix, 0.0).astype(bf), conv_low, 1, 1)
                weighted = grad_mixing * decay
                grad_cross = grad_cross + weighted * step_row
                weighted = weighted * cross
                col = jnp.sum(weighted, axis=0, keepdims=True)
                row = jnp.sum(weighted * step_row, axis=1, keepdims=True)
                row_sums = jnp.where(lane == at, row, row_sums)
                col_sums = jnp.where(place_row == at, col, col_sums)
            grad_conv = grad_mix * skip + halves(backs[0], backs[1])
            back, sums = conv_back(grad_conv, pre, shifted, within, weights)
            out[rows, mh + pair * 128 : mh + (pair + 1) * 128] = back.astype(bf)
            for i, part in enumerate(sums + [skip_sum]):
                chan_sums[i : i + 1, cols] += part
        low[b] = grad_cross.astype(bf)
        col_sums = col_sums.T
        grad_level = row_sums - step * col_sums
        grad_rate_step = dot(tri, grad_level, 0, 0, HIGH)
        grad_step = (col_sums + grad_rate_step * rate) * jax.nn.sigmoid(mixed + side[5:6, :])
        grad_step = jnp.where(inside, grad_step, 0.0)
        misc[rows, :] = grad_step
        side_sums[5:6, :] += jnp.sum(grad_step, axis=0, keepdims=True)
        side_sums[6:7, :] += jnp.sum(grad_rate_step * step, axis=0, keepdims=True) * rate[:1, :]

    def attention(b):
        rows = block_rows(b, slots)
        at = 2 * mh
        query, key, value, probs, waves = attend(projected, rows, at, lens, table, b, slots)
        grad = grads[rows, mh:].astype(bf)
        grad_probs = dot(grad, value, 1, 1)
        out[rows, at + 2 * HD : at + 3 * HD] = dot(probs.astype(bf), grad, 0, 0).astype(bf)
        grad_raw = probs * (grad_probs - jnp.sum(grad_probs * probs, axis=-1, keepdims=True))
        grad_raw = (grad_raw * HD ** (-0.5)).astype(bf)
        out[rows, at : at + HD] = turned_back(dot(grad_raw, key, 1, 0), waves).astype(bf)
        out[rows, at + HD : at + 2 * HD] = turned_back(dot(grad_raw, query, 0, 0), waves).astype(bf)

    def state(b):
        rows = block_rows(b, slots)
        allowed, within = marks(lens, b, slots)
        mixed = projected[rows, 2 * mh + 3 * HD :]
        first, second, pre, shifted = state_parts(mixed, within, side, sh)
        lane = lax.broadcasted_iota(jnp.int32, pre.shape, 1)
        grad_first = dot(summed[b], second, 0, 0)
        grad_second = pltpu.roll(dot(summed[b], first, 1, 0), sh, 1)
        grad = jnp.where(lane < sh, grad_first, jnp.where(lane < 2 * sh, grad_second, 0.0))
        back, sums = conv_back(grad, pre, shifted, within, side)
        out[rows, 2 * mh + 3 * HD :] = jnp.where(lane < 2 * sh, back, misc[rows, :]).astype(bf)
        for i, part in enumerate(sums):
            side_sums[i : i + 1, :] += part

    each_block(0, GROUP, scan)
    begun = blocks_start(low, land, s1, r1)
    each_block(0, GROUP // 2, attention)
    done = blocks_turn(begun, low, land, mine, summed, s2, r2, here)
    each_block(GROUP // 2, GROUP, attention)
    blocks_finish(begun, done)
    each_block(0, GROUP, state)


def mixer_back(lens, projected, chan, side, table, scanned, crossed, grads, sh, ph):
    tokens = projected.shape[0]
    slots = tokens // GROUP
    mh = chan.shape[1]
    vm = pl.BlockSpec(memory_space=VMEM)
    return pl.pallas_call(
        partial(mixer_back_kernel, sh, ph),
        name="mixer_back",
        out_shape=(
            jax.ShapeDtypeStruct(projected.shape, jnp.bfloat16),
            jax.ShapeDtypeStruct(chan.shape, jnp.float32),
            jax.ShapeDtypeStruct(side.shape, jnp.float32),
        ),
        in_specs=[pl.BlockSpec(memory_space=pltpu.SMEM)] + [vm] * 7,
        out_specs=(vm,) * 3,
        scratch_shapes=blocks_scratch(slots)
        + [
            VMEM((GROUP, slots, slots), jnp.bfloat16),
            VMEM((tokens, 128), jnp.float32),
        ],
        compiler_params=params(5, 48),
        cost_estimate=cost(50),
    )(lens, projected, chan, side, table, scanned, crossed, grads)


def swiglu(ff_gate, ff_up):
    return jax.nn.silu(ff_gate) * ff_up


def cut(array, parts, axis=1):
    rows, cols = array.shape
    return array.reshape(rows, parts, cols // parts).transpose(1, 0, 2)


def local(
    tokens,
    cotangent,
    deal_order,
    seq_lengths,
    mixer_norm_gain,
    mamba_gate_weight,
    mamba_input_weight,
    state_weight,
    step_weight,
    conv_input,
    conv_input_bias,
    conv_state,
    conv_state_bias,
    step_bias,
    decay_log,
    skip_scale,
    mamba_out_weight,
    query_weight,
    key_weight,
    value_weight,
    attn_out_weight,
    ff_norm_gain,
    gate_weight,
    up_weight,
    down_weight,
):
    n_row = lax.axis_size("row")
    r = lax.axis_index("row")
    c = lax.axis_index("col")
    t = member(r, MIX)
    n_bits = n_row.bit_length() - 1
    slots, width = tokens.shape[1:]
    bf = jnp.bfloat16
    rows = mamba_gate_weight.shape[0]
    mh = mamba_gate_weight.shape[1] // TP
    qh = query_weight.shape[1] // TP
    kvh = key_weight.shape[1]
    sh = state_weight.shape[1] // (2 * GROUP)
    ph = step_weight.shape[1] // TP
    fh = gate_weight.shape[1] // TP
    used = 2 * mh + qh + 2 * kvh + 2 * sh + ph
    spare = -used % 256

    half = state_weight.shape[1] // 2
    def assemble(slab, after):
        held = [(0, slab)]
        for b in data_bits(n_row, FFN):
            next_held = []
            for mask, part in held:
                if mask:
                    part, unused_value = lax.optimization_barrier((part, after))
                next_held.append((mask | 1 << b, lax.ppermute(part, "row", flips(n_row, 1 << b))))
            held = held + next_held
        return place_slabs(
            [mask for mask, part in held], [part for mask, part in held], n_row
        ).reshape(n_row * rows, slab.shape[2])

    def pick(array, index, axis=0):
        return lax.dynamic_index_in_dim(array, index, axis, keepdims=False)

    def sum_groups(grad, axes, after=None):
        grad = grad.astype(bf)
        bits = data_bits(n_row, axes)
        order = [n_bits - 1 - b for b in bits + [axes[1], axes[0]]]
        if order != sorted(order):
            cutup = grad.reshape((2,) * n_bits + (rows, grad.shape[1]))
            grad = cutup.transpose(order + [n_bits, n_bits + 1]).reshape(grad.shape)
        if after is not None:
            grad, after = lax.optimization_barrier((grad, after))
        by_group = sorted(range(n_row), key=lambda row: [row >> b & 1 for b in bits])
        alike = [
            [row for row in by_group if [row >> b & 1 for b in axes] == [m & 1, m >> 1]]
            for m in range(TP)
        ]
        part = lax.psum_scatter(
            grad, "row", scatter_dimension=0, axis_index_groups=alike, tiled=True
        ).reshape(TP, rows, grad.shape[1])
        return part, after

    meta_all, give, take, x_home, gy_home, normed_one, gy_all, w_mixer, slab_up, slab_down = deal(
        deal_order,
        seq_lengths,
        tokens,
        cotangent,
        mixer_norm_gain[None, :],
        (key_weight, value_weight),
        (mamba_gate_weight, mamba_input_weight, query_weight),
        (state_weight, step_weight, mamba_out_weight, attn_out_weight),
        (gate_weight, up_weight, down_weight),
        2 * sh + ph + spare,
        n_row,
    )
    normed_one = normed_one.reshape(GROUP * slots, width)
    gy_all = gy_all.reshape(GROUP * slots, width)
    w_mixer = w_mixer.reshape(width, -1)
    w_in, w_out = w_mixer[:, : used + spare], w_mixer[:, used + spare :]

    base = r - sum(bit(r, b) * (1 << b) for b in MIX)
    group_meta = jnp.stack([pick(meta_all, base + mask_of(m, MIX)) for m in range(TP)])
    lengths = group_meta[:, 2:4, : seq_lengths.shape[2]].reshape(GROUP, seq_lengths.shape[2])
    half_dim = HD // 2
    inverse = ROPE_BASE ** (-2.0 * jnp.arange(half_dim, dtype=jnp.float32) / HD)
    angles = jnp.arange(slots, dtype=jnp.float32)[:, None] * inverse[None, :]
    cosine, sine = jnp.cos(angles), jnp.sin(angles)
    table = jnp.concatenate([cosine, cosine, -sine, sine], axis=1)

    def piece(array, size, start):
        return lax.dynamic_slice_in_dim(array, start, size, array.ndim - 1)

    eighth = c * TP + t
    chan = jnp.concatenate(
        [
            piece(conv_input, mh, t * mh),
            piece(conv_input_bias[None], mh, t * mh),
            jnp.repeat(piece(skip_scale[None], ph, t * ph), mh // ph, axis=1),
            jnp.zeros((2, mh), jnp.float32),
        ],
        axis=0,
    )
    states = jnp.concatenate([conv_state, conv_state_bias[None]], axis=0)
    states = jnp.concatenate(
        [piece(states, sh, eighth * sh), piece(states, sh, half + eighth * sh)], axis=1
    )
    heads = jnp.concatenate(
        [piece(step_bias[None], ph, t * ph), piece(decay_log[None], ph, t * ph)], axis=0
    )
    after = 128 - 2 * sh - ph
    side = jnp.concatenate(
        [
            jnp.pad(states, ((0, 0), (0, 128 - 2 * sh))),
            jnp.pad(heads, ((0, 0), (2 * sh, after))),
            jnp.zeros((1, 128), jnp.float32),
        ],
        axis=0,
    )

    projected = matmul(normed_one, w_in)
    edges = [0, mh, 2 * mh, 2 * mh + qh, 2 * mh + qh + kvh, 2 * mh + qh + 2 * kvh]
    edges = edges + [edges[-1] + 2 * sh, edges[-1] + 2 * sh + ph]
    branch_in, scanned, crossed = mixer(lengths, projected, chan, side, table, sh, ph)
    branch_part = matmul_trans(branch_in, w_out).astype(bf).reshape(GROUP, slots, width)
    ff_gain = ff_norm_gain[None, :]
    mid, normed_two, w_down = middle(branch_part, x_home, ff_gain, slab_down, n_row)
    normed_two = normed_two.reshape(GROUP * slots, width)
    w_gate_up = assemble(slab_up, branch_part)
    w_down = w_down.reshape(n_row * rows, -1)

    ff_gate_up = matmul(normed_two, w_gate_up)
    ff_gate, ff_up = ff_gate_up[:, :fh], ff_gate_up[:, fh:]
    ff_hidden = swiglu(ff_gate, ff_up).astype(bf)
    grad_hidden = matmul(gy_all, w_down)
    unused_value, pullback = jax.vjp(swiglu, ff_gate, ff_up)
    grad_gate, grad_up = pullback(grad_hidden)
    grad_gate_up = jnp.concatenate([grad_gate.astype(bf), grad_up.astype(bf)], axis=1)
    (grad_ff,) = products(
        [(normed_two, grad_gate_up), (gy_all, ff_hidden)], [(0, 0, 2 * fh), (1, 0, fh)]
    )
    grad_gate_up, grad_ff = lax.optimization_barrier((grad_gate_up, grad_ff))
    ff_sums, unused_value = sum_groups(grad_ff, FFN)
    normed_two_part = (
        matmul_trans(grad_gate_up, w_gate_up).astype(bf).reshape(GROUP, slots, width)
    )
    d_mid, delta_ff_gain, branch_all = turn(
        normed_two_part, mid, gy_home, ff_gain
    )
    branch_all = branch_all.reshape(GROUP * slots, width)

    grad_branch_in = matmul(branch_all, w_out)
    grad_projected, chan_sums, side_sums = mixer_back(
        lengths, projected, chan, side, table, scanned, crossed, grad_branch_in, sh, ph
    )
    grad_mixer, grad_kv = products(
        [(normed_one, grad_projected), (branch_all, branch_in)],
        [(0, 0, edges[3]), (0, edges[5], used + spare), (1, 0, mh + qh)],
        [(0, edges[3], edges[5])],
    )
    grad_projected, grad_mixer, ff_hidden = lax.optimization_barrier(
        (grad_projected, grad_mixer, ff_hidden)
    )
    ff_part = matmul_trans(ff_hidden, w_down).astype(bf).reshape(GROUP, slots, width)
    mixer_sums, unused_value = sum_groups(grad_mixer, MIX)
    normed_one_part = matmul_trans(grad_projected, w_in).astype(bf).reshape(GROUP, slots, width)

    buf, small_all, delta_kv, ff_land = send_home(
        normed_one_part, x_home, d_mid, ff_part, mid, mixer_norm_gain[None, :], take,
        (chan_sums, side_sums, delta_ff_gain),
        grad_kv.reshape(n_row // TP, TP, rows, 2 * kvh), ff_sums, n_row,
    )
    output, grad_tokens, mixer_land, other_land = last(buf, give, mixer_sums, edges[3])
    results = unpack(
        ff_land, mixer_land, other_land, small_all, delta_kv, output, grad_tokens, mh, qh, fh, sh, ph
    )
    flat = (2, 8, 10, 11, 12, 13, 19)
    return tuple(
        array.reshape(array.shape[1]) if i in flat else array for i, array in enumerate(results)
    )


def solution(mesh):
    both = P("row", "col")
    turned = P("col", "row")
    in_specs = (
        P(None, "row", None),
        P(None, "row", None),
        P(None, "row"),
        P(None, "row", None),
        P(),
        both,
        both,
        P("row", None),
        both,
        P(None, "col"),
        P("col"),
        P(),
        P(),
        P("col"),
        P("col"),
        P("col"),
        turned,
        both,
        both,
        both,
        turned,
        P(),
        both,
        both,
        turned,
    )
    out_specs = (
        P(None, "row", None),
        P(None, "row", None),
        P(),
        both,
        both,
        P("row", None),
        both,
        P(None, "col"),
        P("col"),
        P(),
        P(),
        P("col"),
        P("col"),
        P("col"),
        turned,
        both,
        both,
        both,
        turned,
        P(),
        both,
        both,
        turned,
    )
    return jax.shard_map(local, mesh=mesh, in_specs=in_specs, out_specs=out_specs, check_vma=False)
```

```python
from functools import partial

import jax
import jax.numpy as jnp
from jax import lax
from jax.experimental import pallas as pl
from jax.experimental.pallas import tpu as pltpu
from jax.sharding import PartitionSpec as P

HD = 128
TP = 4
GROUP = 2 * TP
CHUNK = 16
EPS = 1e-05
NEG_LARGE = -1e30
ROPE_BASE = 100000000000.0
MESH = pl.DeviceIdType.MESH
HIGH = lax.Precision.HIGHEST
VMEM = pltpu.VMEM
ANY = pltpu.HBM


def matmul(first_op, second_op):
    return jnp.dot(first_op, second_op, preferred_element_type=jnp.float32)


def matmul_trans(first_op, second_op):
    return lax.dot_general(
        first_op, second_op, (((1,), (1,)), ((), ())), preferred_element_type=jnp.float32
    )


def matmul_left(first_op, second_op):
    return lax.dot_general(
        first_op, second_op, (((0,), (0,)), ((), ())), preferred_element_type=jnp.float32
    )


MIX, FFN = (0, 1), (0, 1)


def data_bits(n_row, axes):
    return [b for b in reversed(range(n_row.bit_length() - 1)) if b not in axes]


def bit(row, b):
    return lax.rem(lax.div(row, 1 << b), 2)


def flip(row, b):
    return row + (1 << b) * (1 - 2 * bit(row, b))


def member(row, axes):
    return bit(row, axes[0]) + 2 * bit(row, axes[1])


def partner(row, m, axes):
    if m & 1:
        row = flip(row, axes[0])
    if m & 2:
        row = flip(row, axes[1])
    return row


def turned_row(row, mask):
    for b in range(mask.bit_length()):
        row = flip(row, b) if mask >> b & 1 else row
    return row


def group_of(row, n_row, axes):
    index = 0
    for b in data_bits(n_row, axes):
        index = index * 2 + bit(row, b)
    return index


def flips(n_row, mask):
    return [(row, row ^ mask) for row in range(n_row)]


def mask_of(m, axes):
    return (m & 1) * (1 << axes[0]) + (m // 2) * (1 << axes[1])


def place():
    return lax.axis_index("row"), lax.axis_index("col")


def block_of(m, axes):
    return member(partner(lax.axis_index("row"), m, axes), axes) * 2


def plan_of(axes, slots):
    if axes != (0, 1) or slots % 32:
        return [(0, slots, 2, 1)]
    return [(0, slots // 2, 1, 2), (slots // 2, slots, 2, 1)]


def params(number, megabytes):
    return pltpu.CompilerParams(
        collective_id=number, has_side_effects=True, vmem_limit_bytes=megabytes << 20
    )


def cost(microseconds):
    return pl.CostEstimate(flops=0, transcendentals=0, bytes_accessed=microseconds * 3_400_000)


def remote(src, dst, send, recv, row, col):
    return pltpu.make_async_remote_copy(
        src_ref=src, dst_ref=dst, send_sem=send, recv_sem=recv, device_id=(row, col), device_id_type=MESH
    )


def greet(*groups, cross=False, beyond=()):
    r, c = place()
    barrier = pltpu.get_barrier_semaphore()
    others = [(r, 1 - c)]
    for axes in groups:
        for m in (1, 2, 3) if cross else (1, 2):
            others.append((partner(r, m, axes), c))
            if cross:
                others.append((partner(r, m, axes), 1 - c))
    others = others + [(flip(r, b), c) for b in beyond]
    for other in others:
        pl.semaphore_signal(barrier, inc=1, device_id=other, device_id_type=MESH)
    pl.semaphore_wait(barrier, len(others))


def gather_start(src, out, send, recv, here, axes):
    r, c = place()
    own = member(r, axes) * 2 + c
    copies = [
        pltpu.make_async_copy(src, out.at[own], here),
        remote(src, out.at[own], send.at[0], recv.at[0], r, 1 - c),
    ]
    for p, (low, high, near, far) in enumerate(plan_of(axes, src.shape[0])):
        for k, m in ((1, near), (2, far)):
            copies.append(
                remote(
                    src.at[low:high], out.at[own, low:high], send.at[6 * p + k], recv.at[6 * p + k],
                    partner(r, m, axes), c,
                )
            )
    for copy in copies[2:] + copies[:2]:
        copy.start()
    return copies


def gather_pass(steps, p, k, m, row, col, out, send, recv, axes):
    r, c = place()
    low, high = plan_of(axes, out.shape[1])[p][:2]
    part = out.at[block_of(m, axes) + c, low:high]
    steps.append(remote(part, part, send.at[6 * p + k], recv.at[6 * p + k], row, col))
    steps[-1].start()


def gather_turn(copies, out, send, recv, axes):
    r, c = place()
    steps = []
    for p, (low, high, near, far) in enumerate(plan_of(axes, out.shape[1])):
        copies[2 + 2 * p].wait_recv()
        gather_pass(steps, p, 3, near, partner(r, far, axes), c, out, send, recv, axes)
        gather_pass(steps, p, 4, near, r, 1 - c, out, send, recv, axes)
    return steps


def gather_finish(copies, steps, out, send, recv, axes):
    r, c = place()
    plan = plan_of(axes, out.shape[1])
    for p, (low, high, near, far) in enumerate(plan):
        copies[3 + 2 * p].wait_recv()
        gather_pass(steps, p, 5, far, r, 1 - c, out, send, recv, axes)
    for p in range(len(plan)):
        steps[2 * p].wait_recv()
        gather_pass(steps, p, 6, 3, r, 1 - c, out, send, recv, axes)
    copies[0].wait()
    copies[1].wait()
    for copy in copies[2:] + steps[: 2 * len(plan) : 2]:
        copy.wait_send()
    for i, copy in enumerate(steps):
        if i >= 2 * len(plan) or i % 2:
            copy.wait()


def gather(src, out, send, recv, here, axes):
    copies = gather_start(src, out, send, recv, here, axes)
    gather_finish(copies, gather_turn(copies, out, send, recv, axes), out, send, recv, axes)


ROWS = 16


def by_rows(count, body, first=0):
    def step(i, carry):
        body(pl.ds(pl.multiple_of(i * ROWS, ROWS), ROWS))
        return carry

    lax.fori_loop(first // ROWS, count // ROWS, step, 0)


def scatter_steps(parts, near, held, far, s1, r1, s2, r2, total, axes):
    r, c = place()
    slots = total.shape[0]
    plan = plan_of(axes, slots)
    pairs = {}
    for m in (3, 1, 2, 0):
        pairs[m] = remote(
            parts.at[block_of(m, axes) + 1 - c], near.at[m], s1.at[m], r1.at[m], r, 1 - c
        )
        pairs[m].start()
    sent = {}

    def pair_sum(m, i, low, high):
        block = block_of(m, axes) + c

        def add(rows):
            held[i, rows, :] = (
                parts[block, rows, :].astype(jnp.float32) + near[m, rows, :].astype(jnp.float32)
            ).astype(jnp.bfloat16)

        by_rows(high, add, low)

    def send(i, p, m):
        low, high = plan[p][:2]
        k = 3 * p + i
        sent[i, p] = remote(
            held.at[i, low:high], far.at[i, low:high], s2.at[k], r2.at[k], partner(r, m, axes), c
        )
        sent[i, p].start()

    yield
    pairs[3].wait_recv()
    for p, (low, high, first, then) in enumerate(plan):
        pair_sum(3, 1, low, high)
        send(1, p, then)
    for m in (1, 2):
        pairs[m].wait_recv()
        for p, (low, high, first, then) in enumerate(plan):
            pair_sum(m, 0 if m == then else 2, low, high)
            if m == then:
                send(0, p, then)
    yield
    for p, (low, high, first, then) in enumerate(plan):
        sent[1, p].wait_recv()

        def add(rows):
            held[2, rows, :] = (
                held[2, rows, :].astype(jnp.float32) + far[1, rows, :].astype(jnp.float32)
            ).astype(jnp.bfloat16)

        by_rows(high, add, low)
        send(2, p, first)
    yield
    pairs[0].wait_recv()
    for p in range(len(plan)):
        sent[0, p].wait_recv()
        sent[2, p].wait_recv()
    own = member(r, axes) * 2 + c

    def fold(rows):
        total[rows, :] = (
            parts[own, rows, :].astype(jnp.float32)
            + near[0, rows, :].astype(jnp.float32)
            + far[0, rows, :].astype(jnp.float32)
            + far[2, rows, :].astype(jnp.float32)
        )

    by_rows(slots, fold)
    for copy in list(pairs.values()) + list(sent.values()):
        copy.wait_send()
    yield


def scatter_sum(*args):
    for step in scatter_steps(*args):
        pass


def scatter_scratch(slots, width):
    return [
        VMEM((TP, slots, width), jnp.bfloat16),
        VMEM((TP - 1, slots, width), jnp.bfloat16),
        VMEM((TP - 1, slots, width), jnp.bfloat16),
        pltpu.SemaphoreType.DMA((TP,)),
        pltpu.SemaphoreType.DMA((TP,)),
        pltpu.SemaphoreType.DMA((6,)),
        pltpu.SemaphoreType.DMA((6,)),
    ]


def gather_scratch():
    return [
        pltpu.SemaphoreType.DMA((13,)),
        pltpu.SemaphoreType.DMA((13,)),
        pltpu.SemaphoreType.DMA,
    ]


def strip_views(refs, owner, piece):
    at = 0
    for ref in refs:
        count = ref.shape[1] // TP
        yield ref.at[:, pl.ds(pl.multiple_of(owner * count, 128), count)], piece.at[:, at : at + count]
        at += count


def cut_start(refs, piece, send, recv, here, axes):
    r, c = place()
    for source, target in strip_views(refs, member(r, axes), piece):
        pltpu.make_async_copy(source, target, here).start()
    for m in (3, 1, 2):
        other = partner(r, m, axes)
        for source, target in strip_views(refs, member(other, axes), piece):
            remote(source, target, send.at[m], recv.at[m], other, c).start()


def piece_done(piece, sem):
    pltpu.make_async_copy(piece, piece, sem).wait()


def weight_forward(masks, whole, cols, send, recv):
    r, c = place()
    n_row = lax.axis_size("row")
    bits = data_bits(n_row, MIX)
    copies = []
    for mask in masks:
        at = whole.at[turned_row(r, mask), :, cols]
        crossed = [k for k, b in enumerate(bits) if mask >> b & 1]
        if crossed:
            piece_done(at, recv.at[mask])
        for b in bits[max([-1] + crossed) + 1 :]:
            lands = mask | 1 << b
            copies.append(remote(at, at, send.at[lands], recv.at[lands], flip(r, b), c))
            copies[-1].start()
    return copies


def weight_rounds(n_row, held):
    rounds = []
    for b in data_bits(n_row, MIX):
        rounds.append([mask | 1 << b for mask in held])
        held = held + rounds[-1]
    return rounds


def spread(masks, whole, cols, send, recv):
    r, c = place()
    copies = []
    for mask in masks:
        at = whole.at[turned_row(r, mask), :, cols]
        for m in (3, 1, 2):
            lands = mask | mask_of(m, MIX)
            copies.append(remote(at, at, send.at[lands], recv.at[lands], partner(r, m, MIX), c))
            copies[-1].start()
    return copies


def place_kernel(masks, n_row, *refs):
    slabs, whole, sems = refs[: len(masks)], refs[-2], refs[-1]
    r, c = place()
    copies = []
    for i, mask in enumerate(masks):
        at = whole.at[group_of(turned_row(r, mask), n_row, FFN)]
        copies.append(pltpu.make_async_copy(slabs[i], at, sems.at[i]))
        copies[-1].start()
    for copy in copies:
        copy.wait()


def place_slabs(masks, slabs, n_row):
    return pl.pallas_call(
        partial(place_kernel, masks, n_row),
        name="place",
        out_shape=jax.ShapeDtypeStruct((len(masks),) + slabs[0].shape, slabs[0].dtype),
        in_specs=[pl.BlockSpec(memory_space=ANY)] * len(masks),
        out_specs=pl.BlockSpec(memory_space=ANY),
        scratch_shapes=[pltpu.SemaphoreType.DMA((len(masks),))],
        compiler_params=pltpu.CompilerParams(vmem_limit_bytes=4 << 20),
        cost_estimate=cost(4),
    )(*slabs)


def exchange_rows(buf, land, send, recv):
    r, c = place()
    n_row = lax.axis_size("row")

    def copy(other):
        return remote(
            buf.at[other], land.at[r], send.at[other], recv.at[r], other, c
        )

    def start(off, carry):
        copy(lax.rem(r + off, n_row)).start()
        return carry

    lax.fori_loop(1, n_row, start, 0)


def finish_rows(buf, land, send, recv):
    r, c = place()
    n_row = lax.axis_size("row")

    def finish(off, carry):
        other = lax.rem(r + off, n_row)
        copy = remote(buf.at[other], land.at[other], send.at[other], recv.at[other], other, c)
        copy.wait_send()
        copy.wait_recv()
        return carry

    lax.fori_loop(1, n_row, finish, 0)


def greet_rows(meanwhile=None):
    r, c = place()
    n_row = lax.axis_size("row")
    barrier = pltpu.get_barrier_semaphore()

    def greet(off, carry):
        pl.semaphore_signal(
            barrier, inc=1, device_id=(lax.rem(r + off, n_row), c), device_id_type=MESH
        )
        return carry

    lax.fori_loop(1, n_row, greet, 0)
    pl.semaphore_signal(barrier, inc=1, device_id=(r, 1 - c), device_id_type=MESH)
    if meanwhile is not None:
        meanwhile()
    pl.semaphore_wait(barrier, n_row)


COLS = 512


def permute_out(choice, buf, first, second, slots):
    n_row = buf.shape[0]

    def column(i, carry):
        cols = pl.ds(pl.multiple_of(i * COLS, COLS), COLS)
        picked = matmul(choice[:, :slots], first[:, cols]) + matmul(choice[:, slots:], second[:, cols])
        buf[:, :, cols] = picked.astype(jnp.bfloat16).reshape(n_row, CHUNK, COLS)
        return carry

    lax.fori_loop(0, buf.shape[2] // COLS, column, 0)


def permute_in(choice, land, first, second, slots, then=None):
    n_row = land.shape[0]

    def column(i, carry):
        cols = pl.ds(pl.multiple_of(i * COLS, COLS), COLS)
        got = land[:, :, cols].reshape(n_row * CHUNK, COLS)
        first[:, cols] = matmul_left(choice[:, :slots], got).astype(jnp.bfloat16)
        second[:, cols] = matmul_left(choice[:, slots:], got).astype(jnp.bfloat16)
        if then is not None:
            then(i, cols)
        return carry

    lax.fori_loop(0, land.shape[2] // COLS, column, 0)


def deal_kernel(
    order, lengths, tokens, cotangent, gain, *refs
):
    kv_refs, first_refs, refs = refs[:2], refs[2:5], refs[5:]
    states, steps_in, mamba_out, attn_out, refs = *refs[:4], refs[4:]
    up_refs, down, refs = refs[:2], refs[2], refs[3:]
    meta_all, give, take, x_out, gy_out, normed_all, gy_all, whole, slab_up, slab_down = refs[:10]
    x_mine, g_mine, buf, land, normed = refs[10:15]
    load, msend, mrecv, csend, crecv, nsend, nrecv, nhere, gsend, grecv, ghere = refs[15:26]
    wsend, wrecv, acut, arecv, ahere, bcut, brecv, bhere, usend, urecv, uhere, dsend, drecv, dhere, kv_here = refs[26:41]
    meta, mixed, mamba_turned, attn_turned, down_turned = refs[41:]
    second_refs, down_refs = (mixed, mamba_turned, attn_turned), (down_turned,)
    r, c = place()
    n_row = lax.axis_size("row")
    f = member(r, FFN)
    slots = x_mine.shape[0]
    per_peer = slots // n_row
    loads = [
        pltpu.make_async_copy(tokens.at[c], x_mine, load.at[0]),
        pltpu.make_async_copy(cotangent.at[c], g_mine, load.at[1]),
    ]
    for copy in loads:
        copy.start()
    bf = jnp.bfloat16

    def turn_weight(source, target):
        target[...] = source[...].astype(jnp.float32).T.astype(bf)

    def prepare():
        count = lengths.shape[2]
        meta[...] = jnp.zeros_like(meta)
        meta[0:2, :] = order[...]
        for i in range(2):
            meta[2 + i : 3 + i, 0:count] = lengths[i]
        part = states.shape[1] // 4
        values = states[...].astype(jnp.float32)
        first = jnp.where(c == 0, values[:, :part], values[:, part : 2 * part])
        second = jnp.where(c == 0, values[:, 2 * part : 3 * part], values[:, 3 * part :])
        step_values = steps_in[...].astype(jnp.float32)
        sh, ph = part // TP, step_values.shape[1] // TP
        width = mixed.shape[1] // TP
        for k in range(TP):
            cols = slice(k * sh, (k + 1) * sh)
            strip = [first[:, cols], second[:, cols], step_values[:, k * ph : (k + 1) * ph]]
            strip.append(jnp.zeros((values.shape[0], width - 2 * sh - ph), jnp.float32))
            mixed[:, k * width : (k + 1) * width] = jnp.concatenate(strip, axis=1).astype(bf)
        turn_weight(mamba_out, mamba_turned)
        turn_weight(attn_out, attn_turned)

    greet_rows(prepare)
    group = [mask_of(m, MIX) for m in range(TP)]
    first_cols = sum(ref.shape[1] for ref in first_refs) // TP
    kv_cols = first_cols + sum(ref.shape[1] for ref in kv_refs)
    cuts = (
        (slice(0, first_cols), first_refs, acut, arecv, ahere),
        (slice(kv_cols, whole.shape[2]), second_refs, bcut, brecv, bhere),
    )
    kv = slice(first_cols, kv_cols)

    def meta_copy(other, slot):
        return remote(meta, meta_all.at[slot], msend.at[other], mrecv.at[slot], other, c)

    def start(off, carry):
        meta_copy(lax.rem(r + off, n_row), r).start()
        return carry

    lax.fori_loop(1, n_row, start, 0)
    meta_all[r] = meta[...]
    at = first_cols
    for ref in kv_refs:
        pltpu.make_async_copy(ref, whole.at[r, :, at : at + ref.shape[1]], kv_here).start()
        at += ref.shape[1]
    for cols, refs_of, send, recv, here in cuts:
        cut_start(refs_of, whole.at[r, :, cols], send, recv, here, MIX)
    forwards = []
    for i, (cols, refs_of, send, recv, here) in enumerate(cuts):
        piece_done(whole.at[r, :, cols], here)
        forwards = forwards + weight_forward([0], whole, cols, wsend.at[i], wrecv.at[i])
    piece_done(whole.at[r, :, kv], kv_here)
    forwards = forwards + weight_forward([0], whole, kv, wsend.at[2], wrecv.at[2])

    def finish(off, carry):
        other = lax.rem(r + off, n_row)
        copy = meta_copy(other, other)
        copy.wait_send()
        copy.wait_recv()
        return carry

    lax.fori_loop(1, n_row, finish, 0)

    shift = slots.bit_length() - 1
    row_no = lax.broadcasted_iota(jnp.int32, (CHUNK, slots), 0)
    wanted = jnp.where(row_no < per_peer, row_no, row_no - per_peer).astype(jnp.float32)
    early = row_no < per_peer
    late = (row_no >= per_peer) & (row_no < 2 * per_peer)
    tri = (
        lax.broadcasted_iota(jnp.int32, (slots, slots), 0)
        < lax.broadcasted_iota(jnp.int32, (slots, slots), 1)
    ).astype(jnp.float32).astype(jnp.bfloat16)
    places = lax.broadcasted_iota(jnp.int32, (slots, slots), 0)

    def order_of(block):
        picked = jnp.where(c == 0, block[0:1, :], block[1:2, :])
        return lax.shift_right_logical(picked, shift), picked - lax.shift_left(
            lax.shift_right_logical(picked, shift), shift
        )

    own_source, own_local = order_of(meta[...])

    def select(mask):
        wide = jnp.broadcast_to(mask.astype(jnp.float32), (CHUNK, slots)).astype(jnp.bfloat16)
        rank = matmul(wide, tri)
        return jnp.where(
            (rank == wanted) & (wide.astype(jnp.float32) > 0.5), 1.0, 0.0
        )

    def build(d, carry):
        rows = pl.ds(pl.multiple_of(d * CHUNK, CHUNK), CHUNK)
        source, local = order_of(meta_all[d])
        chosen = select(source == r).astype(jnp.bfloat16)
        at_home = (places == local).astype(jnp.float32).astype(jnp.bfloat16)
        picks = matmul_trans(chosen, at_home)
        give[rows, :slots] = jnp.where(early, picks, 0.0).astype(jnp.bfloat16)
        give[rows, slots:] = jnp.where(late, picks, 0.0).astype(jnp.bfloat16)
        kept = select(own_source == d)
        take[rows, :slots] = jnp.where(early, kept, 0.0).astype(jnp.bfloat16)
        take[rows, slots:] = jnp.where(late, kept, 0.0).astype(jnp.bfloat16)
        return carry

    lax.fori_loop(0, n_row, build, 0)
    for copy in loads:
        copy.wait()
    permute_out(give, buf, x_mine, g_mine, slots)
    exchange_rows(buf, land, csend, crecv)
    land[r] = buf[r]
    for i, (cols, refs_of, send, recv, here) in enumerate(cuts):
        for m in (1, 2, 3):
            piece_done(whole.at[r, :, cols], recv.at[m])
            forwards = forwards + weight_forward([group[m]], whole, cols, wsend.at[i], wrecv.at[i])
    turn_weight(down, down_turned)
    finish_rows(buf, land, csend, crecv)
    permute_in(take, land, x_out, gy_out, slots)

    def norm(rows):
        values = x_out[rows, :].astype(jnp.float32)
        scale = lax.rsqrt(jnp.mean(values * values, axis=-1, keepdims=True) + EPS)
        normed[rows, :] = (values * scale * gain[...]).astype(jnp.bfloat16)

    by_rows(slots, norm)
    first = gather_start(normed, normed_all, nsend, nrecv, nhere, MIX)
    cut_start(up_refs, slab_up.at[f], usend, urecv, uhere, FFN)
    cut_start(down_refs, slab_down.at[f], dsend, drecv, dhere, FFN)
    second = gather_start(gy_out, gy_all, gsend, grecv, ghere, FFN)
    kv_rounds = weight_rounds(n_row, [0])
    steps = []
    for k, masks in enumerate(weight_rounds(n_row, group)):
        forwards = forwards + weight_forward(kv_rounds[k], whole, kv, wsend.at[2], wrecv.at[2])
        for i in (0, 1):
            forwards = forwards + weight_forward(masks, whole, cuts[i][0], wsend.at[i], wrecv.at[i])
            if k == 0 and i == 0:
                steps.append(gather_turn(first, normed_all, nsend, nrecv, MIX))
            if k == 0 and i == 1:
                steps.append(gather_turn(second, gy_all, gsend, grecv, FFN))
        if k == len(kv_rounds) - 1:
            kv_held = [0] + [mask for masks in kv_rounds for mask in masks]
            spreads = spread(kv_held, whole, kv, wsend.at[2], wrecv.at[2])
    gather_finish(first, steps[0], normed_all, nsend, nrecv, MIX)
    gather_finish(second, steps[1], gy_all, gsend, grecv, FFN)
    for copy in forwards:
        copy.wait_send()
    for cols, refs_of, send, recv, here in cuts:
        for m in (1, 2, 3):
            piece_done(whole.at[r, :, cols], send.at[m])
    for copy in spreads:
        copy.wait()
    for slab, send, recv, here in ((slab_up, usend, urecv, uhere), (slab_down, dsend, drecv, dhere)):
        piece_done(slab.at[f], here)
        for m in (1, 2, 3):
            piece_done(slab.at[f], send.at[m])
            piece_done(slab.at[f], recv.at[m])


def deal(order, lengths, tokens, cotangent, gain, kv, first, second, ff, strip, n_row):
    slots, width = tokens.shape[1:]
    bf = jnp.bfloat16
    rows = first[0].shape[0]
    states, steps_in, mamba_out, attn_out = second
    in_cols = sum(array.shape[1] for array in kv) + sum(array.shape[1] for array in first) // TP
    in_cols += strip + (mamba_out.shape[0] + attn_out.shape[0]) // TP
    up_cols, down_cols = 2 * ff[0].shape[1] // TP, ff[2].shape[0] // TP
    vm, hb = pl.BlockSpec(memory_space=VMEM), pl.BlockSpec(memory_space=ANY)
    dma = pltpu.SemaphoreType.DMA
    return pl.pallas_call(
        deal_kernel,
        name="deal",
        out_shape=(
            jax.ShapeDtypeStruct((n_row, 8, 128), jnp.int32),
            jax.ShapeDtypeStruct((n_row * CHUNK, 2 * slots), bf),
            jax.ShapeDtypeStruct((n_row * CHUNK, 2 * slots), bf),
            jax.ShapeDtypeStruct((slots, width), bf),
            jax.ShapeDtypeStruct((slots, width), bf),
            jax.ShapeDtypeStruct((GROUP, slots, width), bf),
            jax.ShapeDtypeStruct((GROUP, slots, width), bf),
            jax.ShapeDtypeStruct((n_row, rows, in_cols), bf),
            jax.ShapeDtypeStruct((TP, rows, up_cols), bf),
            jax.ShapeDtypeStruct((TP, rows, down_cols), bf),
        ),
        in_specs=[vm, vm, hb, hb, vm] + [vm] * 12,
        out_specs=(vm,) * 5 + (hb,) * 5,
        scratch_shapes=[
            VMEM((slots, width), bf),
            VMEM((slots, width), bf),
            VMEM((n_row, CHUNK, width), bf),
            VMEM((n_row, CHUNK, width), bf),
            VMEM((slots, width), bf),
            dma((2,)),
            dma((n_row,)),
            dma((n_row,)),
            dma((n_row,)),
            dma((n_row,)),
        ]
        + gather_scratch()
        + gather_scratch()
        + [dma((3, n_row)), dma((3, n_row))]
        + [dma((TP,)), dma((TP,)), dma] * 4
        + [dma]
        + [
            VMEM((8, 128), jnp.int32),
            VMEM((rows, TP * strip), bf),
            VMEM((rows, mamba_out.shape[0]), bf),
            VMEM((rows, attn_out.shape[0]), bf),
            VMEM((rows, ff[2].shape[0]), bf),
        ],
        compiler_params=params(0, 58),
        cost_estimate=cost(100),
    )(order, lengths, tokens, cotangent, gain, *kv, *first, *second, *ff)


def slab_copy(slab, whole, mask, b, send, recv):
    r, c = place()
    n_row = lax.axis_size("row")
    at = whole.at[group_of(turned_row(r, mask), n_row, FFN)]
    lands = mask | 1 << b
    k = group_index(lands, n_row)
    return remote(at if mask else slab, at, send.at[k], recv.at[k], flip(r, b), c)


def group_index(mask, n_row):
    return sum((mask >> b & 1) << i for i, b in enumerate(data_bits(n_row, FFN)))


def middle_kernel(
    parts, x, gain, slab, mid, normed_all, whole,
    near, out2, far, s1, r1, s2, r2, normed, nsend, nrecv, nhere, wsend, wrecv, where,
):
    r, c = place()
    n_row = lax.axis_size("row")
    bits = data_bits(n_row, FFN)
    greet(*{MIX, FFN}, beyond=bits)
    own = pltpu.make_async_copy(slab, whole.at[group_of(r, n_row, FFN)], where)
    own.start()
    copies = {1 << b: slab_copy(slab, whole, 0, b, wsend, wrecv) for b in bits}
    for copy in copies.values():
        copy.start()
    scatter_sum(parts, near, out2, far, s1, r1, s2, r2, mid, MIX)

    def norm(rows):
        values = x[rows, :].astype(jnp.float32) + mid[rows, :]
        mid[rows, :] = values
        scale = lax.rsqrt(jnp.mean(values * values, axis=-1, keepdims=True) + EPS)
        normed[rows, :] = (values * scale * gain[...]).astype(jnp.bfloat16)

    by_rows(mid.shape[0], norm)
    started = gather_start(normed, normed_all, nsend, nrecv, nhere, FFN)
    passed = gather_turn(started, normed_all, nsend, nrecv, FFN)
    for i, b in enumerate(bits):
        for mask in [mask for mask in copies if mask >> b & 1]:
            copies[mask].wait_recv()
            for later in bits[i + 1 :]:
                lands = mask | 1 << later
                copies[lands] = slab_copy(slab, whole, mask, later, wsend, wrecv)
                copies[lands].start()
    gather_finish(started, passed, normed_all, nsend, nrecv, FFN)
    own.wait()
    for copy in copies.values():
        copy.wait_send()


def middle(parts, x, gain, slab, n_row):
    slots, width = x.shape
    groups = n_row // TP
    vm, hb = pl.BlockSpec(memory_space=VMEM), pl.BlockSpec(memory_space=ANY)
    return pl.pallas_call(
        middle_kernel,
        name="middle",
        out_shape=(
            jax.ShapeDtypeStruct((slots, width), jnp.float32),
            jax.ShapeDtypeStruct((GROUP, slots, width), jnp.bfloat16),
            jax.ShapeDtypeStruct((groups,) + slab.shape, slab.dtype),
        ),
        in_specs=[vm] * 3 + [hb],
        out_specs=(vm, hb, hb),
        scratch_shapes=scatter_scratch(slots, width)
        + [VMEM((slots, width), jnp.bfloat16)]
        + gather_scratch()
        + [
            pltpu.SemaphoreType.DMA((groups,)),
            pltpu.SemaphoreType.DMA((groups,)),
            pltpu.SemaphoreType.DMA,
        ],
        compiler_params=params(1, 30),
        cost_estimate=cost(60),
    )(parts, x, gain, slab)


def norm_back(values, gain, grad):
    inverse = lax.rsqrt(jnp.mean(values * values, axis=-1, keepdims=True) + EPS)
    scaled = grad * gain
    back = inverse * scaled - values * (
        inverse * inverse * inverse * jnp.mean(values * scaled, axis=-1, keepdims=True)
    )
    return back, jnp.sum(grad * values * inverse, axis=0, keepdims=True)


def turn_kernel(
    parts, mid, gy, gain, d_mid, d_gain, branch_all,
    near, out2, far, s1, r1, s2, r2, branch, nsend, nrecv, nhere,
):
    greet(*{MIX, FFN})
    scatter_sum(parts, near, out2, far, s1, r1, s2, r2, d_mid, FFN)
    d_gain[...] = jnp.zeros_like(d_gain)

    def back(rows):
        values = mid[rows, :]
        grad, gain_part = norm_back(values, gain[...], d_mid[rows, :])
        grad = gy[rows, :].astype(jnp.float32) + grad
        d_mid[rows, :] = grad
        branch[rows, :] = grad.astype(jnp.bfloat16)
        d_gain[...] += gain_part

    by_rows(mid.shape[0], back)
    gather(branch, branch_all, nsend, nrecv, nhere, MIX)


def turn(parts, mid, gy, gain):
    slots, width = mid.shape
    return pl.pallas_call(
        turn_kernel,
        name="turn",
        out_shape=(
            jax.ShapeDtypeStruct((slots, width), jnp.float32),
            jax.ShapeDtypeStruct((1, width), jnp.float32),
            jax.ShapeDtypeStruct((GROUP, slots, width), jnp.bfloat16),
        ),
        in_specs=[pl.BlockSpec(memory_space=VMEM)] * 4,
        out_specs=(pl.BlockSpec(memory_space=VMEM),) * 2 + (pl.BlockSpec(memory_space=ANY),),
        scratch_shapes=scatter_scratch(slots, width)
        + [VMEM((slots, width), jnp.bfloat16)]
        + gather_scratch(),
        compiler_params=params(2, 30),
        cost_estimate=cost(60),
    )(parts, mid, gy, gain)


def home_kernel(
    parts, x, d_mid, ff_parts, mid, gain, take, chan_sums, side_sums, ff_gain_sums, kv_parts, ff_sums,
    buf, small_all, kv_sums, ff_land,
    near, out2, far, s1, r1, s2, r2, total, first, second, d_gain, stages, stage_land, tsend, trecv, gsend, grecv, ghere, *more
):
    r, c = place()
    slots, width = x.shape
    bits = data_bits(lax.axis_size("row"), MIX)
    greet_rows()
    kv_near, kv_held, kv_far, kv_s1, kv_r1, kv_s2, kv_r2 = more[3:10]
    ff_total = more[10]
    delivered = deliver(ff_sums, ff_land, *more[:3], FFN)
    steps = scatter_steps(parts, near, out2, far, s1, r1, s2, r2, total, MIX)
    ff_steps = scatter_steps(ff_parts, *more[11:], ff_total, FFN)
    for pair in zip(steps, ff_steps):
        pass
    d_gain[...] = jnp.zeros_like(d_gain)

    def back(rows):
        values = x[rows, :].astype(jnp.float32)
        grad, gain_part = norm_back(values, gain[...], total[rows, :])
        second[rows, :] = (d_mid[rows, :] + grad).astype(jnp.bfloat16)
        first[rows, :] = (ff_total[rows, :] + mid[rows, :]).astype(jnp.bfloat16)
        d_gain[...] += gain_part

    by_rows(slots, back)
    at = 0
    for sums in (chan_sums, side_sums, ff_gain_sums, d_gain):
        for i in range(sums.shape[0]):
            for k in range(sums.shape[1] // 128):
                stages[0, at : at + 1, :] = sums[i : i + 1, k * 128 : (k + 1) * 128]
                at += 1

    def stage_copy(i):
        return remote(
            stages.at[i], stage_land.at[i], tsend.at[i], trecv.at[i], flip(r, bits[i]), c
        )

    stage_copy(0).start()
    permute_out(take, buf, first, second, slots)
    own = member(r, MIX)
    groups = kv_parts.shape[0]
    kv_sent = []
    for m in (3, 1, 2):
        other = partner(r, m, MIX)
        kv_sent.append(
            remote(kv_parts.at[:, member(other, MIX)], kv_near.at[m], kv_s1.at[m], kv_r1.at[m], other, c)
        )
        kv_sent[-1].start()
    for i in range(len(bits)):
        stage_copy(i).wait()
        stages[i + 1] = stages[i] + stage_land[i]
        if i + 1 < len(bits):
            stage_copy(i + 1).start()
    started = gather_start(stages.at[len(bits)], small_all, gsend, grecv, ghere, MIX)
    for copy in kv_sent:
        copy.wait()
    passed = gather_turn(started, small_all, gsend, grecv, MIX)

    def kv_pair(g):
        kv_held[g] = (
            kv_parts[g, own].astype(jnp.float32)
            + kv_near[1, g].astype(jnp.float32)
            + kv_near[2, g].astype(jnp.float32)
            + kv_near[3, g].astype(jnp.float32)
        ).astype(jnp.bfloat16)

    each_block(0, groups, kv_pair)
    kv_far_sent = []
    for k in range(1, groups):
        other = turned_row(r, sum((1 << b) * (k >> i & 1) for i, b in enumerate(bits)))
        kv_far_sent.append(
            remote(
                kv_held.at[group_of(other, lax.axis_size("row"), MIX)],
                kv_far.at[k], kv_s2.at[k], kv_r2.at[k], other, c,
            )
        )
        kv_far_sent[-1].start()
    gather_finish(started, passed, small_all, gsend, grecv, MIX)
    for copy in kv_far_sent:
        copy.wait()
    kv_total = kv_held[group_of(r, lax.axis_size("row"), MIX)].astype(jnp.float32)
    for k in range(1, groups):
        kv_total = kv_total + kv_far[k].astype(jnp.float32)
    kv_sums[...] = kv_total
    for copy in delivered:
        copy.wait()


def deliver(sums, land, send, recv, here, axes):
    r, c = place()
    own = member(r, axes)
    copies = [pltpu.make_async_copy(sums.at[own], land.at[own], here)]
    for m in (3, 1, 2):
        other = partner(r, m, axes)
        copies.append(
            remote(sums.at[member(other, axes)], land.at[own], send.at[m], recv.at[m], other, c)
        )
    for copy in copies:
        copy.start()
    return copies


def deliver_scratch():
    dma = pltpu.SemaphoreType.DMA
    return [dma((TP,)), dma((TP,)), dma]


def last_kernel(
    at, buf, give, sums, output, gradient, sums_land, other,
    land, first, second, csend, crecv, here, osend, orecv, s1, r1, h1, send, recv,
):
    r, c = place()
    greet_rows()
    exchange_rows(buf, land, csend, crecv)
    delivered = deliver(sums, sums_land, s1, r1, h1, MIX)
    land[r] = buf[r]
    for copy in delivered:
        copy.wait()
    across = remote(sums_land.at[:, :, at : at + 128], other, send, recv, r, 1 - c)
    across.start()
    finish_rows(buf, land, csend, crecv)

    def home_copies(i, cols):
        copies = []
        for k, (mine, out) in enumerate(((first, output), (second, gradient))):
            source, target = mine.at[:, cols], out.at[c, :, cols]
            copies.append(pltpu.make_async_copy(source, target, here.at[k, i]))
            copies.append(remote(source, target, osend.at[k, i], orecv.at[k, i], r, 1 - c))
        return copies

    def send_column(i, cols):
        for copy in home_copies(i, cols):
            copy.start()

    permute_in(give, land, first, second, first.shape[0], send_column)

    def finish(i, carry):
        for copy in home_copies(i, pl.ds(pl.multiple_of(i * COLS, COLS), COLS)):
            copy.wait()
        return carry

    lax.fori_loop(0, first.shape[1] // COLS, finish, 0)
    across.wait()


def last(buf, give, sums, at):
    n_row, chunk, width = buf.shape
    slots = give.shape[1] // 2
    vm, hb = pl.BlockSpec(memory_space=VMEM), pl.BlockSpec(memory_space=ANY)
    dma = pltpu.SemaphoreType.DMA
    bf = jnp.bfloat16
    return pl.pallas_call(
        partial(last_kernel, at),
        name="last",
        out_shape=(
            jax.ShapeDtypeStruct((2, slots, width), bf),
            jax.ShapeDtypeStruct((2, slots, width), bf),
            jax.ShapeDtypeStruct(sums.shape, sums.dtype),
            jax.ShapeDtypeStruct(sums.shape[:2] + (128,), sums.dtype),
        ),
        in_specs=[vm, vm, hb],
        out_specs=(hb,) * 4,
        scratch_shapes=[
            VMEM(buf.shape, bf),
            VMEM((slots, width), bf),
            VMEM((slots, width), bf),
            dma((n_row,)),
            dma((n_row,)),
        ]
        + [dma((2, width // COLS))] * 3
        + deliver_scratch()
        + [dma, dma],
        compiler_params=params(6, 48),
        cost_estimate=cost(35),
    )(buf, give, sums)


def products_kernel(parts, *refs):
    pairs = len(refs) - len(parts)
    for part, out in zip(parts, refs[pairs:]):
        at = 0
        for i, low, high in part:
            left, right = refs[2 * i], refs[2 * i + 1]
            out[:, at : at + high - low] = dot(left[...], right[:, low:high], 0, 0).astype(out.dtype)
            at += high - low


def products(pairs, *parts):
    tokens, width = pairs[0][0].shape
    tile = min(512, width)
    specs = []
    for left, right in pairs:
        specs.append(pl.BlockSpec((tokens, tile), lambda i: (0, i)))
        specs.append(pl.BlockSpec(right.shape, lambda i: (0, 0)))
    totals = [sum(high - low for i, low, high in part) for part in parts]
    return pl.pallas_call(
        partial(products_kernel, parts),
        name="products",
        grid=(width // tile,),
        out_shape=tuple(jax.ShapeDtypeStruct((width, total), jnp.bfloat16) for total in totals),
        in_specs=specs,
        out_specs=tuple(pl.BlockSpec((tile, total), lambda i: (i, 0)) for total in totals),
        compiler_params=pltpu.CompilerParams(vmem_limit_bytes=40 << 20),
        cost_estimate=cost(10),
    )(*[array for pair in pairs for array in pair])


def unpack_kernel(
    sh, ph, ff, mixer, misc, small, kv, home_out, home_grad,
    output, gradient, mixer_gain, mamba_gate, mamba_input, state, step, conv_k, conv_b, state_k, state_b,
    step_bias, decay, skip, mamba_out, query, key, value, attn_out, ff_gain, gate, up, down, sems,
):
    c = lax.axis_index("col")
    f32 = jnp.float32
    copies = [
        pltpu.make_async_copy(home_out, output, sems.at[0]),
        pltpu.make_async_copy(home_grad, gradient, sems.at[1]),
    ]
    for copy in copies:
        copy.start()
    mh = mamba_gate.shape[1] // TP
    fh = gate.shape[1] // TP
    qh = query.shape[1] // TP
    kvh = key.shape[1]
    at = 2 * mh + qh
    out = mixer.shape[2] - mh - qh
    for m in range(TP):
        def cols(size):
            return slice(m * size, (m + 1) * size)

        gate[:, cols(fh)] = ff[m, :, :fh].astype(f32)
        up[:, cols(fh)] = ff[m, :, fh : 2 * fh].astype(f32)
        down[cols(fh), :] = ff[m, :, 2 * fh :].astype(f32).T
        mamba_gate[:, cols(mh)] = mixer[m, :, :mh].astype(f32)
        mamba_input[:, cols(mh)] = mixer[m, :, mh : 2 * mh].astype(f32)
        query[:, cols(qh)] = mixer[m, :, 2 * mh : at].astype(f32)
        mamba_out[cols(mh), :] = mixer[m, :, out : out + mh].astype(f32).T
        attn_out[cols(qh), :] = mixer[m, :, out + mh :].astype(f32).T
    key[...] = kv[:, :kvh]
    value[...] = kv[:, kvh:]

    mine = [mixer[m, :, at : at + 128].astype(f32) for m in range(TP)]
    other = [misc[m].astype(f32) for m in range(TP)]
    by_col = [
        [jnp.where(c == col, mine[m], other[m]) for m in range(TP)] for col in range(2)
    ]
    state[...] = jnp.concatenate(
        [
            by_col[col][m][:, part * sh : (part + 1) * sh]
            for part in range(2)
            for col in range(2)
            for m in range(TP)
        ],
        axis=1,
    )
    step[...] = jnp.concatenate([part[:, 2 * sh : 2 * sh + ph] for part in mine], axis=1)

    lanes = mh // 128
    channels = [
        jnp.concatenate(
            [
                small[2 * m + c, i * lanes + k : i * lanes + k + 1, :]
                for m in range(TP)
                for k in range(lanes)
            ],
            axis=1,
        )
        for i in range(6)
    ]
    for i in range(4):
        conv_k[i : i + 1, :] = channels[i]
    conv_b[...] = channels[4][0]
    per_head = mh // ph
    shape = (TP * mh, TP * ph)
    heads = lax.broadcasted_iota(jnp.int32, shape, 1) * per_head
    channel = lax.broadcasted_iota(jnp.int32, shape, 0)
    picks = ((channel >= heads) & (channel < heads + per_head)).astype(f32)
    skip[...] = dot(jnp.broadcast_to(channels[5], (8, TP * mh)), picks, 1, 0, HIGH)[:1, :]
    start = 8 * lanes
    sides = [[small[2 * m + col, start : start + 8, :] for m in range(TP)] for col in range(2)]
    states = jnp.concatenate(
        [
            sides[col][m][:, part * sh : (part + 1) * sh]
            for part in range(2)
            for col in range(2)
            for m in range(TP)
        ],
        axis=1,
    )
    state_k[...] = states[:4, :]
    state_b[...] = states[4]
    own_heads = jnp.concatenate(
        [jnp.where(c == 0, sides[0][m], sides[1][m])[:, 2 * sh : 2 * sh + ph] for m in range(TP)], axis=1
    )
    step_bias[...] = own_heads[5:6, :]
    decay[...] = own_heads[6:7, :]
    start = start + 8
    for gain in (ff_gain, mixer_gain):
        count = gain.shape[0] // 128
        total = sum(small[i, start : start + count, :] for i in range(GROUP))
        for k in range(count):
            gain[k * 128 : (k + 1) * 128] = total[k]
        start = start + count
    for copy in copies:
        copy.wait()


def unpack(ff, mixer, misc, small, kv, output, gradient, mh, qh, fh, sh, ph):
    rows, width = ff.shape[1], output.shape[2]
    kvh = kv.shape[1] // 2
    vm, hb = pl.BlockSpec(memory_space=VMEM), pl.BlockSpec(memory_space=ANY)
    f32 = jnp.float32
    shapes = [
        (width,),
        (rows, TP * mh),
        (rows, TP * mh),
        (rows, 2 * GROUP * sh),
        (rows, TP * ph),
        (4, TP * mh),
        (TP * mh,),
        (4, 2 * GROUP * sh),
        (2 * GROUP * sh,),
        (1, TP * ph),
        (1, TP * ph),
        (1, TP * ph),
        (TP * mh, rows),
        (rows, TP * qh),
        (rows, kvh),
        (rows, kvh),
        (TP * qh, rows),
        (width,),
        (rows, TP * fh),
        (rows, TP * fh),
        (TP * fh, rows),
    ]
    return pl.pallas_call(
        partial(unpack_kernel, sh, ph),
        name="unpack",
        out_shape=tuple(jax.ShapeDtypeStruct(a.shape, a.dtype) for a in (output, gradient))
        + tuple(jax.ShapeDtypeStruct(shape, f32) for shape in shapes),
        in_specs=[vm] * 5 + [hb] * 2,
        out_specs=(hb,) * 2 + (vm,) * len(shapes),
        scratch_shapes=[pltpu.SemaphoreType.DMA((2,))],
        compiler_params=pltpu.CompilerParams(vmem_limit_bytes=40 << 20),
        cost_estimate=cost(8),
    )(ff, mixer, misc, small, kv, output, gradient)


def send_home(parts, x, d_mid, ff_parts, mid, gain, take, small, kv_parts, ff_sums, n_row):
    slots, width = x.shape
    bf = jnp.bfloat16
    size = sum(part.size for part in small) // 128 + width // 128
    phases = len(data_bits(n_row, MIX))
    return pl.pallas_call(
        home_kernel,
        name="home",
        out_shape=(
            jax.ShapeDtypeStruct((n_row, CHUNK, width), bf),
            jax.ShapeDtypeStruct((GROUP, size, 128), jnp.float32),
            jax.ShapeDtypeStruct(kv_parts.shape[2:], jnp.float32),
            jax.ShapeDtypeStruct(ff_sums.shape, bf),
        ),
        in_specs=[pl.BlockSpec(memory_space=VMEM)] * 11 + [pl.BlockSpec(memory_space=ANY)],
        out_specs=(
            pl.BlockSpec(memory_space=VMEM),
            pl.BlockSpec(memory_space=ANY),
            pl.BlockSpec(memory_space=VMEM),
            pl.BlockSpec(memory_space=ANY),
        ),
        scratch_shapes=scatter_scratch(slots, width)
        + [
            VMEM((slots, width), jnp.float32),
            VMEM((slots, width), bf),
            VMEM((slots, width), bf),
            VMEM((1, width), jnp.float32),
            VMEM((phases + 1, size, 128), jnp.float32),
            VMEM((phases, size, 128), jnp.float32),
            pltpu.SemaphoreType.DMA((phases,)),
            pltpu.SemaphoreType.DMA((phases,)),
        ]
        + gather_scratch()
        + deliver_scratch()
        + [
            VMEM((TP, kv_parts.shape[0]) + kv_parts.shape[2:], bf),
            VMEM((kv_parts.shape[0],) + kv_parts.shape[2:], bf),
            VMEM((kv_parts.shape[0],) + kv_parts.shape[2:], bf),
            pltpu.SemaphoreType.DMA((TP,)),
            pltpu.SemaphoreType.DMA((TP,)),
            pltpu.SemaphoreType.DMA((kv_parts.shape[0],)),
            pltpu.SemaphoreType.DMA((kv_parts.shape[0],)),
            VMEM((slots, width), jnp.float32),
        ]
        + scatter_scratch(slots, width),
        compiler_params=params(3, 48),
        cost_estimate=cost(75),
    )(parts, x, d_mid, ff_parts, mid, gain, take, *small, kv_parts, ff_sums)


def blocks_start(low, land, s1, r1):
    r, c = place()
    copies = []
    for m, f in CROSSED:
        col = 1 - c if f else c
        k = m * 2 + f
        copies.append(
            remote(low.at[block_of(m, MIX) + col], land.at[k], s1.at[k], r1.at[k], partner(r, m, MIX), col)
        )
        copies[-1].start()
    return copies


def blocks_turn(first, low, land, mine, total, s2, r2, here):
    r, c = place()
    own = member(r, MIX) * 2 + c
    for copy in first:
        copy.wait_recv()
    summed = low[own].astype(jnp.float32)
    for m, f in CROSSED:
        summed = summed + land[m * 2 + f].astype(jnp.float32)
    mine[...] = summed.astype(jnp.bfloat16)
    copies = [pltpu.make_async_copy(mine, total.at[own], here)]
    for m, f in CROSSED:
        k = m * 2 + f
        copies.append(
            remote(mine, total.at[own], s2.at[k], r2.at[k], partner(r, m, MIX), 1 - c if f else c)
        )
    for copy in copies:
        copy.start()
    return copies


def blocks_finish(first, second):
    for copy in first:
        copy.wait_send()
    for copy in second:
        copy.wait()


CROSSED = [(m, f) for m in (3, 1, 2) for f in (0, 1)] + [(0, 1)]


def blocks_scratch(slots):
    dma = pltpu.SemaphoreType.DMA
    return [
        VMEM((GROUP, slots, slots), jnp.bfloat16),
        VMEM((GROUP, slots, slots), jnp.bfloat16),
        VMEM((slots, slots), jnp.bfloat16),
        dma((GROUP,)),
        dma((GROUP,)),
        dma((GROUP,)),
        dma((GROUP,)),
        dma,
    ]


def dot(first_op, second_op, first_dim, second_dim, precision=None):
    return lax.dot_general(
        first_op,
        second_op,
        (((first_dim,), (second_dim,)), ((), ())),
        precision=precision,
        preferred_element_type=jnp.float32,
    )


def block_rows(b, slots):
    return pl.ds(pl.multiple_of(b * slots, slots), slots)


def marks(lens, b, slots):
    row = lax.broadcasted_iota(jnp.int32, (slots, slots), 0)
    col = lax.broadcasted_iota(jnp.int32, (slots, slots), 1)
    row_segment, col_segment, within = jnp.zeros_like(row), jnp.zeros_like(row), row
    end = 0
    for k in range(lens.shape[1] - 1):
        end = end + lens[b, k]
        row_segment = row_segment + (row >= end).astype(jnp.int32)
        col_segment = col_segment + (col >= end).astype(jnp.int32)
        within = jnp.where(row >= end, row - end, within)
    return (row_segment == col_segment) & (row >= col), within


def conv_pre(values, within, weights):
    width = values.shape[1]
    shifted = [values]
    for k in range(1, 4):
        valid = within[:, :1] >= k
        shifted.append(jnp.where(valid, pltpu.roll(values, k, 0), 0.0))
    pre = weights[4:5, :]
    for k in range(4):
        pre = pre + weights[3 - k : 4 - k, :] * shifted[k]
    return pre, shifted


def conv_back(grad, pre, shifted, within, weights):
    slots = grad.shape[0]
    gate = jax.nn.sigmoid(pre)
    e = grad * gate * (1.0 + pre * (1.0 - gate))
    sums = [jnp.sum(e * shifted[3 - i], axis=0, keepdims=True) for i in range(4)]
    sums.append(jnp.sum(e, axis=0, keepdims=True))
    back = weights[3:4, :] * e
    for k in range(1, 4):
        valid = within[:, :1] >= k
        back = back + weights[3 - k : 4 - k, :] * pltpu.roll(jnp.where(valid, e, 0.0), slots - k, 0)
    return back, sums


def softplus(values):
    return jnp.maximum(values, 0.0) + jnp.log1p(jnp.exp(-jnp.abs(values)))


def steps_and_levels(mixed, side, low, count):
    slots, width = mixed.shape
    lane = lax.broadcasted_iota(jnp.int32, (slots, width), 1)
    inside = (lane >= low) & (lane < low + count)
    step = jnp.where(inside, softplus(mixed + side[5:6, :]), 0.0)
    rate = jnp.where(inside, -jnp.exp(side[6:7, :]), 0.0)
    row = lax.broadcasted_iota(jnp.int32, (slots, slots), 0)
    col = lax.broadcasted_iota(jnp.int32, (slots, slots), 1)
    tri = (row >= col).astype(jnp.float32)
    level = dot(tri, step * rate, 1, 0, HIGH)
    return step, rate, level, tri, inside


def halves(first, second):
    lane = lax.broadcasted_iota(jnp.int32, first.shape, 1)
    return jnp.where(lane < first.shape[1] // 2, first, second)


def state_parts(mixed, within, side, sh):
    pre, shifted = conv_pre(mixed, within, side)
    act = pre * jax.nn.sigmoid(pre)
    lane = lax.broadcasted_iota(jnp.int32, act.shape, 1)
    first = jnp.where(lane < sh, act, 0.0).astype(jnp.bfloat16)
    second = jnp.where(lane < sh, pltpu.roll(act, act.shape[1] - sh, 1), 0.0).astype(jnp.bfloat16)
    return first, second, pre, shifted


def turned_pair(values, waves):
    half = values.shape[1] // 2
    return values * waves[:, : 2 * half] + pltpu.roll(values, half, 1) * waves[:, 2 * half :]


def turned_back(values, waves):
    half = values.shape[1] // 2
    return values * waves[:, : 2 * half] - pltpu.roll(values, half, 1) * waves[:, 2 * half :]


def wave_rows(within, table):
    slots = within.shape[0]
    picks = (within == lax.broadcasted_iota(jnp.int32, (slots, slots), 1)).astype(jnp.float32)
    return dot(picks, table[...], 1, 0, HIGH)


def attend(projected, rows, at, lens, table, b, slots):
    allowed, within = marks(lens, b, slots)
    waves = wave_rows(within, table)
    query = turned_pair(projected[rows, at : at + HD], waves).astype(jnp.bfloat16)
    key = turned_pair(projected[rows, at + HD : at + 2 * HD], waves).astype(jnp.bfloat16)
    value = projected[rows, at + 2 * HD : at + 3 * HD].astype(jnp.bfloat16)
    scores = jnp.where(allowed, dot(query, key, 1, 1) * HD ** (-0.5), NEG_LARGE)
    exps = jnp.exp(scores - jnp.max(scores, axis=-1, keepdims=True))
    probs = exps / jnp.sum(exps, axis=-1, keepdims=True)
    return query, key, value, probs, waves


def each_block(first, last, body):
    def step(b, carry):
        body(b)
        return carry

    lax.fori_loop(first, last, step, 0)


def mixer_kernel(
    sh, ph, lens, projected, chan, side, table, branch, scanned, crossed,
    low, land, mine, s1, r1, s2, r2, here, conv,
):
    slots = crossed.shape[1]
    mh = chan.shape[1]
    heads_at = 2 * sh
    greet(MIX, cross=True)

    def before(b):
        rows = block_rows(b, slots)
        allowed, within = marks(lens, b, slots)
        pre, unused = conv_pre(projected[rows, mh : 2 * mh], within, chan)
        conv[rows, :] = pre * jax.nn.sigmoid(pre)
        mixed = projected[rows, 2 * mh + 3 * HD :]
        first, second, unused, unused = state_parts(mixed, within, side, sh)
        low[b] = dot(second, first, 1, 1).astype(jnp.bfloat16)

    def attention(b):
        rows = block_rows(b, slots)
        query, key, value, probs, waves = attend(projected, rows, 2 * mh, lens, table, b, slots)
        branch[rows, mh:] = dot(probs.astype(jnp.bfloat16), value, 1, 0).astype(jnp.bfloat16)

    def after(b):
        rows = block_rows(b, slots)
        allowed, within = marks(lens, b, slots)
        mixed = projected[rows, 2 * mh + 3 * HD :]
        step, rate, level, tri, inside = steps_and_levels(mixed, side, heads_at, ph)
        step_t, level_t = step.T, level.T
        cross = crossed[b].astype(jnp.float32)
        for pair in range(ph // 2):
            cols = slice(pair * 128, (pair + 1) * 128)
            convs = conv[rows, cols]
            conv_low = convs.astype(jnp.bfloat16)
            outs = []
            for h in (2 * pair, 2 * pair + 1):
                at = heads_at + h
                spread = level[:, at : at + 1] - level_t[at : at + 1, :]
                decay = jnp.exp(jnp.where(allowed, spread, NEG_LARGE))
                mixing = cross * decay * step_t[at : at + 1, :]
                outs.append(dot(mixing.astype(jnp.bfloat16), conv_low, 1, 0))
            total = halves(outs[0], outs[1])
            scanned[rows, cols] = total
            gate = projected[rows, cols]
            gated = (total + chan[5:6, cols] * convs) * (gate * jax.nn.sigmoid(gate))
            branch[rows, cols] = gated.astype(jnp.bfloat16)

    each_block(0, GROUP, before)
    first = blocks_start(low, land, s1, r1)
    each_block(0, GROUP // 2, attention)
    second = blocks_turn(first, low, land, mine, crossed, s2, r2, here)
    each_block(GROUP // 2, GROUP, attention)
    blocks_finish(first, second)
    each_block(0, GROUP, after)


def mixer(lens, projected, chan, side, table, sh, ph):
    tokens = projected.shape[0]
    slots = tokens // GROUP
    mh = chan.shape[1]
    vm = pl.BlockSpec(memory_space=VMEM)
    return pl.pallas_call(
        partial(mixer_kernel, sh, ph),
        name="mixer",
        out_shape=(
            jax.ShapeDtypeStruct((tokens, mh + HD), jnp.bfloat16),
            jax.ShapeDtypeStruct((tokens, mh), jnp.float32),
            jax.ShapeDtypeStruct((GROUP, slots, slots), jnp.bfloat16),
        ),
        in_specs=[pl.BlockSpec(memory_space=pltpu.SMEM)] + [vm] * 4,
        out_specs=(vm,) * 3,
        scratch_shapes=blocks_scratch(slots) + [VMEM((tokens, mh), jnp.float32)],
        compiler_params=params(4, 40),
        cost_estimate=cost(30),
    )(lens, projected, chan, side, table)


def mixer_back_kernel(
    sh, ph, lens, projected, chan, side, table, scanned, crossed, grads,
    out, chan_sums, side_sums,
    low, land, mine, s1, r1, s2, r2, here, summed, misc,
):
    slots = crossed.shape[1]
    mh = chan.shape[1]
    heads_at = 2 * sh
    bf = jnp.bfloat16
    greet(MIX, cross=True)
    chan_sums[...] = jnp.zeros_like(chan_sums)
    side_sums[...] = jnp.zeros_like(side_sums)

    def scan(b):
        rows = block_rows(b, slots)
        allowed, within = marks(lens, b, slots)
        mixed = projected[rows, 2 * mh + 3 * HD :]
        step, rate, level, tri, inside = steps_and_levels(mixed, side, heads_at, ph)
        step_t, level_t = step.T, level.T
        cross = crossed[b].astype(jnp.float32)
        lane = lax.broadcasted_iota(jnp.int32, (slots, 128), 1)
        place_row = lax.broadcasted_iota(jnp.int32, (slots, slots), 0)
        grad_cross = jnp.zeros((slots, slots), jnp.float32)
        row_sums = jnp.zeros((slots, slots), jnp.float32)
        col_sums = jnp.zeros((slots, slots), jnp.float32)
        for pair in range(ph // 2):
            cols = slice(pair * 128, (pair + 1) * 128)
            weights = chan[:, cols]
            pre, shifted = conv_pre(
                projected[rows, mh + pair * 128 : mh + (pair + 1) * 128], within, weights
            )
            convs = pre * jax.nn.sigmoid(pre)
            conv_low = convs.astype(bf)
            gate = projected[rows, cols]
            sig = jax.nn.sigmoid(gate)
            grad = grads[rows, cols]
            skip = weights[5:6, :]
            grad_mix = grad * (gate * sig)
            out[rows, cols] = (
                grad * (scanned[rows, cols] + skip * convs) * (sig * (1.0 + gate * (1.0 - sig)))
            ).astype(bf)
            skip_sum = jnp.sum(grad_mix * convs, axis=0, keepdims=True)
            grad_low = grad_mix.astype(bf)
            backs = []
            for f in (0, 1):
                at = heads_at + 2 * pair + f
                mask = lane < 64 if f == 0 else lane >= 64
                spread = level[:, at : at + 1] - level_t[at : at + 1, :]
                decay = jnp.exp(jnp.where(allowed, spread, NEG_LARGE))
                step_row = step_t[at : at + 1, :]
                mixing = cross * decay * step_row
                backs.append(dot(mixing.astype(bf), grad_low, 0, 0))
                grad_mixing = dot(jnp.where(mask, grad_mix, 0.0).astype(bf), conv_low, 1, 1)
                weighted = grad_mixing * decay
                grad_cross = grad_cross + weighted * step_row
                weighted = weighted * cross
                col = jnp.sum(weighted, axis=0, keepdims=True)
                row = jnp.sum(weighted * step_row, axis=1, keepdims=True)
                row_sums = jnp.where(lane == at, row, row_sums)
                col_sums = jnp.where(place_row == at, col, col_sums)
            grad_conv = grad_mix * skip + halves(backs[0], backs[1])
            back, sums = conv_back(grad_conv, pre, shifted, within, weights)
            out[rows, mh + pair * 128 : mh + (pair + 1) * 128] = back.astype(bf)
            for i, part in enumerate(sums + [skip_sum]):
                chan_sums[i : i + 1, cols] += part
        low[b] = grad_cross.astype(bf)
        col_sums = col_sums.T
        grad_level = row_sums - step * col_sums
        grad_rate_step = dot(tri, grad_level, 0, 0, HIGH)
        grad_step = (col_sums + grad_rate_step * rate) * jax.nn.sigmoid(mixed + side[5:6, :])
        grad_step = jnp.where(inside, grad_step, 0.0)
        misc[rows, :] = grad_step
        side_sums[5:6, :] += jnp.sum(grad_step, axis=0, keepdims=True)
        side_sums[6:7, :] += jnp.sum(grad_rate_step * step, axis=0, keepdims=True) * rate[:1, :]

    def attention(b):
        rows = block_rows(b, slots)
        at = 2 * mh
        query, key, value, probs, waves = attend(projected, rows, at, lens, table, b, slots)
        grad = grads[rows, mh:].astype(bf)
        grad_probs = dot(grad, value, 1, 1)
        out[rows, at + 2 * HD : at + 3 * HD] = dot(probs.astype(bf), grad, 0, 0).astype(bf)
        grad_raw = probs * (grad_probs - jnp.sum(grad_probs * probs, axis=-1, keepdims=True))
        grad_raw = (grad_raw * HD ** (-0.5)).astype(bf)
        out[rows, at : at + HD] = turned_back(dot(grad_raw, key, 1, 0), waves).astype(bf)
        out[rows, at + HD : at + 2 * HD] = turned_back(dot(grad_raw, query, 0, 0), waves).astype(bf)

    def state(b):
        rows = block_rows(b, slots)
        allowed, within = marks(lens, b, slots)
        mixed = projected[rows, 2 * mh + 3 * HD :]
        first, second, pre, shifted = state_parts(mixed, within, side, sh)
        lane = lax.broadcasted_iota(jnp.int32, pre.shape, 1)
        grad_first = dot(summed[b], second, 0, 0)
        grad_second = pltpu.roll(dot(summed[b], first, 1, 0), sh, 1)
        grad = jnp.where(lane < sh, grad_first, jnp.where(lane < 2 * sh, grad_second, 0.0))
        back, sums = conv_back(grad, pre, shifted, within, side)
        out[rows, 2 * mh + 3 * HD :] = jnp.where(lane < 2 * sh, back, misc[rows, :]).astype(bf)
        for i, part in enumerate(sums):
            side_sums[i : i + 1, :] += part

    each_block(0, GROUP, scan)
    begun = blocks_start(low, land, s1, r1)
    each_block(0, GROUP // 2, attention)
    done = blocks_turn(begun, low, land, mine, summed, s2, r2, here)
    each_block(GROUP // 2, GROUP, attention)
    blocks_finish(begun, done)
    each_block(0, GROUP, state)


def mixer_back(lens, projected, chan, side, table, scanned, crossed, grads, sh, ph):
    tokens = projected.shape[0]
    slots = tokens // GROUP
    mh = chan.shape[1]
    vm = pl.BlockSpec(memory_space=VMEM)
    return pl.pallas_call(
        partial(mixer_back_kernel, sh, ph),
        name="mixer_back",
        out_shape=(
            jax.ShapeDtypeStruct(projected.shape, jnp.bfloat16),
            jax.ShapeDtypeStruct(chan.shape, jnp.float32),
            jax.ShapeDtypeStruct(side.shape, jnp.float32),
        ),
        in_specs=[pl.BlockSpec(memory_space=pltpu.SMEM)] + [vm] * 7,
        out_specs=(vm,) * 3,
        scratch_shapes=blocks_scratch(slots)
        + [
            VMEM((GROUP, slots, slots), jnp.bfloat16),
            VMEM((tokens, 128), jnp.float32),
        ],
        compiler_params=params(5, 48),
        cost_estimate=cost(50),
    )(lens, projected, chan, side, table, scanned, crossed, grads)


def swiglu(ff_gate, ff_up):
    return jax.nn.silu(ff_gate) * ff_up


def cut(array, parts, axis=1):
    rows, cols = array.shape
    return array.reshape(rows, parts, cols // parts).transpose(1, 0, 2)


def local(
    tokens,
    cotangent,
    deal_order,
    seq_lengths,
    mixer_norm_gain,
    mamba_gate_weight,
    mamba_input_weight,
    state_weight,
    step_weight,
    conv_input,
    conv_input_bias,
    conv_state,
    conv_state_bias,
    step_bias,
    decay_log,
    skip_scale,
    mamba_out_weight,
    query_weight,
    key_weight,
    value_weight,
    attn_out_weight,
    ff_norm_gain,
    gate_weight,
    up_weight,
    down_weight,
):
    n_row = lax.axis_size("row")
    r = lax.axis_index("row")
    c = lax.axis_index("col")
    t = member(r, MIX)
    n_bits = n_row.bit_length() - 1
    slots, width = tokens.shape[1:]
    bf = jnp.bfloat16
    rows = mamba_gate_weight.shape[0]
    mh = mamba_gate_weight.shape[1] // TP
    qh = query_weight.shape[1] // TP
    kvh = key_weight.shape[1]
    sh = state_weight.shape[1] // (2 * GROUP)
    ph = step_weight.shape[1] // TP
    fh = gate_weight.shape[1] // TP
    used = 2 * mh + qh + 2 * kvh + 2 * sh + ph
    spare = -used % 256

    half = state_weight.shape[1] // 2
    def assemble(slab, after):
        held = [(0, slab)]
        for b in data_bits(n_row, FFN):
            next_held = []
            for mask, part in held:
                if mask:
                    part, unused_value = lax.optimization_barrier((part, after))
                next_held.append((mask | 1 << b, lax.ppermute(part, "row", flips(n_row, 1 << b))))
            held = held + next_held
        return place_slabs(
            [mask for mask, part in held], [part for mask, part in held], n_row
        ).reshape(n_row * rows, slab.shape[2])

    def pick(array, index, axis=0):
        return lax.dynamic_index_in_dim(array, index, axis, keepdims=False)

    def sum_groups(grad, axes, after=None):
        grad = grad.astype(bf)
        bits = data_bits(n_row, axes)
        order = [n_bits - 1 - b for b in bits + [axes[1], axes[0]]]
        if order != sorted(order):
            cutup = grad.reshape((2,) * n_bits + (rows, grad.shape[1]))
            grad = cutup.transpose(order + [n_bits, n_bits + 1]).reshape(grad.shape)
        if after is not None:
            grad, after = lax.optimization_barrier((grad, after))
        by_group = sorted(range(n_row), key=lambda row: [row >> b & 1 for b in bits])
        alike = [
            [row for row in by_group if [row >> b & 1 for b in axes] == [m & 1, m >> 1]]
            for m in range(TP)
        ]
        part = lax.psum_scatter(
            grad, "row", scatter_dimension=0, axis_index_groups=alike, tiled=True
        ).reshape(TP, rows, grad.shape[1])
        return part, after

    meta_all, give, take, x_home, gy_home, normed_one, gy_all, w_mixer, slab_up, slab_down = deal(
        deal_order,
        seq_lengths,
        tokens,
        cotangent,
        mixer_norm_gain[None, :],
        (key_weight, value_weight),
        (mamba_gate_weight, mamba_input_weight, query_weight),
        (state_weight, step_weight, mamba_out_weight, attn_out_weight),
        (gate_weight, up_weight, down_weight),
        2 * sh + ph + spare,
        n_row,
    )
    normed_one = normed_one.reshape(GROUP * slots, width)
    gy_all = gy_all.reshape(GROUP * slots, width)
    w_mixer = w_mixer.reshape(width, -1)
    w_in, w_out = w_mixer[:, : used + spare], w_mixer[:, used + spare :]

    base = r - sum(bit(r, b) * (1 << b) for b in MIX)
    group_meta = jnp.stack([pick(meta_all, base + mask_of(m, MIX)) for m in range(TP)])
    lengths = group_meta[:, 2:4, : seq_lengths.shape[2]].reshape(GROUP, seq_lengths.shape[2])
    half_dim = HD // 2
    inverse = ROPE_BASE ** (-2.0 * jnp.arange(half_dim, dtype=jnp.float32) / HD)
    angles = jnp.arange(slots, dtype=jnp.float32)[:, None] * inverse[None, :]
    cosine, sine = jnp.cos(angles), jnp.sin(angles)
    table = jnp.concatenate([cosine, cosine, -sine, sine], axis=1)

    def piece(array, size, start):
        return lax.dynamic_slice_in_dim(array, start, size, array.ndim - 1)

    eighth = c * TP + t
    chan = jnp.concatenate(
        [
            piece(conv_input, mh, t * mh),
            piece(conv_input_bias[None], mh, t * mh),
            jnp.repeat(piece(skip_scale[None], ph, t * ph), mh // ph, axis=1),
            jnp.zeros((2, mh), jnp.float32),
        ],
        axis=0,
    )
    states = jnp.concatenate([conv_state, conv_state_bias[None]], axis=0)
    states = jnp.concatenate(
        [piece(states, sh, eighth * sh), piece(states, sh, half + eighth * sh)], axis=1
    )
    heads = jnp.concatenate(
        [piece(step_bias[None], ph, t * ph), piece(decay_log[None], ph, t * ph)], axis=0
    )
    after = 128 - 2 * sh - ph
    side = jnp.concatenate(
        [
            jnp.pad(states, ((0, 0), (0, 128 - 2 * sh))),
            jnp.pad(heads, ((0, 0), (2 * sh, after))),
            jnp.zeros((1, 128), jnp.float32),
        ],
        axis=0,
    )

    projected = matmul(normed_one, w_in)
    edges = [0, mh, 2 * mh, 2 * mh + qh, 2 * mh + qh + kvh, 2 * mh + qh + 2 * kvh]
    edges = edges + [edges[-1] + 2 * sh, edges[-1] + 2 * sh + ph]
    branch_in, scanned, crossed = mixer(lengths, projected, chan, side, table, sh, ph)
    branch_part = matmul_trans(branch_in, w_out).astype(bf).reshape(GROUP, slots, width)
    ff_gain = ff_norm_gain[None, :]
    mid, normed_two, w_down = middle(branch_part, x_home, ff_gain, slab_down, n_row)
    normed_two = normed_two.reshape(GROUP * slots, width)
    w_gate_up = assemble(slab_up, branch_part)
    w_down = w_down.reshape(n_row * rows, -1)

    ff_gate_up = matmul(normed_two, w_gate_up)
    ff_gate, ff_up = ff_gate_up[:, :fh], ff_gate_up[:, fh:]
    ff_hidden = swiglu(ff_gate, ff_up).astype(bf)
    grad_hidden = matmul(gy_all, w_down)
    unused_value, pullback = jax.vjp(swiglu, ff_gate, ff_up)
    grad_gate, grad_up = pullback(grad_hidden)
    grad_gate_up = jnp.concatenate([grad_gate.astype(bf), grad_up.astype(bf)], axis=1)
    (grad_ff,) = products(
        [(normed_two, grad_gate_up), (gy_all, ff_hidden)], [(0, 0, 2 * fh), (1, 0, fh)]
    )
    grad_gate_up, grad_ff = lax.optimization_barrier((grad_gate_up, grad_ff))
    ff_sums, unused_value = sum_groups(grad_ff, FFN)
    normed_two_part = (
        matmul_trans(grad_gate_up, w_gate_up).astype(bf).reshape(GROUP, slots, width)
    )
    d_mid, delta_ff_gain, branch_all = turn(
        normed_two_part, mid, gy_home, ff_gain
    )
    branch_all = branch_all.reshape(GROUP * slots, width)

    grad_branch_in = matmul(branch_all, w_out)
    grad_projected, chan_sums, side_sums = mixer_back(
        lengths, projected, chan, side, table, scanned, crossed, grad_branch_in, sh, ph
    )
    grad_mixer, grad_kv = products(
        [(normed_one, grad_projected), (branch_all, branch_in)],
        [(0, 0, edges[3]), (0, edges[5], used + spare), (1, 0, mh + qh)],
        [(0, edges[3], edges[5])],
    )
    grad_projected, grad_mixer, ff_hidden = lax.optimization_barrier(
        (grad_projected, grad_mixer, ff_hidden)
    )
    ff_part = matmul_trans(ff_hidden, w_down).astype(bf).reshape(GROUP, slots, width)
    mixer_sums, unused_value = sum_groups(grad_mixer, MIX)
    normed_one_part = matmul_trans(grad_projected, w_in).astype(bf).reshape(GROUP, slots, width)

    buf, small_all, delta_kv, ff_land = send_home(
        normed_one_part, x_home, d_mid, ff_part, mid, mixer_norm_gain[None, :], take,
        (chan_sums, side_sums, delta_ff_gain),
        grad_kv.reshape(n_row // TP, TP, rows, 2 * kvh), ff_sums, n_row,
    )
    output, grad_tokens, mixer_land, other_land = last(buf, give, mixer_sums, edges[3])
    results = unpack(
        ff_land, mixer_land, other_land, small_all, delta_kv, output, grad_tokens, mh, qh, fh, sh, ph
    )
    flat = (11, 12, 13)
    return tuple(
        array.reshape(array.shape[1]) if i in flat else array for i, array in enumerate(results)
    )


def solution(mesh):
    both = P("row", "col")
    turned = P("col", "row")
    in_specs = (
        P(None, "row", None),
        P(None, "row", None),
        P(None, "row"),
        P(None, "row", None),
        P(),
        both,
        both,
        P("row", None),
        both,
        P(None, "col"),
        P("col"),
        P(),
        P(),
        P("col"),
        P("col"),
        P("col"),
        turned,
        both,
        both,
        both,
        turned,
        P(),
        both,
        both,
        turned,
    )
    out_specs = (
        P(None, "row", None),
        P(None, "row", None),
        P(),
        both,
        both,
        P("row", None),
        both,
        P(None, "col"),
        P("col"),
        P(),
        P(),
        P("col"),
        P("col"),
        P("col"),
        turned,
        both,
        both,
        both,
        turned,
        P(),
        both,
        both,
        turned,
    )
    return jax.shard_map(local, mesh=mesh, in_specs=in_specs, out_specs=out_specs, check_vma=False)
```
